32 devices in a mesh: item: 8 (over z, x), seq: 4 (over y, core).
Axes of the slice: x: 2, y: 2, z: 4, core: 2. Of those that a mesh axis runs over, the one named last changes fastest.
Arguments:
- inputs: bfloat16 [8, 3072, 768], P('item', 'seq'), may hold values from -6 to 6
- d_output: bfloat16 [8, 3072, 768], P('item', 'seq'), may hold values from -6 to 6
- glob_count: int32 [8], P('item'), may hold values from 2 to 4
- glob_pos: int32 [8, 4], P('item'), may hold values from 0 to 47, as said below
- rand_blocks: int32 [8, 12, 48, 3], P('item', 'seq'), may hold values from 0 to 47
- w_qkv: float32 [768, 2304], P('item'), may hold values from -0.21875 to 0.21875
- w_out: float32 [768, 768], P('item'), may hold values from -0.875 to 0.875
- w_up: float32 [768, 3072], P('item'), may hold values from -0.21875 to 0.21875
- w_down: float32 [3072, 768], P('item'), may hold values from -0.109375 to 0.109375
- small_params: float32 [12, 768], replicated
- first_qkv: float32 [768, 2304], P('item'), may hold values from -0.00024414062 to 0.00024414062
- second_qkv: float32 [768, 2304], P('item'), may hold values from 1.4110135e-10 to 5.644054e-10
- first_out: float32 [768, 768], P('item'), may hold values from -0.00024414062 to 0.00024414062
- second_out: float32 [768, 768], P('item'), may hold values from 1.4110135e-10 to 5.644054e-10
- first_up: float32 [768, 3072], P('item'), may hold values from -0.00024414062 to 0.00024414062
- second_up: float32 [768, 3072], P('item'), may hold values from 1.4110135e-10 to 5.644054e-10
- first_down: float32 [3072, 768], P('item'), may hold values from -0.00024414062 to 0.00024414062
- second_down: float32 [3072, 768], P('item'), may hold values from 1.4110135e-10 to 5.644054e-10
- first_small: float32 [12, 768], replicated, may hold values from -0.0007324219 to 0.0007324219
- second_small: float32 [12, 768], replicated, may hold values from 1.2699122e-09 to 5.0796487e-09
Outputs:
- outputs: bfloat16 [8, 3072, 768], P('item', 'seq')
- d_inputs: float32 [8, 3072, 768], P('item', 'seq')
- grad_norm: float32 [], replicated
- new_w_qkv: float32 [768, 2304], P('item')
- new_first_qkv: float32 [768, 2304], P('item')
- new_second_qkv: float32 [768, 2304], P('item')
- new_w_out: float32 [768, 768], P('item')
- new_first_out: float32 [768, 768], P('item')
- new_second_out: float32 [768, 768], P('item')
- new_w_up: float32 [768, 3072], P('item')
- new_first_up: float32 [768, 3072], P('item')
- new_second_up: float32 [768, 3072], P('item')
- new_w_down: float32 [3072, 768], P('item')
- new_first_down: float32 [3072, 768], P('item')
- new_second_down: float32 [3072, 768], P('item')
- new_small: float32 [12, 768], replicated
- new_first_small: float32 [12, 768], replicated
- new_second_small: float32 [12, 768], replicated
The draws below stay inside these ranges and needn't reach their ends.
Inputs may be any that keep to these rules, and one draw needn't show every extreme that they name: `glob_pos`: each row holds distinct blocks; its first two entries are block 0 and block 47; only the first glob_count entries of a row are global.
All inputs are finite; a program needn't handle non-finite values.
Results may differ from the reference program's by a relative error of at most 0.012.
The reference program's roundings to bfloat16 on the way count: a program that leaves them out, or rounds other values in their place, can miss the bound.
Values may be sent and summed in bfloat16 or wider, within the bound.
A program may use at most 192 MiB of HBM per device.

```python
import math
import jax
import jax.numpy as jnp
from jax import lax

D = 768
HEADS = 12
HEAD_DIM = 64
FF = 3072
BLOCK = 64
RAND = 3
GMAX = 4
SMALL_ROWS = 12
ADAM_STEP = 10
SEQ_LEN = 3072
NB = 48
ITEMS = 8


def draw_glob_pos(key, part):
    row_keys = jax.random.split(key, ITEMS)

    def one_row(row_key):
        middle = jax.random.permutation(row_key, NB - 2)[:GMAX - 2] + 1
        ends = jnp.array([0, NB - 1], jnp.int32)
        return jnp.concatenate([ends, middle.astype(jnp.int32)])
    return jax.vmap(one_row)(row_keys)


def draw_small_params(key, part):
    gain_key, bias_key = jax.random.split(jax.random.fold_in(key, 7))
    row_ids = jnp.arange(SMALL_ROWS)[:, None]
    feature_place = jnp.arange(D, dtype=jnp.float32)[None, :] / (D - 1)
    unit_place = (jnp.arange(SMALL_ROWS * D, dtype=jnp.float32).reshape(SMALL_ROWS, D) - 8 * D) / (FF - 1)
    gain_ramp = jnp.exp((feature_place - 0.5) * 2.0 * jnp.log(2.0))
    bias_ramp = jnp.where(row_ids >= 8, -1.5 + 3.0 * unit_place, 0.0)
    is_gain = (row_ids == 0) | (row_ids == 5)
    gains = jnp.clip(1.0 + 0.15 * jax.random.normal(gain_key, (SMALL_ROWS, D), jnp.float32), 0.5, 1.5)
    biases = jnp.clip(0.2 * jax.random.normal(bias_key, (SMALL_ROWS, D), jnp.float32), -0.8, 0.8)
    gains = jnp.where(row_ids == 0, gains * gain_ramp, gains)
    biases = biases + bias_ramp
    return jnp.where(is_gain, gains, biases).astype(jnp.float32)


def touch_ends(values, rng, least, high):
    longest = values.shape.index(max(values.shape))
    spots = []
    for shift in (0, 1):
        where = [jax.random.randint(jax.random.fold_in(rng, axis), (), 0, length) for axis, length in enumerate(values.shape)]
        where[longest] = (where[longest] + shift) % values.shape[longest]
        spots.append(tuple(where))
    return values.at[spots[0]].set(least).at[spots[1]].set(high)


def levels(rng, dims, cuts, least, top_value):
    level = 1.0
    for axis_at, blocks in cuts:
        draws = jax.random.uniform(jax.random.fold_in(jax.random.fold_in(rng, 6), axis_at), (blocks,), jnp.float32, least / len(cuts), top_value / len(cuts))
        level = level * jnp.repeat(jnp.exp(draws), dims[axis_at] // blocks).reshape((-1,) + (1,) * (len(dims) - 1 - axis_at))
    return level


def bell_draw(own_key, extent, scale, bound, cuts=(), kind=jnp.bfloat16):
    values = jax.random.normal(own_key, extent, jnp.float32) * scale
    if len(cuts) > 0:
        values = levels(own_key, extent, cuts, -0.22, 0.18) * values
    return jnp.clip(values, min=-bound, max=bound).astype(kind)


def setup_inputs(seed: int = 0) -> dict:
    key_list = jax.random.split(jax.random.key(seed), 21)
    return {
        "inputs": bell_draw(key_list[0], (ITEMS, SEQ_LEN, D), 1.0, 6.0, ((0, 8), (1, 4))),
        "d_output": bell_draw(key_list[1], (ITEMS, SEQ_LEN, D), 1.0, 6.0, ((0, 8), (1, 4))),
        "glob_count": touch_ends(jax.random.randint(key_list[2], (ITEMS,), 2, GMAX + 1), jax.random.fold_in(key_list[2], 1), 2, GMAX).astype(jnp.int32),
        "glob_pos": draw_glob_pos(jax.random.fold_in(key_list[20], 71), 0),
        "rand_blocks": touch_ends(jax.random.randint(key_list[4], (ITEMS, HEADS, NB, RAND), 0, NB), jax.random.fold_in(key_list[4], 1), 0, NB - 1).astype(jnp.int32),
        "w_qkv": bell_draw(key_list[5], (D, 3 * D), D ** -0.5, 0.21875, ((0, 8),), jnp.float32),
        "w_out": bell_draw(key_list[6], (D, D), (D // 16) ** -0.5, 0.875, ((0, 8),), jnp.float32),
        "w_up": bell_draw(key_list[7], (D, FF), D ** -0.5, 0.21875, ((0, 8),), jnp.float32),
        "w_down": bell_draw(key_list[8], (FF, D), FF ** -0.5, 0.109375, ((0, 8),), jnp.float32),
        "small_params": draw_small_params(jax.random.fold_in(key_list[20], 71), 0),
        "first_qkv": bell_draw(key_list[10], (D, 3 * D), (0.111 * (4 * D * D + 2 * D * FF + 12 * D) ** -0.5), 0.00024414062, ((0, 8),), jnp.float32),
        "second_qkv": jnp.clip(jnp.exp(math.log(5.644054112963204e-10) - 1.3862944 * jax.random.uniform(key_list[11], (D, 3 * D), jnp.float32) ** levels(key_list[11], (D, 3 * D), ((0, 8),), -0.2, 0.2)), 1.411013528240801e-10, 5.644054112963204e-10),
        "first_out": bell_draw(key_list[12], (D, D), (0.111 * (4 * D * D + 2 * D * FF + 12 * D) ** -0.5), 0.00024414062, ((0, 8),), jnp.float32),
        "second_out": jnp.clip(jnp.exp(math.log(5.644054112963204e-10) - 1.3862944 * jax.random.uniform(key_list[13], (D, D), jnp.float32) ** levels(key_list[13], (D, D), ((0, 8),), -0.2, 0.2)), 1.411013528240801e-10, 5.644054112963204e-10),
        "first_up": bell_draw(key_list[14], (D, FF), (0.111 * (4 * D * D + 2 * D * FF + 12 * D) ** -0.5), 0.00024414062, ((0, 8),), jnp.float32),
        "second_up": jnp.clip(jnp.exp(math.log(5.644054112963204e-10) - 1.3862944 * jax.random.uniform(key_list[15], (D, FF), jnp.float32) ** levels(key_list[15], (D, FF), ((0, 8),), -0.2, 0.2)), 1.411013528240801e-10, 5.644054112963204e-10),
        "first_down": bell_draw(key_list[16], (FF, D), (0.111 * (4 * D * D + 2 * D * FF + 12 * D) ** -0.5), 0.00024414062, ((0, 8),), jnp.float32),
        "second_down": jnp.clip(jnp.exp(math.log(5.644054112963204e-10) - 1.3862944 * jax.random.uniform(key_list[17], (FF, D), jnp.float32) ** levels(key_list[17], (FF, D), ((0, 8),), -0.2, 0.2)), 1.411013528240801e-10, 5.644054112963204e-10),
        "first_small": bell_draw(key_list[18], (SMALL_ROWS, D), (0.333 * (4 * D * D + 2 * D * FF + 12 * D) ** -0.5), 0.0007324219, (), jnp.float32),
        "second_small": jnp.clip(jnp.exp(jax.random.uniform(key_list[19], (SMALL_ROWS, D), jnp.float32, math.log(1.2699121754167209e-09), math.log(5.0796487016668834e-09))), 1.2699121754167209e-09, 5.0796487016668834e-09),
    }


@jax.custom_vjp
def low(v):
    return lax.optimization_barrier(v.astype(jnp.bfloat16)).astype(jnp.float32)

@jax.custom_vjp
def low_back(v):
    return v

def low_keep(v):
    return (low(v), None)

def low_pass(kept, grad):
    return (grad,)

def back_keep(v):
    return (v, None)

def back_low(kept, grad):
    return (low(grad),)
low.defvjp(low_keep, low_pass)
low_back.defvjp(back_keep, back_low)
norm_epsilon = 1e-06
beta_first = 0.9
beta_second = 0.999
adam_epsilon = 1e-08
learn_rate = 0.1
small_rate = 0.5
weight_decay = 0.01
clip_level = 1.0
masked_value = -1e+30
highest = lax.Precision.HIGHEST

def layer_norm(values, gain, bias):
    average = lax.optimization_barrier(jnp.mean(values, -1, keepdims=True))
    centered = values - average
    spread = lax.optimization_barrier(jnp.mean(centered * centered, -1, keepdims=True))
    return centered * lax.rsqrt(spread + norm_epsilon) * gain + bias

def block_allowed(count, positions, random_table):
    nblocks = random_table.shape[1]
    block_ids = jnp.arange(nblocks, dtype=jnp.int32)
    active = jnp.arange(positions.shape[0], dtype=jnp.int32) < count
    is_global = jnp.any((positions[:, None] == block_ids[None, :]) & active[:, None], axis=0)
    window = jnp.abs(block_ids[:, None] - block_ids[None, :]) <= 1
    chosen = jnp.any(random_table[:, :, :, None] == block_ids[None, None, None, :], axis=2)
    return window[None] | chosen | is_global[None, :, None] | is_global[None, None, :]

def attention(qkv, allowed):
    seq_len = qkv.shape[0]
    q_rows = min(512, seq_len)
    split_parts = qkv.reshape(seq_len, 3, HEADS, HEAD_DIM).transpose(2, 1, 0, 3)
    offsets = jnp.arange(seq_len // q_rows, dtype=jnp.int32) * q_rows

    def one_head(packed):
        parts, head_allowed = packed
        q_head, k_head, v_head = (parts[0], parts[1], parts[2])

        def rows_of(offset):
            q_block = lax.dynamic_slice_in_dim(q_head, offset, q_rows, 0)
            allowed_rows = lax.dynamic_slice_in_dim(head_allowed, offset // BLOCK, q_rows // BLOCK, 0)
            scores = low_back(jnp.dot(q_block, k_head.T, precision=highest) * HEAD_DIM ** (-0.5))
            shaped = scores.reshape(q_rows // BLOCK, BLOCK, seq_len // BLOCK, BLOCK)
            shaped = jnp.where(allowed_rows[:, None, :, None], shaped, masked_value).reshape(q_rows, seq_len)
            attn_prob = jax.nn.softmax(shaped, axis=-1)
            return jnp.dot(low(attn_prob), v_head, precision=highest)
        mixed_rows = lax.map(jax.checkpoint(rows_of), offsets)
        return mixed_rows.reshape(seq_len, HEAD_DIM)
    mixed = lax.map(one_head, (split_parts, allowed))
    return mixed.transpose(1, 0, 2).reshape(seq_len, HEADS * HEAD_DIM)

def item_forward(tokens, wq, wo, wu, wd, small, count, positions, table):
    zero_bias = jnp.zeros((D,), jnp.float32)
    qkv_bias = jnp.concatenate([small[2], zero_bias, small[3]])
    qkv = jnp.dot(low(tokens), wq, precision=highest) + qkv_bias
    qkv = low_back(low(qkv))
    allowed = block_allowed(count, positions, table)
    mixed = low_back(low(attention(qkv, allowed)))
    attn_out = low_back(jnp.dot(mixed, wo, precision=highest) + small[4])
    hidden = layer_norm(tokens + attn_out, small[0], small[1])
    up_pre = low_back(jnp.dot(low(hidden), wu, precision=highest) + small[8:12].reshape(FF))
    active = jax.nn.gelu(up_pre, approximate=False)
    ffn_out = low_back(jnp.dot(low(active), wd, precision=highest) + small[7])
    return layer_norm(hidden + ffn_out, small[5], small[6])

def adam_update(weight, first, second, grad, decay, rate):
    first_new = beta_first * first + (1.0 - beta_first) * grad
    second_new = beta_second * second + (1.0 - beta_second) * grad * grad
    first_hat = first_new / (1.0 - beta_first ** ADAM_STEP)
    second_hat = second_new / (1.0 - beta_second ** ADAM_STEP)
    weight_new = weight - rate * (first_hat / (jnp.sqrt(second_hat) + adam_epsilon) + decay * weight)
    return (weight_new, first_new, second_new)

def reference(inputs, d_output, glob_count, glob_pos, rand_blocks, w_qkv, w_out, w_up, w_down, small_params, first_qkv, second_qkv, first_out, second_out, first_up, second_up, first_down, second_down, first_small, second_small):

    def forward(tokens, wq, wo, wu, wd, small):
        wq, wo, wu, wd = (low(wq), low(wo), low(wu), low(wd))

        def one_item(packed):
            row_tokens, count, positions, table = packed
            return item_forward(row_tokens, wq, wo, wu, wd, small, count, positions, table)
        return lax.map(jax.checkpoint(one_item), (tokens, glob_count, glob_pos, rand_blocks))
    outputs, pull_back = jax.vjp(forward, inputs.astype(jnp.float32), w_qkv, w_out, w_up, w_down, small_params)
    d_inputs, g_qkv, g_out, g_up, g_down, g_small = pull_back(d_output.astype(jnp.float32))
    squares = jnp.sum(g_qkv * g_qkv) + jnp.sum(g_out * g_out) + jnp.sum(g_up * g_up) + jnp.sum(g_down * g_down) + jnp.sum(g_small * g_small)
    grad_norm = jnp.sqrt(squares)
    factor = jnp.minimum(1.0, clip_level / (grad_norm + 1e-06))
    new_qkv = adam_update(w_qkv, first_qkv, second_qkv, g_qkv * factor, weight_decay, learn_rate)
    new_out = adam_update(w_out, first_out, second_out, g_out * factor, weight_decay, learn_rate)
    new_up = adam_update(w_up, first_up, second_up, g_up * factor, weight_decay, learn_rate)
    new_down = adam_update(w_down, first_down, second_down, g_down * factor, weight_decay, learn_rate)
    new_small = adam_update(small_params, first_small, second_small, g_small * factor, 0.0, small_rate)
    return (outputs.astype(jnp.bfloat16), d_inputs, grad_norm, new_qkv[0], new_qkv[1], new_qkv[2], new_out[0], new_out[1], new_out[2], new_up[0], new_up[1], new_up[2], new_down[0], new_down[1], new_down[2], new_small[0], new_small[1], new_small[2])
```

```python
import functools

import jax
import jax.numpy as jnp
from jax import lax
from jax.experimental import pallas as pl
from jax.experimental.pallas import tpu as pltpu
from jax.sharding import PartitionSpec as P

ADAM_STEP = 10
norm_epsilon = 1e-06
beta_first = 0.9
beta_second = 0.999
adam_epsilon = 1e-08
learn_rate = 0.1
small_rate = 0.5
weight_decay = 0.01
clip_level = 1.0


HD=64; BL=64; NEG=-1e30
bf16=jnp.bfloat16; f32=jnp.float32
NT=(((1,),(1,)),((),()))
TN=(((0,),(0,)),((),()))

def slots(count, positions, table):
    H,NB,R=table.shape; G=positions.shape[0]
    a=jnp.arange(NB,dtype=jnp.int32)
    win=jnp.stack([a-1,a,a+1],-1)
    act=jnp.arange(G,dtype=jnp.int32)<count
    parts=jnp.concatenate([jnp.broadcast_to(win[None],(H,NB,3)),
        jnp.broadcast_to(jnp.where(act,positions,-1)[None,None],(H,NB,G)),table],-1)
    S=3+G+R
    ok=(parts>=0)&(parts<NB)
    same=parts[...,:,None]==parts[...,None,:]
    earlier=jnp.arange(S)[:,None]>jnp.arange(S)[None,:]
    dup=jnp.any(same&earlier,-1)
    isg=jnp.any((positions[None,:]==a[:,None])&act[None],-1)
    ok=ok&~dup&~isg[None,:,None]
    idx=jnp.clip(parts,0,NB-1)
    bias=jnp.where(ok,0.0,NEG).astype(f32)
    bias=jnp.broadcast_to(bias[...,None],(H,NB,S,BL)).reshape(H*NB,S*BL)
    return idx.reshape(-1), bias

def lo_lanes(rows):
    return lax.broadcasted_iota(jnp.int32,(rows,2*HD),1)<HD

def pick(block,h,which):
    low=lo_lanes(block.shape[0])
    keep_low=(h%2==1) if which=='q' else (h%2==0)
    return jnp.where(low if keep_low else ~low, block, jnp.zeros_like(block))

def fwd_kernel(H,NB,S,G,CH,idx_ref,gl_ref,qkv_ref,bias_ref,out_ref,lse_ref,sbuf):
    n=NB*BL
    def finish(r,outs,lses):
        low=lo_lanes(BL)
        for p in range((H+1)//2):
            if 2*p+1<H:
                out_ref[pl.ds(r,BL),p*128:(p+1)*128]=jnp.where(low,outs[2*p],outs[2*p+1]).astype(bf16)
            else:
                out_ref[pl.ds(r,BL),p*128:p*128+HD]=outs[2*p][:,:HD].astype(bf16)
        lane=lax.broadcasted_iota(jnp.int32,(BL,128),1)
        acc=jnp.zeros((BL,128),f32)
        for h in range(H): acc=jnp.where(lane==h,lses[h],acc)
        lse_ref[pl.ds(r,BL),:]=acc
    def qblk(r,h):
        return pick(qkv_ref[pl.ds(r,BL),(H+h//2)*128:(H+h//2+1)*128],h,'q')
    def body(a,_):
        r=pl.multiple_of(a*BL,BL)
        outs=[];lses=[]
        for h in range(H):
            kv=jnp.concatenate([qkv_ref[pl.ds(pl.multiple_of(idx_ref[(h*NB+a)*S+j]*BL,BL),BL),h*128:(h+1)*128] for j in range(S)],0)
            s=lax.dot_general(qblk(r,h),kv,NT,preferred_element_type=f32)+bias_ref[pl.ds(h*NB+a,1),:]
            m=jnp.max(s,-1,keepdims=True)
            e=jnp.exp(s-m)
            l=jnp.sum(e,-1,keepdims=True)
            p=(e*(1.0/l)).astype(bf16)
            outs.append(jnp.dot(p,kv,preferred_element_type=f32))
            lses.append(m+jnp.log(l))
        finish(r,outs,lses)
        return 0
    lax.fori_loop(0,NB,body,0,unroll=UNROLL)
    def gbody(g,_):
        r=pl.multiple_of(gl_ref[1+g]*BL,BL)
        outs=[];lses=[]
        for h in range(H):
            q=qblk(r,h)
            mm=None
            for c in range(n//CH):
                s=lax.dot_general(q,qkv_ref[c*CH:(c+1)*CH,h*128:(h+1)*128],NT,preferred_element_type=f32)
                sbuf[h,:,c*CH:(c+1)*CH]=s
                mc=jnp.max(s,-1,keepdims=True)
                mm=mc if mm is None else jnp.maximum(mm,mc)
            l=0.;
            for c in range(n//CH):
                e=jnp.exp(sbuf[h,:,c*CH:(c+1)*CH]-mm)
                sbuf[h,:,c*CH:(c+1)*CH]=e
                l=l+jnp.sum(e,-1,keepdims=True)
            il=1.0/l
            o=0.
            for c in range(n//CH):
                p=(sbuf[h,:,c*CH:(c+1)*CH]*il).astype(bf16)
                o=o+jnp.dot(p,qkv_ref[c*CH:(c+1)*CH,h*128:(h+1)*128],preferred_element_type=f32)
            outs.append(o); lses.append(mm+jnp.log(l))
        finish(r,outs,lses)
        return 0
    lax.fori_loop(0,gl_ref[0],gbody,0)
UNROLL=1
def attn_fwd(idx,gl,qkv,bias,H,NB,S):
    n=NB*BL
    V=pl.BlockSpec(memory_space=pltpu.VMEM); SM=pl.BlockSpec(memory_space=pltpu.SMEM)
    return pl.pallas_call(functools.partial(fwd_kernel,H,NB,S,0,512),
        out_shape=(jax.ShapeDtypeStruct((n,H*HD),bf16),jax.ShapeDtypeStruct((n,128),f32)),
        in_specs=[SM,SM,V,V],out_specs=(V,V),
        scratch_shapes=[pltpu.VMEM((H,BL,n),f32)],
        compiler_params=pltpu.CompilerParams(vmem_limit_bytes=56<<20),name="attn_fwd")(idx,gl,qkv,bias)

def bwd_kernel(H,NB,S,CH,idx_ref,gl_ref,qkv_ref,g_ref,lse_ref,bias_ref,out_ref,acc,pbuf,dbuf):
    n=NB*BL
    QP=(H+1)//2
    def zero(i,_):
        acc[pl.ds(pl.multiple_of(i*256,256),256),:]=jnp.zeros((256,H*128),f32)
        return 0
    lax.fori_loop(0,n//256,zero,0)
    def xblk(r,h):
        q=pick(qkv_ref[pl.ds(r,BL),(H+h//2)*128:(H+h//2+1)*128],h,'q')
        w=min(128,H*HD-(h//2)*128)
        g=g_ref[pl.ds(r,BL),(h//2)*128:(h//2)*128+w]
        if w<128: g=jnp.concatenate([g,jnp.zeros((BL,128-w),bf16)],1)
        else: g=pick(g,h,'g')
        return jnp.concatenate([q,g],0)
    def finish(r,dqs):
        low=lo_lanes(BL)
        for p in range(QP):
            hi=dqs[2*p]; lo=dqs[2*p+1] if 2*p+1<H else jnp.zeros_like(hi)
            out_ref[pl.ds(r,BL),(H+p)*128:(H+p+1)*128]=jnp.where(low,lo,hi).astype(bf16)
    def body(a,_):
        r=pl.multiple_of(a*BL,BL)
        dqs=[]
        for h in range(H):
            x=xblk(r,h)
            rows=[pl.multiple_of(idx_ref[(h*NB+a)*S+j]*BL,BL) for j in range(S)]
            kv=jnp.concatenate([qkv_ref[pl.ds(rows[j],BL),h*128:(h+1)*128] for j in range(S)],0)
            sd=lax.dot_general(x,kv,NT,preferred_element_type=f32)
            p=jnp.exp(sd[:BL]+bias_ref[pl.ds(h*NB+a,1),:]-lse_ref[pl.ds(r,BL),h:h+1])
            dp=sd[BL:]
            inner=jnp.sum(dp*p,-1,keepdims=True)
            ds=p*(dp-inner)
            w=jnp.concatenate([ds.astype(bf16),p.astype(bf16)],0)
            dqs.append(jnp.dot(w[:BL],kv,preferred_element_type=f32))
            dkv=lax.dot_general(w,x,TN,preferred_element_type=f32)
            for j in range(S):
                acc[pl.ds(rows[j],BL),h*128:(h+1)*128]+=dkv[j*BL:(j+1)*BL]
        finish(r,dqs)
        return 0
    lax.fori_loop(0,NB,body,0,unroll=UNROLL)
    def gbody(g,_):
        r=pl.multiple_of(gl_ref[1+g]*BL,BL)
        dqs=[]
        for h in range(H):
            x=xblk(r,h)
            lse=lse_ref[pl.ds(r,BL),h:h+1]
            inner=0.
            for c in range(n//CH):
                cs=slice(c*CH,(c+1)*CH)
                sd=lax.dot_general(x,qkv_ref[cs,h*128:(h+1)*128],NT,preferred_element_type=f32)
                p=jnp.exp(sd[:BL]-lse); dp=sd[BL:]
                pbuf[h,:,cs]=p; dbuf[h,:,cs]=dp
                inner=inner+jnp.sum(dp*p,-1,keepdims=True)
            dq=0.
            for c in range(n//CH):
                cs=slice(c*CH,(c+1)*CH)
                p=pbuf[h,:,cs]
                ds=(p*(dbuf[h,:,cs]-inner)).astype(bf16)
                w=jnp.concatenate([ds,p.astype(bf16)],0)
                dq=dq+jnp.dot(ds,qkv_ref[cs,h*128:(h+1)*128],preferred_element_type=f32)
                acc[cs,h*128:(h+1)*128]+=lax.dot_general(w,x,TN,preferred_element_type=f32)
            dqs.append(dq)
        finish(r,dqs)
        return 0
    lax.fori_loop(0,gl_ref[0],gbody,0)
    def flush(i,_):
        rr=pl.ds(pl.multiple_of(i*256,256),256)
        out_ref[rr,:H*128]=acc[rr,:].astype(bf16)
        return 0
    lax.fori_loop(0,n//256,flush,0)

def attn_bwd(idx,gl,qkv,g,lse,bias,H,NB,S):
    n=NB*BL
    V=pl.BlockSpec(memory_space=pltpu.VMEM); SM=pl.BlockSpec(memory_space=pltpu.SMEM)
    return pl.pallas_call(functools.partial(bwd_kernel,H,NB,S,512),
        out_shape=jax.ShapeDtypeStruct((n,(H+(H+1)//2)*128),bf16),
        in_specs=[SM,SM,V,V,V,V],out_specs=V,
        scratch_shapes=[pltpu.VMEM((n,H*128),f32),pltpu.VMEM((H,BL,n),f32),pltpu.VMEM((H,BL,n),f32)],
        compiler_params=pltpu.CompilerParams(vmem_limit_bytes=56<<20),name="attn_bwd")(idx,gl,qkv,g,lse,bias)


def layer_norm(values, gain, bias):
    average = jnp.mean(values, -1, keepdims=True)
    centered = values - average
    spread = jnp.mean(centered * centered, -1, keepdims=True)
    return centered * lax.rsqrt(spread + norm_epsilon) * gain + bias


def exact_gelu(values):
    return jax.nn.gelu(values, approximate=False)


def packed_columns(own):
    heads = own.shape[2]
    cols = []
    for h in range(heads):
        pair = [own[:, 2, h], own[:, 1, h]]
        cols += pair if h % 2 == 0 else pair[::-1]
    for p in range((heads + 1) // 2):
        odd = own[:, 0, 2 * p + 1] if 2 * p + 1 < heads else jnp.zeros_like(own[:, 0, 0])
        cols += [odd * HD**-0.5, own[:, 0, 2 * p] * HD**-0.5]
    return jnp.concatenate(cols, -1)


def natural_columns(values, heads):
    parts = [[], [], []]
    for h in range(heads):
        first, second = values[:, h * 128 : h * 128 + HD], values[:, h * 128 + HD : h * 128 + 128]
        base = (heads + h // 2) * 128
        if h % 2 == 0:
            parts[2].append(first)
            parts[1].append(second)
            parts[0].append(values[:, base + HD : base + 128] * HD**-0.5)
        else:
            parts[1].append(first)
            parts[2].append(second)
            parts[0].append(values[:, base : base + HD] * HD**-0.5)
    return jnp.concatenate(parts[0] + parts[1] + parts[2], -1)


def adam_update(weight, first, second, grad, decay, rate):
    first_new = beta_first * first + (1.0 - beta_first) * grad
    second_new = beta_second * second + (1.0 - beta_second) * grad * grad
    first_hat = first_new / (1.0 - beta_first**ADAM_STEP)
    second_hat = second_new / (1.0 - beta_second**ADAM_STEP)
    weight_new = weight - rate * (
        first_hat / (jnp.sqrt(second_hat) + adam_epsilon) + decay * weight
    )
    return (weight_new, first_new, second_new)


def on_device(
    inputs,
    d_output,
    glob_count,
    glob_pos,
    rand_blocks,
    w_qkv,
    w_out,
    w_up,
    w_down,
    small_params,
    first_qkv,
    second_qkv,
    first_out,
    second_out,
    first_up,
    second_up,
    first_down,
    second_down,
    first_small,
    second_small,
):
    items_n, tok_rows, width = inputs.shape
    groups = lax.axis_size("seq")
    place = lax.axis_index("seq")
    heads = rand_blocks.shape[1]
    nblocks = rand_blocks.shape[2]
    head_width = heads * HD
    positions_n = tok_rows * groups
    row_count = tok_rows
    slots_n = 3 + glob_pos.shape[1] + rand_blocks.shape[3]

    own = lax.dynamic_index_in_dim(
        w_qkv.reshape(-1, 3, groups, heads, HD), place, 2, keepdims=False
    )
    slab = lax.all_gather(packed_columns(own).astype(bf16), "item", axis=0, tiled=True)
    full_out, full_up, full_down = (
        lax.all_gather(w_out.astype(bf16), "item", axis=0, tiled=True),
        lax.all_gather(w_up.astype(bf16), "item", axis=0, tiled=True),
        lax.all_gather(w_down.astype(bf16), "item", axis=0, tiled=True),
    )
    bias3 = jnp.stack([small_params[2], jnp.zeros((width,), f32), small_params[3]])
    own_bias = lax.dynamic_index_in_dim(
        bias3.reshape(1, 3, groups, heads, HD), place, 2, keepdims=False
    )
    slab_bias = packed_columns(own_bias)
    tokens_b = inputs.reshape(tok_rows, width)
    tokens_all = lax.all_gather(tokens_b, "seq", axis=0, tiled=True)
    tokens_f = tokens_b.astype(f32)
    qkv = (jnp.dot(tokens_all, slab, preferred_element_type=f32) + slab_bias).astype(bf16)
    idx, bias = slots(glob_count[0], glob_pos[0], rand_blocks[0])
    gl = jnp.concatenate([glob_count, glob_pos[0]])
    mixed_heads, lse = attn_fwd(idx, gl, qkv, bias, heads, nblocks, slots_n)
    mixed = lax.all_to_all(mixed_heads, "seq", split_axis=0, concat_axis=1, tiled=True)
    attn_out = jnp.dot(mixed, full_out, preferred_element_type=f32) + small_params[4]
    hidden, norm_one_back = jax.vjp(
        layer_norm, tokens_f + attn_out, small_params[0], small_params[1]
    )
    hidden_b = hidden.astype(bf16)
    up_pre = jnp.dot(hidden_b, full_up, preferred_element_type=f32) + small_params[8:12].reshape(-1)
    active, gelu_back = jax.vjp(exact_gelu, up_pre)
    active_b = active.astype(bf16)
    ffn_out = jnp.dot(active_b, full_down, preferred_element_type=f32) + small_params[7]
    outputs, norm_two_back = jax.vjp(layer_norm, hidden + ffn_out, small_params[5], small_params[6])
    grad_second, grad_gain_two, grad_bias_two = norm_two_back(
        d_output.reshape(row_count, width).astype(f32)
    )
    grad_ffn = grad_second.astype(bf16)
    grad_w_down = jnp.einsum("rf,rd->fd", active_b, grad_ffn, preferred_element_type=f32)
    grad_active = jnp.einsum("rd,fd->rf", grad_ffn, full_down, preferred_element_type=f32)
    (grad_up_pre,) = gelu_back(grad_active)
    grad_up_b = grad_up_pre.astype(bf16)
    grad_w_up = jnp.einsum("rd,rf->df", hidden_b, grad_up_b, preferred_element_type=f32)
    grad_hidden = grad_second + jnp.einsum(
        "rf,df->rd", grad_up_b, full_up, preferred_element_type=f32
    )
    grad_first, grad_gain_one, grad_bias_one = norm_one_back(grad_hidden)
    grad_attn = grad_first.astype(bf16)
    grad_w_out = jnp.einsum("rm,rd->md", mixed, grad_attn, preferred_element_type=f32)
    grad_mixed = jnp.einsum("rd,md->rm", grad_attn, full_out, preferred_element_type=f32).astype(
        bf16
    )
    grad_heads = lax.all_to_all(grad_mixed, "seq", split_axis=1, concat_axis=0, tiled=True)
    grad_qkv = attn_bwd(idx, gl, qkv, grad_heads, lse, bias, heads, nblocks, slots_n)
    grad_slab = jnp.einsum("rd,re->de", tokens_all, grad_qkv, preferred_element_type=f32)
    grad_tokens = jnp.einsum("re,de->rd", grad_qkv, slab, preferred_element_type=f32).astype(bf16)
    grad_inputs = grad_first + lax.psum_scatter(
        grad_tokens, "seq", scatter_dimension=0, tiled=True
    ).astype(f32)
    slab_sum = natural_columns(jnp.sum(grad_qkv.astype(f32), 0)[None], heads)[0]
    bias_grads = lax.dynamic_update_index_in_dim(
        jnp.zeros((3, groups, heads * HD), f32), slab_sum.reshape(3, heads * HD), place, 1
    ).reshape(3, width)
    small_rows = jnp.stack(
        [
            grad_gain_one,
            grad_bias_one,
            bias_grads[0],
            bias_grads[2],
            jnp.sum(grad_attn.astype(f32), 0),
            grad_gain_two,
            grad_bias_two,
            jnp.sum(grad_ffn.astype(f32), 0),
        ]
    )
    small_part = jnp.concatenate(
        [small_rows, jnp.sum(grad_up_b.astype(f32), 0).reshape(4, width)], 0
    )
    small_total = lax.psum(small_part, ("item", "seq"))
    shard_down = lax.psum_scatter(grad_w_down.astype(bf16), "item", scatter_dimension=0, tiled=True)
    shard_up = lax.psum_scatter(grad_w_up.astype(bf16), "item", scatter_dimension=0, tiled=True)
    shard_out = lax.psum_scatter(grad_w_out.astype(bf16), "item", scatter_dimension=0, tiled=True)
    shard_slab = lax.psum_scatter(grad_slab.astype(bf16), "item", scatter_dimension=0, tiled=True)
    shard_slab = natural_columns(shard_slab.astype(f32), heads).reshape(-1, 3, 1, heads * HD)
    shard_qkv = lax.all_gather(shard_slab, "seq", axis=2, tiled=True).reshape(-1, 3 * width)
    shard_out, shard_up, shard_down = lax.psum(
        (shard_out.astype(f32), shard_up.astype(f32), shard_down.astype(f32)), "seq"
    )
    local_squares = (
        jnp.sum(shard_qkv * shard_qkv)
        + jnp.sum(shard_out * shard_out)
        + jnp.sum(shard_up * shard_up)
        + jnp.sum(shard_down * shard_down)
    )
    matrix_squares = lax.psum(local_squares, "item")
    grad_norm = jnp.sqrt(matrix_squares + jnp.sum(small_total * small_total))
    factor = jnp.minimum(1.0, clip_level / (grad_norm + 1e-06))
    new_qkv = adam_update(
        w_qkv, first_qkv, second_qkv, shard_qkv * factor, weight_decay, learn_rate
    )
    new_out = adam_update(
        w_out, first_out, second_out, shard_out * factor, weight_decay, learn_rate
    )
    new_up = adam_update(w_up, first_up, second_up, shard_up * factor, weight_decay, learn_rate)
    new_down = adam_update(
        w_down, first_down, second_down, shard_down * factor, weight_decay, learn_rate
    )
    new_small = adam_update(
        small_params, first_small, second_small, small_total * factor, 0.0, small_rate
    )
    return (
        outputs.astype(bf16).reshape(items_n, tok_rows, width),
        grad_inputs.reshape(items_n, tok_rows, width),
        grad_norm,
        new_qkv[0],
        new_qkv[1],
        new_qkv[2],
        new_out[0],
        new_out[1],
        new_out[2],
        new_up[0],
        new_up[1],
        new_up[2],
        new_down[0],
        new_down[1],
        new_down[2],
        new_small[0],
        new_small[1],
        new_small[2],
    )


def solution(mesh):
    return jax.shard_map(
        on_device,
        mesh=mesh,
        in_specs=(
            P("item", "seq", None),
            P("item", "seq", None),
            P("item"),
            P("item", None),
            P("item", "seq", None, None),
            P("item", None),
            P("item", None),
            P("item", None),
            P("item", None),
            P(),
            P("item", None),
            P("item", None),
            P("item", None),
            P("item", None),
            P("item", None),
            P("item", None),
            P("item", None),
            P("item", None),
            P(),
            P(),
        ),
        out_specs=(
            P("item", "seq", None),
            P("item", "seq", None),
            P(),
            P("item", None),
            P("item", None),
            P("item", None),
            P("item", None),
            P("item", None),
            P("item", None),
            P("item", None),
            P("item", None),
            P("item", None),
            P("item", None),
            P("item", None),
            P("item", None),
            P(),
            P(),
            P(),
        ),
        check_vma=False,
    )
```

```python
import functools

import jax
import jax.numpy as jnp
from jax import lax
from jax.experimental import pallas as pl
from jax.experimental.pallas import tpu as pltpu
from jax.sharding import PartitionSpec as P

ADAM_STEP = 10
norm_epsilon = 1e-06
beta_first = 0.9
beta_second = 0.999
adam_epsilon = 1e-08
learn_rate = 0.1
small_rate = 0.5
weight_decay = 0.01
clip_level = 1.0


HD = 64
BL = 64
NEG = -1e30
bf16 = jnp.bfloat16
f32 = jnp.float32
NT = (((1,), (1,)), ((), ()))
TN = (((0,), (0,)), ((), ()))


def slots(count, positions, table, place):
    heads, nblocks, picks = table.shape
    chunk = nblocks // 4
    globals_n = positions.shape[0]
    here = jnp.arange(nblocks, dtype=jnp.int32)

    def turned(b):
        return ((b // chunk) ^ place) * chunk + b % chunk

    block = turned(here)
    rows = table.reshape(heads, 2, 2, chunk, picks)
    rows = jnp.where(place % 2 == 1, rows[:, :, ::-1], rows)
    rows = jnp.where(place // 2 == 1, rows[:, ::-1], rows).reshape(heads, nblocks, picks)
    window = jnp.stack([block - 1, block, block + 1], -1)
    active = jnp.arange(globals_n, dtype=jnp.int32) < count
    parts = jnp.concatenate(
        [
            jnp.broadcast_to(window[None], (heads, nblocks, 3)),
            jnp.broadcast_to(jnp.where(active, positions, -1)[None, None], (heads, nblocks, globals_n)),
            rows,
        ],
        -1,
    )
    count_slots = 3 + globals_n + picks
    valid = (parts >= 0) & (parts < nblocks)
    same = parts[..., :, None] == parts[..., None, :]
    earlier = jnp.arange(count_slots)[:, None] > jnp.arange(count_slots)[None, :]
    repeated = jnp.any(same & earlier, -1)
    is_global = jnp.any((positions[None, :] == block[:, None]) & active[None], -1)
    valid = valid & ~repeated & ~is_global[None, :, None]
    idx = turned(jnp.clip(parts, 0, nblocks - 1))
    bias = jnp.where(valid, 0.0, NEG).astype(f32)
    bias = jnp.broadcast_to(bias[..., None], (heads, nblocks, count_slots, BL))
    glob = jnp.concatenate([count[None], turned(positions)])
    return idx.reshape(-1), bias.reshape(heads * nblocks, count_slots * BL), glob


def low_lanes(rows):
    return lax.broadcasted_iota(jnp.int32, (rows, 2 * HD), 1) < HD


def pick(block, keep_low):
    low = low_lanes(block.shape[0])
    return jnp.where(low if keep_low else ~low, block, jnp.zeros_like(block))


def fwd_kernel(dims, idx_ref, gl_ref, qkv_ref, bias_ref, *rest):
    heads, nblocks, slots_n, first, parts, chunk, wide = dims
    out_refs, lse_ref, sbuf = rest[:parts], rest[parts], rest[parts + 1]
    n = nblocks * BL
    lane = lax.broadcasted_iota(jnp.int32, (BL, 128), 1)

    def finish(out_ref, at, row, outs, lses):
        low = low_lanes(BL)
        for p in range((heads + 1) // 2):
            if 2 * p + 1 < heads:
                both = jnp.where(low, outs[2 * p], outs[2 * p + 1])
                out_ref[pl.ds(at, BL), p * 128 : (p + 1) * 128] = both.astype(bf16)
            else:
                out_ref[pl.ds(at, BL), p * 128 : p * 128 + HD] = outs[2 * p][:, :HD].astype(bf16)
        total = jnp.zeros((BL, 128), f32)
        for h in range(heads):
            total = jnp.where(lane == h, lses[h], total)
        lse_ref[pl.ds(row, BL), :] = total

    def queries(r, h):
        return pick(qkv_ref[pl.ds(r, BL), (heads + h // 2) * 128 : (heads + h // 2 + 1) * 128], h % 2 == 1)

    for part in range(parts):

        def body(b, _):
            a = first + part * chunk + b
            r = pl.multiple_of(a * BL, BL)
            outs, lses = [], []
            for h in range(heads):
                base = (h * nblocks + a) * slots_n
                kv = jnp.concatenate(
                    [
                        qkv_ref[pl.ds(pl.multiple_of(idx_ref[base + j] * BL, BL), BL), h * 128 : (h + 1) * 128]
                        for j in range(slots_n)
                    ],
                    0,
                )
                s = lax.dot_general(queries(r, h), kv, NT, preferred_element_type=f32)
                s = s + bias_ref[pl.ds(h * nblocks + a, 1), :]
                m = jnp.max(s, -1, keepdims=True)
                e = jnp.exp(s - m)
                l = jnp.sum(e, -1, keepdims=True)
                p = (e * (1.0 / l)).astype(bf16)
                outs.append(jnp.dot(p, kv, preferred_element_type=f32))
                lses.append(m + jnp.log(l))
            at = pl.multiple_of(b * BL, BL)
            finish(out_refs[part], at, pl.multiple_of(part * chunk * BL + at, BL), outs, lses)
            return 0

        lax.fori_loop(0, chunk, body, 0)

    def whole_row(g, _):
        a = gl_ref[1 + g]
        local = a - first

        @pl.when((local >= 0) & (local < parts * chunk))
        def _():
            r = pl.multiple_of(a * BL, BL)
            outs, lses = [], []
            for h in range(heads):
                q = queries(r, h)
                m = None
                for c in range(n // wide):
                    cs = slice(c * wide, (c + 1) * wide)
                    s = lax.dot_general(q, qkv_ref[cs, h * 128 : (h + 1) * 128], NT, preferred_element_type=f32)
                    sbuf[h, :, cs] = s
                    mc = jnp.max(s, -1, keepdims=True)
                    m = mc if m is None else jnp.maximum(m, mc)
                l = 0.0
                for c in range(n // wide):
                    cs = slice(c * wide, (c + 1) * wide)
                    e = jnp.exp(sbuf[h, :, cs] - m)
                    sbuf[h, :, cs] = e
                    l = l + jnp.sum(e, -1, keepdims=True)
                inv = 1.0 / l
                o = 0.0
                for c in range(n // wide):
                    cs = slice(c * wide, (c + 1) * wide)
                    p = (sbuf[h, :, cs] * inv).astype(bf16)
                    o = o + jnp.dot(p, qkv_ref[cs, h * 128 : (h + 1) * 128], preferred_element_type=f32)
                outs.append(o)
                lses.append(m + jnp.log(l))
            row = pl.multiple_of(local * BL, BL)
            for part in range(parts):

                @pl.when(local // chunk == part)
                def _():
                    finish(out_refs[part], pl.multiple_of(row - part * chunk * BL, BL), row, outs, lses)

        return 0

    lax.fori_loop(0, gl_ref[0], whole_row, 0)


def attn_fwd(idx, gl, qkv, bias, heads, first_part, parts):
    n = qkv.shape[0]
    nblocks = n // BL
    chunk = nblocks // 4
    slots_n = bias.shape[1] // BL
    vmem = pl.BlockSpec(memory_space=pltpu.VMEM)
    smem = pl.BlockSpec(memory_space=pltpu.SMEM)
    dims = (heads, nblocks, slots_n, first_part * chunk, parts, chunk, 512)
    return pl.pallas_call(
        functools.partial(fwd_kernel, dims),
        out_shape=tuple([jax.ShapeDtypeStruct((n // 4, heads * HD), bf16)] * parts)
        + (jax.ShapeDtypeStruct((parts * n // 4, 128), f32),),
        in_specs=[smem, smem, vmem, vmem],
        out_specs=tuple([vmem] * (parts + 1)),
        scratch_shapes=[pltpu.VMEM((heads, BL, n), f32)],
        compiler_params=pltpu.CompilerParams(vmem_limit_bytes=56 << 20),
        cost_estimate=pl.CostEstimate(flops=10 * parts * 10**9, bytes_accessed=10**7, transcendentals=0),
        name="attn_fwd",
    )(idx, gl, qkv, bias)


def bwd_kernel(dims, idx_ref, gl_ref, qkv_ref, bias_ref, *rest):
    heads, nblocks, slots_n, first, parts, chunk, wide, begin, end = dims
    g_refs, rest = rest[:parts], rest[parts:]
    lse_ref, rest = rest[0], rest[1:]
    if not begin:
        acc_in, dq_in, rest = rest[0], rest[1], rest[2:]
    if end:
        out_ref, acc, pbuf, dbuf = rest
    else:
        acc, dq_ref, pbuf, dbuf = rest
    n = nblocks * BL
    pairs = (heads + 1) // 2
    kvw = heads * 128

    def start(i, _):
        rr = pl.ds(pl.multiple_of(i * 256, 256), 256)
        if begin:
            acc[rr, :] = jnp.zeros((256, kvw), f32)
        else:
            acc[rr, :] = acc_in[rr, :]
        return 0

    lax.fori_loop(0, n // 256, start, 0)
    if end and not begin:
        out_ref[0 : first * BL, kvw:] = dq_in[...]

    def grads(g_ref, at, h):
        w = min(128, heads * HD - (h // 2) * 128)
        g = g_ref[pl.ds(at, BL), (h // 2) * 128 : (h // 2) * 128 + w]
        if w < 128:
            return jnp.concatenate([g, jnp.zeros((BL, 128 - w), bf16)], 1)
        return pick(g, h % 2 == 0)

    def queries(r, h):
        return pick(qkv_ref[pl.ds(r, BL), (heads + h // 2) * 128 : (heads + h // 2 + 1) * 128], h % 2 == 1)

    def finish(r, dqs):
        low = low_lanes(BL)
        for p in range(pairs):
            high = dqs[2 * p]
            odd = dqs[2 * p + 1] if 2 * p + 1 < heads else jnp.zeros_like(high)
            both = jnp.where(low, odd, high).astype(bf16)
            if end:
                out_ref[pl.ds(r, BL), kvw + p * 128 : kvw + (p + 1) * 128] = both
            else:
                dq_ref[pl.ds(pl.multiple_of(r - first * BL, BL), BL), p * 128 : (p + 1) * 128] = both

    for part in range(parts):

        def body(b, _):
            a = first + part * chunk + b
            r = pl.multiple_of(a * BL, BL)
            at = pl.multiple_of(b * BL, BL)
            row = pl.multiple_of(part * chunk * BL + at, BL)
            dqs = []
            for h in range(heads):
                hs = slice(h * 128, (h + 1) * 128)
                x = jnp.concatenate([queries(r, h), grads(g_refs[part], at, h)], 0)
                base = (h * nblocks + a) * slots_n
                rows = [pl.multiple_of(idx_ref[base + j] * BL, BL) for j in range(slots_n)]
                kv = jnp.concatenate([qkv_ref[pl.ds(rows[j], BL), hs] for j in range(slots_n)], 0)
                sd = lax.dot_general(x, kv, NT, preferred_element_type=f32)
                p = jnp.exp(sd[:BL] + bias_ref[pl.ds(h * nblocks + a, 1), :] - lse_ref[pl.ds(row, BL), h : h + 1])
                dp = sd[BL:]
                ds = p * (dp - jnp.sum(dp * p, -1, keepdims=True))
                w = jnp.concatenate([ds.astype(bf16), p.astype(bf16)], 0)
                dqs.append(jnp.dot(w[:BL], kv, preferred_element_type=f32))
                dkv = lax.dot_general(w, x, TN, preferred_element_type=f32)
                for j in range(slots_n):
                    acc[pl.ds(rows[j], BL), hs] += dkv[j * BL : (j + 1) * BL]
            finish(r, dqs)
            return 0

        lax.fori_loop(0, chunk, body, 0)

    def whole_row(g, _):
        a = gl_ref[1 + g]
        local = a - first
        for part in range(parts):

            @pl.when((local >= part * chunk) & (local < (part + 1) * chunk))
            def _():
                r = pl.multiple_of(a * BL, BL)
                row = pl.multiple_of(local * BL, BL)
                at = pl.multiple_of((local - part * chunk) * BL, BL)
                dqs = []
                for h in range(heads):
                    hs = slice(h * 128, (h + 1) * 128)
                    x = jnp.concatenate([queries(r, h), grads(g_refs[part], at, h)], 0)
                    lse = lse_ref[pl.ds(row, BL), h : h + 1]
                    inner = 0.0
                    for c in range(n // wide):
                        cs = slice(c * wide, (c + 1) * wide)
                        sd = lax.dot_general(x, qkv_ref[cs, hs], NT, preferred_element_type=f32)
                        p = jnp.exp(sd[:BL] - lse)
                        dp = sd[BL:]
                        pbuf[h, :, cs] = p
                        dbuf[h, :, cs] = dp
                        inner = inner + jnp.sum(dp * p, -1, keepdims=True)
                    dq = 0.0
                    for c in range(n // wide):
                        cs = slice(c * wide, (c + 1) * wide)
                        p = pbuf[h, :, cs]
                        ds = (p * (dbuf[h, :, cs] - inner)).astype(bf16)
                        w = jnp.concatenate([ds, p.astype(bf16)], 0)
                        dq = dq + jnp.dot(ds, qkv_ref[cs, hs], preferred_element_type=f32)
                        acc[cs, hs] += lax.dot_general(w, x, TN, preferred_element_type=f32)
                    dqs.append(dq)
                finish(r, dqs)

        return 0

    lax.fori_loop(0, gl_ref[0], whole_row, 0)
    if end:

        def flush(i, _):
            rr = pl.ds(pl.multiple_of(i * 256, 256), 256)
            out_ref[rr, :kvw] = acc[rr, :].astype(bf16)
            return 0

        lax.fori_loop(0, n // 256, flush, 0)


def attn_bwd(idx, gl, qkv, bias, grads, lse, heads, first_part, carried, end):
    n = qkv.shape[0]
    nblocks = n // BL
    chunk = nblocks // 4
    slots_n = bias.shape[1] // BL
    parts = len(grads)
    vmem = pl.BlockSpec(memory_space=pltpu.VMEM)
    smem = pl.BlockSpec(memory_space=pltpu.SMEM)
    dims = (heads, nblocks, slots_n, first_part * chunk, parts, chunk, 512, not carried, end)
    pairs = (heads + 1) // 2
    scratch = [pltpu.VMEM((heads, BL, n), f32)] * 2
    if end:
        out_shape = jax.ShapeDtypeStruct((n, (heads + pairs) * 128), bf16)
        out_specs = vmem
        scratch = [pltpu.VMEM((n, heads * 128), f32)] + scratch
    else:
        out_shape = (
            jax.ShapeDtypeStruct((n, heads * 128), f32),
            jax.ShapeDtypeStruct((parts * n // 4, pairs * 128), bf16),
        )
        out_specs = (vmem, vmem)
    return pl.pallas_call(
        functools.partial(bwd_kernel, dims),
        out_shape=out_shape,
        in_specs=[smem, smem] + [vmem] * (3 + parts + len(carried)),
        out_specs=out_specs,
        scratch_shapes=scratch,
        compiler_params=pltpu.CompilerParams(vmem_limit_bytes=60 << 20),
        cost_estimate=pl.CostEstimate(flops=11 * parts * 10**9, bytes_accessed=10**7, transcendentals=0),
        name="attn_bwd",
    )(idx, gl, qkv, bias, *grads, lse, *carried)


MESH_ID = pl.DeviceIdType.MESH


def flip(index, number):
    total = 0
    for bit in (1, 2, 4):
        digit = (index // bit) % 2
        total = total + bit * ((1 - digit) if number & bit else digit)
    return total


def greet(item, place, items):
    barrier = pltpu.get_barrier_semaphore()
    for t in range(1, 4):
        pl.semaphore_signal(barrier, inc=1, device_id=(item, flip(place, t)), device_id_type=MESH_ID)
    for k in range(1, items):
        pl.semaphore_signal(barrier, inc=1, device_id=(flip(item, k), place), device_id_type=MESH_ID)
    pl.semaphore_wait(barrier, 3 + items - 1)


def tail_kernel(
    items, query_columns, x0, x1, x2, x3, gq_ref, slab_ref, first_ref, small_ref, shard_ref,
    din_ref, group_ref, total_ref, squares_ref,
    near_out, near_in, far_out, far_in, grad_v, part_out, part_in, small_in, small_mid, small_items, sq_out, sq_in, sq_mid, sq_items,
    near_send, near_recv, far_send, far_recv, part_send, part_recv, sg_send, sg_recv, si_send, si_recv,
    gr_send, gr_recv, qg_send, qg_recv, qi_send, qi_recv,
):
    xs = (x0, x1, x2, x3)
    item, place = lax.axis_index("item"), lax.axis_index("seq")
    tokens, width = x0.shape
    rows = width // items
    tile = 256
    chunks = tokens // tile
    columns = gq_ref.shape[1]
    small_rows = small_ref.shape[0]
    greet(item, place, items)

    def to_group(src, dst, send, recv, t):
        return pltpu.make_async_remote_copy(
            src_ref=src, dst_ref=dst, send_sem=send, recv_sem=recv,
            device_id=(item, flip(place, t)), device_id_type=MESH_ID,
        )

    def to_item(src, dst, send, recv, k):
        return pltpu.make_async_remote_copy(
            src_ref=src, dst_ref=dst, send_sem=send, recv_sem=recv,
            device_id=(flip(item, k), place), device_id_type=MESH_ID,
        )

    small_copies = [to_group(small_ref, small_in.at[t], sg_send.at[t], sg_recv.at[t], t) for t in range(1, 4)]
    for copy in small_copies:
        copy.start()

    def token_part(t, c):
        return lax.dot_general(
            gq_ref[t * tokens + c * tile : t * tokens + (c + 1) * tile, :], slab_ref[...], NT, preferred_element_type=f32
        )

    near_copies = {}
    far_copies = []

    def send_near(t):
        for c in range(chunks):
            cs = pl.ds(c * tile, tile)
            near_out[t // 2, c * tile : (c + 1) * tile, :] = token_part(t, c).astype(bf16)
            copy = to_group(
                near_out.at[t // 2, cs], near_in.at[t // 2, cs], near_send.at[t // 2, c], near_recv.at[t // 2, c], 1
            )
            copy.start()
            near_copies[(t // 2, c)] = copy

    send_near(3)
    for c in range(chunks):
        cs = slice(c * tile, (c + 1) * tile)
        part = token_part(2, c)
        near_copies[(1, c)].wait_recv()
        far_out[cs, :] = (part.astype(bf16).astype(f32) + near_in[1, cs, :].astype(f32)).astype(bf16)
        copy = to_group(far_out.at[pl.ds(c * tile, tile)], far_in.at[pl.ds(c * tile, tile)], far_send.at[c], far_recv.at[c], 2)
        copy.start()
        far_copies.append(copy)

    def slab_rows(r, _):
        at = pl.multiple_of(r * tile, tile)
        part = 0.0
        for t in range(4):
            part = part + lax.dot_general(
                xs[t][:, pl.ds(at, tile)], gq_ref[t * tokens : (t + 1) * tokens, :], TN, preferred_element_type=f32
            )
        grad_v[pl.ds(at, tile), :] = part
        return 0

    lax.fori_loop(0, width // tile, slab_rows, 0)

    def sums(r, line):
        at = pl.multiple_of(r * tile, tile)
        return line + jnp.sum(gq_ref[pl.ds(at, tile), :].astype(f32), 0, keepdims=True)

    line = lax.fori_loop(0, 4 * chunks, sums, jnp.zeros((1, columns), f32))
    high = line.astype(bf16)
    rest = (line - high.astype(f32)).astype(bf16)
    which = lax.broadcasted_iota(jnp.int32, (16, columns), 0)
    lines = jnp.where(which == 0, high.astype(f32), jnp.where(which == 1, rest.astype(f32), 0.0)).astype(bf16)
    part_copies = []
    for k in list(range(items - 1, 0, -1)) + [0]:
        at = pl.multiple_of(flip(item, k) * rows, 8)
        part_out[k, 0:rows, :] = grad_v[pl.ds(at, rows), :].astype(bf16)
        part_out[k, rows : rows + 16, :] = lines
        if k:
            copy = to_item(part_out.at[k], part_in.at[k], part_send.at[k], part_recv.at[k], k)
            copy.start()
            part_copies.append(copy)

    for copy in small_copies:
        copy.wait()
    small_mid[...] = small_ref[...] + small_in[1] + small_in[2] + small_in[3]
    item_copies = [to_item(small_mid, small_items.at[k], si_send.at[k], si_recv.at[k], k) for k in range(1, items)]
    for copy in item_copies:
        copy.start()

    send_near(1)
    for c in range(chunks):
        cs = slice(c * tile, (c + 1) * tile)
        din_ref[cs, :] = first_ref[cs, :] + token_part(0, c).astype(bf16).astype(f32)

    def square_sum(values):
        return jnp.sum(jnp.sum(values * values, 0, keepdims=True), -1, keepdims=True)

    squares = square_sum(shard_ref[...])
    for copy in part_copies:
        copy.wait()
    own = part_out[0].astype(f32)
    for k in range(1, items):
        own = own + part_in[k].astype(f32)
    group_ref[0] = own
    group_copies = [to_group(group_ref.at[0], group_ref.at[t], gr_send.at[t], gr_recv.at[t], t) for t in (2, 1)]
    for copy in group_copies:
        copy.start()
    column = lax.broadcasted_iota(jnp.int32, (1, columns), 1)
    squares = squares + square_sum(own[0:rows] * jnp.where(column < query_columns, 1.0, HD**-0.5))
    sq_out[...] = jnp.broadcast_to(squares, (8, 128))
    sq_copies = [to_group(sq_out, sq_in.at[t], qg_send.at[t], qg_recv.at[t], t) for t in range(1, 4)]
    for copy in sq_copies:
        copy.start()
    for copy in sq_copies:
        copy.wait()
    sq_mid[...] = sq_out[...] + sq_in[1] + sq_in[2] + sq_in[3]
    sq_item_copies = [to_item(sq_mid, sq_items.at[k], qi_send.at[k], qi_recv.at[k], k) for k in range(1, items)]
    for copy in sq_item_copies:
        copy.start()

    group_copies[0].wait()
    cross = to_group(group_ref.at[2], group_ref.at[3], gr_send.at[3], gr_recv.at[3], 1)
    cross.start()
    for copy in item_copies:
        copy.wait()
    total = small_mid[...]
    for k in range(1, items):
        total = total + small_items[k]
    total_ref[...] = total
    for c in range(chunks):
        cs = slice(c * tile, (c + 1) * tile)
        near_copies[(1, c)].wait_send()
        near_copies[(0, c)].wait()
        far_copies[c].wait()
        din_ref[cs, :] = din_ref[cs, :] + near_in[0, cs, :].astype(f32) + far_in[cs, :].astype(f32)
    for copy in sq_item_copies:
        copy.wait()
    answer = sq_mid[...]
    for k in range(1, items):
        answer = answer + sq_items[k]
    squares_ref[...] = answer
    group_copies[1].wait()
    cross.wait()


def tail(xs, gq, slab, first, small, shard, items, query_columns):
    tokens, width = xs[0].shape
    columns = gq.shape[1]
    rows = width // items
    vmem = pl.BlockSpec(memory_space=pltpu.VMEM)
    dma = pltpu.SemaphoreType.DMA
    chunks = tokens // 256
    return pl.pallas_call(
        functools.partial(tail_kernel, items, query_columns),
        out_shape=(
            jax.ShapeDtypeStruct((tokens, width), f32),
            jax.ShapeDtypeStruct((4, rows + 16, columns), f32),
            jax.ShapeDtypeStruct(small.shape, f32),
            jax.ShapeDtypeStruct((8, 128), f32),
        ),
        in_specs=[vmem] * 9,
        out_specs=(vmem,) * 4,
        scratch_shapes=[
            pltpu.VMEM((2, tokens, width), bf16),
            pltpu.VMEM((2, tokens, width), bf16),
            pltpu.VMEM((tokens, width), bf16),
            pltpu.VMEM((tokens, width), bf16),
            pltpu.VMEM((width, columns), f32),
            pltpu.VMEM((items, rows + 16, columns), bf16),
            pltpu.VMEM((items, rows + 16, columns), bf16),
            pltpu.VMEM((4,) + small.shape, f32),
            pltpu.VMEM(small.shape, f32),
            pltpu.VMEM((items,) + small.shape, f32),
            pltpu.VMEM((8, 128), f32),
            pltpu.VMEM((4, 8, 128), f32),
            pltpu.VMEM((8, 128), f32),
            pltpu.VMEM((items, 8, 128), f32),
            dma((2, chunks)), dma((2, chunks)), dma((chunks,)), dma((chunks,)),
            dma((items,)), dma((items,)), dma((4,)), dma((4,)), dma((items,)), dma((items,)),
            dma((4,)), dma((4,)), dma((4,)), dma((4,)), dma((items,)), dma((items,)),
        ],
        compiler_params=pltpu.CompilerParams(vmem_limit_bytes=60 << 20, collective_id=3, has_side_effects=True),
        cost_estimate=pl.CostEstimate(flops=60 * 10**9, bytes_accessed=10**7, transcendentals=0),
        name="tail",
    )(*xs, gq, slab, first, small, shard)
def project_kernel(item_of, tile, *refs):
    items = len(refs) - 7
    xs, pieces, bias_ref, out_ref, slab_ref = refs[:4], refs[4:-3], refs[-3], refs[-2], refs[-1]
    item = item_of()
    rows = pieces[0].shape[0]
    for k in range(items):
        at = pl.multiple_of((item ^ k) * rows, 16)
        slab_ref[pl.ds(at, rows), :] = pieces[k][...]
    tokens = xs[0].shape[0]
    for t in range(4):

        def body(r, _):
            at = pl.multiple_of(r * tile, tile)
            part = jnp.dot(xs[t][pl.ds(at, tile), :], slab_ref[...], preferred_element_type=f32)
            out_ref[pl.ds(pl.multiple_of(t * tokens + at, tile), tile), :] = (part + bias_ref[...]).astype(bf16)
            return 0

        lax.fori_loop(0, tokens // tile, body, 0)


def project(item_of, xs, pieces, bias):
    tokens, width = xs[0].shape
    rows, columns = pieces[0].shape
    vmem = pl.BlockSpec(memory_space=pltpu.VMEM)
    return pl.pallas_call(
        functools.partial(project_kernel, item_of, 256),
        out_shape=(
            jax.ShapeDtypeStruct((4 * tokens, columns), bf16),
            jax.ShapeDtypeStruct((rows * len(pieces), columns), bf16),
        ),
        in_specs=[vmem] * (5 + len(pieces)),
        out_specs=(vmem, vmem),
        compiler_params=pltpu.CompilerParams(vmem_limit_bytes=48 << 20),
        cost_estimate=pl.CostEstimate(flops=6 * 10**9, bytes_accessed=10**7, transcendentals=0),
        name="project",
    )(*xs, *pieces, bias)


def token_grad_kernel(tile, gq_ref, slab_ref, keep_ref, send_ref):
    tokens = keep_ref.shape[1]
    for t in (1, 3, 0, 2):
        out_ref = send_ref if t % 2 else keep_ref

        def body(r, _):
            at = pl.multiple_of(r * tile, tile)
            part = lax.dot_general(
                gq_ref[pl.ds(pl.multiple_of(t * tokens + at, tile), tile), :],
                slab_ref[...],
                NT,
                preferred_element_type=f32,
            )
            out_ref[t // 2, pl.ds(at, tile), :] = part.astype(bf16)
            return 0

        lax.fori_loop(0, tokens // tile, body, 0)


def token_grads(gq, slab):
    tokens, width = gq.shape[0] // 4, slab.shape[0]
    vmem = pl.BlockSpec(memory_space=pltpu.VMEM)
    half = jax.ShapeDtypeStruct((2, tokens, width), bf16)
    return pl.pallas_call(
        functools.partial(token_grad_kernel, 256),
        out_shape=(half, half),
        in_specs=[vmem] * 2,
        out_specs=(vmem, vmem),
        compiler_params=pltpu.CompilerParams(vmem_limit_bytes=48 << 20),
        cost_estimate=pl.CostEstimate(flops=6 * 10**9, bytes_accessed=10**7, transcendentals=0),
        name="token_grads",
    )(gq, slab)


def slab_grad_kernel(item_of, items, *refs):
    xs, gq_ref, sums_ref, part_refs, total = refs[:4], refs[4], refs[5], refs[6 : 6 + items], refs[6 + items]
    item = item_of()
    tokens, width = xs[0].shape
    rows = width // items
    tile = 256
    for t in range(4):

        def body(r, _):
            at = pl.multiple_of(r * tile, tile)
            part = lax.dot_general(
                xs[t][:, pl.ds(at, tile)], gq_ref[t * tokens : (t + 1) * tokens, :], TN, preferred_element_type=f32
            )
            if t == 0:
                total[pl.ds(at, tile), :] = part
            else:
                total[pl.ds(at, tile), :] += part
            return 0

        lax.fori_loop(0, width // tile, body, 0)
    for k in range(items):
        part_refs[k][...] = total[pl.ds(pl.multiple_of((item ^ k) * rows, 8), rows), :].astype(bf16)

    def sums(r, total_row):
        at = pl.multiple_of(r * tile, tile)
        return total_row + jnp.sum(gq_ref[pl.ds(at, tile), :].astype(f32), 0, keepdims=True)

    sums_ref[...] = lax.fori_loop(0, gq_ref.shape[0] // tile, sums, jnp.zeros((1, gq_ref.shape[1]), f32))


def slab_grads(item_of, xs, gq, items):
    tokens, width = xs[0].shape
    columns = gq.shape[1]
    vmem = pl.BlockSpec(memory_space=pltpu.VMEM)
    return pl.pallas_call(
        functools.partial(slab_grad_kernel, item_of, items),
        out_shape=(jax.ShapeDtypeStruct((1, columns), f32),)
        + tuple([jax.ShapeDtypeStruct((width // items, columns), bf16)] * items),
        in_specs=[vmem] * 5,
        out_specs=tuple([vmem] * (1 + items)),
        scratch_shapes=[pltpu.VMEM((width, columns), f32)],
        compiler_params=pltpu.CompilerParams(vmem_limit_bytes=48 << 20),
        cost_estimate=pl.CostEstimate(flops=6 * 10**9, bytes_accessed=10**7, transcendentals=0),
        name="slab_grads",
    )(*xs, gq)


def gelu_parts(u):
    half = 0.5 * (1.0 + lax.erf(u * 0.7071067811865476))
    return u * half, half + u * jnp.exp(-0.5 * u * u) * 0.3989422804014327


def middle_kernel(
    dims, where_am_i, own_ref, far_ref, near_ref, x_ref, mixed_ref, dout_ref, small_ref,
    out_ref, first_ref, gmix_ref, grads_ref, sgrad_ref,
    wo_v, wu_v, wd_v, xhat_v, hid_v, act_v, slope_v, ffn_v, gffn_v, gup_v, dhid_v, rstd_v, stage_d, stage_u, stage_o,
    wsem, gsem,
):
    items, rows, width, tile = dims
    item, place = where_am_i()
    third = rows // 3
    tokens = x_ref.shape[0]
    tiles = tokens // tile
    group_rows = width // 4
    sources = (own_ref, near_ref.at[0], far_ref, near_ref.at[1])

    def load(which):
        for t in range(4):
            q = place ^ t
            for k in range(items):
                j = item ^ k
                src = sources[t].at[k]
                if which == 0:
                    pltpu.make_async_copy(src.at[pl.ds(2 * rows, third)], wo_v.at[j, pl.ds(pl.multiple_of(q * third, 16), third)], wsem.at[0]).start()
                elif which == 1:
                    pltpu.make_async_copy(src.at[pl.ds(0, rows)], wu_v.at[q, pl.ds(pl.multiple_of(j * rows, 16), rows)], wsem.at[1]).start()
                else:
                    pltpu.make_async_copy(src.at[pl.ds(rows, rows)], wd_v.at[j // 2, pl.ds(pl.multiple_of((j % 2) * 4 * rows + q * rows, 16), rows)], wsem.at[2]).start()

    for which in range(3):
        load(which)

    def rowsl(r):
        return pl.ds(pl.multiple_of(r * tile, tile), tile)

    def wo_rows(q):
        return jnp.concatenate([wo_v[2 * q, 0:rows], wo_v[2 * q + 1, 0:rows]], 0)

    pltpu.make_async_copy(wo_v, wo_v, wsem.at[0]).wait()

    def norm_one(r, _):
        rs = rowsl(r)
        total = x_ref[rs, :].astype(f32) + small_ref[4:5, :]
        for t in range(4):
            total += jnp.dot(mixed_ref[t, rs, :], wo_rows(place ^ t), preferred_element_type=f32)
        centered = total - jnp.mean(total, -1, keepdims=True)
        rstd = lax.rsqrt(jnp.mean(centered * centered, -1, keepdims=True) + norm_epsilon)
        xhat = centered * rstd
        xhat_v[rs, :] = xhat
        rstd_v[rs, :] = jnp.broadcast_to(rstd, (tile, 128))
        hid_v[rs, :] = (xhat * small_ref[0:1, :] + small_ref[1:2, :]).astype(bf16)
        return 0

    lax.fori_loop(0, tiles, norm_one, 0)
    pltpu.make_async_copy(wu_v, wu_v, wsem.at[1]).wait()
    pltpu.make_async_copy(wd_v, wd_v, wsem.at[2]).wait()

    def ffn(n, _):
        p, r = n // tiles, n % tiles
        rs = rowsl(r)
        up = jnp.dot(hid_v[rs, :], wu_v[p], preferred_element_type=f32) + small_ref[pl.ds(8 + p, 1), :]
        act, slope = gelu_parts(up)
        act = act.astype(bf16)
        act_v[p, rs, :] = act
        slope_v[p, rs, :] = slope
        part = jnp.dot(act, wd_v[p], preferred_element_type=f32)

        @pl.when(p == 0)
        def _():
            ffn_v[rs, :] = part

        @pl.when(p > 0)
        def _():
            ffn_v[rs, :] += part

        return 0

    lax.fori_loop(0, 4 * tiles, ffn, 0)
    zero = jnp.zeros((1, width), f32)

    def norm_two(r, sums):
        rs = rowsl(r)
        dg, db, dd = sums
        hidden = xhat_v[rs, :] * small_ref[0:1, :] + small_ref[1:2, :]
        total = hidden + (ffn_v[rs, :] + small_ref[7:8, :])
        centered = total - jnp.mean(total, -1, keepdims=True)
        rstd = lax.rsqrt(jnp.mean(centered * centered, -1, keepdims=True) + norm_epsilon)
        xhat = centered * rstd
        out_ref[rs, :] = (xhat * small_ref[5:6, :] + small_ref[6:7, :]).astype(bf16)
        dy = dout_ref[rs, :].astype(f32)
        dg = dg + jnp.sum(dy * xhat, 0, keepdims=True)
        db = db + jnp.sum(dy, 0, keepdims=True)
        dx = dy * small_ref[5:6, :]
        dx = rstd * (dx - jnp.mean(dx, -1, keepdims=True) - xhat * jnp.mean(dx * xhat, -1, keepdims=True))
        dhid_v[rs, :] = dx
        short = dx.astype(bf16)
        gffn_v[rs, :] = short
        dd = dd + jnp.sum(short.astype(f32), 0, keepdims=True)
        return dg, db, dd

    dg2, db2, dd = lax.fori_loop(0, tiles, norm_two, (zero, zero, zero))
    sgrad_ref[...] = jnp.zeros_like(sgrad_ref)
    sgrad_ref[5:6, :] = dg2
    sgrad_ref[6:7, :] = db2
    sgrad_ref[7:8, :] = dd
    nt = (((1,), (1,)), ((), ()))
    tn = (((0,), (0,)), ((), ()))
    pieces = width // tile

    def wait_stage(ref, sem):
        pltpu.make_async_copy(ref, ref, sem).wait()

    def back(p, _):
        def back_rows(r, total):
            rs = rowsl(r)
            ga = lax.dot_general(gffn_v[rs, :], wd_v[p], nt, preferred_element_type=f32)
            gup = (ga * slope_v[p, rs, :]).astype(bf16)
            gup_v[rs, :] = gup
            dhid_v[rs, :] += lax.dot_general(gup, wu_v[p], nt, preferred_element_type=f32)
            return total + jnp.sum(gup.astype(f32), 0, keepdims=True)

        sgrad_ref[pl.ds(8 + p, 1), :] = lax.fori_loop(0, tiles, back_rows, zero)

        @pl.when(p > 0)
        def _():
            wait_stage(stage_d, gsem.at[0])
            wait_stage(stage_u, gsem.at[1])

        for m in range(pieces):
            cs = slice(m * tile, (m + 1) * tile)
            stage_d[cs, :] = lax.dot_general(act_v[p, :, cs], gffn_v[...], tn, preferred_element_type=f32).astype(bf16)
        for jj in range(2):
            for q in range(4):
                src = stage_d.at[pl.ds(jj * 4 * rows + q * rows, rows)]
                dst = grads_ref.at[q ^ place, (2 * p + jj) ^ item, pl.ds(rows, rows)]
                pltpu.make_async_copy(src, dst, gsem.at[0]).start()
        for m in range(pieces):
            cs = slice(m * tile, (m + 1) * tile)
            stage_u[cs, :] = lax.dot_general(hid_v[:, cs], gup_v[...], tn, preferred_element_type=f32).astype(bf16)
        for j in range(items):
            src = stage_u.at[pl.ds(j * rows, rows)]
            dst = grads_ref.at[p ^ place, j ^ item, pl.ds(0, rows)]
            pltpu.make_async_copy(src, dst, gsem.at[1]).start()
        return 0

    lax.fori_loop(0, 4, back, 0)

    def norm_back(r, sums):
        rs = rowsl(r)
        dg, db, da = sums
        dy = dhid_v[rs, :]
        xhat = xhat_v[rs, :]
        dg = dg + jnp.sum(dy * xhat, 0, keepdims=True)
        db = db + jnp.sum(dy, 0, keepdims=True)
        dx = dy * small_ref[0:1, :]
        dx = rstd_v[rs, 0:1] * (dx - jnp.mean(dx, -1, keepdims=True) - xhat * jnp.mean(dx * xhat, -1, keepdims=True))
        first_ref[rs, :] = dx
        short = dx.astype(bf16)
        hid_v[rs, :] = short
        da = da + jnp.sum(short.astype(f32), 0, keepdims=True)
        for t in range(4):
            gmix_ref[t, rs, :] = lax.dot_general(short, wo_rows(place ^ t), nt, preferred_element_type=f32).astype(bf16)
        return dg, db, da

    dg1, db1, da = lax.fori_loop(0, tiles, norm_back, (zero, zero, zero))
    sgrad_ref[0:1, :] = dg1
    sgrad_ref[1:2, :] = db1
    sgrad_ref[4:5, :] = da
    for j in range(items):
        stage_o[j, pl.ds(rows, third)] = jnp.zeros((third, width), bf16)
    for t in range(4):
        q = place ^ t
        part = lax.dot_general(mixed_ref[t], hid_v[...], tn, preferred_element_type=f32).astype(bf16)
        stage_o[2 * q, pl.ds(0, rows)] = part[:rows]
        stage_o[2 * q + 1, pl.ds(0, rows)] = part[rows:]
    for j in range(items):
        for u in range(4):
            src = stage_o.at[j, pl.ds(u * third, third)]
            dst = grads_ref.at[u ^ place, j ^ item, pl.ds(2 * rows, third)]
            pltpu.make_async_copy(src, dst, gsem.at[2]).start()
    wait_stage(stage_d, gsem.at[0])
    wait_stage(stage_u, gsem.at[1])
    wait_stage(stage_o, gsem.at[2])


def middle(where_am_i, own, far, near, x, mixed, dout, small, tile=256):
    items, quarter, width = own.shape
    rows = quarter * 3 // 7
    tokens = x.shape[0]
    any_space = pl.BlockSpec(memory_space=pl.ANY)
    vmem = pl.BlockSpec(memory_space=pltpu.VMEM)
    square = (tokens, width)
    return pl.pallas_call(
        functools.partial(middle_kernel, (items, rows, width, tile), where_am_i),
        out_shape=(
            jax.ShapeDtypeStruct(square, bf16),
            jax.ShapeDtypeStruct(square, f32),
            jax.ShapeDtypeStruct((4, tokens, width // 4), bf16),
            jax.ShapeDtypeStruct((4, items, quarter, width), bf16),
            jax.ShapeDtypeStruct(small.shape, f32),
        ),
        in_specs=[any_space] * 3 + [vmem] * 4,
        out_specs=(vmem, vmem, vmem, any_space, vmem),
        scratch_shapes=[
            pltpu.VMEM((items, 4 * rows // 3, width), bf16),
            pltpu.VMEM((4, width, width), bf16),
            pltpu.VMEM((4, width, width), bf16),
            pltpu.VMEM(square, f32),
            pltpu.VMEM(square, bf16),
            pltpu.VMEM((4, tokens, width), bf16),
            pltpu.VMEM((4, tokens, width), f32),
            pltpu.VMEM(square, f32),
            pltpu.VMEM(square, bf16),
            pltpu.VMEM(square, bf16),
            pltpu.VMEM(square, f32),
            pltpu.VMEM((tokens, 128), f32),
            pltpu.VMEM((width, width), bf16),
            pltpu.VMEM((width, width), bf16),
            pltpu.VMEM((items, 4 * rows // 3, width), bf16),
            pltpu.SemaphoreType.DMA((3,)),
            pltpu.SemaphoreType.DMA((3,)),
        ],
        compiler_params=pltpu.CompilerParams(vmem_limit_bytes=60 << 20),
        cost_estimate=pl.CostEstimate(flops=60 * 10**9, bytes_accessed=10**7, transcendentals=0),
        name="middle",
    )(own, far, near, x, mixed, dout, small)


def swap(values, axis, bit):
    size = lax.axis_size(axis)
    return lax.ppermute(values, axis, [(i, i ^ bit) for i in range(size)])


def take(values, at, dim):
    return lax.dynamic_index_in_dim(values, at, dim, keepdims=False)


def add_short(a, b):
    return (a.astype(f32) + b.astype(f32)).astype(bf16)


def in_order(pieces, place):
    pieces = pieces.reshape(2, 2, *pieces.shape[1:])
    pieces = jnp.where(place % 2 == 1, pieces[:, ::-1], pieces)
    pieces = jnp.where(place // 2 == 1, pieces[::-1], pieces)
    return pieces.reshape(4, *pieces.shape[2:])


def from_group(shard):
    pair = jnp.stack([shard, swap(shard, "seq", 2)])
    near = swap(pair, "seq", 1)
    return jnp.stack([pair[0], near[0], pair[1], near[1]])


def layer_norm(values, gain, bias):
    average = jnp.mean(values, -1, keepdims=True)
    centered = values - average
    spread = jnp.mean(centered * centered, -1, keepdims=True)
    return centered * lax.rsqrt(spread + norm_epsilon) * gain + bias


def exact_gelu(values):
    return jax.nn.gelu(values, approximate=False)


def packed_columns(own):
    heads = own.shape[2]
    cols = []
    for h in range(heads):
        pair = [own[:, 2, h], own[:, 1, h]]
        cols += pair if h % 2 == 0 else pair[::-1]
    for p in range((heads + 1) // 2):
        odd = own[:, 0, 2 * p + 1] if 2 * p + 1 < heads else jnp.zeros_like(own[:, 0, 0])
        cols += [odd * HD**-0.5, own[:, 0, 2 * p] * HD**-0.5]
    return jnp.concatenate(cols, -1)


def natural_columns(values, heads):
    parts = [[], [], []]
    for h in range(heads):
        first, second = values[:, h * 128 : h * 128 + HD], values[:, h * 128 + HD : h * 128 + 128]
        base = (heads + h // 2) * 128
        if h % 2 == 0:
            parts[2].append(first)
            parts[1].append(second)
            parts[0].append(values[:, base + HD : base + 128] * HD**-0.5)
        else:
            parts[1].append(first)
            parts[2].append(second)
            parts[0].append(values[:, base : base + HD] * HD**-0.5)
    return jnp.concatenate(parts[0] + parts[1] + parts[2], -1)


def adam_update(weight, first, second, grad, decay, rate):
    first_new = beta_first * first + (1.0 - beta_first) * grad
    second_new = beta_second * second + (1.0 - beta_second) * grad * grad
    first_hat = first_new / (1.0 - beta_first**ADAM_STEP)
    second_hat = second_new / (1.0 - beta_second**ADAM_STEP)
    weight_new = weight - rate * (
        first_hat / (jnp.sqrt(second_hat) + adam_epsilon) + decay * weight
    )
    return (weight_new, first_new, second_new)


def on_device(
    inputs,
    d_output,
    glob_count,
    glob_pos,
    rand_blocks,
    w_qkv,
    w_out,
    w_up,
    w_down,
    small_params,
    first_qkv,
    second_qkv,
    first_out,
    second_out,
    first_up,
    second_up,
    first_down,
    second_down,
    first_small,
    second_small,
):
    items_n, tok_rows, width = inputs.shape
    groups = lax.axis_size("seq")
    items = lax.axis_size("item")
    place = lax.axis_index("seq")
    heads = rand_blocks.shape[1]
    rows = w_out.shape[0]
    third = rows // 3

    def where_am_i():
        return lax.axis_index("item"), lax.axis_index("seq")

    def item_of():
        return lax.axis_index("item")

    own = take(w_qkv.reshape(-1, 3, groups, heads, HD), place, 2)
    piece = packed_columns(own).astype(bf16)
    pieces = [piece] + [swap(piece, "item", k) for k in range(1, items)]
    tokens_b = inputs.reshape(tok_rows, width)
    tokens_far = swap(tokens_b, "seq", 2)
    tokens_near = swap(tokens_b, "seq", 1)
    tokens_cross = swap(tokens_far, "seq", 1)
    xs = [tokens_b, tokens_near, tokens_far, tokens_cross]
    quarter = jnp.concatenate(
        [
            take(w_up.reshape(rows, 4, width), place, 1),
            take(w_down.reshape(4, rows, width), place, 0),
            take(w_out.reshape(3, third, width), jnp.minimum(place, 2), 0),
        ],
        0,
    ).astype(bf16)
    w_parts = [quarter] + [swap(quarter, "item", k) for k in range(1, items)]
    bias3 = jnp.stack([small_params[2], jnp.zeros((width,), f32), small_params[3]])
    slab_bias = packed_columns(take(bias3.reshape(1, 3, groups, heads, HD), place, 2))
    qkv, slab = project(item_of, xs, pieces, slab_bias)
    w_parts, qkv = lax.optimization_barrier((w_parts, qkv))
    idx, bias, gl = slots(glob_count[0], glob_pos[0], rand_blocks[0], place)
    mix2, mix3, lse_far = attn_fwd(idx, gl, qkv, bias, heads, 2, 2)
    w_parts, mix2, mix3, qkv = lax.optimization_barrier((w_parts, mix2, mix3, qkv))
    w_own = jnp.stack(w_parts)
    w_far = swap(w_own, "seq", 2)
    mix0, mix1, lse_near = attn_fwd(idx, gl, qkv, bias, heads, 0, 2)
    w_own, w_far, mix0, mix1, mix2, mix3 = lax.optimization_barrier(
        (w_own, w_far, mix0, mix1, mix2, mix3)
    )
    w_near = swap(jnp.stack([w_own, w_far]), "seq", 1)
    mixed = jnp.stack([mix0, swap(mix1, "seq", 1), swap(mix2, "seq", 2), swap(mix3, "seq", 3)])
    outputs, grad_first, grad_mixed, parts, small_part = middle(
        where_am_i, w_own, w_far, w_near, tokens_b, mixed, d_output.reshape(tok_rows, width), small_params
    )
    grads_in = [grad_mixed[0]] + [swap(grad_mixed[t], "seq", t) for t in range(1, 4)]
    parts = parts.reshape(2, 2, *parts.shape[1:])
    pair_sum = add_short(parts[:, 0], swap(parts[:, 1], "seq", 1))
    far_half = swap(pair_sum[1], "seq", 2)
    acc, dq_near = attn_bwd(idx, gl, qkv, bias, grads_in[:2], lse_near, heads, 0, (), False)
    far_half, acc, dq_near = lax.optimization_barrier((far_half, acc, dq_near))
    far_sum = add_short(pair_sum[0], far_half)
    received = [swap(far_sum[k], "item", k) for k in range(1, items)]
    grad_qkv = attn_bwd(idx, gl, qkv, bias, grads_in[2:], lse_far, heads, 2, (acc, dq_near), True)
    received, far_sum, grad_qkv = lax.optimization_barrier((received, far_sum, grad_qkv))
    shard = far_sum[0].astype(f32)
    for k in range(1, items):
        shard = shard + received[k - 1].astype(f32)
    small16 = jnp.pad(small_part, ((0, 4), (0, 0)))
    grad_inputs, slab_group, small_total, squares = tail(xs, grad_qkv, slab, grad_first, small16, shard, items, heads * 128)
    slab_group = in_order(slab_group, place)
    lines = natural_columns(slab_group[:, rows] + slab_group[:, rows + 1], heads).reshape(groups, 3, heads * HD)
    lines = lines.transpose(1, 0, 2).reshape(3, width)
    small_total = small_total[:12].at[2].set(lines[0]).at[3].set(lines[2])
    matrix_squares = squares[0, 0]
    group = in_order(from_group(shard), place)
    shard_up = group[:, :rows].transpose(1, 0, 2).reshape(rows, 4 * width)
    shard_down = group[:, rows : 2 * rows].reshape(4 * rows, width)
    shard_out = group[:3, 2 * rows :].reshape(rows, width)
    shard_qkv = (
        natural_columns(slab_group[:, :rows].reshape(groups * rows, -1), heads)
        .reshape(groups, rows, 3, heads * HD)
        .transpose(1, 2, 0, 3)
        .reshape(rows, 3 * width)
    )
    grad_norm = jnp.sqrt(matrix_squares + jnp.sum(small_total * small_total))
    factor = jnp.minimum(1.0, clip_level / (grad_norm + 1e-06))
    new_qkv = adam_update(
        w_qkv, first_qkv, second_qkv, shard_qkv * factor, weight_decay, learn_rate
    )
    new_out = adam_update(
        w_out, first_out, second_out, shard_out * factor, weight_decay, learn_rate
    )
    new_up = adam_update(w_up, first_up, second_up, shard_up * factor, weight_decay, learn_rate)
    new_down = adam_update(
        w_down, first_down, second_down, shard_down * factor, weight_decay, learn_rate
    )
    new_small = adam_update(
        small_params, first_small, second_small, small_total * factor, 0.0, small_rate
    )
    return (
        outputs.astype(bf16).reshape(items_n, tok_rows, width),
        grad_inputs.reshape(items_n, tok_rows, width),
        grad_norm,
        new_qkv[0],
        new_qkv[1],
        new_qkv[2],
        new_out[0],
        new_out[1],
        new_out[2],
        new_up[0],
        new_up[1],
        new_up[2],
        new_down[0],
        new_down[1],
        new_down[2],
        new_small[0],
        new_small[1],
        new_small[2],
    )


def on_device_many(
    inputs,
    d_output,
    glob_count,
    glob_pos,
    rand_blocks,
    w_qkv,
    w_out,
    w_up,
    w_down,
    small_params,
    first_qkv,
    second_qkv,
    first_out,
    second_out,
    first_up,
    second_up,
    first_down,
    second_down,
    first_small,
    second_small,
):
    items_n, tok_rows, width = inputs.shape
    groups = lax.axis_size("seq")
    place = lax.axis_index("seq")
    heads = rand_blocks.shape[1]
    row_count = tok_rows

    own = lax.dynamic_index_in_dim(
        w_qkv.reshape(-1, 3, groups, heads, HD), place, 2, keepdims=False
    )
    slab = lax.all_gather(packed_columns(own).astype(bf16), "item", axis=0, tiled=True)
    full_out, full_up, full_down = (
        lax.all_gather(w_out.astype(bf16), "item", axis=0, tiled=True),
        lax.all_gather(w_up.astype(bf16), "item", axis=0, tiled=True),
        lax.all_gather(w_down.astype(bf16), "item", axis=0, tiled=True),
    )
    bias3 = jnp.stack([small_params[2], jnp.zeros((width,), f32), small_params[3]])
    own_bias = lax.dynamic_index_in_dim(
        bias3.reshape(1, 3, groups, heads, HD), place, 2, keepdims=False
    )
    slab_bias = packed_columns(own_bias)
    tokens_b = inputs.reshape(tok_rows, width)
    tokens_all = lax.all_gather(tokens_b, "seq", axis=0, tiled=True)
    tokens_f = tokens_b.astype(f32)
    qkv = (jnp.dot(tokens_all, slab, preferred_element_type=f32) + slab_bias).astype(bf16)
    idx, bias, gl = slots(glob_count[0], glob_pos[0], rand_blocks[0], jnp.int32(0))
    *mixed_parts, lse = attn_fwd(idx, gl, qkv, bias, heads, 0, 4)
    mixed_heads = jnp.concatenate(mixed_parts, 0)
    mixed = lax.all_to_all(mixed_heads, "seq", split_axis=0, concat_axis=1, tiled=True)
    attn_out = jnp.dot(mixed, full_out, preferred_element_type=f32) + small_params[4]
    hidden, norm_one_back = jax.vjp(
        layer_norm, tokens_f + attn_out, small_params[0], small_params[1]
    )
    hidden_b = hidden.astype(bf16)
    up_pre = jnp.dot(hidden_b, full_up, preferred_element_type=f32) + small_params[8:12].reshape(-1)
    active, gelu_back = jax.vjp(exact_gelu, up_pre)
    active_b = active.astype(bf16)
    ffn_out = jnp.dot(active_b, full_down, preferred_element_type=f32) + small_params[7]
    outputs, norm_two_back = jax.vjp(layer_norm, hidden + ffn_out, small_params[5], small_params[6])
    grad_second, grad_gain_two, grad_bias_two = norm_two_back(
        d_output.reshape(row_count, width).astype(f32)
    )
    grad_ffn = grad_second.astype(bf16)
    grad_w_down = jnp.einsum("rf,rd->fd", active_b, grad_ffn, preferred_element_type=f32)
    grad_active = jnp.einsum("rd,fd->rf", grad_ffn, full_down, preferred_element_type=f32)
    (grad_up_pre,) = gelu_back(grad_active)
    grad_up_b = grad_up_pre.astype(bf16)
    grad_w_up = jnp.einsum("rd,rf->df", hidden_b, grad_up_b, preferred_element_type=f32)
    grad_hidden = grad_second + jnp.einsum(
        "rf,df->rd", grad_up_b, full_up, preferred_element_type=f32
    )
    grad_first, grad_gain_one, grad_bias_one = norm_one_back(grad_hidden)
    grad_attn = grad_first.astype(bf16)
    grad_w_out = jnp.einsum("rm,rd->md", mixed, grad_attn, preferred_element_type=f32)
    grad_mixed = jnp.einsum("rd,md->rm", grad_attn, full_out, preferred_element_type=f32).astype(
        bf16
    )
    grad_heads = lax.all_to_all(grad_mixed, "seq", split_axis=1, concat_axis=0, tiled=True)
    grads_in = [grad_heads[t * tok_rows : (t + 1) * tok_rows] for t in range(4)]
    grad_qkv = attn_bwd(idx, gl, qkv, bias, grads_in, lse, heads, 0, (), True)
    grad_slab = jnp.einsum("rd,re->de", tokens_all, grad_qkv, preferred_element_type=f32)
    grad_tokens = jnp.einsum("re,de->rd", grad_qkv, slab, preferred_element_type=f32).astype(bf16)
    grad_inputs = grad_first + lax.psum_scatter(
        grad_tokens, "seq", scatter_dimension=0, tiled=True
    ).astype(f32)
    slab_sum = natural_columns(jnp.sum(grad_qkv.astype(f32), 0)[None], heads)[0]
    bias_grads = lax.dynamic_update_index_in_dim(
        jnp.zeros((3, groups, heads * HD), f32), slab_sum.reshape(3, heads * HD), place, 1
    ).reshape(3, width)
    small_rows = jnp.stack(
        [
            grad_gain_one,
            grad_bias_one,
            bias_grads[0],
            bias_grads[2],
            jnp.sum(grad_attn.astype(f32), 0),
            grad_gain_two,
            grad_bias_two,
            jnp.sum(grad_ffn.astype(f32), 0),
        ]
    )
    small_part = jnp.concatenate(
        [small_rows, jnp.sum(grad_up_b.astype(f32), 0).reshape(4, width)], 0
    )
    small_total = lax.psum(small_part, ("item", "seq"))
    shard_down = lax.psum_scatter(grad_w_down.astype(bf16), "item", scatter_dimension=0, tiled=True)
    shard_up = lax.psum_scatter(grad_w_up.astype(bf16), "item", scatter_dimension=0, tiled=True)
    shard_out = lax.psum_scatter(grad_w_out.astype(bf16), "item", scatter_dimension=0, tiled=True)
    shard_slab = lax.psum_scatter(grad_slab.astype(bf16), "item", scatter_dimension=0, tiled=True)
    shard_slab = natural_columns(shard_slab.astype(f32), heads).reshape(-1, 3, 1, heads * HD)
    shard_qkv = lax.all_gather(shard_slab, "seq", axis=2, tiled=True).reshape(-1, 3 * width)
    shard_out, shard_up, shard_down = lax.psum(
        (shard_out.astype(f32), shard_up.astype(f32), shard_down.astype(f32)), "seq"
    )
    local_squares = (
        jnp.sum(shard_qkv * shard_qkv)
        + jnp.sum(shard_out * shard_out)
        + jnp.sum(shard_up * shard_up)
        + jnp.sum(shard_down * shard_down)
    )
    matrix_squares = lax.psum(local_squares, "item")
    grad_norm = jnp.sqrt(matrix_squares + jnp.sum(small_total * small_total))
    factor = jnp.minimum(1.0, clip_level / (grad_norm + 1e-06))
    new_qkv = adam_update(
        w_qkv, first_qkv, second_qkv, shard_qkv * factor, weight_decay, learn_rate
    )
    new_out = adam_update(
        w_out, first_out, second_out, shard_out * factor, weight_decay, learn_rate
    )
    new_up = adam_update(w_up, first_up, second_up, shard_up * factor, weight_decay, learn_rate)
    new_down = adam_update(
        w_down, first_down, second_down, shard_down * factor, weight_decay, learn_rate
    )
    new_small = adam_update(
        small_params, first_small, second_small, small_total * factor, 0.0, small_rate
    )
    return (
        outputs.astype(bf16).reshape(items_n, tok_rows, width),
        grad_inputs.reshape(items_n, tok_rows, width),
        grad_norm,
        new_qkv[0],
        new_qkv[1],
        new_qkv[2],
        new_out[0],
        new_out[1],
        new_out[2],
        new_up[0],
        new_up[1],
        new_up[2],
        new_down[0],
        new_down[1],
        new_down[2],
        new_small[0],
        new_small[1],
        new_small[2],
    )


def solution(mesh):
    few = mesh.shape["item"] == 8 and mesh.shape["seq"] == 4
    return jax.shard_map(
        on_device if few else on_device_many,
        mesh=mesh,
        in_specs=(
            P("item", "seq", None),
            P("item", "seq", None),
            P("item"),
            P("item", None),
            P("item", "seq", None, None),
            P("item", None),
            P("item", None),
            P("item", None),
            P("item", None),
            P(),
            P("item", None),
            P("item", None),
            P("item", None),
            P("item", None),
            P("item", None),
            P("item", None),
            P("item", None),
            P("item", None),
            P(),
            P(),
        ),
        out_specs=(
            P("item", "seq", None),
            P("item", "seq", None),
            P(),
            P("item", None),
            P("item", None),
            P("item", None),
            P("item", None),
            P("item", None),
            P("item", None),
            P("item", None),
            P("item", None),
            P("item", None),
            P("item", None),
            P("item", None),
            P("item", None),
            P(),
            P(),
            P(),
        ),
        check_vma=False,
    )
```

```python
import functools

import jax
import jax.numpy as jnp
from jax import lax
from jax.experimental import pallas as pl
from jax.experimental.pallas import tpu as pltpu
from jax.sharding import PartitionSpec as P

ADAM_STEP = 10
norm_epsilon = 1e-06
beta_first = 0.9
beta_second = 0.999
adam_epsilon = 1e-08
learn_rate = 0.1
small_rate = 0.5
weight_decay = 0.01
clip_level = 1.0


def adam_update(weight, first, second, grad, decay, rate):
    first_new = beta_first * first + (1.0 - beta_first) * grad
    second_new = beta_second * second + (1.0 - beta_second) * grad * grad
    first_hat = first_new / (1.0 - beta_first**ADAM_STEP)
    second_hat = second_new / (1.0 - beta_second**ADAM_STEP)
    weight_new = weight - rate * (
        first_hat / (jnp.sqrt(second_hat) + adam_epsilon) + decay * weight
    )
    return (weight_new, first_new, second_new)


HD = 64
BL = 64
NEG = -1e30
bf16 = jnp.bfloat16
f32 = jnp.float32
NT = (((1,), (1,)), ((), ()))
TN = (((0,), (0,)), ((), ()))


def slots(count, positions, table, place):
    heads, nblocks, picks = table.shape
    chunk = nblocks // 4
    globals_n = positions.shape[0]
    here = jnp.arange(nblocks, dtype=jnp.int32)

    def turned(b):
        return ((b // chunk) ^ place) * chunk + b % chunk

    block = turned(here)
    rows = table.reshape(heads, 2, 2, chunk, picks)
    rows = jnp.where(place % 2 == 1, rows[:, :, ::-1], rows)
    rows = jnp.where(place // 2 == 1, rows[:, ::-1], rows).reshape(heads, nblocks, picks)
    window = jnp.stack([block - 1, block, block + 1], -1)
    active = jnp.arange(globals_n, dtype=jnp.int32) < count
    parts = jnp.concatenate(
        [
            jnp.broadcast_to(window[None], (heads, nblocks, 3)),
            jnp.broadcast_to(jnp.where(active, positions, -1)[None, None], (heads, nblocks, globals_n)),
            rows,
        ],
        -1,
    )
    count_slots = 3 + globals_n + picks
    valid = (parts >= 0) & (parts < nblocks)
    same = parts[..., :, None] == parts[..., None, :]
    earlier = jnp.arange(count_slots)[:, None] > jnp.arange(count_slots)[None, :]
    repeated = jnp.any(same & earlier, -1)
    is_global = jnp.any((positions[None, :] == block[:, None]) & active[None], -1)
    valid = valid & ~repeated & ~is_global[None, :, None]
    idx = turned(jnp.clip(parts, 0, nblocks - 1))
    bias = jnp.where(valid, 0.0, NEG).astype(f32)
    bias = jnp.broadcast_to(bias[..., None], (heads, nblocks, count_slots, BL))
    glob = jnp.concatenate([count[None], turned(positions)])
    return idx.reshape(-1), bias.reshape(heads * nblocks, count_slots * BL), glob


def low_lanes(rows):
    return lax.broadcasted_iota(jnp.int32, (rows, 2 * HD), 1) < HD


def pick(block, keep_low):
    low = low_lanes(block.shape[0])
    return jnp.where(low if keep_low else ~low, block, jnp.zeros_like(block))


def fwd_kernel(dims, idx_ref, gl_ref, qkv_ref, bias_ref, *rest):
    heads, nblocks, slots_n, first, parts, chunk, wide = dims
    out_refs, lse_ref, sbuf, s_v, e_v, l_v, out_v = rest[:parts], rest[parts], *rest[parts + 1 :]
    n = nblocks * BL
    lane = lax.broadcasted_iota(jnp.int32, (BL, 128), 1)

    def finish(row, outs, lses):
        low = low_lanes(BL)
        for p in range((heads + 1) // 2):
            if 2 * p + 1 < heads:
                both = jnp.where(low, outs[2 * p], outs[2 * p + 1])
                out_v[pl.ds(row, BL), p * 128 : (p + 1) * 128] = both.astype(bf16)
            else:
                out_v[pl.ds(row, BL), p * 128 : p * 128 + HD] = outs[2 * p][:, :HD].astype(bf16)
        total = jnp.zeros((BL, 128), f32)
        for h in range(heads):
            total = jnp.where(lane == h, lses[h], total)
        lse_ref[pl.ds(row, BL), :] = total

    def queries(r, h):
        return pick(qkv_ref[pl.ds(r, BL), (heads + h // 2) * 128 : (heads + h // 2 + 1) * 128], h % 2 == 1)

    blocks = parts * chunk

    def clamp(b):
        return jnp.minimum(jnp.maximum(b, 0), blocks - 1)

    def gathered(a, h):
        base = (h * nblocks + a) * slots_n
        return jnp.concatenate(
            [
                qkv_ref[pl.ds(pl.multiple_of(idx_ref[base + j] * BL, BL), BL), h * 128 : (h + 1) * 128]
                for j in range(slots_n)
            ],
            0,
        )

    def body(b, _):
        last, now, new = clamp(b - 2), clamp(b - 1), clamp(b)
        outs, lses = [], []
        for h in range(heads):
            o = jnp.dot(e_v[h], gathered(first + last, h), preferred_element_type=f32)
            outs.append(o)
            lses.append(l_v[h])
        finish(pl.multiple_of(last * BL, BL), outs, lses)
        for h in range(heads):
            s = s_v[h] + bias_ref[pl.ds(h * nblocks + first + now, 1), :]
            m = jnp.max(s, -1, keepdims=True)
            e = jnp.exp(s - m)
            l = jnp.sum(e, -1, keepdims=True)
            e_v[h] = (e * (1.0 / l)).astype(bf16)
            l_v[h] = jnp.broadcast_to(m + jnp.log(l), (BL, 128))
        for h in range(heads):
            a = first + new
            s_v[h] = lax.dot_general(
                queries(pl.multiple_of(a * BL, BL), h), gathered(a, h), NT, preferred_element_type=f32
            )
        return 0

    lax.fori_loop(0, blocks + 2, body, 0)

    def whole_row(g, _):
        a = gl_ref[1 + g]
        local = a - first

        @pl.when((local >= 0) & (local < parts * chunk))
        def _():
            r = pl.multiple_of(a * BL, BL)
            outs, lses = [], []
            for h in range(heads):
                q = queries(r, h)
                m = None
                for c in range(n // wide):
                    cs = slice(c * wide, (c + 1) * wide)
                    s = lax.dot_general(q, qkv_ref[cs, h * 128 : (h + 1) * 128], NT, preferred_element_type=f32)
                    sbuf[h, :, cs] = s
                    mc = jnp.max(s, -1, keepdims=True)
                    m = mc if m is None else jnp.maximum(m, mc)
                l = 0.0
                for c in range(n // wide):
                    cs = slice(c * wide, (c + 1) * wide)
                    e = jnp.exp(sbuf[h, :, cs] - m)
                    sbuf[h, :, cs] = e
                    l = l + jnp.sum(e, -1, keepdims=True)
                inv = 1.0 / l
                o = 0.0
                for c in range(n // wide):
                    cs = slice(c * wide, (c + 1) * wide)
                    p = (sbuf[h, :, cs] * inv).astype(bf16)
                    o = o + jnp.dot(p, qkv_ref[cs, h * 128 : (h + 1) * 128], preferred_element_type=f32)
                outs.append(o)
                lses.append(m + jnp.log(l))
            finish(pl.multiple_of(local * BL, BL), outs, lses)

        return 0

    lax.fori_loop(0, gl_ref[0], whole_row, 0)
    for part in range(parts):
        out_refs[part][...] = out_v[part * chunk * BL : (part + 1) * chunk * BL, :]


def attn_fwd(idx, gl, qkv, bias, heads, first_part, parts):
    n = qkv.shape[0]
    nblocks = n // BL
    chunk = nblocks // 4
    slots_n = bias.shape[1] // BL
    vmem = pl.BlockSpec(memory_space=pltpu.VMEM)
    smem = pl.BlockSpec(memory_space=pltpu.SMEM)
    dims = (heads, nblocks, slots_n, first_part * chunk, parts, chunk, 512)
    return pl.pallas_call(
        functools.partial(fwd_kernel, dims),
        out_shape=tuple([jax.ShapeDtypeStruct((n // 4, heads * HD), bf16)] * parts)
        + (jax.ShapeDtypeStruct((parts * n // 4, 128), f32),),
        in_specs=[smem, smem, vmem, vmem],
        out_specs=tuple([vmem] * (parts + 1)),
        scratch_shapes=[
            pltpu.VMEM((heads, BL, n), f32),
            pltpu.VMEM((heads, BL, slots_n * BL), f32),
            pltpu.VMEM((heads, BL, slots_n * BL), bf16),
            pltpu.VMEM((heads, BL, 128), f32),
            pltpu.VMEM((parts * n // 4, heads * HD), bf16),
        ],
        compiler_params=pltpu.CompilerParams(vmem_limit_bytes=56 << 20),
        cost_estimate=pl.CostEstimate(flops=10 * parts * 10**9, bytes_accessed=10**7, transcendentals=0),
        name="attn_fwd",
    )(idx, gl, qkv, bias)


def bwd_kernel(dims, idx_ref, gl_ref, qkv_ref, bias_ref, *rest):
    heads, nblocks, slots_n, first, parts, chunk, wide, begin, end = dims
    g_refs, rest = rest[:parts], rest[parts:]
    lse_ref, rest = rest[0], rest[1:]
    if not begin:
        acc_in, dq_in, rest = rest[0], rest[1], rest[2:]
    if end:
        out_ref, acc, pbuf, dbuf, sd_v, w_v, g_v = rest
    else:
        acc, dq_ref, pbuf, dbuf, sd_v, w_v, g_v = rest
    n = nblocks * BL
    pairs = (heads + 1) // 2
    kvw = heads * 128

    def start(i, _):
        rr = pl.ds(pl.multiple_of(i * 256, 256), 256)
        if begin:
            acc[rr, :] = jnp.zeros((256, kvw), f32)
        else:
            acc[rr, :] = acc_in[rr, :]
        return 0

    lax.fori_loop(0, n // 256, start, 0)
    if end and not begin:
        out_ref[0 : first * BL, kvw:] = dq_in[...]

    for part in range(parts):
        g_v[part * chunk * BL : (part + 1) * chunk * BL, :] = g_refs[part][...]

    def grads(at, h):
        w = min(128, heads * HD - (h // 2) * 128)
        g = g_v[pl.ds(at, BL), (h // 2) * 128 : (h // 2) * 128 + w]
        if w < 128:
            return jnp.concatenate([g, jnp.zeros((BL, 128 - w), bf16)], 1)
        return pick(g, h % 2 == 0)

    def queries(r, h):
        return pick(qkv_ref[pl.ds(r, BL), (heads + h // 2) * 128 : (heads + h // 2 + 1) * 128], h % 2 == 1)

    def finish(r, dqs):
        low = low_lanes(BL)
        for p in range(pairs):
            high = dqs[2 * p]
            odd = dqs[2 * p + 1] if 2 * p + 1 < heads else jnp.zeros_like(high)
            both = jnp.where(low, odd, high).astype(bf16)
            if end:
                out_ref[pl.ds(r, BL), kvw + p * 128 : kvw + (p + 1) * 128] = both
            else:
                dq_ref[pl.ds(pl.multiple_of(r - first * BL, BL), BL), p * 128 : (p + 1) * 128] = both

    blocks = parts * chunk

    def clamp(b):
        return jnp.minimum(jnp.maximum(b, 0), blocks - 1)

    def slot_rows(a, h):
        base = (h * nblocks + a) * slots_n
        return [pl.multiple_of(idx_ref[base + j] * BL, BL) for j in range(slots_n)]

    def stacked(b, h):
        r = pl.multiple_of((first + b) * BL, BL)
        return jnp.concatenate([queries(r, h), grads(pl.multiple_of(b * BL, BL), h)], 0)

    def body(b, _):
        last, now, new = clamp(b - 2), clamp(b - 1), clamp(b)
        dqs = []
        for h in range(heads):
            hs = slice(h * 128, (h + 1) * 128)
            rows = slot_rows(first + last, h)
            kv = jnp.concatenate([qkv_ref[pl.ds(rows[j], BL), hs] for j in range(slots_n)], 0)
            dqs.append(jnp.dot(w_v[h, :BL], kv, preferred_element_type=f32))
            dkv = lax.dot_general(w_v[h], stacked(last, h), TN, preferred_element_type=f32)
            dkv = jnp.where(b >= 2, dkv, 0.0)
            for j in range(slots_n):
                acc[pl.ds(rows[j], BL), hs] += dkv[j * BL : (j + 1) * BL]
        finish(pl.multiple_of((first + last) * BL, BL), dqs)
        for h in range(heads):
            sd = sd_v[h]
            row = pl.multiple_of(now * BL, BL)
            p = jnp.exp(
                sd[:BL] + bias_ref[pl.ds(h * nblocks + first + now, 1), :] - lse_ref[pl.ds(row, BL), h : h + 1]
            )
            dp = sd[BL:]
            ds = p * (dp - jnp.sum(dp * p, -1, keepdims=True))
            w_v[h, :BL] = ds.astype(bf16)
            w_v[h, BL:] = p.astype(bf16)
        for h in range(heads):
            rows = slot_rows(first + new, h)
            kv = jnp.concatenate(
                [qkv_ref[pl.ds(rows[j], BL), h * 128 : (h + 1) * 128] for j in range(slots_n)], 0
            )
            sd_v[h] = lax.dot_general(stacked(new, h), kv, NT, preferred_element_type=f32)
        return 0

    sd_v[...] = jnp.zeros_like(sd_v)
    w_v[...] = jnp.zeros_like(w_v)
    lax.fori_loop(0, blocks + 2, body, 0)

    def whole_row(g, _):
        a = gl_ref[1 + g]
        local = a - first

        @pl.when((local >= 0) & (local < parts * chunk))
        def _():
            r = pl.multiple_of(a * BL, BL)
            row = pl.multiple_of(local * BL, BL)
            dqs = []
            for h in range(heads):
                hs = slice(h * 128, (h + 1) * 128)
                x = jnp.concatenate([queries(r, h), grads(row, h)], 0)
                lse = lse_ref[pl.ds(row, BL), h : h + 1]
                inner = 0.0
                for c in range(n // wide):
                    cs = slice(c * wide, (c + 1) * wide)
                    sd = lax.dot_general(x, qkv_ref[cs, hs], NT, preferred_element_type=f32)
                    p = jnp.exp(sd[:BL] - lse)
                    dp = sd[BL:]
                    pbuf[h, :, cs] = p
                    dbuf[h, :, cs] = dp
                    inner = inner + jnp.sum(dp * p, -1, keepdims=True)
                dq = 0.0
                for c in range(n // wide):
                    cs = slice(c * wide, (c + 1) * wide)
                    p = pbuf[h, :, cs]
                    ds = (p * (dbuf[h, :, cs] - inner)).astype(bf16)
                    w = jnp.concatenate([ds, p.astype(bf16)], 0)
                    dq = dq + jnp.dot(ds, qkv_ref[cs, hs], preferred_element_type=f32)
                    acc[cs, hs] += lax.dot_general(w, x, TN, preferred_element_type=f32)
                dqs.append(dq)
            finish(r, dqs)

        return 0

    lax.fori_loop(0, gl_ref[0], whole_row, 0)
    if end:

        def flush(i, _):
            rr = pl.ds(pl.multiple_of(i * 256, 256), 256)
            out_ref[rr, :kvw] = acc[rr, :].astype(bf16)
            return 0

        lax.fori_loop(0, n // 256, flush, 0)


def attn_bwd(idx, gl, qkv, bias, grads, lse, heads, first_part, carried, end):
    n = qkv.shape[0]
    nblocks = n // BL
    chunk = nblocks // 4
    slots_n = bias.shape[1] // BL
    parts = len(grads)
    vmem = pl.BlockSpec(memory_space=pltpu.VMEM)
    smem = pl.BlockSpec(memory_space=pltpu.SMEM)
    dims = (heads, nblocks, slots_n, first_part * chunk, parts, chunk, 512, not carried, end)
    pairs = (heads + 1) // 2
    scratch = [pltpu.VMEM((heads, BL, n), f32)] * 2 + [
        pltpu.VMEM((heads, 2 * BL, slots_n * BL), f32),
        pltpu.VMEM((heads, 2 * BL, slots_n * BL), bf16),
        pltpu.VMEM((parts * n // 4, heads * HD), bf16),
    ]
    if end:
        out_shape = jax.ShapeDtypeStruct((n, (heads + pairs) * 128), bf16)
        out_specs = vmem
        scratch = [pltpu.VMEM((n, heads * 128), f32)] + scratch
    else:
        out_shape = (
            jax.ShapeDtypeStruct((n, heads * 128), f32),
            jax.ShapeDtypeStruct((parts * n // 4, pairs * 128), bf16),
        )
        out_specs = (vmem, vmem)
    return pl.pallas_call(
        functools.partial(bwd_kernel, dims),
        out_shape=out_shape,
        in_specs=[smem, smem] + [vmem] * (3 + parts + len(carried)),
        out_specs=out_specs,
        scratch_shapes=scratch,
        compiler_params=pltpu.CompilerParams(vmem_limit_bytes=60 << 20),
        cost_estimate=pl.CostEstimate(flops=11 * parts * 10**9, bytes_accessed=10**7, transcendentals=0),
        name="attn_bwd",
    )(idx, gl, qkv, bias, *grads, lse, *carried)


MESH_ID = pl.DeviceIdType.MESH


def flip(index, number):
    total = 0
    for bit in (1, 2, 4):
        digit = (index // bit) % 2
        total = total + bit * ((1 - digit) if number & bit else digit)
    return total


def blend(a, b):
    return sum(bit * (((a // bit) % 2 + (b // bit) % 2) % 2) for bit in (1, 2, 4))


def greet(item, place, items):
    barrier = pltpu.get_barrier_semaphore()
    for t in range(1, 4):
        pl.semaphore_signal(barrier, inc=1, device_id=(item, flip(place, t)), device_id_type=MESH_ID)
    for k in range(1, items):
        pl.semaphore_signal(barrier, inc=1, device_id=(flip(item, k), place), device_id_type=MESH_ID)
    pl.semaphore_wait(barrier, 3 + items - 1)


def tail_kernel(
    items, query_columns, x0, x1, x2, x3, gq_ref, slab_ref, first_ref, small_ref, pk_ref, pr_ref, qk_ref, qr_ref,
    din_ref, group_ref, sgroup_ref, total_ref, squares_ref,
    near_out, near_in, far_out, far_in, grad_v, side_out, side_in, part_out, part_in, z_out, z_in, small_in, small_mid, small_items, sq_out, sq_in, sq_mid, sq_items,
    near_send, near_recv, far_send, far_recv, side_send, side_recv, part_send, part_recv, z_send, z_recv, sg_send, sg_recv, si_send, si_recv,
    gr_send, gr_recv, sl_send, sl_recv, qg_send, qg_recv, qi_send, qi_recv,
):
    xs = (x0, x1, x2, x3)
    item, place = lax.axis_index("item"), lax.axis_index("seq")
    tokens, width = x0.shape
    rows = width // items
    tile = 256
    chunks = tokens // tile
    columns = gq_ref.shape[1]
    levels = items // 2
    up_rows = pk_ref.shape[1]
    greet(item, place, items)

    def to_group(src, dst, send, recv, t):
        return pltpu.make_async_remote_copy(
            src_ref=src, dst_ref=dst, send_sem=send, recv_sem=recv,
            device_id=(item, flip(place, t)), device_id_type=MESH_ID,
        )

    def to_item(src, dst, send, recv, k):
        return pltpu.make_async_remote_copy(
            src_ref=src, dst_ref=dst, send_sem=send, recv_sem=recv,
            device_id=(flip(item, k), place), device_id_type=MESH_ID,
        )

    small_copies = [to_group(small_ref, small_in.at[t], sg_send.at[t], sg_recv.at[t], t) for t in range(1, 4)]
    for copy in small_copies:
        copy.start()

    z_copies = []
    for kz in range(levels - 1, 0, -1):
        z_out[kz, 0:up_rows, :] = (pk_ref[kz].astype(f32) + pr_ref[kz].astype(f32)).astype(bf16)
        z_out[kz, up_rows:, :] = (qk_ref[kz].astype(f32) + qr_ref[kz].astype(f32)).astype(bf16)
        copy = to_item(z_out.at[kz], z_in.at[kz], z_send.at[kz], z_recv.at[kz], 2 * kz)
        copy.start()
        z_copies.append(copy)

    def token_part(t, c):
        return lax.dot_general(
            gq_ref[t * tokens + c * tile : t * tokens + (c + 1) * tile, :], slab_ref[...], NT, preferred_element_type=f32
        )

    near_copies = {}
    far_copies = []

    def send_near(t):
        for c in range(chunks):
            cs = pl.ds(c * tile, tile)
            near_out[t // 2, c * tile : (c + 1) * tile, :] = token_part(t, c).astype(bf16)
            copy = to_group(
                near_out.at[t // 2, cs], near_in.at[t // 2, cs], near_send.at[t // 2, c], near_recv.at[t // 2, c], 1
            )
            copy.start()
            near_copies[(t // 2, c)] = copy

    send_near(3)
    for c in range(chunks):
        cs = slice(c * tile, (c + 1) * tile)
        part = token_part(2, c)
        near_copies[(1, c)].wait_recv()
        far_out[cs, :] = (part.astype(bf16).astype(f32) + near_in[1, cs, :].astype(f32)).astype(bf16)
        copy = to_group(far_out.at[pl.ds(c * tile, tile)], far_in.at[pl.ds(c * tile, tile)], far_send.at[c], far_recv.at[c], 2)
        copy.start()
        far_copies.append(copy)

    def slab_rows(r, _):
        at = pl.multiple_of(r * tile, tile)
        part = 0.0
        for t in range(4):
            part = part + lax.dot_general(
                xs[t][:, pl.ds(at, tile)], gq_ref[t * tokens : (t + 1) * tokens, :], TN, preferred_element_type=f32
            )
        grad_v[pl.ds(at, tile), :] = part
        return 0

    lax.fori_loop(0, width // tile, slab_rows, 0)

    def sums(r, line):
        at = pl.multiple_of(r * tile, tile)
        return line + jnp.sum(gq_ref[pl.ds(at, tile), :].astype(f32), 0, keepdims=True)

    line = lax.fori_loop(0, 4 * chunks, sums, jnp.zeros((1, columns), f32))
    high = line.astype(bf16)
    rest = (line - high.astype(f32)).astype(bf16)
    which = lax.broadcasted_iota(jnp.int32, (16, columns), 0)
    lines = jnp.where(which == 0, high.astype(f32), jnp.where(which == 1, rest.astype(f32), 0.0)).astype(bf16)
    level = item // 2
    side = item % 2

    def slab_part(kz, kx):
        at = pl.multiple_of((2 * flip(level, kz) + (side + kx) % 2) * rows, 8)
        return grad_v[pl.ds(at, rows), :]

    side_copies = []
    for kz in range(levels - 1, -1, -1):
        side_out[kz, 0:rows, :] = slab_part(kz, 1).astype(bf16)
        side_out[kz, rows : rows + 16, :] = lines
        copy = to_item(side_out.at[kz], side_in.at[kz], side_send.at[kz], side_recv.at[kz], 1)
        copy.start()
        side_copies.append((kz, copy))

    for copy in small_copies:
        copy.wait()
    small_mid[...] = small_ref[...] + small_in[1] + small_in[2] + small_in[3]
    item_copies = [to_item(small_mid, small_items.at[k], si_send.at[k], si_recv.at[k], k) for k in range(1, items)]
    for copy in item_copies:
        copy.start()

    send_near(1)
    for c in range(chunks):
        cs = slice(c * tile, (c + 1) * tile)
        din_ref[cs, :] = first_ref[cs, :] + token_part(0, c).astype(bf16).astype(f32)

    def square_sum(values):
        return jnp.sum(jnp.sum(values * values, 0, keepdims=True), -1, keepdims=True)

    part_copies = []
    for kz, copy in side_copies:
        copy.wait()
        part = slab_part(kz, 0) + side_in[kz, 0:rows, :].astype(f32)
        both = lines.astype(f32) + side_in[kz, rows : rows + 16, :].astype(f32)
        if kz:
            part_out[kz, 0:rows, :] = part.astype(bf16)
            whole = jnp.sum(both, 0, keepdims=True)
            short = whole.astype(bf16).astype(f32)
            which_row = jnp.where(which == 0, short, jnp.where(which == 1, whole - short, 0.0))
            part_out[kz, rows : rows + 16, :] = which_row.astype(bf16)
            copy = to_item(part_out.at[kz], part_in.at[kz], part_send.at[kz], part_recv.at[kz], 2 * kz)
            copy.start()
            part_copies.append(copy)
        else:
            own_part, own_lines = part, both

    for copy in z_copies:
        copy.wait()

    up = pk_ref[0].astype(f32) + pr_ref[0].astype(f32)
    down = qk_ref[0].astype(f32) + qr_ref[0].astype(f32)
    for kz in range(1, levels):
        up = up + z_in[kz, 0:up_rows, :].astype(f32)
        down = down + z_in[kz, up_rows:, :].astype(f32)
    group_ref[0, 0:up_rows, :] = up
    group_ref[0, up_rows:, :] = down
    big_copies = [to_group(group_ref.at[0], group_ref.at[t], gr_send.at[t], gr_recv.at[t], t) for t in (2, 1)]
    for copy in big_copies:
        copy.start()
    squares = square_sum(up) + square_sum(down)
    for copy in part_copies:
        copy.wait()
    own = jnp.concatenate([own_part, own_lines], 0)
    for kz in range(1, levels):
        own = own + part_in[kz].astype(f32)
    sgroup_ref[0] = own
    group_copies = [to_group(sgroup_ref.at[0], sgroup_ref.at[t], sl_send.at[t], sl_recv.at[t], t) for t in (2, 1)]
    for copy in group_copies:
        copy.start()
    column = lax.broadcasted_iota(jnp.int32, (1, columns), 1)
    squares = squares + square_sum(own[0:rows] * jnp.where(column < query_columns, 1.0, HD**-0.5))
    sq_out[...] = jnp.broadcast_to(squares, (8, 128))
    sq_copies = [to_group(sq_out, sq_in.at[t], qg_send.at[t], qg_recv.at[t], t) for t in range(1, 4)]
    for copy in sq_copies:
        copy.start()
    for copy in sq_copies:
        copy.wait()
    sq_mid[...] = sq_out[...] + sq_in[1] + sq_in[2] + sq_in[3]
    sq_item_copies = [to_item(sq_mid, sq_items.at[k], qi_send.at[k], qi_recv.at[k], k) for k in range(1, items)]
    for copy in sq_item_copies:
        copy.start()

    group_copies[0].wait()
    cross = to_group(sgroup_ref.at[2], sgroup_ref.at[3], sl_send.at[3], sl_recv.at[3], 1)
    cross.start()
    big_copies[0].wait()
    big_cross = to_group(group_ref.at[2], group_ref.at[3], gr_send.at[3], gr_recv.at[3], 1)
    big_cross.start()
    for copy in item_copies:
        copy.wait()
    total = small_mid[...]
    for k in range(1, items):
        total = total + small_items[k]
    total_ref[...] = total
    for c in range(chunks):
        cs = slice(c * tile, (c + 1) * tile)
        near_copies[(1, c)].wait_send()
        near_copies[(0, c)].wait()
        far_copies[c].wait()
        din_ref[cs, :] = din_ref[cs, :] + near_in[0, cs, :].astype(f32) + far_in[cs, :].astype(f32)
    for copy in sq_item_copies:
        copy.wait()
    answer = sq_mid[...]
    for k in range(1, items):
        answer = answer + sq_items[k]
    squares_ref[...] = answer
    group_copies[1].wait()
    cross.wait()
    big_copies[1].wait()
    big_cross.wait()


def tail(xs, gq, slab, first, small, shards, items, query_columns):
    tokens, width = xs[0].shape
    columns = gq.shape[1]
    rows = width // items
    vmem = pl.BlockSpec(memory_space=pltpu.VMEM)
    dma = pltpu.SemaphoreType.DMA
    chunks, levels = tokens // 256, items // 2
    quarter = shards[0].shape[1] + shards[2].shape[1]
    slab_part = (levels, rows + 16, columns)
    return pl.pallas_call(
        functools.partial(tail_kernel, items, query_columns),
        out_shape=(
            jax.ShapeDtypeStruct((tokens, width), f32),
            jax.ShapeDtypeStruct((4, quarter, width), f32),
            jax.ShapeDtypeStruct((4, rows + 16, columns), f32),
            jax.ShapeDtypeStruct(small.shape, f32),
            jax.ShapeDtypeStruct((8, 128), f32),
        ),
        in_specs=[vmem] * 12,
        out_specs=(vmem,) * 5,
        scratch_shapes=[
            pltpu.VMEM((2, tokens, width), bf16),
            pltpu.VMEM((2, tokens, width), bf16),
            pltpu.VMEM((tokens, width), bf16),
            pltpu.VMEM((tokens, width), bf16),
            pltpu.VMEM((width, columns), f32),
            pltpu.VMEM(slab_part, bf16),
            pltpu.VMEM(slab_part, bf16),
            pltpu.VMEM(slab_part, bf16),
            pltpu.VMEM(slab_part, bf16),
            pltpu.VMEM((levels, quarter, width), bf16),
            pltpu.VMEM((levels, quarter, width), bf16),
            pltpu.VMEM((4,) + small.shape, f32),
            pltpu.VMEM(small.shape, f32),
            pltpu.VMEM((items,) + small.shape, f32),
            pltpu.VMEM((8, 128), f32),
            pltpu.VMEM((4, 8, 128), f32),
            pltpu.VMEM((8, 128), f32),
            pltpu.VMEM((items, 8, 128), f32),
            dma((2, chunks)), dma((2, chunks)), dma((chunks,)), dma((chunks,)),
            dma((levels,)), dma((levels,)), dma((levels,)), dma((levels,)), dma((levels,)), dma((levels,)),
            dma((4,)), dma((4,)), dma((items,)), dma((items,)),
            dma((4,)), dma((4,)), dma((4,)), dma((4,)), dma((4,)), dma((4,)), dma((items,)), dma((items,)),
        ],
        compiler_params=pltpu.CompilerParams(vmem_limit_bytes=60 << 20, collective_id=3, has_side_effects=True),
        cost_estimate=pl.CostEstimate(flops=60 * 10**9, bytes_accessed=10**7, transcendentals=0),
        name="tail",
    )(*xs, gq, slab, first, small, *shards)


def update_kernel(
    place_of, heads, group_ref, sgroup_ref, total_ref, squares_ref,
    wq, fq, sq, wo, fo, so, wu, fu, su, wd, fd, sd, ws, fs, ss,
    norm_ref, nwq, nfq, nsq, nwo, nfo, nso, nwu, nfu, nsu, nwd, nfd, nsd, nws, nfs, nss,
    grad_q, grad_s,
):
    place = place_of()
    rows, width = wo.shape
    third = rows // 3
    small_rows = ws.shape[0]
    grad_s[...] = total_ref[...]
    for q in range(4):
        t = flip(place, q)
        piece = sgroup_ref.at[t]
        for h in range(heads):
            at = (q * heads + h) * HD
            pair = h * 128
            value, key = (pair, pair + HD) if h % 2 == 0 else (pair + HD, pair)
            query = (heads + h // 2) * 128 + (HD if h % 2 == 0 else 0)
            for part, base, scale in ((0, query, HD**-0.5), (1, key, 1.0), (2, value, 1.0)):
                grad_q[:, part * width + at : part * width + at + HD] = piece[0:rows, base : base + HD] * scale
            for row, base, scale in ((2, query, HD**-0.5), (3, value, 1.0)):
                line = piece[rows : rows + 16, base : base + HD]
                grad_s[row : row + 1, at : at + HD] = (line[0:1] + line[1:2]) * scale
    small = grad_s[0:small_rows, :]
    squares = jnp.sum(jnp.sum(small * small, 0, keepdims=True), -1, keepdims=True) + squares_ref[0:1, 0:1]
    norm = jnp.sqrt(squares)
    norm_ref[...] = norm
    factor = jnp.minimum(1.0, clip_level / (norm + 1e-06))

    def apply(refs, index, grad, decay, rate):
        w, f, s, nw, nf, ns = refs
        new = adam_update(w[index], f[index], s[index], grad * factor, decay, rate)
        nw[index], nf[index], ns[index] = new

    everything = (slice(None), slice(None))
    apply((ws, fs, ss, nws, nfs, nss), everything, small, 0.0, small_rate)
    for part in range(3):
        cs = slice(part * width, (part + 1) * width)
        apply((wq, fq, sq, nwq, nfq, nsq), (slice(None), cs), grad_q[:, cs], weight_decay, learn_rate)
    for q in range(4):
        t = flip(place, q)
        cs = slice(q * width, (q + 1) * width)
        apply((wu, fu, su, nwu, nfu, nsu), (slice(None), cs), group_ref[t, 0:rows, :], weight_decay, learn_rate)
        if q < 3:
            os = (slice(q * third, (q + 1) * third), slice(None))
            apply((wo, fo, so, nwo, nfo, nso), os, group_ref[t, rows : rows + third, :], weight_decay, learn_rate)
        ds = (slice(q * rows, (q + 1) * rows), slice(None))
        apply((wd, fd, sd, nwd, nfd, nsd), ds, group_ref[t, rows + third :, :], weight_decay, learn_rate)


def update(place_of, heads, group, sgroup, total, squares, states):
    vmem = pl.BlockSpec(memory_space=pltpu.VMEM)
    rows = states[3].shape[0]
    return pl.pallas_call(
        functools.partial(update_kernel, place_of, heads),
        out_shape=(jax.ShapeDtypeStruct((1, 1), f32),) + tuple(jax.ShapeDtypeStruct(a.shape, f32) for a in states),
        in_specs=[vmem] * (4 + len(states)),
        out_specs=(vmem,) * (1 + len(states)),
        scratch_shapes=[pltpu.VMEM(states[0].shape, f32), pltpu.VMEM(total.shape, f32)],
        compiler_params=pltpu.CompilerParams(vmem_limit_bytes=60 << 20),
        cost_estimate=pl.CostEstimate(flops=10**9, bytes_accessed=25 * 10**6, transcendentals=0),
        name="update",
    )(group, sgroup, total, squares, *states)


def head_kernel(
    items, x_ref, piece_ref, quarter_ref, bias_ref,
    near_ref, far_ref, cross_ref, qkv_ref, slab_ref, line_ref, side_ref, wfar_ref,
    pieces_v, x_send, x_recv, far_send, far_recv, cross_send, cross_recv,
    s_up_send, s_up_recv, s_down_send, s_down_recv, s_side_send, s_side_recv,
    w_up_send, w_up_recv, w_down_send, w_down_recv, w_side_send, w_side_recv, w_own, y_send, y_recv,
):
    item, place = lax.axis_index("item"), lax.axis_index("seq")
    side, level = item % 2, item // 2
    levels = items // 2
    tokens = x_ref.shape[0]
    rows = piece_ref.shape[0]
    tile = 256
    chunks = tokens // tile
    greet(item, place, items)

    def to_group(src, dst, send, recv, t):
        return pltpu.make_async_remote_copy(
            src_ref=src, dst_ref=dst, send_sem=send, recv_sem=recv,
            device_id=(item, flip(place, t)), device_id_type=MESH_ID,
        )

    class Flow:
        def __init__(self, slot, side_slot, other_slot, arrived, sems):
            self.slot, self.side_slot, self.other_slot, self.arrived = slot, side_slot, other_slot, arrived
            self.up_send, self.up_recv, self.down_send, self.down_recv, self.side_send, self.side_recv = sems

        def up(self, d):
            part = self.slot(-d)
            return pltpu.make_async_remote_copy(
                src_ref=part, dst_ref=part, send_sem=self.up_send.at[d], recv_sem=self.up_recv.at[d],
                device_id=(item + 2, place), device_id_type=MESH_ID,
            )

        def down(self, d):
            part = self.slot(d)
            return pltpu.make_async_remote_copy(
                src_ref=part, dst_ref=part, send_sem=self.down_send.at[d], recv_sem=self.down_recv.at[d],
                device_id=(item - 2, place), device_id_type=MESH_ID,
            )

        def across(self, d):
            part = self.slot(d)
            return pltpu.make_async_remote_copy(
                src_ref=part, dst_ref=self.side_slot(d), send_sem=self.side_send.at[level + d], recv_sem=self.side_recv.at[level + d],
                device_id=(item + 1 - 2 * side, place), device_id_type=MESH_ID,
            )

        def begin(self):
            @pl.when(level < levels - 1)
            def _():
                self.up(0).start()

            @pl.when(level > 0)
            def _():
                self.down(0).start()

            self.across(0).start()
            self.arrived(0)

        def step(self, d):
            @pl.when(level >= d)
            def _():
                part = self.slot(-d)
                pltpu.make_async_remote_copy(
                    src_ref=part, dst_ref=part, send_sem=self.up_send.at[d - 1], recv_sem=self.up_recv.at[d - 1],
                    device_id=(item + 1 - 2 * side, place), device_id_type=MESH_ID,
                ).wait_recv()

                @pl.when(level < levels - 1)
                def _():
                    self.up(d).start()

                self.across(-d).start()
                self.arrived(-d)

            @pl.when(level < levels - d)
            def _():
                part = self.slot(d)
                pltpu.make_async_remote_copy(
                    src_ref=part, dst_ref=part, send_sem=self.down_send.at[d - 1], recv_sem=self.down_recv.at[d - 1],
                    device_id=(item + 1 - 2 * side, place), device_id_type=MESH_ID,
                ).wait_recv()

                @pl.when(level > 0)
                def _():
                    self.down(d).start()

                self.across(d).start()
                self.arrived(d)

        def other_side(self):
            for z in range(levels):
                part = self.other_slot(z)
                pltpu.make_async_remote_copy(
                    src_ref=part, dst_ref=part, send_sem=self.side_send.at[z], recv_sem=self.side_recv.at[z],
                    device_id=(item + 1 - 2 * side, place), device_id_type=MESH_ID,
                ).wait_recv()

        def finish(self):
            for d in range(levels - 1):

                @pl.when((level >= d) & (level < levels - 1))
                def _():
                    self.up(d).wait_send()

                @pl.when((level < levels - d) & (level > 0))
                def _():
                    self.down(d).wait_send()

            for z in range(levels):
                part = self.slot(z - level)
                pltpu.make_async_remote_copy(
                    src_ref=part, dst_ref=part, send_sem=self.side_send.at[z], recv_sem=self.side_recv.at[z],
                    device_id=(item + 1 - 2 * side, place), device_id_type=MESH_ID,
                ).wait_send()

    def far_copy(z):
        return to_group(line_ref.at[z], wfar_ref.at[z], y_send.at[z], y_recv.at[z], 2)

    def piece_slot(d):
        return pieces_v.at[item + 2 * d]

    slab_flow = Flow(piece_slot, piece_slot, lambda z: pieces_v.at[2 * z + 1 - side], lambda d: None, (s_up_send, s_up_recv, s_down_send, s_down_recv, s_side_send, s_side_recv))
    w_flow = Flow(
        lambda d: line_ref.at[level + d], lambda d: side_ref.at[level + d], lambda z: side_ref.at[z],
        lambda d: far_copy(level + d).start(), (w_up_send, w_up_recv, w_down_send, w_down_recv, w_side_send, w_side_recv))
    own = pltpu.make_async_copy(quarter_ref, line_ref.at[level], w_own.at[0])
    own.start()
    pieces_v[item] = piece_ref[...]
    slab_flow.begin()
    far_copies, near_copies, cross_copies = [], [], []
    for c in range(chunks):
        cs = pl.ds(c * tile, tile)
        far_copies.append(to_group(x_ref.at[cs], far_ref.at[cs], far_send.at[c], far_recv.at[c], 2))
        far_copies[-1].start()
    near_copies = [to_group(x_ref, near_ref, x_send.at[0], x_recv.at[0], 1)]
    near_copies[0].start()
    for d in range(1, levels):
        slab_flow.step(d)
    own.wait()
    w_flow.begin()
    slab_flow.other_side()
    for j in range(items):
        slab_ref[j * rows : (j + 1) * rows, :] = pieces_v[j]

    def project_rows(src, t, c):
        part = jnp.dot(src[c * tile : (c + 1) * tile, :], slab_ref[...], preferred_element_type=f32)
        at = t * tokens + c * tile
        qkv_ref[at : at + tile, :] = (part + bias_ref[...]).astype(bf16)

    def pass_on(c):
        cs = pl.ds(c * tile, tile)
        far_copies[c].wait_recv()
        copy = to_group(far_ref.at[cs], cross_ref.at[cs], cross_send.at[c], cross_recv.at[c], 1)
        copy.start()
        cross_copies.append(copy)

    for c in range(chunks):
        project_rows(x_ref, 0, c)
        pass_on(c)
        if c + 1 < levels:
            w_flow.step(c + 1)
        if c == 0:
            near_copies[0].wait_recv()
        project_rows(near_ref, 1, c)
        project_rows(far_ref, 2, c)
        cross_copies[c].wait_recv()
        project_rows(cross_ref, 3, c)
    for d in range(chunks + 1, levels):
        w_flow.step(d)
    w_flow.other_side()
    near_copies[0].wait_send()
    for c in range(chunks):
        far_copies[c].wait_send()
        cross_copies[c].wait_send()
    for z in range(levels):
        far_copy(z).wait()
    slab_flow.finish()
    w_flow.finish()


def head(x, piece, quarter, bias, items):
    tokens, width = x.shape
    rows, columns = piece.shape
    vmem = pl.BlockSpec(memory_space=pltpu.VMEM)
    any_space = pl.BlockSpec(memory_space=pl.ANY)
    dma = pltpu.SemaphoreType.DMA
    chunks, levels = tokens // 256, items // 2
    tokens_shape = jax.ShapeDtypeStruct((tokens, width), bf16)
    return pl.pallas_call(
        functools.partial(head_kernel, items),
        out_shape=(
            tokens_shape, tokens_shape, tokens_shape,
            jax.ShapeDtypeStruct((4 * tokens, columns), bf16),
            jax.ShapeDtypeStruct((rows * items, columns), bf16),
        )
        + (jax.ShapeDtypeStruct((items // 2,) + quarter.shape, bf16),) * 3,
        in_specs=[vmem, vmem, any_space, vmem],
        out_specs=(vmem,) * 5 + (any_space,) * 3,
        scratch_shapes=[
            pltpu.VMEM((items, rows, columns), bf16),
            dma((1,)), dma((1,)), dma((chunks,)), dma((chunks,)), dma((chunks,)), dma((chunks,)),
        ]
        + [dma((levels,))] * 12
        + [dma((1,)), dma((levels,)), dma((levels,))],
        compiler_params=pltpu.CompilerParams(vmem_limit_bytes=48 << 20, collective_id=1, has_side_effects=True),
        cost_estimate=pl.CostEstimate(flops=40 * 10**9, bytes_accessed=10**7, transcendentals=0),
        name="head",
    )(x, piece, quarter, bias)


def gelu_parts(u):
    half = 0.5 * (1.0 + lax.erf(u * 0.7071067811865476))
    return u * half, half + u * jnp.exp(-0.5 * u * u) * 0.3989422804014327


def middle_kernel(
    dims, line_ref, side_ref, fline_ref, fside_ref, x_ref, mix0_ref, mix1_ref, mix2_ref, mix3_ref, dout_ref, small_ref,
    out_ref, first_ref, gmix0_ref, gmix1_ref, gmix2_ref, gmix3_ref, pkeep_ref, psend_ref, qkeep_ref, qsend_ref, sgrad_ref,
    wo_v, wu_v, wd_v, xhat_v, hid_v, act_v, slope_v, ffn_v, gffn_v, gup_v, dhid_v, rstd_v, stage_d, stage_u, stage_o,
    got_u, got_d, got_o, mixn_v,
    wsem, wsend, wrecv, mix_send, mix_recv, usend, urecv, dsend, drecv, osend, orecv, flush,
):
    items, rows, width, tile = dims
    item, place = lax.axis_index("item"), lax.axis_index("seq")
    side, level = item % 2, item // 2
    core, far = place % 2, place // 2
    third = rows // 3
    tokens = x_ref.shape[0]
    tiles = tokens // tile
    near = (item, flip(place, 1))
    barrier = pltpu.get_barrier_semaphore()
    pl.semaphore_signal(barrier, inc=1, device_id=near, device_id_type=MESH_ID)
    pl.semaphore_wait(barrier, 1)

    def remote(src, dst, send, recv):
        return pltpu.make_async_remote_copy(
            src_ref=src, dst_ref=dst, send_sem=send, recv_sem=recv, device_id=near, device_id_type=MESH_ID
        )

    mix_copy = remote(mix1_ref, mixn_v, mix_send.at[0], mix_recv.at[0])
    mix_copy.start()

    def load(which):
        for t in (0, 2):
            q = flip(place, t)
            for n in range(items):
                z, kx = n // 2, n % 2
                j = 2 * z + (side + kx) % 2
                src = ((line_ref, side_ref) if t == 0 else (fline_ref, fside_ref))[kx].at[z]
                if which == 0:
                    src = src.at[pl.ds(2 * rows, third)]
                    dst = wo_v.at[j, pl.ds(pl.multiple_of(q * third, 16), third)]
                elif which == 1:
                    src = src.at[pl.ds(0, rows)]
                    dst = wu_v.at[q, pl.ds(pl.multiple_of(j * rows, 16), rows)]
                else:
                    src = src.at[pl.ds(rows, rows)]
                    dst = wd_v.at[j // 2, pl.ds(pl.multiple_of((j % 2) * 4 * rows + q * rows, 16), rows)]
                remote(src, dst, wsend.at[which], wrecv.at[which]).start()
                pltpu.make_async_copy(src, dst, wsem.at[which]).start()

    for which in range(3):
        load(which)

    def loaded(which):
        half = (wo_v.at[pl.ds(0, items // 2)], wu_v.at[pl.ds(0, 2)], wd_v.at[pl.ds(0, 2)])[which]
        pltpu.make_async_copy(half, half, wsem.at[which]).wait()
        remote(half, half, wsend.at[which], wrecv.at[which]).wait_recv()

    def rowsl(r):
        return pl.ds(pl.multiple_of(r * tile, tile), tile)

    def wo_rows(q):
        return jnp.concatenate([wo_v[2 * q, 0:rows], wo_v[2 * q + 1, 0:rows]], 0)

    mixes = (mix0_ref, mixn_v, mix2_ref, mix3_ref)
    gmixes = (gmix0_ref, gmix1_ref, gmix2_ref, gmix3_ref)
    mix_copy.wait_recv()
    loaded(0)

    def norm_one(r, _):
        rs = rowsl(r)
        total = x_ref[rs, :].astype(f32) + small_ref[4:5, :]
        for t in range(4):
            total += jnp.dot(mixes[t][rs, :], wo_rows(flip(place, t)), preferred_element_type=f32)
        centered = total - jnp.mean(total, -1, keepdims=True)
        rstd = lax.rsqrt(jnp.mean(centered * centered, -1, keepdims=True) + norm_epsilon)
        xhat = centered * rstd
        xhat_v[rs, :] = xhat
        rstd_v[rs, :] = jnp.broadcast_to(rstd, (tile, 128))
        hid_v[rs, :] = (xhat * small_ref[0:1, :] + small_ref[1:2, :]).astype(bf16)
        return 0

    lax.fori_loop(0, tiles, norm_one, 0)
    loaded(1)
    loaded(2)

    def ffn(n, _):
        p, r = n // tiles, n % tiles
        rs = rowsl(r)
        up = jnp.dot(hid_v[rs, :], wu_v[p], preferred_element_type=f32) + small_ref[pl.ds(8 + p, 1), :]
        act, slope = gelu_parts(up)
        act = act.astype(bf16)
        act_v[p, rs, :] = act
        slope_v[p, rs, :] = slope
        part = jnp.dot(act, wd_v[p], preferred_element_type=f32)

        @pl.when(p == 0)
        def _():
            ffn_v[rs, :] = part

        @pl.when(p > 0)
        def _():
            ffn_v[rs, :] += part

        return 0

    lax.fori_loop(0, 4 * tiles, ffn, 0)
    zero = jnp.zeros((1, width), f32)

    def norm_two(r, sums):
        rs = rowsl(r)
        dg, db, dd = sums
        hidden = xhat_v[rs, :] * small_ref[0:1, :] + small_ref[1:2, :]
        total = hidden + (ffn_v[rs, :] + small_ref[7:8, :])
        centered = total - jnp.mean(total, -1, keepdims=True)
        rstd = lax.rsqrt(jnp.mean(centered * centered, -1, keepdims=True) + norm_epsilon)
        xhat = centered * rstd
        out_ref[rs, :] = (xhat * small_ref[5:6, :] + small_ref[6:7, :]).astype(bf16)
        dy = dout_ref[rs, :].astype(f32)
        dg = dg + jnp.sum(dy * xhat, 0, keepdims=True)
        db = db + jnp.sum(dy, 0, keepdims=True)
        dx = dy * small_ref[5:6, :]
        dx = rstd * (dx - jnp.mean(dx, -1, keepdims=True) - xhat * jnp.mean(dx * xhat, -1, keepdims=True))
        dhid_v[rs, :] = dx
        short = dx.astype(bf16)
        gffn_v[rs, :] = short
        dd = dd + jnp.sum(short.astype(f32), 0, keepdims=True)
        return dg, db, dd

    dg2, db2, dd = lax.fori_loop(0, tiles, norm_two, (zero, zero, zero))
    sgrad_ref[...] = jnp.zeros_like(sgrad_ref)
    sgrad_ref[5:6, :] = dg2
    sgrad_ref[6:7, :] = db2
    sgrad_ref[7:8, :] = dd
    nt = (((1,), (1,)), ((), ()))
    tn = (((0,), (0,)), ((), ()))
    pieces = width // tile

    def in_p(yrel, j, row, count):
        kx, kz = (j % 2 + side) % 2, flip(level, j // 2)
        return (pkeep_ref, psend_ref)[yrel].at[kx, kz, pl.ds(row, count)]

    def finish_chunk(p, par):
        remote(got_d.at[p], got_d.at[p], dsend.at[p], drecv.at[p]).wait_recv()
        for jj in range(2):
            for yy in range(2):
                at = pl.multiple_of((4 * jj + 2 * yy + core) * rows, 16)
                total = stage_d[par, pl.ds(at, rows), :].astype(f32) + got_d[p, jj, yy].astype(f32)
                got_d[p, jj, yy] = total.astype(bf16)
                for kx, ref in enumerate((qkeep_ref, qsend_ref)):

                    @pl.when((jj + side) % 2 == kx)
                    def _():
                        dst = ref.at[(yy + far) % 2, blend(level, p)]
                        pltpu.make_async_copy(got_d.at[p, jj, yy], dst, flush.at[0]).start()

        half = p // 2

        @pl.when(p % 2 == core)
        def _():
            remote(got_u.at[half], got_u.at[half], usend.at[half], urecv.at[half]).wait_recv()
            for m in range(tiles):
                ms = slice(m * tile, (m + 1) * tile)
                got_u[half, ms, :] = (stage_u[par, ms, :].astype(f32) + got_u[half, ms, :].astype(f32)).astype(bf16)
            for yrel in range(2):

                @pl.when((half + far) % 2 == yrel)
                def _():
                    for j in range(items):
                        src = got_u.at[half, pl.ds(j * rows, rows)]
                        pltpu.make_async_copy(src, in_p(yrel, j, 0, rows), flush.at[1]).start()

    def back(p, _):
        par = p % 2

        def back_rows(r, total):
            rs = rowsl(r)
            ga = lax.dot_general(gffn_v[rs, :], wd_v[p], nt, preferred_element_type=f32)
            gup = (ga * slope_v[p, rs, :]).astype(bf16)
            gup_v[rs, :] = gup
            dhid_v[rs, :] += lax.dot_general(gup, wu_v[p], nt, preferred_element_type=f32)
            return total + jnp.sum(gup.astype(f32), 0, keepdims=True)

        sgrad_ref[pl.ds(8 + p, 1), :] = lax.fori_loop(0, tiles, back_rows, zero)

        @pl.when(p >= 2)
        def _():
            remote(got_d.at[p - 2], got_d.at[p - 2], dsend.at[p - 2], drecv.at[p - 2]).wait_send()

            @pl.when(p % 2 != core)
            def _():
                half = p // 2 - 1
                remote(got_u.at[half], got_u.at[half], usend.at[half], urecv.at[half]).wait_send()

        for m in range(pieces):
            cs = slice(m * tile, (m + 1) * tile)
            stage_d[par, cs, :] = lax.dot_general(act_v[p, :, cs], gffn_v[...], tn, preferred_element_type=f32).astype(bf16)
        for jj in range(2):
            for yy in range(2):
                at = pl.multiple_of((4 * jj + 2 * yy + 1 - core) * rows, 16)
                remote(stage_d.at[par, pl.ds(at, rows)], got_d.at[p, jj, yy], dsend.at[p], drecv.at[p]).start()
        for m in range(pieces):
            cs = slice(m * tile, (m + 1) * tile)
            stage_u[par, cs, :] = lax.dot_general(hid_v[:, cs], gup_v[...], tn, preferred_element_type=f32).astype(bf16)

        @pl.when(p % 2 != core)
        def _():
            remote(stage_u.at[par], got_u.at[p // 2], usend.at[p // 2], urecv.at[p // 2]).start()

        @pl.when(p > 0)
        def _():
            finish_chunk(p - 1, 1 - par)

        return 0

    lax.fori_loop(0, 4, back, 0)

    def norm_back(r, sums):
        rs = rowsl(r)
        dg, db, da = sums
        dy = dhid_v[rs, :]
        xhat = xhat_v[rs, :]
        dg = dg + jnp.sum(dy * xhat, 0, keepdims=True)
        db = db + jnp.sum(dy, 0, keepdims=True)
        dx = dy * small_ref[0:1, :]
        dx = rstd_v[rs, 0:1] * (dx - jnp.mean(dx, -1, keepdims=True) - xhat * jnp.mean(dx * xhat, -1, keepdims=True))
        first_ref[rs, :] = dx
        short = dx.astype(bf16)
        hid_v[rs, :] = short
        da = da + jnp.sum(short.astype(f32), 0, keepdims=True)
        for t in range(4):
            gmixes[t][rs, :] = lax.dot_general(
                short, wo_rows(flip(place, t)), nt, preferred_element_type=f32
            ).astype(bf16)
        return dg, db, da

    dg1, db1, da = lax.fori_loop(0, tiles, norm_back, (zero, zero, zero))
    sgrad_ref[0:1, :] = dg1
    sgrad_ref[1:2, :] = db1
    sgrad_ref[4:5, :] = da
    for j in range(items):
        stage_o[j, pl.ds(rows, third)] = jnp.zeros((third, width), bf16)
    for t in range(4):
        q = flip(place, t)
        part = lax.dot_general(mixes[t][...], hid_v[...], tn, preferred_element_type=f32).astype(bf16)
        stage_o[2 * q, pl.ds(0, rows)] = part[:rows]
        stage_o[2 * q + 1, pl.ds(0, rows)] = part[rows:]
    o_copies = []
    for yy in range(2):
        at = pl.multiple_of((2 * yy + 1 - core) * third, 16)
        copy = remote(stage_o.at[:, pl.ds(at, third)], got_o.at[yy], osend.at[yy], orecv.at[yy])
        copy.start()
        o_copies.append(copy)
    finish_chunk(3, 1)
    for yy in range(2):
        o_copies[yy].wait_recv()
        at = pl.multiple_of((2 * yy + core) * third, 16)
        for j in range(items):
            total = stage_o[j, pl.ds(at, third)].astype(f32) + got_o[yy, j].astype(f32)
            got_o[yy, j] = total.astype(bf16)
        for yrel in range(2):

            @pl.when((yy + far) % 2 == yrel)
            def _():
                for j in range(items):
                    pltpu.make_async_copy(got_o.at[yy, j], in_p(yrel, j, rows, third), flush.at[2]).start()

    mix_copy.wait_send()
    for which in range(3):
        half = (wo_v.at[pl.ds(0, items // 2)], wu_v.at[pl.ds(0, 2)], wd_v.at[pl.ds(0, 2)])[which]
        remote(half, half, wsend.at[which], wrecv.at[which]).wait_send()
    for p in (2, 3):
        remote(got_d.at[p], got_d.at[p], dsend.at[p], drecv.at[p]).wait_send()
    remote(got_u.at[1], got_u.at[1], usend.at[1], urecv.at[1]).wait_send()
    for yy in range(2):
        o_copies[yy].wait_send()
    pltpu.make_async_copy(got_d, got_d, flush.at[0]).wait()
    pltpu.make_async_copy(got_u, got_u, flush.at[1]).wait()
    pltpu.make_async_copy(got_o, got_o, flush.at[2]).wait()


def middle(weights, x, mixes, dout, small, tile=256):
    levels, quarter, width = weights[0].shape
    items = 2 * levels
    rows = quarter * 3 // 7
    third = rows // 3
    tokens = x.shape[0]
    any_space = pl.BlockSpec(memory_space=pl.ANY)
    vmem = pl.BlockSpec(memory_space=pltpu.VMEM)
    square = (tokens, width)
    dma = pltpu.SemaphoreType.DMA
    head_part = jax.ShapeDtypeStruct((tokens, width // 4), bf16)
    p_shape = jax.ShapeDtypeStruct((2, items // 2, rows + third, width), bf16)
    q_shape = jax.ShapeDtypeStruct((2, items // 2, rows, width), bf16)
    return pl.pallas_call(
        functools.partial(middle_kernel, (items, rows, width, tile)),
        out_shape=(
            jax.ShapeDtypeStruct(square, bf16),
            jax.ShapeDtypeStruct(square, f32),
            head_part, head_part, head_part, head_part,
            p_shape, p_shape, q_shape, q_shape,
            jax.ShapeDtypeStruct(small.shape, f32),
        ),
        in_specs=[any_space] * 4 + [vmem] * 7,
        out_specs=(vmem,) * 6 + (any_space,) * 4 + (vmem,),
        scratch_shapes=[
            pltpu.VMEM((items, 4 * third, width), bf16),
            pltpu.VMEM((4, width, width), bf16),
            pltpu.VMEM((4, width, width), bf16),
            pltpu.VMEM(square, f32),
            pltpu.VMEM(square, bf16),
            pltpu.VMEM((4, tokens, width), bf16),
            pltpu.VMEM((4, tokens, width), f32),
            pltpu.VMEM(square, f32),
            pltpu.VMEM(square, bf16),
            pltpu.VMEM(square, bf16),
            pltpu.VMEM(square, f32),
            pltpu.VMEM((tokens, 128), f32),
            pltpu.VMEM((2, width, width), bf16),
            pltpu.VMEM((2, width, width), bf16),
            pltpu.VMEM((items, 4 * third, width), bf16),
            pltpu.VMEM((2, width, width), bf16),
            pltpu.VMEM((4, 2, 2, rows, width), bf16),
            pltpu.VMEM((2, items, third, width), bf16),
            pltpu.VMEM((tokens, width // 4), bf16),
            dma((3,)), dma((3,)), dma((3,)), dma((1,)), dma((1,)), dma((2,)), dma((2,)), dma((4,)), dma((4,)),
            dma((2,)), dma((2,)), dma((3,)),
        ],
        compiler_params=pltpu.CompilerParams(vmem_limit_bytes=61 << 20, collective_id=2, has_side_effects=True),
        cost_estimate=pl.CostEstimate(flops=60 * 10**9, bytes_accessed=10**7, transcendentals=0),
        name="middle",
    )(*weights, x, *mixes, dout, small)


def swap(values, axis, bit):
    size = lax.axis_size(axis)
    return lax.ppermute(values, axis, [(i, i ^ bit) for i in range(size)])


def take(values, at, dim):
    return lax.dynamic_index_in_dim(values, at, dim, keepdims=False)


def add_short(a, b):
    return (a.astype(f32) + b.astype(f32)).astype(bf16)


def layer_norm(values, gain, bias):
    average = jnp.mean(values, -1, keepdims=True)
    centered = values - average
    spread = jnp.mean(centered * centered, -1, keepdims=True)
    return centered * lax.rsqrt(spread + norm_epsilon) * gain + bias


def exact_gelu(values):
    return jax.nn.gelu(values, approximate=False)


def packed_columns(own):
    heads = own.shape[2]
    cols = []
    for h in range(heads):
        pair = [own[:, 2, h], own[:, 1, h]]
        cols += pair if h % 2 == 0 else pair[::-1]
    for p in range((heads + 1) // 2):
        odd = own[:, 0, 2 * p + 1] if 2 * p + 1 < heads else jnp.zeros_like(own[:, 0, 0])
        cols += [odd * HD**-0.5, own[:, 0, 2 * p] * HD**-0.5]
    return jnp.concatenate(cols, -1)


def natural_columns(values, heads):
    parts = [[], [], []]
    for h in range(heads):
        first, second = values[:, h * 128 : h * 128 + HD], values[:, h * 128 + HD : h * 128 + 128]
        base = (heads + h // 2) * 128
        if h % 2 == 0:
            parts[2].append(first)
            parts[1].append(second)
            parts[0].append(values[:, base + HD : base + 128] * HD**-0.5)
        else:
            parts[1].append(first)
            parts[2].append(second)
            parts[0].append(values[:, base : base + HD] * HD**-0.5)
    return jnp.concatenate(parts[0] + parts[1] + parts[2], -1)


def on_device(
    inputs,
    d_output,
    glob_count,
    glob_pos,
    rand_blocks,
    w_qkv,
    w_out,
    w_up,
    w_down,
    small_params,
    first_qkv,
    second_qkv,
    first_out,
    second_out,
    first_up,
    second_up,
    first_down,
    second_down,
    first_small,
    second_small,
):
    _, tok_rows, width = inputs.shape
    groups = lax.axis_size("seq")
    items = lax.axis_size("item")
    place = lax.axis_index("seq")
    heads = rand_blocks.shape[1]
    rows = w_out.shape[0]
    third = rows // 3

    own = take(w_qkv.reshape(-1, 3, groups, heads, HD), place, 2)
    piece = packed_columns(own).astype(bf16)
    tokens_b = inputs.reshape(tok_rows, width)
    quarter = jnp.concatenate(
        [
            take(w_up.reshape(rows, 4, width), place, 1),
            take(w_down.reshape(4, rows, width), place, 0),
            take(w_out.reshape(3, third, width), jnp.minimum(place, 2), 0),
        ],
        0,
    ).astype(bf16)
    bias3 = jnp.stack([small_params[2], jnp.zeros((width,), f32), small_params[3]])
    slab_bias = packed_columns(take(bias3.reshape(1, 3, groups, heads, HD), place, 2))
    *others, qkv, slab, w_line, w_side, w_far = head(tokens_b, piece, quarter, slab_bias, items)
    xs = [tokens_b, *others]
    w_far_side = swap(w_side, "seq", 2)
    idx, bias, gl = slots(glob_count[0], glob_pos[0], rand_blocks[0], place)
    mix2, mix3, lse_far = attn_fwd(idx, gl, qkv, bias, heads, 2, 2)
    mix2_in, mix3_in = swap(mix2, "seq", 2), swap(mix3, "seq", 3)
    mix0, mix1, lse_near = attn_fwd(idx, gl, qkv, bias, heads, 0, 2)
    w_far_side, mix0, mix1, mix2_in, mix3_in = lax.optimization_barrier((w_far_side, mix0, mix1, mix2_in, mix3_in))
    outputs, grad_first, *grad_mixed, p_keep, p_send, q_keep, q_send, small_part = middle(
        (w_line, w_side, w_far, w_far_side), tokens_b, (mix0, mix1, mix2_in, mix3_in), d_output.reshape(tok_rows, width), small_params
    )
    grads_in = [grad_mixed[0]] + [swap(grad_mixed[t], "seq", t) for t in range(1, 4)]
    p_in = swap(p_send, "seq", 2)
    q_in = swap(q_send, "item", 1)
    acc, dq_near = attn_bwd(idx, gl, qkv, bias, grads_in[:2], lse_near, heads, 0, (), False)
    p_in, q_in, acc, dq_near = lax.optimization_barrier((p_in, q_in, acc, dq_near))
    p_next = swap(add_short(p_keep[1], p_in[1]), "item", 1)
    q_next = swap(add_short(q_keep[1], q_in[1]), "seq", 2)
    p_here, q_here = add_short(p_keep[0], p_in[0]), add_short(q_keep[0], q_in[0])
    grad_qkv = attn_bwd(idx, gl, qkv, bias, grads_in[2:], lse_far, heads, 2, (acc, dq_near), True)
    p_next, q_next, grad_qkv = lax.optimization_barrier((p_next, q_next, grad_qkv))
    small16 = jnp.pad(small_part, ((0, 4), (0, 0)))
    grad_inputs, group, slab_group, small_total, squares = tail(
        xs, grad_qkv, slab, grad_first, small16, (p_here, p_next, q_here, q_next), items, heads * 128
    )
    norm, *states = update(
        lambda: lax.axis_index("seq"),
        heads,
        group,
        slab_group,
        small_total,
        squares,
        (
            w_qkv, first_qkv, second_qkv, w_out, first_out, second_out, w_up, first_up, second_up,
            w_down, first_down, second_down, small_params, first_small, second_small,
        ),
    )
    return (outputs[None], grad_inputs[None], norm.reshape(()), *states)


def on_device_many(
    inputs,
    d_output,
    glob_count,
    glob_pos,
    rand_blocks,
    w_qkv,
    w_out,
    w_up,
    w_down,
    small_params,
    first_qkv,
    second_qkv,
    first_out,
    second_out,
    first_up,
    second_up,
    first_down,
    second_down,
    first_small,
    second_small,
):
    items_n, tok_rows, width = inputs.shape
    groups = lax.axis_size("seq")
    place = lax.axis_index("seq")
    heads = rand_blocks.shape[1]
    row_count = tok_rows

    own = lax.dynamic_index_in_dim(
        w_qkv.reshape(-1, 3, groups, heads, HD), place, 2, keepdims=False
    )
    slab = lax.all_gather(packed_columns(own).astype(bf16), "item", axis=0, tiled=True)
    full_out, full_up, full_down = (
        lax.all_gather(w_out.astype(bf16), "item", axis=0, tiled=True),
        lax.all_gather(w_up.astype(bf16), "item", axis=0, tiled=True),
        lax.all_gather(w_down.astype(bf16), "item", axis=0, tiled=True),
    )
    bias3 = jnp.stack([small_params[2], jnp.zeros((width,), f32), small_params[3]])
    own_bias = lax.dynamic_index_in_dim(
        bias3.reshape(1, 3, groups, heads, HD), place, 2, keepdims=False
    )
    slab_bias = packed_columns(own_bias)
    tokens_b = inputs.reshape(tok_rows, width)
    tokens_all = lax.all_gather(tokens_b, "seq", axis=0, tiled=True)
    tokens_f = tokens_b.astype(f32)
    qkv = (jnp.dot(tokens_all, slab, preferred_element_type=f32) + slab_bias).astype(bf16)
    idx, bias, gl = slots(glob_count[0], glob_pos[0], rand_blocks[0], jnp.int32(0))
    *mixed_parts, lse = attn_fwd(idx, gl, qkv, bias, heads, 0, 4)
    mixed_heads = jnp.concatenate(mixed_parts, 0)
    mixed = lax.all_to_all(mixed_heads, "seq", split_axis=0, concat_axis=1, tiled=True)
    attn_out = jnp.dot(mixed, full_out, preferred_element_type=f32) + small_params[4]
    hidden, norm_one_back = jax.vjp(
        layer_norm, tokens_f + attn_out, small_params[0], small_params[1]
    )
    hidden_b = hidden.astype(bf16)
    up_pre = jnp.dot(hidden_b, full_up, preferred_element_type=f32) + small_params[8:12].reshape(-1)
    active, gelu_back = jax.vjp(exact_gelu, up_pre)
    active_b = active.astype(bf16)
    ffn_out = jnp.dot(active_b, full_down, preferred_element_type=f32) + small_params[7]
    outputs, norm_two_back = jax.vjp(layer_norm, hidden + ffn_out, small_params[5], small_params[6])
    grad_second, grad_gain_two, grad_bias_two = norm_two_back(
        d_output.reshape(row_count, width).astype(f32)
    )
    grad_ffn = grad_second.astype(bf16)
    grad_w_down = jnp.einsum("rf,rd->fd", active_b, grad_ffn, preferred_element_type=f32)
    grad_active = jnp.einsum("rd,fd->rf", grad_ffn, full_down, preferred_element_type=f32)
    (grad_up_pre,) = gelu_back(grad_active)
    grad_up_b = grad_up_pre.astype(bf16)
    grad_w_up = jnp.einsum("rd,rf->df", hidden_b, grad_up_b, preferred_element_type=f32)
    grad_hidden = grad_second + jnp.einsum(
        "rf,df->rd", grad_up_b, full_up, preferred_element_type=f32
    )
    grad_first, grad_gain_one, grad_bias_one = norm_one_back(grad_hidden)
    grad_attn = grad_first.astype(bf16)
    grad_w_out = jnp.einsum("rm,rd->md", mixed, grad_attn, preferred_element_type=f32)
    grad_mixed = jnp.einsum("rd,md->rm", grad_attn, full_out, preferred_element_type=f32).astype(
        bf16
    )
    grad_heads = lax.all_to_all(grad_mixed, "seq", split_axis=1, concat_axis=0, tiled=True)
    grads_in = [grad_heads[t * tok_rows : (t + 1) * tok_rows] for t in range(4)]
    grad_qkv = attn_bwd(idx, gl, qkv, bias, grads_in, lse, heads, 0, (), True)
    grad_slab = jnp.einsum("rd,re->de", tokens_all, grad_qkv, preferred_element_type=f32)
    grad_tokens = jnp.einsum("re,de->rd", grad_qkv, slab, preferred_element_type=f32).astype(bf16)
    grad_inputs = grad_first + lax.psum_scatter(
        grad_tokens, "seq", scatter_dimension=0, tiled=True
    ).astype(f32)
    slab_sum = natural_columns(jnp.sum(grad_qkv.astype(f32), 0)[None], heads)[0]
    bias_grads = lax.dynamic_update_index_in_dim(
        jnp.zeros((3, groups, heads * HD), f32), slab_sum.reshape(3, heads * HD), place, 1
    ).reshape(3, width)
    small_rows = jnp.stack(
        [
            grad_gain_one,
            grad_bias_one,
            bias_grads[0],
            bias_grads[2],
            jnp.sum(grad_attn.astype(f32), 0),
            grad_gain_two,
            grad_bias_two,
            jnp.sum(grad_ffn.astype(f32), 0),
        ]
    )
    small_part = jnp.concatenate(
        [small_rows, jnp.sum(grad_up_b.astype(f32), 0).reshape(4, width)], 0
    )
    small_total = lax.psum(small_part, ("item", "seq"))
    shard_down = lax.psum_scatter(grad_w_down.astype(bf16), "item", scatter_dimension=0, tiled=True)
    shard_up = lax.psum_scatter(grad_w_up.astype(bf16), "item", scatter_dimension=0, tiled=True)
    shard_out = lax.psum_scatter(grad_w_out.astype(bf16), "item", scatter_dimension=0, tiled=True)
    shard_slab = lax.psum_scatter(grad_slab.astype(bf16), "item", scatter_dimension=0, tiled=True)
    shard_slab = natural_columns(shard_slab.astype(f32), heads).reshape(-1, 3, 1, heads * HD)
    shard_qkv = lax.all_gather(shard_slab, "seq", axis=2, tiled=True).reshape(-1, 3 * width)
    shard_out, shard_up, shard_down = lax.psum(
        (shard_out.astype(f32), shard_up.astype(f32), shard_down.astype(f32)), "seq"
    )
    local_squares = (
        jnp.sum(shard_qkv * shard_qkv)
        + jnp.sum(shard_out * shard_out)
        + jnp.sum(shard_up * shard_up)
        + jnp.sum(shard_down * shard_down)
    )
    matrix_squares = lax.psum(local_squares, "item")
    grad_norm = jnp.sqrt(matrix_squares + jnp.sum(small_total * small_total))
    factor = jnp.minimum(1.0, clip_level / (grad_norm + 1e-06))
    new_qkv = adam_update(
        w_qkv, first_qkv, second_qkv, shard_qkv * factor, weight_decay, learn_rate
    )
    new_out = adam_update(
        w_out, first_out, second_out, shard_out * factor, weight_decay, learn_rate
    )
    new_up = adam_update(w_up, first_up, second_up, shard_up * factor, weight_decay, learn_rate)
    new_down = adam_update(
        w_down, first_down, second_down, shard_down * factor, weight_decay, learn_rate
    )
    new_small = adam_update(
        small_params, first_small, second_small, small_total * factor, 0.0, small_rate
    )
    return (
        outputs.astype(bf16).reshape(items_n, tok_rows, width),
        grad_inputs.reshape(items_n, tok_rows, width),
        grad_norm,
        new_qkv[0],
        new_qkv[1],
        new_qkv[2],
        new_out[0],
        new_out[1],
        new_out[2],
        new_up[0],
        new_up[1],
        new_up[2],
        new_down[0],
        new_down[1],
        new_down[2],
        new_small[0],
        new_small[1],
        new_small[2],
    )


def solution(mesh):
    few = mesh.shape["item"] == 8 and mesh.shape["seq"] == 4
    return jax.shard_map(
        on_device if few else on_device_many,
        mesh=mesh,
        in_specs=(
            P("item", "seq", None),
            P("item", "seq", None),
            P("item"),
            P("item", None),
            P("item", "seq", None, None),
            P("item", None),
            P("item", None),
            P("item", None),
            P("item", None),
            P(),
            P("item", None),
            P("item", None),
            P("item", None),
            P("item", None),
            P("item", None),
            P("item", None),
            P("item", None),
            P("item", None),
            P(),
            P(),
        ),
        out_specs=(
            P("item", "seq", None),
            P("item", "seq", None),
            P(),
            P("item", None),
            P("item", None),
            P("item", None),
            P("item", None),
            P("item", None),
            P("item", None),
            P("item", None),
            P("item", None),
            P("item", None),
            P("item", None),
            P("item", None),
            P("item", None),
            P(),
            P(),
            P(),
        ),
        check_vma=False,
    )
```

```python
import functools

import jax
import jax.numpy as jnp
from jax import lax
from jax.experimental import pallas as pl
from jax.experimental.pallas import tpu as pltpu
from jax.sharding import PartitionSpec as P

ADAM_STEP = 10
norm_epsilon = 1e-06
beta_first = 0.9
beta_second = 0.999
adam_epsilon = 1e-08
learn_rate = 0.1
small_rate = 0.5
weight_decay = 0.01
clip_level = 1.0


def adam_update(weight, first, second, grad, decay, rate):
    first_new = beta_first * first + (1.0 - beta_first) * grad
    second_new = beta_second * second + (1.0 - beta_second) * grad * grad
    first_hat = first_new / (1.0 - beta_first**ADAM_STEP)
    second_hat = second_new / (1.0 - beta_second**ADAM_STEP)
    weight_new = weight - rate * (
        first_hat / (jnp.sqrt(second_hat) + adam_epsilon) + decay * weight
    )
    return (weight_new, first_new, second_new)


HD = 64
BL = 64
NEG = -1e30
bf16 = jnp.bfloat16
f32 = jnp.float32
NT = (((1,), (1,)), ((), ()))
TN = (((0,), (0,)), ((), ()))


def slots(count, positions, table, place):
    heads, nblocks, picks = table.shape
    chunk = nblocks // 4
    globals_n = positions.shape[0]
    here = jnp.arange(nblocks, dtype=jnp.int32)

    def turned(b):
        return ((b // chunk) ^ place) * chunk + b % chunk

    block = turned(here)
    rows = table.reshape(heads, 2, 2, chunk, picks)
    rows = jnp.where(place % 2 == 1, rows[:, :, ::-1], rows)
    rows = jnp.where(place // 2 == 1, rows[:, ::-1], rows).reshape(heads, nblocks, picks)
    window = jnp.stack([block - 1, block, block + 1], -1)
    active = jnp.arange(globals_n, dtype=jnp.int32) < count
    parts = jnp.concatenate(
        [
            jnp.broadcast_to(window[None], (heads, nblocks, 3)),
            jnp.broadcast_to(jnp.where(active, positions, -1)[None, None], (heads, nblocks, globals_n)),
            rows,
        ],
        -1,
    )
    count_slots = 3 + globals_n + picks
    valid = (parts >= 0) & (parts < nblocks)
    same = parts[..., :, None] == parts[..., None, :]
    earlier = jnp.arange(count_slots)[:, None] > jnp.arange(count_slots)[None, :]
    repeated = jnp.any(same & earlier, -1)
    is_global = jnp.any((positions[None, :] == block[:, None]) & active[None], -1)
    valid = valid & ~repeated & ~is_global[None, :, None]
    idx = turned(jnp.clip(parts, 0, nblocks - 1))
    bias = jnp.where(valid, 0.0, NEG).astype(f32)
    bias = jnp.broadcast_to(bias[..., None], (heads, nblocks, count_slots, BL))
    glob = jnp.concatenate([count[None], turned(positions)])
    return idx.reshape(-1), bias.reshape(heads * nblocks, count_slots * BL), glob


def low_lanes(rows):
    return lax.broadcasted_iota(jnp.int32, (rows, 2 * HD), 1) < HD


def pick(block, keep_low):
    low = low_lanes(block.shape[0])
    return jnp.where(low if keep_low else ~low, block, jnp.zeros_like(block))


def fwd_kernel(dims, idx_ref, gl_ref, qkv_ref, bias_ref, *rest):
    heads, nblocks, slots_n, first, parts, chunk, wide = dims
    out_refs, lse_ref, sbuf, s_v, e_v, l_v, out_v = rest[:parts], rest[parts], *rest[parts + 1 :]
    n = nblocks * BL
    lane = lax.broadcasted_iota(jnp.int32, (BL, 128), 1)

    def finish(row, outs, lses):
        low = low_lanes(BL)
        for p in range((heads + 1) // 2):
            if 2 * p + 1 < heads:
                both = jnp.where(low, outs[2 * p], outs[2 * p + 1])
                out_v[pl.ds(row, BL), p * 128 : (p + 1) * 128] = both.astype(bf16)
            else:
                out_v[pl.ds(row, BL), p * 128 : p * 128 + HD] = outs[2 * p][:, :HD].astype(bf16)
        total = jnp.zeros((BL, 128), f32)
        for h in range(heads):
            total = jnp.where(lane == h, lses[h], total)
        lse_ref[pl.ds(row, BL), :] = total

    def queries(r, h):
        return pick(qkv_ref[pl.ds(r, BL), (heads + h // 2) * 128 : (heads + h // 2 + 1) * 128], h % 2 == 1)

    blocks = parts * chunk

    def clamp(b):
        return jnp.minimum(jnp.maximum(b, 0), blocks - 1)

    def gathered(a, h):
        base = (h * nblocks + a) * slots_n
        return jnp.concatenate(
            [
                qkv_ref[pl.ds(pl.multiple_of(idx_ref[base + j] * BL, BL), BL), h * 128 : (h + 1) * 128]
                for j in range(slots_n)
            ],
            0,
        )

    def body(b, _):
        last, now, new = clamp(b - 2), clamp(b - 1), clamp(b)
        outs, lses = [], []
        for h in range(heads):
            o = jnp.dot(e_v[h], gathered(first + last, h), preferred_element_type=f32)
            outs.append(o)
            lses.append(l_v[h])
        finish(pl.multiple_of(last * BL, BL), outs, lses)
        for h in range(heads):
            s = s_v[h] + bias_ref[pl.ds(h * nblocks + first + now, 1), :]
            m = jnp.max(s, -1, keepdims=True)
            e = jnp.exp(s - m)
            l = jnp.sum(e, -1, keepdims=True)
            e_v[h] = (e * (1.0 / l)).astype(bf16)
            l_v[h] = jnp.broadcast_to(m + jnp.log(l), (BL, 128))
        for h in range(heads):
            a = first + new
            s_v[h] = lax.dot_general(
                queries(pl.multiple_of(a * BL, BL), h), gathered(a, h), NT, preferred_element_type=f32
            )
        return 0

    lax.fori_loop(0, blocks + 2, body, 0)

    def whole_row(g, _):
        a = gl_ref[1 + g]
        local = a - first

        @pl.when((local >= 0) & (local < parts * chunk))
        def _():
            r = pl.multiple_of(a * BL, BL)
            outs, lses = [], []
            for h in range(heads):
                q = queries(r, h)
                m = None
                for c in range(n // wide):
                    cs = slice(c * wide, (c + 1) * wide)
                    s = lax.dot_general(q, qkv_ref[cs, h * 128 : (h + 1) * 128], NT, preferred_element_type=f32)
                    sbuf[h, :, cs] = s
                    mc = jnp.max(s, -1, keepdims=True)
                    m = mc if m is None else jnp.maximum(m, mc)
                l = 0.0
                for c in range(n // wide):
                    cs = slice(c * wide, (c + 1) * wide)
                    e = jnp.exp(sbuf[h, :, cs] - m)
                    sbuf[h, :, cs] = e
                    l = l + jnp.sum(e, -1, keepdims=True)
                inv = 1.0 / l
                o = 0.0
                for c in range(n // wide):
                    cs = slice(c * wide, (c + 1) * wide)
                    p = (sbuf[h, :, cs] * inv).astype(bf16)
                    o = o + jnp.dot(p, qkv_ref[cs, h * 128 : (h + 1) * 128], preferred_element_type=f32)
                outs.append(o)
                lses.append(m + jnp.log(l))
            finish(pl.multiple_of(local * BL, BL), outs, lses)

        return 0

    lax.fori_loop(0, gl_ref[0], whole_row, 0)
    for part in range(parts):
        out_refs[part][...] = out_v[part * chunk * BL : (part + 1) * chunk * BL, :]


def attn_fwd(idx, gl, qkv, bias, heads, first_part, parts):
    n = qkv.shape[0]
    nblocks = n // BL
    chunk = nblocks // 4
    slots_n = bias.shape[1] // BL
    vmem = pl.BlockSpec(memory_space=pltpu.VMEM)
    smem = pl.BlockSpec(memory_space=pltpu.SMEM)
    dims = (heads, nblocks, slots_n, first_part * chunk, parts, chunk, 512)
    return pl.pallas_call(
        functools.partial(fwd_kernel, dims),
        out_shape=tuple([jax.ShapeDtypeStruct((n // 4, heads * HD), bf16)] * parts)
        + (jax.ShapeDtypeStruct((parts * n // 4, 128), f32),),
        in_specs=[smem, smem, vmem, vmem],
        out_specs=tuple([vmem] * (parts + 1)),
        scratch_shapes=[
            pltpu.VMEM((heads, BL, n), f32),
            pltpu.VMEM((heads, BL, slots_n * BL), f32),
            pltpu.VMEM((heads, BL, slots_n * BL), bf16),
            pltpu.VMEM((heads, BL, 128), f32),
            pltpu.VMEM((parts * n // 4, heads * HD), bf16),
        ],
        compiler_params=pltpu.CompilerParams(vmem_limit_bytes=24 << 20),
        cost_estimate=pl.CostEstimate(flops=10 * parts * 10**9, bytes_accessed=10**7, transcendentals=0),
        name="attn_fwd",
    )(idx, gl, qkv, bias)


def bwd_kernel(dims, idx_ref, gl_ref, qkv_ref, bias_ref, *rest):
    heads, nblocks, slots_n, first, parts, chunk, wide, begin, end = dims
    g_refs, rest = rest[:parts], rest[parts:]
    lse_ref, rest = rest[0], rest[1:]
    if not begin:
        acc_in, dq_in, rest = rest[0], rest[1], rest[2:]
    if end:
        out_ref, acc, pbuf, dbuf, sd_v, w_v, g_v = rest
    else:
        acc, dq_ref, pbuf, dbuf, sd_v, w_v, g_v = rest
    n = nblocks * BL
    pairs = (heads + 1) // 2
    kvw = heads * 128

    def start(i, _):
        rr = pl.ds(pl.multiple_of(i * 256, 256), 256)
        if begin:
            acc[rr, :] = jnp.zeros((256, kvw), f32)
        else:
            acc[rr, :] = acc_in[rr, :]
        return 0

    lax.fori_loop(0, n // 256, start, 0)
    if end and not begin:
        out_ref[0 : first * BL, kvw:] = dq_in[...]

    for part in range(parts):
        g_v[part * chunk * BL : (part + 1) * chunk * BL, :] = g_refs[part][...]

    def grads(at, h):
        w = min(128, heads * HD - (h // 2) * 128)
        g = g_v[pl.ds(at, BL), (h // 2) * 128 : (h // 2) * 128 + w]
        if w < 128:
            return jnp.concatenate([g, jnp.zeros((BL, 128 - w), bf16)], 1)
        return pick(g, h % 2 == 0)

    def queries(r, h):
        return pick(qkv_ref[pl.ds(r, BL), (heads + h // 2) * 128 : (heads + h // 2 + 1) * 128], h % 2 == 1)

    def finish(r, dqs):
        low = low_lanes(BL)
        for p in range(pairs):
            high = dqs[2 * p]
            odd = dqs[2 * p + 1] if 2 * p + 1 < heads else jnp.zeros_like(high)
            both = jnp.where(low, odd, high).astype(bf16)
            if end:
                out_ref[pl.ds(r, BL), kvw + p * 128 : kvw + (p + 1) * 128] = both
            else:
                dq_ref[pl.ds(pl.multiple_of(r - first * BL, BL), BL), p * 128 : (p + 1) * 128] = both

    blocks = parts * chunk

    def clamp(b):
        return jnp.minimum(jnp.maximum(b, 0), blocks - 1)

    def slot_rows(a, h):
        base = (h * nblocks + a) * slots_n
        return [pl.multiple_of(idx_ref[base + j] * BL, BL) for j in range(slots_n)]

    def stacked(b, h):
        r = pl.multiple_of((first + b) * BL, BL)
        return jnp.concatenate([queries(r, h), grads(pl.multiple_of(b * BL, BL), h)], 0)

    def body(b, _):
        last, now, new = clamp(b - 2), clamp(b - 1), clamp(b)
        dqs = []
        for h in range(heads):
            hs = slice(h * 128, (h + 1) * 128)
            rows = slot_rows(first + last, h)
            kv = jnp.concatenate([qkv_ref[pl.ds(rows[j], BL), hs] for j in range(slots_n)], 0)
            dqs.append(jnp.dot(w_v[h, :BL], kv, preferred_element_type=f32))
            dkv = lax.dot_general(w_v[h], stacked(last, h), TN, preferred_element_type=f32)
            dkv = jnp.where(b >= 2, dkv, 0.0)
            for j in range(slots_n):
                acc[pl.ds(rows[j], BL), hs] += dkv[j * BL : (j + 1) * BL]
        finish(pl.multiple_of((first + last) * BL, BL), dqs)
        for h in range(heads):
            sd = sd_v[h]
            row = pl.multiple_of(now * BL, BL)
            p = jnp.exp(
                sd[:BL] + bias_ref[pl.ds(h * nblocks + first + now, 1), :] - lse_ref[pl.ds(row, BL), h : h + 1]
            )
            dp = sd[BL:]
            ds = p * (dp - jnp.sum(dp * p, -1, keepdims=True))
            w_v[h, :BL] = ds.astype(bf16)
            w_v[h, BL:] = p.astype(bf16)
        for h in range(heads):
            rows = slot_rows(first + new, h)
            kv = jnp.concatenate(
                [qkv_ref[pl.ds(rows[j], BL), h * 128 : (h + 1) * 128] for j in range(slots_n)], 0
            )
            sd_v[h] = lax.dot_general(stacked(new, h), kv, NT, preferred_element_type=f32)
        return 0

    sd_v[...] = jnp.zeros_like(sd_v)
    w_v[...] = jnp.zeros_like(w_v)
    lax.fori_loop(0, blocks + 2, body, 0)

    def whole_row(g, _):
        a = gl_ref[1 + g]
        local = a - first

        @pl.when((local >= 0) & (local < parts * chunk))
        def _():
            r = pl.multiple_of(a * BL, BL)
            row = pl.multiple_of(local * BL, BL)
            dqs = []
            for h in range(heads):
                hs = slice(h * 128, (h + 1) * 128)
                x = jnp.concatenate([queries(r, h), grads(row, h)], 0)
                lse = lse_ref[pl.ds(row, BL), h : h + 1]
                inner = 0.0
                for c in range(n // wide):
                    cs = slice(c * wide, (c + 1) * wide)
                    sd = lax.dot_general(x, qkv_ref[cs, hs], NT, preferred_element_type=f32)
                    p = jnp.exp(sd[:BL] - lse)
                    dp = sd[BL:]
                    pbuf[h, :, cs] = p
                    dbuf[h, :, cs] = dp
                    inner = inner + jnp.sum(dp * p, -1, keepdims=True)
                dq = 0.0
                for c in range(n // wide):
                    cs = slice(c * wide, (c + 1) * wide)
                    p = pbuf[h, :, cs]
                    ds = (p * (dbuf[h, :, cs] - inner)).astype(bf16)
                    w = jnp.concatenate([ds, p.astype(bf16)], 0)
                    dq = dq + jnp.dot(ds, qkv_ref[cs, hs], preferred_element_type=f32)
                    acc[cs, hs] += lax.dot_general(w, x, TN, preferred_element_type=f32)
                dqs.append(dq)
            finish(r, dqs)

        return 0

    lax.fori_loop(0, gl_ref[0], whole_row, 0)
    if end:

        def flush(i, _):
            rr = pl.ds(pl.multiple_of(i * 256, 256), 256)
            out_ref[rr, :kvw] = acc[rr, :].astype(bf16)
            return 0

        lax.fori_loop(0, n // 256, flush, 0)


def attn_bwd(idx, gl, qkv, bias, grads, lse, heads, first_part, carried, end):
    n = qkv.shape[0]
    nblocks = n // BL
    chunk = nblocks // 4
    slots_n = bias.shape[1] // BL
    parts = len(grads)
    vmem = pl.BlockSpec(memory_space=pltpu.VMEM)
    smem = pl.BlockSpec(memory_space=pltpu.SMEM)
    dims = (heads, nblocks, slots_n, first_part * chunk, parts, chunk, 512, not carried, end)
    pairs = (heads + 1) // 2
    scratch = [pltpu.VMEM((heads, BL, n), f32)] * 2 + [
        pltpu.VMEM((heads, 2 * BL, slots_n * BL), f32),
        pltpu.VMEM((heads, 2 * BL, slots_n * BL), bf16),
        pltpu.VMEM((parts * n // 4, heads * HD), bf16),
    ]
    if end:
        out_shape = jax.ShapeDtypeStruct((n, (heads + pairs) * 128), bf16)
        out_specs = vmem
        scratch = [pltpu.VMEM((n, heads * 128), f32)] + scratch
    else:
        out_shape = (
            jax.ShapeDtypeStruct((n, heads * 128), f32),
            jax.ShapeDtypeStruct((parts * n // 4, pairs * 128), bf16),
        )
        out_specs = (vmem, vmem)
    return pl.pallas_call(
        functools.partial(bwd_kernel, dims),
        out_shape=out_shape,
        in_specs=[smem, smem] + [vmem] * (3 + parts + len(carried)),
        out_specs=out_specs,
        scratch_shapes=scratch,
        compiler_params=pltpu.CompilerParams(vmem_limit_bytes=36 << 20),
        cost_estimate=pl.CostEstimate(flops=11 * parts * 10**9, bytes_accessed=10**7, transcendentals=0),
        name="attn_bwd",
    )(idx, gl, qkv, bias, *grads, lse, *carried)


MESH_ID = pl.DeviceIdType.MESH


def flip(index, number):
    total = 0
    for bit in (1, 2, 4):
        digit = (index // bit) % 2
        total = total + bit * ((1 - digit) if number & bit else digit)
    return total


def blend(a, b):
    return sum(bit * (((a // bit) % 2 + (b // bit) % 2) % 2) for bit in (1, 2, 4))


def greet(item, place, items):
    barrier = pltpu.get_barrier_semaphore()
    for t in range(1, 4):
        pl.semaphore_signal(barrier, inc=1, device_id=(item, flip(place, t)), device_id_type=MESH_ID)
    for k in range(1, items):
        pl.semaphore_signal(barrier, inc=1, device_id=(flip(item, k), place), device_id_type=MESH_ID)
    pl.semaphore_wait(barrier, 3 + items - 1)


def tail_kernel(
    items, query_columns, x0, x1, x2, x3, gq_ref, slab_ref, first_ref, small_ref, uk_ref, ur_ref, dk_ref, d1_ref, d2_ref, d3_ref,
    din_ref, group_ref, sgroup_ref, total_ref, squares_ref,
    near_out, near_in, far_out, far_in, grad_v, side_out, side_in, part_out, part_in, z_out, z_in, d_out, d_in, small_in, small_mid, small_side, small_both, small_items, small_sum, sq_out, sq_in, sq_mid, sq_items,
    near_send, near_recv, far_send, far_recv, side_send, side_recv, part_send, part_recv, z_send, z_recv, d_send, d_recv, sg_send, sg_recv, sx_send, sx_recv, si_send, si_recv, st_send, st_recv,
    gr_send, gr_recv, sl_send, sl_recv, qg_send, qg_recv, qi_send, qi_recv,
):
    xs = (x0, x1, x2, x3)
    item, place = lax.axis_index("item"), lax.axis_index("seq")
    tokens, width = x0.shape
    rows = width // items
    tile = tokens // 2
    chunks = tokens // tile
    columns = gq_ref.shape[1]
    levels = items // 2
    up_rows = uk_ref.shape[1]
    greet(item, place, items)

    def to_group(src, dst, send, recv, t):
        return pltpu.make_async_remote_copy(
            src_ref=src, dst_ref=dst, send_sem=send, recv_sem=recv,
            device_id=(item, flip(place, t)), device_id_type=MESH_ID,
        )

    def to_item(src, dst, send, recv, k):
        return pltpu.make_async_remote_copy(
            src_ref=src, dst_ref=dst, send_sem=send, recv_sem=recv,
            device_id=(flip(item, k), place), device_id_type=MESH_ID,
        )

    small_copies = [
        to_group(small_ref.at[flip(place, t)], small_in.at[t], sg_send.at[t], sg_recv.at[t], t) for t in range(1, 4)
    ]
    for copy in small_copies:
        copy.start()

    z_copies = []
    for kz in range(levels - 1, 0, -1):
        z_out[kz] = uk_ref[kz] + ur_ref[kz]
        copy = to_item(z_out.at[kz], z_in.at[kz], z_send.at[kz], z_recv.at[kz], 2 * kz)
        copy.start()
        z_copies.append(copy)

    def down_sum(kx):
        return (
            dk_ref[kx].astype(f32) + d1_ref[kx].astype(f32) + d2_ref[kx].astype(f32) + d3_ref[kx].astype(f32)
        )

    d_out[...] = down_sum(1).astype(bf16)
    d_copy = to_item(d_out, d_in, d_send.at[0], d_recv.at[0], 1)
    d_copy.start()

    def token_part(t, c):
        return lax.dot_general(
            gq_ref[t * tokens + c * tile : t * tokens + (c + 1) * tile, :], slab_ref[...], NT, preferred_element_type=f32
        )

    near_copies = {}
    far_copies = []

    def send_near(t, *which):
        for c in which:
            cs = pl.ds(c * tile, tile)
            near_out[t // 2, c * tile : (c + 1) * tile, :] = token_part(t, c).astype(bf16)
            copy = to_group(
                near_out.at[t // 2, cs], near_in.at[t // 2, cs], near_send.at[t // 2, c], near_recv.at[t // 2, c], 1
            )
            copy.start()
            near_copies[(t // 2, c)] = copy

    def send_far(c):
        cs = slice(c * tile, (c + 1) * tile)
        part = token_part(2, c)
        near_copies[(1, c)].wait_recv()
        far_out[cs, :] = (part.astype(bf16).astype(f32) + near_in[1, cs, :].astype(f32)).astype(bf16)
        copy = to_group(far_out.at[pl.ds(c * tile, tile)], far_in.at[pl.ds(c * tile, tile)], far_send.at[c], far_recv.at[c], 2)
        copy.start()
        far_copies.append(copy)

    send_near(3, 0)
    send_far(0)
    for copy in small_copies:
        copy.wait()
    small_mid[...] = small_ref[place] + small_in[1] + small_in[2] + small_in[3]
    small_x = to_item(small_mid, small_side, sx_send.at[0], sx_recv.at[0], 1)
    small_x.start()
    grads = 0.0
    for t in range(4):
        grads = grads + lax.dot_general(
            xs[t][...], gq_ref[t * tokens : (t + 1) * tokens, :], TN, preferred_element_type=f32
        )
    grad_v[...] = grads

    def sums(r, line):
        at = pl.multiple_of(r * tile, tile)
        return line + jnp.sum(gq_ref[pl.ds(at, tile), :].astype(f32), 0, keepdims=True)

    line = lax.fori_loop(0, 4 * chunks, sums, jnp.zeros((1, columns), f32))
    high = line.astype(bf16)
    rest = (line - high.astype(f32)).astype(bf16)
    which = lax.broadcasted_iota(jnp.int32, (16, columns), 0)
    lines = jnp.where(which == 0, high.astype(f32), jnp.where(which == 1, rest.astype(f32), 0.0)).astype(bf16)
    level = item // 2
    side = item % 2

    def slab_part(kz, kx):
        at = pl.multiple_of((2 * flip(level, kz) + (side + kx) % 2) * rows, 8)
        return grad_v[pl.ds(at, rows), :]

    side_copies = []
    for kz in range(levels - 1, -1, -1):
        side_out[kz, 0:rows, :] = slab_part(kz, 1).astype(bf16)
        side_out[kz, rows : rows + 16, :] = lines
        copy = to_item(side_out.at[kz], side_in.at[kz], side_send.at[kz], side_recv.at[kz], 1)
        copy.start()
        side_copies.append((kz, copy))

    send_near(3, 1)
    send_far(1)
    small_x.wait()
    small_both[...] = small_mid[...] + small_side[...]
    item_copies = [
        to_item(small_both, small_items.at[kz], si_send.at[kz], si_recv.at[kz], 2 * kz) for kz in range(1, levels)
    ]
    for copy in item_copies:
        copy.start()

    send_near(1, *range(chunks))
    for c in range(chunks):
        cs = slice(c * tile, (c + 1) * tile)
        din_ref[cs, :] = first_ref[cs, :] + token_part(0, c).astype(bf16).astype(f32)

    for copy in item_copies:
        copy.wait()
    small_sum[...] = small_both[...] + small_items[1] + small_items[2] + small_items[3]
    total_ref[place] = small_sum[...]
    total_copies = [to_group(small_sum, total_ref.at[place], st_send.at[t], st_recv.at[t], t) for t in range(1, 4)]
    for copy in total_copies:
        copy.start()

    def square_sum(values):
        return jnp.sum(jnp.sum(values * values, 0, keepdims=True), -1, keepdims=True)

    part_copies = []
    for kz, copy in side_copies:
        copy.wait()
        part = slab_part(kz, 0) + side_in[kz, 0:rows, :].astype(f32)
        both = lines.astype(f32) + side_in[kz, rows : rows + 16, :].astype(f32)
        if kz:
            part_out[kz, 0:rows, :] = part.astype(bf16)
            whole = jnp.sum(both, 0, keepdims=True)
            short = whole.astype(bf16).astype(f32)
            which_row = jnp.where(which == 0, short, jnp.where(which == 1, whole - short, 0.0))
            part_out[kz, rows : rows + 16, :] = which_row.astype(bf16)
            copy = to_item(part_out.at[kz], part_in.at[kz], part_send.at[kz], part_recv.at[kz], 2 * kz)
            copy.start()
            part_copies.append(copy)
        else:
            own_part, own_lines = part, both

    for copy in z_copies:
        copy.wait()

    up = uk_ref[0].astype(f32) + ur_ref[0].astype(f32)
    for kz in range(1, levels):
        up = up + z_in[kz].astype(f32)
    d_copy.wait()
    down = down_sum(0) + d_in[...].astype(f32)
    group_ref[0, 0:up_rows, :] = up.astype(bf16)
    group_ref[0, up_rows:, :] = down.astype(bf16)
    squares = square_sum(up) + square_sum(down)
    for copy in part_copies:
        copy.wait()
    own = jnp.concatenate([own_part, own_lines], 0)
    for kz in range(1, levels):
        own = own + part_in[kz].astype(f32)
    sgroup_ref[0] = own
    group_copies = [to_group(sgroup_ref.at[0], sgroup_ref.at[t], sl_send.at[t], sl_recv.at[t], t) for t in (2, 1)]
    for copy in group_copies:
        copy.start()
    column = lax.broadcasted_iota(jnp.int32, (1, columns), 1)
    squares = squares + square_sum(own[0:rows] * jnp.where(column < query_columns, 1.0, HD**-0.5))
    sq_out[...] = jnp.broadcast_to(squares, (8, 128))
    sq_copies = [to_group(sq_out, sq_in.at[t], qg_send.at[t], qg_recv.at[t], t) for t in range(1, 4)]
    for copy in sq_copies:
        copy.start()
    big_copies = [to_group(group_ref.at[0], group_ref.at[t], gr_send.at[t], gr_recv.at[t], t) for t in (2, 1)]
    for copy in big_copies:
        copy.start()
    for copy in sq_copies:
        copy.wait()
    sq_mid[...] = sq_out[...] + sq_in[1] + sq_in[2] + sq_in[3]
    sq_item_copies = [to_item(sq_mid, sq_items.at[k], qi_send.at[k], qi_recv.at[k], k) for k in range(1, items)]
    for copy in sq_item_copies:
        copy.start()

    group_copies[0].wait()
    cross = to_group(sgroup_ref.at[2], sgroup_ref.at[3], sl_send.at[3], sl_recv.at[3], 1)
    cross.start()
    big_copies[0].wait()
    big_cross = to_group(group_ref.at[2], group_ref.at[3], gr_send.at[3], gr_recv.at[3], 1)
    big_cross.start()
    for t in range(1, 4):
        total_copies[t - 1].wait_send()
        to_group(small_sum, total_ref.at[flip(place, t)], st_send.at[t], st_recv.at[t], t).wait_recv()
    for c in range(chunks):
        cs = slice(c * tile, (c + 1) * tile)
        near_copies[(1, c)].wait_send()
        near_copies[(0, c)].wait()
        far_copies[c].wait()
        din_ref[cs, :] = din_ref[cs, :] + near_in[0, cs, :].astype(f32) + far_in[cs, :].astype(f32)
    for copy in sq_item_copies:
        copy.wait()
    answer = sq_mid[...]
    for k in range(1, items):
        answer = answer + sq_items[k]
    squares_ref[...] = answer
    group_copies[1].wait()
    cross.wait()
    big_copies[1].wait()
    big_cross.wait()


def tail(xs, gq, slab, first, small, shards, items, query_columns):
    tokens, width = xs[0].shape
    columns = gq.shape[1]
    rows = width // items
    vmem = pl.BlockSpec(memory_space=pltpu.VMEM)
    dma = pltpu.SemaphoreType.DMA
    chunks, levels = 2, items // 2
    up_rows = shards[0].shape[1]
    quarter = up_rows + rows
    slab_part = (levels, rows + 16, columns)
    return pl.pallas_call(
        functools.partial(tail_kernel, items, query_columns),
        out_shape=(
            jax.ShapeDtypeStruct((tokens, width), f32),
            jax.ShapeDtypeStruct((4, quarter, width), bf16),
            jax.ShapeDtypeStruct((4, rows + 16, columns), f32),
            jax.ShapeDtypeStruct(small.shape, f32),
            jax.ShapeDtypeStruct((8, 128), f32),
        ),
        in_specs=[vmem] * 14,
        out_specs=(vmem,) * 5,
        scratch_shapes=[
            pltpu.VMEM((2, tokens, width), bf16),
            pltpu.VMEM((2, tokens, width), bf16),
            pltpu.VMEM((tokens, width), bf16),
            pltpu.VMEM((tokens, width), bf16),
            pltpu.VMEM((width, columns), f32),
            pltpu.VMEM(slab_part, bf16),
            pltpu.VMEM(slab_part, bf16),
            pltpu.VMEM(slab_part, bf16),
            pltpu.VMEM(slab_part, bf16),
            pltpu.VMEM((levels, up_rows, width), bf16),
            pltpu.VMEM((levels, up_rows, width), bf16),
            pltpu.VMEM((rows, width), bf16),
            pltpu.VMEM((rows, width), bf16),
            pltpu.VMEM((4, 8, width), f32),
            pltpu.VMEM((8, width), f32),
            pltpu.VMEM((8, width), f32),
            pltpu.VMEM((8, width), f32),
            pltpu.VMEM((levels, 8, width), f32),
            pltpu.VMEM((8, width), f32),
            pltpu.VMEM((8, 128), f32),
            pltpu.VMEM((4, 8, 128), f32),
            pltpu.VMEM((8, 128), f32),
            pltpu.VMEM((items, 8, 128), f32),
            dma((2, chunks)), dma((2, chunks)), dma((chunks,)), dma((chunks,)),
            dma((levels,)), dma((levels,)), dma((levels,)), dma((levels,)), dma((levels,)), dma((levels,)), dma((1,)), dma((1,)),
            dma((4,)), dma((4,)), dma((1,)), dma((1,)), dma((levels,)), dma((levels,)), dma((4,)), dma((4,)),
            dma((4,)), dma((4,)), dma((4,)), dma((4,)), dma((4,)), dma((4,)), dma((items,)), dma((items,)),
        ],
        compiler_params=pltpu.CompilerParams(vmem_limit_bytes=42 << 20, collective_id=3, has_side_effects=True),
        cost_estimate=pl.CostEstimate(flops=60 * 10**9, bytes_accessed=10**7, transcendentals=0),
        name="tail",
    )(*xs, gq, slab, first, small, *shards)


def update_kernel(
    place_of, heads, group_ref, sgroup_ref, total_ref, squares_ref,
    wq, fq, sq, wo, fo, so, wu, fu, su, wd, fd, sd, ws, fs, ss,
    norm_ref, nwq, nfq, nsq, nwo, nfo, nso, nwu, nfu, nsu, nwd, nfd, nsd, nws, nfs, nss,
    grad_q, grad_s,
):
    place = place_of()
    rows, width = wo.shape
    third = rows // 3
    small_rows = ws.shape[0]
    for row in range(ws.shape[0]):
        grad_s[row : row + 1, :] = total_ref[row // 3, row % 3 : row % 3 + 1, :]
    for q in range(4):
        t = flip(place, q)
        piece = sgroup_ref.at[t]
        for h in range(heads):
            at = (q * heads + h) * HD
            pair = h * 128
            value, key = (pair, pair + HD) if h % 2 == 0 else (pair + HD, pair)
            query = (heads + h // 2) * 128 + (HD if h % 2 == 0 else 0)
            for part, base, scale in ((0, query, HD**-0.5), (1, key, 1.0), (2, value, 1.0)):
                grad_q[:, part * width + at : part * width + at + HD] = piece[0:rows, base : base + HD] * scale
            for row, base, scale in ((2, query, HD**-0.5), (3, value, 1.0)):
                line = piece[rows : rows + 16, base : base + HD]
                grad_s[row : row + 1, at : at + HD] = (line[0:1] + line[1:2]) * scale
    small = grad_s[0:small_rows, :]
    squares = jnp.sum(jnp.sum(small * small, 0, keepdims=True), -1, keepdims=True) + squares_ref[0:1, 0:1]
    norm = jnp.sqrt(squares)
    norm_ref[...] = norm
    factor = jnp.minimum(1.0, clip_level / (norm + 1e-06))

    def apply(refs, index, grad, decay, rate):
        w, f, s, nw, nf, ns = refs
        new = adam_update(w[index], f[index], s[index], grad * factor, decay, rate)
        nw[index], nf[index], ns[index] = new

    everything = (slice(None), slice(None))
    apply((ws, fs, ss, nws, nfs, nss), everything, small, 0.0, small_rate)
    for part in range(3):
        cs = slice(part * width, (part + 1) * width)
        apply((wq, fq, sq, nwq, nfq, nsq), (slice(None), cs), grad_q[:, cs], weight_decay, learn_rate)
    for q in range(4):
        t = flip(place, q)
        cs = slice(q * width, (q + 1) * width)
        apply((wu, fu, su, nwu, nfu, nsu), (slice(None), cs), group_ref[t, 0:rows, :].astype(f32), weight_decay, learn_rate)
        if q < 3:
            os = (slice(q * third, (q + 1) * third), slice(None))
            apply((wo, fo, so, nwo, nfo, nso), os, group_ref[t, rows : rows + third, :].astype(f32), weight_decay, learn_rate)
        ds = (slice(q * rows, (q + 1) * rows), slice(None))
        apply((wd, fd, sd, nwd, nfd, nsd), ds, group_ref[t, rows + third :, :].astype(f32), weight_decay, learn_rate)


def update(place_of, heads, group, sgroup, total, squares, states):
    vmem = pl.BlockSpec(memory_space=pltpu.VMEM)
    rows = states[3].shape[0]
    return pl.pallas_call(
        functools.partial(update_kernel, place_of, heads),
        out_shape=(jax.ShapeDtypeStruct((1, 1), f32),) + tuple(jax.ShapeDtypeStruct(a.shape, f32) for a in states),
        in_specs=[vmem] * (4 + len(states)),
        out_specs=(vmem,) * (1 + len(states)),
        scratch_shapes=[pltpu.VMEM(states[0].shape, f32), pltpu.VMEM((16, total.shape[2]), f32)],
        compiler_params=pltpu.CompilerParams(vmem_limit_bytes=60 << 20),
        cost_estimate=pl.CostEstimate(flops=10**9, bytes_accessed=25 * 10**6, transcendentals=0),
        name="update",
    )(group, sgroup, total, squares, *states)


def line_place(z):
    return (z + 2) % 3 + (z // 3) * (3 - (z + 2) % 3)


def head_kernel(
    items, heads, x_ref, wq_ref, small_ref, wo_ref, wu_ref, wd_ref,
    near_out, far_out, cross_out, qkv_out, slab_out, line_ref, side_ref, wfar_ref,
    near_ref, far_ref, cross_ref, qkv_ref, slab_ref, piece_ref, bias_ref, raw_v, quarter_ref, pieces_v, x_send, x_recv, far_send, far_recv, cross_send, cross_recv,
    s_up_send, s_up_recv, s_down_send, s_down_recv, s_side_send, s_side_recv,
    w_up_send, w_up_recv, w_down_send, w_down_recv, w_side_send, w_side_recv, w_own, y_send, y_recv, keep_sem, raw_sem, qkv_sem,
):
    item, place = lax.axis_index("item"), lax.axis_index("seq")
    side, level = item % 2, item // 2
    levels = items // 2
    tokens = x_ref.shape[0]
    rows, width = wo_ref.shape
    third = rows // 3
    raws = (
        (wu_ref.at[:, pl.ds(pl.multiple_of(place * width, 128), width)], 0, rows),
        (wd_ref.at[pl.ds(pl.multiple_of(place * rows, 8), rows)], rows, rows),
        (wo_ref.at[pl.ds(pl.multiple_of((place - place // 3) * third, 8), third)], 2 * rows, third),
    )
    for n, (src, at, count) in enumerate(raws):
        pltpu.make_async_copy(src, raw_v.at[pl.ds(at, count)], raw_sem.at[n]).start()
    bias_ref[...] = jnp.zeros_like(bias_ref)
    piece_ref[...] = jnp.zeros_like(piece_ref)
    for g in range(4):

        @pl.when(place == g)
        def _():
            for h in range(heads):
                at = (g * heads + h) * HD
                pair = h * 128
                value, key = (pair, pair + HD) if h % 2 == 0 else (pair + HD, pair)
                query = (heads + h // 2) * 128 + (HD if h % 2 == 0 else 0)
                for part, base, scale in ((0, query, HD**-0.5), (1, key, 1.0), (2, value, 1.0)):
                    cut = wq_ref[:, part * width + at : part * width + at + HD]
                    piece_ref[:, base : base + HD] = (cut * scale).astype(bf16)
                bias_ref[:, query : query + HD] = small_ref[2:3, at : at + HD] * HD**-0.5
                bias_ref[:, value : value + HD] = small_ref[3:4, at : at + HD]

    tile = 256
    chunks = tokens // tile
    greet(item, place, items)

    def to_group(src, dst, send, recv, t):
        return pltpu.make_async_remote_copy(
            src_ref=src, dst_ref=dst, send_sem=send, recv_sem=recv,
            device_id=(item, flip(place, t)), device_id_type=MESH_ID,
        )

    class Flow:
        def __init__(self, slot, side_slot, other_slot, arrived, sems):
            self.slot, self.side_slot, self.other_slot, self.arrived = slot, side_slot, other_slot, arrived
            self.up_send, self.up_recv, self.down_send, self.down_recv, self.side_send, self.side_recv = sems

        def up(self, d):
            part = self.slot(-d)
            return pltpu.make_async_remote_copy(
                src_ref=part, dst_ref=part, send_sem=self.up_send.at[d], recv_sem=self.up_recv.at[d],
                device_id=(item + 2, place), device_id_type=MESH_ID,
            )

        def down(self, d):
            part = self.slot(d)
            return pltpu.make_async_remote_copy(
                src_ref=part, dst_ref=part, send_sem=self.down_send.at[d], recv_sem=self.down_recv.at[d],
                device_id=(item - 2, place), device_id_type=MESH_ID,
            )

        def across(self, d):
            part = self.slot(d)
            return pltpu.make_async_remote_copy(
                src_ref=part, dst_ref=self.side_slot(d), send_sem=self.side_send.at[level + d], recv_sem=self.side_recv.at[level + d],
                device_id=(item + 1 - 2 * side, place), device_id_type=MESH_ID,
            )

        def begin(self):
            @pl.when(level < levels - 1)
            def _():
                self.up(0).start()

            @pl.when(level > 0)
            def _():
                self.down(0).start()

            self.across(0).start()
            self.arrived(0)

        def step(self, d):
            @pl.when(level >= d)
            def _():
                part = self.slot(-d)
                pltpu.make_async_remote_copy(
                    src_ref=part, dst_ref=part, send_sem=self.up_send.at[d - 1], recv_sem=self.up_recv.at[d - 1],
                    device_id=(item + 1 - 2 * side, place), device_id_type=MESH_ID,
                ).wait_recv()

                @pl.when(level < levels - 1)
                def _():
                    self.up(d).start()

                self.across(-d).start()
                self.arrived(-d)

            @pl.when(level < levels - d)
            def _():
                part = self.slot(d)
                pltpu.make_async_remote_copy(
                    src_ref=part, dst_ref=part, send_sem=self.down_send.at[d - 1], recv_sem=self.down_recv.at[d - 1],
                    device_id=(item + 1 - 2 * side, place), device_id_type=MESH_ID,
                ).wait_recv()

                @pl.when(level > 0)
                def _():
                    self.down(d).start()

                self.across(d).start()
                self.arrived(d)

        def other_side(self):
            for z in range(levels):
                part = self.other_slot(z)
                pltpu.make_async_remote_copy(
                    src_ref=part, dst_ref=part, send_sem=self.side_send.at[z], recv_sem=self.side_recv.at[z],
                    device_id=(item + 1 - 2 * side, place), device_id_type=MESH_ID,
                ).wait_recv()

        def finish(self):
            for d in range(levels - 1):

                @pl.when((level >= d) & (level < levels - 1))
                def _():
                    self.up(d).wait_send()

                @pl.when((level < levels - d) & (level > 0))
                def _():
                    self.down(d).wait_send()

            for z in range(levels):
                part = self.slot(z - level)
                pltpu.make_async_remote_copy(
                    src_ref=part, dst_ref=part, send_sem=self.side_send.at[z], recv_sem=self.side_recv.at[z],
                    device_id=(item + 1 - 2 * side, place), device_id_type=MESH_ID,
                ).wait_send()

    def far_copy(z):
        at = line_place(z)
        return to_group(line_ref.at[at], wfar_ref.at[at], y_send.at[at], y_recv.at[at], 2)

    def to_far(z):
        @pl.when((z > 0) & (z < levels - 1))
        def _():
            far_copy(z).start()

    def piece_slot(d):
        return pieces_v.at[item + 2 * d]

    slab_flow = Flow(piece_slot, piece_slot, lambda z: pieces_v.at[2 * z + 1 - side], lambda d: None, (s_up_send, s_up_recv, s_down_send, s_down_recv, s_side_send, s_side_recv))
    w_flow = Flow(
        lambda d: line_ref.at[line_place(level + d)], lambda d: side_ref.at[line_place(level + d)],
        lambda z: side_ref.at[line_place(z)], lambda d: to_far(level + d), (w_up_send, w_up_recv, w_down_send, w_down_recv, w_side_send, w_side_recv))
    pieces_v[item] = piece_ref[...]
    slab_flow.begin()
    far_copies, near_copies, cross_copies = [], [], []
    for c in range(chunks):
        cs = pl.ds(c * tile, tile)
        far_copies.append(to_group(x_ref.at[cs], far_ref.at[cs], far_send.at[c], far_recv.at[c], 2))
        far_copies[-1].start()
    near_copies = [to_group(x_ref, near_ref, x_send.at[0], x_recv.at[0], 1)]
    near_copies[0].start()
    for n, (src, at, count) in enumerate(raws):
        pltpu.make_async_copy(src, raw_v.at[pl.ds(at, count)], raw_sem.at[n]).wait()
    quarter_ref[...] = raw_v[...].astype(bf16)
    own = pltpu.make_async_copy(quarter_ref, line_ref.at[line_place(level)], w_own.at[0])
    own.start()
    for d in range(1, levels):
        slab_flow.step(d)
    own.wait()
    w_flow.begin()
    slab_flow.other_side()
    for j in range(items):
        slab_ref[j * rows : (j + 1) * rows, :] = pieces_v[j]

    keeps = [pltpu.make_async_copy(slab_ref, slab_out, keep_sem.at[0])]
    keeps[0].start()

    def project_rows(src, t, c):
        part = jnp.dot(src[c * tile : (c + 1) * tile, :], slab_ref[...], preferred_element_type=f32)
        at = t * tokens + c * tile
        qkv_ref[at : at + tile, :] = (part + bias_ref[...]).astype(bf16)
        copy = pltpu.make_async_copy(qkv_ref.at[pl.ds(at, tile)], qkv_out.at[pl.ds(at, tile)], qkv_sem.at[t, c])
        copy.start()
        keeps.append(copy)

    def pass_on(c):
        cs = pl.ds(c * tile, tile)
        far_copies[c].wait_recv()
        copy = to_group(far_ref.at[cs], cross_ref.at[cs], cross_send.at[c], cross_recv.at[c], 1)
        copy.start()
        cross_copies.append(copy)

    for c in range(chunks):
        project_rows(x_ref, 0, c)
        pass_on(c)
        if c + 1 < levels:
            w_flow.step(c + 1)
        if c == 0:
            near_copies[0].wait_recv()
            keeps.append(pltpu.make_async_copy(near_ref, near_out, keep_sem.at[1]))
            keeps[-1].start()
        project_rows(near_ref, 1, c)
        project_rows(far_ref, 2, c)
        cross_copies[c].wait_recv()
        project_rows(cross_ref, 3, c)
    keeps.append(pltpu.make_async_copy(far_ref, far_out, keep_sem.at[2]))
    keeps.append(pltpu.make_async_copy(cross_ref, cross_out, keep_sem.at[3]))
    for copy in keeps[-2:]:
        copy.start()
    for d in range(chunks + 1, levels):
        w_flow.step(d)
    w_flow.other_side()
    near_copies[0].wait_send()
    for c in range(chunks):
        far_copies[c].wait_send()
        cross_copies[c].wait_send()
    for z in range(1, levels - 1):
        far_copy(z).wait()
    for copy in keeps:
        copy.wait()
    slab_flow.finish()
    w_flow.finish()


def head(x, wq, small, wo, wu, wd, items, heads):
    tokens, width = x.shape
    rows = wo.shape[0]
    columns = (heads + (heads + 1) // 2) * 128
    quarter = (2 * rows + rows // 3, width)
    vmem = pl.BlockSpec(memory_space=pltpu.VMEM)
    hbm = pl.BlockSpec(memory_space=pltpu.HBM)
    dma = pltpu.SemaphoreType.DMA
    chunks, levels = tokens // 256, items // 2
    tokens_shape = jax.ShapeDtypeStruct((tokens, width), bf16)
    return pl.pallas_call(
        functools.partial(head_kernel, items, heads),
        out_shape=(
            tokens_shape, tokens_shape, tokens_shape,
            jax.ShapeDtypeStruct((4 * tokens, columns), bf16),
            jax.ShapeDtypeStruct((rows * items, columns), bf16),
            jax.ShapeDtypeStruct((levels,) + quarter, bf16),
            jax.ShapeDtypeStruct((levels,) + quarter, bf16),
            jax.ShapeDtypeStruct((levels - 2,) + quarter, bf16),
        ),
        in_specs=[vmem] * 3 + [hbm] * 3,
        out_specs=(hbm,) * 8,
        scratch_shapes=[pltpu.VMEM((tokens, width), bf16)] * 3
        + [
            pltpu.VMEM((4 * tokens, columns), bf16),
            pltpu.VMEM((rows * items, columns), bf16),
            pltpu.VMEM((rows, columns), bf16),
            pltpu.VMEM((1, columns), f32),
            pltpu.VMEM(quarter, f32),
            pltpu.VMEM(quarter, bf16),
            pltpu.VMEM((items, rows, columns), bf16),
            dma((1,)), dma((1,)), dma((chunks,)), dma((chunks,)), dma((chunks,)), dma((chunks,)),
        ]
        + [dma((levels,))] * 12
        + [dma((1,)), dma((levels,)), dma((levels,)), dma((4,)), dma((3,)), dma((4, chunks))],
        compiler_params=pltpu.CompilerParams(vmem_limit_bytes=61 << 20, collective_id=1, has_side_effects=True),
        cost_estimate=pl.CostEstimate(flops=40 * 10**9, bytes_accessed=10**7, transcendentals=0),
        name="head",
    )(x, wq, small, wo, wu, wd)


def gelu_parts(u):
    half = 0.5 * (1.0 + lax.erf(u * 0.7071067811865476))
    return u * half, half + u * jnp.exp(-0.5 * u * u) * 0.3989422804014327


def middle_kernel(
    dims, line_ref, side_ref, fmid_ref, fends_ref, gmid_ref, gends_ref, x_ref, mix0_ref, mix1_ref, mix2_ref, mix3_ref, dout_ref, small_ref,
    out_ref, first_ref, gmix0_ref, gmix1_ref, gmix2_ref, gmix3_ref, ukeep_ref, usend_ref, dkeep_ref, dfar_ref, dsend_ref, sgrad_ref,
    wo_v, wu_v, wd_v, xhat_v, hid_v, act_v, slope_v, ffn_v, gffn_v, gup_v, rstd_v, stage_d, stage_u,
    got_u, got_d, got_o, mixn_v,
    wsem, wsend, wrecv, mix_send, mix_recv, usend, urecv, dsend, drecv, osend, orecv, flush, fsend, frecv,
):
    items, rows, width, tile = dims
    item, place = lax.axis_index("item"), lax.axis_index("seq")
    side, level = item % 2, item // 2
    core, far = place % 2, place // 2
    third = rows // 3
    tokens = x_ref.shape[0]
    tiles = tokens // tile
    near = (item, flip(place, 1))
    barrier = pltpu.get_barrier_semaphore()
    across = (item, flip(place, 2))
    for device in (near, across):
        pl.semaphore_signal(barrier, inc=1, device_id=device, device_id_type=MESH_ID)
    pl.semaphore_wait(barrier, 2)

    def remote(src, dst, send, recv):
        return pltpu.make_async_remote_copy(
            src_ref=src, dst_ref=dst, send_sem=send, recv_sem=recv, device_id=near, device_id_type=MESH_ID
        )

    mix_copy = remote(mix1_ref, mixn_v, mix_send.at[0], mix_recv.at[0])
    mix_copy.start()

    def load(which):
        for t in (0, 2):
            q = flip(place, t)
            for n in range(items):
                z, kx = n // 2, n % 2
                j = 2 * z + (side + kx) % 2
                at = line_place(z)
                if t == 0:
                    src = (line_ref, side_ref)[kx].at[at]
                elif at < items // 2 - 2:
                    src = (fmid_ref, gmid_ref)[kx].at[at]
                else:
                    src = (fends_ref, gends_ref)[kx].at[at - (items // 2 - 2)]
                if which == 0:
                    src = src.at[pl.ds(2 * rows, third)]
                    dst = wo_v.at[j, pl.ds(pl.multiple_of(q * third, 16), third)]
                elif which == 1:
                    src = src.at[pl.ds(0, rows)]
                    dst = wu_v.at[q, pl.ds(pl.multiple_of(j * rows, 16), rows)]
                else:
                    src = src.at[pl.ds(rows, rows)]
                    dst = wd_v.at[j // 2, pl.ds(pl.multiple_of((j % 2) * 4 * rows + q * rows, 16), rows)]
                remote(src, dst, wsend.at[which], wrecv.at[which]).start()
                pltpu.make_async_copy(src, dst, wsem.at[which]).start()

    for which in range(3):
        load(which)

    def loaded(which):
        half = (wo_v.at[pl.ds(0, items // 2)], wu_v.at[pl.ds(0, 2)], wd_v.at[pl.ds(0, 2)])[which]
        pltpu.make_async_copy(half, half, wsem.at[which]).wait()
        remote(half, half, wsend.at[which], wrecv.at[which]).wait_recv()

    def rowsl(r):
        return pl.ds(pl.multiple_of(r * tile, tile), tile)

    def wo_rows(q):
        return jnp.concatenate([wo_v[2 * q, 0:rows], wo_v[2 * q + 1, 0:rows]], 0)

    mixes = (mix0_ref, mixn_v, mix2_ref, mix3_ref)
    gmixes = (gmix0_ref, gmix1_ref, gmix2_ref, gmix3_ref)
    mix_copy.wait_recv()
    loaded(0)

    def norm_one(r, _):
        rs = rowsl(r)
        total = x_ref[rs, :].astype(f32) + small_ref[4:5, :]
        for t in range(4):
            total += jnp.dot(mixes[t][rs, :], wo_rows(flip(place, t)), preferred_element_type=f32)
        centered = total - jnp.mean(total, -1, keepdims=True)
        rstd = lax.rsqrt(jnp.mean(centered * centered, -1, keepdims=True) + norm_epsilon)
        xhat = centered * rstd
        xhat_v[rs, :] = xhat
        rstd_v[rs, :] = jnp.broadcast_to(rstd, (tile, 128))
        hid_v[rs, :] = (xhat * small_ref[0:1, :] + small_ref[1:2, :]).astype(bf16)
        return 0

    lax.fori_loop(0, tiles, norm_one, 0)
    loaded(1)
    loaded(2)

    def ffn(n, _):
        p, r = n // tiles, n % tiles
        rs = rowsl(r)
        up = jnp.dot(hid_v[rs, :], wu_v[p], preferred_element_type=f32) + small_ref[pl.ds(8 + p, 1), :]
        act, slope = gelu_parts(up)
        act = act.astype(bf16)
        act_v[p, rs, :] = act
        slope_v[p, rs, :] = slope
        part = jnp.dot(act, wd_v[p], preferred_element_type=f32)

        @pl.when(p == 0)
        def _():
            ffn_v[rs, :] = part

        @pl.when(p > 0)
        def _():
            ffn_v[rs, :] += part

        return 0

    lax.fori_loop(0, 4 * tiles, ffn, 0)
    zero = jnp.zeros((1, width), f32)

    def norm_two(r, sums):
        rs = rowsl(r)
        dg, db, dd = sums
        hidden = xhat_v[rs, :] * small_ref[0:1, :] + small_ref[1:2, :]
        total = hidden + (ffn_v[rs, :] + small_ref[7:8, :])
        centered = total - jnp.mean(total, -1, keepdims=True)
        rstd = lax.rsqrt(jnp.mean(centered * centered, -1, keepdims=True) + norm_epsilon)
        xhat = centered * rstd
        out_ref[rs, :] = (xhat * small_ref[5:6, :] + small_ref[6:7, :]).astype(bf16)
        dy = dout_ref[rs, :].astype(f32)
        dg = dg + jnp.sum(dy * xhat, 0, keepdims=True)
        db = db + jnp.sum(dy, 0, keepdims=True)
        dx = dy * small_ref[5:6, :]
        dx = rstd * (dx - jnp.mean(dx, -1, keepdims=True) - xhat * jnp.mean(dx * xhat, -1, keepdims=True))
        ffn_v[rs, :] = dx
        short = dx.astype(bf16)
        gffn_v[rs, :] = short
        dd = dd + jnp.sum(short.astype(f32), 0, keepdims=True)
        return dg, db, dd

    dg2, db2, dd = lax.fori_loop(0, tiles, norm_two, (zero, zero, zero))
    sgrad_ref[...] = jnp.zeros_like(sgrad_ref)
    sgrad_ref[1, 2:3, :] = dg2
    sgrad_ref[2, 0:1, :] = db2
    sgrad_ref[2, 1:2, :] = dd
    nt = (((1,), (1,)), ((), ()))
    tn = (((0,), (0,)), ((), ()))
    pieces = width // tile

    def spread(src, yrel, row, count, sem):
        for n in range(items):
            z, kx = n // 2, n % 2
            j = 2 * z + (side + kx) % 2
            dst = (ukeep_ref, usend_ref)[kx].at[yrel, flip(level, z), pl.ds(row, count)]
            pltpu.make_async_copy(src(j), dst, sem).start()

    def chunk_at(n):
        return blend(level, 3 - n)

    def finish_chunk(n, par):
        p = chunk_at(n)
        remote(got_d.at[p], got_d.at[p], dsend.at[p], drecv.at[p]).wait_recv()
        for jj in range(2):
            for yy in range(2):
                at = pl.multiple_of((4 * jj + 2 * yy + core) * rows, 16)
                got_d[p, jj, yy] = stage_d[par, pl.ds(at, rows), :] + got_d[p, jj, yy]

        kz = 3 - n
        for jj in range(2):
            kx = (jj + side) % 2
            for yy in range(2):

                @pl.when(far == yy)
                def _():
                    pltpu.make_async_copy(got_d.at[p, jj, yy], dkeep_ref.at[kz, kx], flush.at[0]).start()

                    @pl.when(n < 2)
                    def _():
                        pltpu.make_async_remote_copy(
                            src_ref=got_d.at[p, jj, 1 - yy], dst_ref=dfar_ref.at[n, kx],
                            send_sem=fsend.at[n], recv_sem=frecv.at[n], device_id=across, device_id_type=MESH_ID,
                        ).start()

                    @pl.when(n >= 2)
                    def _():
                        pltpu.make_async_copy(got_d.at[p, jj, 1 - yy], dsend_ref.at[n - 2, kx], flush.at[3]).start()

        half = p // 2

        @pl.when(p % 2 == core)
        def _():
            remote(got_u.at[half], got_u.at[half], usend.at[half], urecv.at[half]).wait_recv()
            for m in range(tiles):
                ms = slice(m * tile, (m + 1) * tile)
                got_u[half, ms, :] = stage_u[par, ms, :] + got_u[half, ms, :]
            spread(
                lambda j: got_u.at[half, pl.ds(pl.multiple_of(j * rows, 16), rows)],
                (half + far) % 2, 0, rows, flush.at[1],
            )

    def back(n, _):
        par = n % 2
        p = chunk_at(n)

        def back_rows(r, total):
            rs = rowsl(r)
            ga = lax.dot_general(gffn_v[rs, :], wd_v[p], nt, preferred_element_type=f32)
            gup = (ga * slope_v[p, rs, :]).astype(bf16)
            gup_v[rs, :] = gup
            ffn_v[rs, :] += lax.dot_general(gup, wu_v[p], nt, preferred_element_type=f32)
            return total + jnp.sum(gup.astype(f32), 0, keepdims=True)

        sgrad_ref[(8 + p) // 3, pl.ds((8 + p) % 3, 1), :] = lax.fori_loop(0, tiles, back_rows, zero)

        @pl.when(n >= 2)
        def _():
            before = chunk_at(n - 2)
            remote(got_d.at[before], got_d.at[before], dsend.at[before], drecv.at[before]).wait_send()

            @pl.when(p % 2 != core)
            def _():
                half = before // 2
                remote(got_u.at[half], got_u.at[half], usend.at[half], urecv.at[half]).wait_send()

        for m in range(pieces):
            cs = slice(m * tile, (m + 1) * tile)
            stage_d[par, cs, :] = lax.dot_general(act_v[p, :, cs], gffn_v[...], tn, preferred_element_type=f32).astype(bf16)
        for jj in range(2):
            for yy in range(2):
                at = pl.multiple_of((4 * jj + 2 * yy + 1 - core) * rows, 16)
                remote(stage_d.at[par, pl.ds(at, rows)], got_d.at[p, jj, yy], dsend.at[p], drecv.at[p]).start()
        for m in range(pieces):
            cs = slice(m * tile, (m + 1) * tile)
            stage_u[par, cs, :] = lax.dot_general(hid_v[:, cs], gup_v[...], tn, preferred_element_type=f32).astype(bf16)

        @pl.when(p % 2 != core)
        def _():
            remote(stage_u.at[par], got_u.at[p // 2], usend.at[p // 2], urecv.at[p // 2]).start()

        @pl.when(n > 0)
        def _():
            finish_chunk(n - 1, 1 - par)

        return 0

    lax.fori_loop(0, 4, back, 0)
    finish_chunk(3, 1)

    def norm_back(r, sums):
        rs = rowsl(r)
        dg, db, da = sums
        dy = ffn_v[rs, :]
        xhat = xhat_v[rs, :]
        dg = dg + jnp.sum(dy * xhat, 0, keepdims=True)
        db = db + jnp.sum(dy, 0, keepdims=True)
        dx = dy * small_ref[0:1, :]
        dx = rstd_v[rs, 0:1] * (dx - jnp.mean(dx, -1, keepdims=True) - xhat * jnp.mean(dx * xhat, -1, keepdims=True))
        first_ref[rs, :] = dx
        short = dx.astype(bf16)
        hid_v[rs, :] = short
        da = da + jnp.sum(short.astype(f32), 0, keepdims=True)
        for t in range(4):
            gmixes[t][rs, :] = lax.dot_general(
                short, wo_rows(flip(place, t)), nt, preferred_element_type=f32
            ).astype(bf16)
        return dg, db, da

    dg1, db1, da = lax.fori_loop(0, tiles, norm_back, (zero, zero, zero))
    sgrad_ref[0, 0:1, :] = dg1
    sgrad_ref[0, 1:2, :] = db1
    sgrad_ref[1, 1:2, :] = da
    for j in range(items):
        wo_v[j, pl.ds(rows, third)] = jnp.zeros((third, width), bf16)
    for t in range(4):
        q = flip(place, t)
        part = lax.dot_general(mixes[t][...], hid_v[...], tn, preferred_element_type=f32).astype(bf16)
        wo_v[2 * q, pl.ds(0, rows)] = part[:rows]
        wo_v[2 * q + 1, pl.ds(0, rows)] = part[rows:]
    o_copies = []
    for yy in range(2):
        at = pl.multiple_of((2 * yy + 1 - core) * third, 16)
        copy = remote(wo_v.at[:, pl.ds(at, third)], got_o.at[yy], osend.at[yy], orecv.at[yy])
        copy.start()
        o_copies.append(copy)
    for yy in range(2):
        o_copies[yy].wait_recv()
        at = pl.multiple_of((2 * yy + core) * third, 16)
        for j in range(items):
            got_o[yy, j] = wo_v[j, pl.ds(at, third)] + got_o[yy, j]
        spread(lambda j: got_o.at[yy, j], (yy + far) % 2, rows, third, flush.at[2])

    mix_copy.wait_send()
    for which in range(3):
        half = (wo_v.at[pl.ds(0, items // 2)], wu_v.at[pl.ds(0, 2)], wd_v.at[pl.ds(0, 2)])[which]
        remote(half, half, wsend.at[which], wrecv.at[which]).wait_send()
    for n in (2, 3):
        p = chunk_at(n)
        remote(got_d.at[p], got_d.at[p], dsend.at[p], drecv.at[p]).wait_send()

        @pl.when(p % 2 != core)
        def _():
            remote(got_u.at[p // 2], got_u.at[p // 2], usend.at[p // 2], urecv.at[p // 2]).wait_send()

    for yy in range(2):
        o_copies[yy].wait_send()
    pltpu.make_async_copy(dkeep_ref, dkeep_ref, flush.at[0]).wait()
    pltpu.make_async_copy(dsend_ref, dsend_ref, flush.at[3]).wait()
    for n in range(2):
        sent = dfar_ref.at[n]
        copy = pltpu.make_async_remote_copy(
            src_ref=sent, dst_ref=sent, send_sem=fsend.at[n], recv_sem=frecv.at[n],
            device_id=across, device_id_type=MESH_ID,
        )
        copy.wait_send()
        copy.wait_recv()
    pltpu.make_async_copy(got_u, got_u, flush.at[1]).wait()
    pltpu.make_async_copy(got_o, got_o, flush.at[2]).wait()


def middle(weights, x, mixes, dout, small, tile=768):
    levels, quarter, width = weights[0].shape
    items = 2 * levels
    rows = quarter * 3 // 7
    third = rows // 3
    tokens = x.shape[0]
    any_space = pl.BlockSpec(memory_space=pltpu.HBM)
    vmem = pl.BlockSpec(memory_space=pltpu.VMEM)
    square = (tokens, width)
    dma = pltpu.SemaphoreType.DMA
    head_part = jax.ShapeDtypeStruct((tokens, width // 4), bf16)
    u_shape = jax.ShapeDtypeStruct((2, levels, rows + third, width), bf16)
    d_half = jax.ShapeDtypeStruct((2, 2, rows, width), bf16)
    d_shape = jax.ShapeDtypeStruct((levels, 2, rows, width), bf16)
    return pl.pallas_call(
        functools.partial(middle_kernel, (items, rows, width, tile)),
        out_shape=(
            jax.ShapeDtypeStruct(square, bf16),
            jax.ShapeDtypeStruct(square, f32),
            head_part, head_part, head_part, head_part,
            u_shape, u_shape, d_shape, d_half, d_half,
            jax.ShapeDtypeStruct((4, 8, width), f32),
        ),
        in_specs=[any_space] * 6 + [vmem] * 7,
        out_specs=(vmem,) * 6 + (any_space,) * 5 + (vmem,),
        scratch_shapes=[
            pltpu.VMEM((items, 4 * third, width), bf16),
            pltpu.VMEM((4, width, width), bf16),
            pltpu.VMEM((4, width, width), bf16),
            pltpu.VMEM(square, f32),
            pltpu.VMEM(square, bf16),
            pltpu.VMEM((4, tokens, width), bf16),
            pltpu.VMEM((4, tokens, width), f32),
            pltpu.VMEM(square, f32),
            pltpu.VMEM(square, bf16),
            pltpu.VMEM(square, bf16),
            pltpu.VMEM((tokens, 128), f32),
            pltpu.VMEM((2, width, width), bf16),
            pltpu.VMEM((2, width, width), bf16),
            pltpu.VMEM((2, width, width), bf16),
            pltpu.VMEM((4, 2, 2, rows, width), bf16),
            pltpu.VMEM((2, items, third, width), bf16),
            pltpu.VMEM((tokens, width // 4), bf16),
            dma((3,)), dma((3,)), dma((3,)), dma((1,)), dma((1,)), dma((2,)), dma((2,)), dma((4,)), dma((4,)),
            dma((2,)), dma((2,)), dma((4,)), dma((2,)), dma((2,)),
        ],
        compiler_params=pltpu.CompilerParams(vmem_limit_bytes=61 << 20, collective_id=2, has_side_effects=True),
        cost_estimate=pl.CostEstimate(flops=60 * 10**9, bytes_accessed=10**7, transcendentals=0),
        name="middle",
    )(*weights, x, *mixes, dout, small)


def swap(values, axis, bit):
    size = lax.axis_size(axis)
    return lax.ppermute(values, axis, [(i, i ^ bit) for i in range(size)])


def take(values, at, dim):
    return lax.dynamic_index_in_dim(values, at, dim, keepdims=False)


def add_short(a, b):
    return (a.astype(f32) + b.astype(f32)).astype(bf16)


def layer_norm(values, gain, bias):
    average = jnp.mean(values, -1, keepdims=True)
    centered = values - average
    spread = jnp.mean(centered * centered, -1, keepdims=True)
    return centered * lax.rsqrt(spread + norm_epsilon) * gain + bias


def exact_gelu(values):
    return jax.nn.gelu(values, approximate=False)


def packed_columns(own):
    heads = own.shape[2]
    cols = []
    for h in range(heads):
        pair = [own[:, 2, h], own[:, 1, h]]
        cols += pair if h % 2 == 0 else pair[::-1]
    for p in range((heads + 1) // 2):
        odd = own[:, 0, 2 * p + 1] if 2 * p + 1 < heads else jnp.zeros_like(own[:, 0, 0])
        cols += [odd * HD**-0.5, own[:, 0, 2 * p] * HD**-0.5]
    return jnp.concatenate(cols, -1)


def natural_columns(values, heads):
    parts = [[], [], []]
    for h in range(heads):
        first, second = values[:, h * 128 : h * 128 + HD], values[:, h * 128 + HD : h * 128 + 128]
        base = (heads + h // 2) * 128
        if h % 2 == 0:
            parts[2].append(first)
            parts[1].append(second)
            parts[0].append(values[:, base + HD : base + 128] * HD**-0.5)
        else:
            parts[1].append(first)
            parts[2].append(second)
            parts[0].append(values[:, base : base + HD] * HD**-0.5)
    return jnp.concatenate(parts[0] + parts[1] + parts[2], -1)


def on_device(
    inputs,
    d_output,
    glob_count,
    glob_pos,
    rand_blocks,
    w_qkv,
    w_out,
    w_up,
    w_down,
    small_params,
    first_qkv,
    second_qkv,
    first_out,
    second_out,
    first_up,
    second_up,
    first_down,
    second_down,
    first_small,
    second_small,
):
    _, tok_rows, width = inputs.shape
    items = lax.axis_size("item")
    place = lax.axis_index("seq")
    heads = rand_blocks.shape[1]

    tokens_b = inputs.reshape(tok_rows, width)
    *others, qkv, slab, w_line, w_side, w_far = head(
        tokens_b, w_qkv, small_params, w_out, w_up, w_down, items, heads
    )
    xs = [tokens_b, *others]
    w_far_ends = swap(w_line[2:], "seq", 2)
    w_side_mid = swap(w_far, "item", 1)
    idx, bias, gl = slots(glob_count[0], glob_pos[0], rand_blocks[0], place)
    mix2, mix3, lse_far = attn_fwd(idx, gl, qkv, bias, heads, 2, 2)
    w_far_ends, w_side_mid, mix2, mix3, qkv = lax.optimization_barrier((w_far_ends, w_side_mid, mix2, mix3, qkv))
    mix2_in, mix3_in = swap(mix2, "seq", 2), swap(mix3, "seq", 3)
    w_side_ends = swap(w_far_ends, "item", 1)
    mix0, mix1, lse_near = attn_fwd(idx, gl, qkv, bias, heads, 0, 2)
    w_side_ends, mix0, mix1, mix2_in, mix3_in = lax.optimization_barrier((w_side_ends, mix0, mix1, mix2_in, mix3_in))
    outputs, grad_first, *grad_mixed, u_keep, u_send, d_keep, d_far, d_send, small_part = middle(
        (w_line, w_side, w_far, w_far_ends, w_side_mid, w_side_ends), tokens_b, (mix0, mix1, mix2_in, mix3_in), d_output.reshape(tok_rows, width), small_params
    )
    grads_in = [grad_mixed[0]] + [swap(grad_mixed[t], "seq", t) for t in range(1, 4)]
    u_in = swap(u_send, "item", 1)
    d_in = swap(d_send, "seq", 2)
    d_next = [swap(add_short(d_keep[3 - n], d_far[n]), "item", 2 * (3 - n)) for n in range(2)]
    acc, dq_near = attn_bwd(idx, gl, qkv, bias, grads_in[:2], lse_near, heads, 0, (), False)
    u_in, d_in, d_next, acc, dq_near = lax.optimization_barrier((u_in, d_in, d_next, acc, dq_near))
    u_next = swap(add_short(u_keep[1], u_in[1]), "seq", 2)
    d_last = swap(add_short(d_keep[1], d_in[0]), "item", 2)
    u_here = add_short(u_keep[0], u_in[0])
    d_here = add_short(d_keep[0], d_in[1])
    grad_qkv = attn_bwd(idx, gl, qkv, bias, grads_in[2:], lse_far, heads, 2, (acc, dq_near), True)
    d_last, u_next, grad_qkv = lax.optimization_barrier((d_last, u_next, grad_qkv))
    grad_inputs, group, slab_group, small_total, squares = tail(
        xs, grad_qkv, slab, grad_first, small_part, (u_here, u_next, d_here, d_last, *d_next), items, heads * 128
    )
    norm, *states = update(
        lambda: lax.axis_index("seq"),
        heads,
        group,
        slab_group,
        small_total,
        squares,
        (
            w_qkv, first_qkv, second_qkv, w_out, first_out, second_out, w_up, first_up, second_up,
            w_down, first_down, second_down, small_params, first_small, second_small,
        ),
    )
    return (outputs[None], grad_inputs[None], norm.reshape(()), *states)


def on_device_many(
    inputs,
    d_output,
    glob_count,
    glob_pos,
    rand_blocks,
    w_qkv,
    w_out,
    w_up,
    w_down,
    small_params,
    first_qkv,
    second_qkv,
    first_out,
    second_out,
    first_up,
    second_up,
    first_down,
    second_down,
    first_small,
    second_small,
):
    items_n, tok_rows, width = inputs.shape
    groups = lax.axis_size("seq")
    place = lax.axis_index("seq")
    heads = rand_blocks.shape[1]
    row_count = tok_rows

    own = lax.dynamic_index_in_dim(
        w_qkv.reshape(-1, 3, groups, heads, HD), place, 2, keepdims=False
    )
    slab = lax.all_gather(packed_columns(own).astype(bf16), "item", axis=0, tiled=True)
    full_out, full_up, full_down = (
        lax.all_gather(w_out.astype(bf16), "item", axis=0, tiled=True),
        lax.all_gather(w_up.astype(bf16), "item", axis=0, tiled=True),
        lax.all_gather(w_down.astype(bf16), "item", axis=0, tiled=True),
    )
    bias3 = jnp.stack([small_params[2], jnp.zeros((width,), f32), small_params[3]])
    own_bias = lax.dynamic_index_in_dim(
        bias3.reshape(1, 3, groups, heads, HD), place, 2, keepdims=False
    )
    slab_bias = packed_columns(own_bias)
    tokens_b = inputs.reshape(tok_rows, width)
    tokens_all = lax.all_gather(tokens_b, "seq", axis=0, tiled=True)
    tokens_f = tokens_b.astype(f32)
    qkv = (jnp.dot(tokens_all, slab, preferred_element_type=f32) + slab_bias).astype(bf16)
    idx, bias, gl = slots(glob_count[0], glob_pos[0], rand_blocks[0], jnp.int32(0))
    *mixed_parts, lse = attn_fwd(idx, gl, qkv, bias, heads, 0, 4)
    mixed_heads = jnp.concatenate(mixed_parts, 0)
    mixed = lax.all_to_all(mixed_heads, "seq", split_axis=0, concat_axis=1, tiled=True)
    attn_out = jnp.dot(mixed, full_out, preferred_element_type=f32) + small_params[4]
    hidden, norm_one_back = jax.vjp(
        layer_norm, tokens_f + attn_out, small_params[0], small_params[1]
    )
    hidden_b = hidden.astype(bf16)
    up_pre = jnp.dot(hidden_b, full_up, preferred_element_type=f32) + small_params[8:12].reshape(-1)
    active, gelu_back = jax.vjp(exact_gelu, up_pre)
    active_b = active.astype(bf16)
    ffn_out = jnp.dot(active_b, full_down, preferred_element_type=f32) + small_params[7]
    outputs, norm_two_back = jax.vjp(layer_norm, hidden + ffn_out, small_params[5], small_params[6])
    grad_second, grad_gain_two, grad_bias_two = norm_two_back(
        d_output.reshape(row_count, width).astype(f32)
    )
    grad_ffn = grad_second.astype(bf16)
    grad_w_down = jnp.einsum("rf,rd->fd", active_b, grad_ffn, preferred_element_type=f32)
    grad_active = jnp.einsum("rd,fd->rf", grad_ffn, full_down, preferred_element_type=f32)
    (grad_up_pre,) = gelu_back(grad_active)
    grad_up_b = grad_up_pre.astype(bf16)
    grad_w_up = jnp.einsum("rd,rf->df", hidden_b, grad_up_b, preferred_element_type=f32)
    grad_hidden = grad_second + jnp.einsum(
        "rf,df->rd", grad_up_b, full_up, preferred_element_type=f32
    )
    grad_first, grad_gain_one, grad_bias_one = norm_one_back(grad_hidden)
    grad_attn = grad_first.astype(bf16)
    grad_w_out = jnp.einsum("rm,rd->md", mixed, grad_attn, preferred_element_type=f32)
    grad_mixed = jnp.einsum("rd,md->rm", grad_attn, full_out, preferred_element_type=f32).astype(
        bf16
    )
    grad_heads = lax.all_to_all(grad_mixed, "seq", split_axis=1, concat_axis=0, tiled=True)
    grads_in = [grad_heads[t * tok_rows : (t + 1) * tok_rows] for t in range(4)]
    grad_qkv = attn_bwd(idx, gl, qkv, bias, grads_in, lse, heads, 0, (), True)
    grad_slab = jnp.einsum("rd,re->de", tokens_all, grad_qkv, preferred_element_type=f32)
    grad_tokens = jnp.einsum("re,de->rd", grad_qkv, slab, preferred_element_type=f32).astype(bf16)
    grad_inputs = grad_first + lax.psum_scatter(
        grad_tokens, "seq", scatter_dimension=0, tiled=True
    ).astype(f32)
    slab_sum = natural_columns(jnp.sum(grad_qkv.astype(f32), 0)[None], heads)[0]
    bias_grads = lax.dynamic_update_index_in_dim(
        jnp.zeros((3, groups, heads * HD), f32), slab_sum.reshape(3, heads * HD), place, 1
    ).reshape(3, width)
    small_rows = jnp.stack(
        [
            grad_gain_one,
            grad_bias_one,
            bias_grads[0],
            bias_grads[2],
            jnp.sum(grad_attn.astype(f32), 0),
            grad_gain_two,
            grad_bias_two,
            jnp.sum(grad_ffn.astype(f32), 0),
        ]
    )
    small_part = jnp.concatenate(
        [small_rows, jnp.sum(grad_up_b.astype(f32), 0).reshape(4, width)], 0
    )
    small_total = lax.psum(small_part, ("item", "seq"))
    shard_down = lax.psum_scatter(grad_w_down.astype(bf16), "item", scatter_dimension=0, tiled=True)
    shard_up = lax.psum_scatter(grad_w_up.astype(bf16), "item", scatter_dimension=0, tiled=True)
    shard_out = lax.psum_scatter(grad_w_out.astype(bf16), "item", scatter_dimension=0, tiled=True)
    shard_slab = lax.psum_scatter(grad_slab.astype(bf16), "item", scatter_dimension=0, tiled=True)
    shard_slab = natural_columns(shard_slab.astype(f32), heads).reshape(-1, 3, 1, heads * HD)
    shard_qkv = lax.all_gather(shard_slab, "seq", axis=2, tiled=True).reshape(-1, 3 * width)
    shard_out, shard_up, shard_down = lax.psum(
        (shard_out.astype(f32), shard_up.astype(f32), shard_down.astype(f32)), "seq"
    )
    local_squares = (
        jnp.sum(shard_qkv * shard_qkv)
        + jnp.sum(shard_out * shard_out)
        + jnp.sum(shard_up * shard_up)
        + jnp.sum(shard_down * shard_down)
    )
    matrix_squares = lax.psum(local_squares, "item")
    grad_norm = jnp.sqrt(matrix_squares + jnp.sum(small_total * small_total))
    factor = jnp.minimum(1.0, clip_level / (grad_norm + 1e-06))
    new_qkv = adam_update(
        w_qkv, first_qkv, second_qkv, shard_qkv * factor, weight_decay, learn_rate
    )
    new_out = adam_update(
        w_out, first_out, second_out, shard_out * factor, weight_decay, learn_rate
    )
    new_up = adam_update(w_up, first_up, second_up, shard_up * factor, weight_decay, learn_rate)
    new_down = adam_update(
        w_down, first_down, second_down, shard_down * factor, weight_decay, learn_rate
    )
    new_small = adam_update(
        small_params, first_small, second_small, small_total * factor, 0.0, small_rate
    )
    return (
        outputs.astype(bf16).reshape(items_n, tok_rows, width),
        grad_inputs.reshape(items_n, tok_rows, width),
        grad_norm,
        new_qkv[0],
        new_qkv[1],
        new_qkv[2],
        new_out[0],
        new_out[1],
        new_out[2],
        new_up[0],
        new_up[1],
        new_up[2],
        new_down[0],
        new_down[1],
        new_down[2],
        new_small[0],
        new_small[1],
        new_small[2],
    )


def solution(mesh):
    few = mesh.shape["item"] == 8 and mesh.shape["seq"] == 4
    return jax.shard_map(
        on_device if few else on_device_many,
        mesh=mesh,
        in_specs=(
            P("item", "seq", None),
            P("item", "seq", None),
            P("item"),
            P("item", None),
            P("item", "seq", None, None),
            P("item", None),
            P("item", None),
            P("item", None),
            P("item", None),
            P(),
            P("item", None),
            P("item", None),
            P("item", None),
            P("item", None),
            P("item", None),
            P("item", None),
            P("item", None),
            P("item", None),
            P(),
            P(),
        ),
        out_specs=(
            P("item", "seq", None),
            P("item", "seq", None),
            P(),
            P("item", None),
            P("item", None),
            P("item", None),
            P("item", None),
            P("item", None),
            P("item", None),
            P("item", None),
            P("item", None),
            P("item", None),
            P("item", None),
            P("item", None),
            P("item", None),
            P(),
            P(),
            P(),
        ),
        check_vma=False,
    )
```

```python
import functools

import jax
import jax.numpy as jnp
from jax import lax
from jax.experimental import pallas as pl
from jax.experimental.pallas import tpu as pltpu
from jax.sharding import PartitionSpec as P

ADAM_STEP = 10
norm_epsilon = 1e-06
beta_first = 0.9
beta_second = 0.999
adam_epsilon = 1e-08
learn_rate = 0.1
small_rate = 0.5
weight_decay = 0.01
clip_level = 1.0


def adam_update(weight, first, second, grad, decay, rate):
    first_new = beta_first * first + (1.0 - beta_first) * grad
    second_new = beta_second * second + (1.0 - beta_second) * grad * grad
    first_hat = first_new / (1.0 - beta_first**ADAM_STEP)
    second_hat = second_new / (1.0 - beta_second**ADAM_STEP)
    weight_new = weight - rate * (
        first_hat / (jnp.sqrt(second_hat) + adam_epsilon) + decay * weight
    )
    return (weight_new, first_new, second_new)


HD = 64
BL = 64
NEG = -1e30
bf16 = jnp.bfloat16
f32 = jnp.float32
NT = (((1,), (1,)), ((), ()))
TN = (((0,), (0,)), ((), ()))


def slots(count, positions, table, place):
    heads, nblocks, picks = table.shape
    chunk = nblocks // 4
    globals_n = positions.shape[0]
    here = jnp.arange(nblocks, dtype=jnp.int32)

    def turned(b):
        return ((b // chunk) ^ place) * chunk + b % chunk

    block = turned(here)
    rows = table.reshape(heads, 2, 2, chunk, picks)
    rows = jnp.where(place % 2 == 1, rows[:, :, ::-1], rows)
    rows = jnp.where(place // 2 == 1, rows[:, ::-1], rows).reshape(heads, nblocks, picks)
    window = jnp.stack([block - 1, block, block + 1], -1)
    active = jnp.arange(globals_n, dtype=jnp.int32) < count
    parts = jnp.concatenate(
        [
            jnp.broadcast_to(window[None], (heads, nblocks, 3)),
            jnp.broadcast_to(jnp.where(active, positions, -1)[None, None], (heads, nblocks, globals_n)),
            rows,
        ],
        -1,
    )
    count_slots = 3 + globals_n + picks
    valid = (parts >= 0) & (parts < nblocks)
    same = parts[..., :, None] == parts[..., None, :]
    earlier = jnp.arange(count_slots)[:, None] > jnp.arange(count_slots)[None, :]
    repeated = jnp.any(same & earlier, -1)
    is_global = jnp.any((positions[None, :] == block[:, None]) & active[None], -1)
    valid = valid & ~repeated & ~is_global[None, :, None]
    idx = turned(jnp.clip(parts, 0, nblocks - 1))
    bias = jnp.where(valid, 0.0, NEG).astype(f32)
    bias = jnp.broadcast_to(bias[..., None], (heads, nblocks, count_slots, BL))
    glob = jnp.concatenate([count[None], turned(positions)])
    return idx.reshape(-1), bias.reshape(heads * nblocks, count_slots * BL), glob


def low_lanes(rows):
    return lax.broadcasted_iota(jnp.int32, (rows, 2 * HD), 1) < HD


def pick(block, keep_low):
    low = low_lanes(block.shape[0])
    return jnp.where(low if keep_low else ~low, block, jnp.zeros_like(block))


def fwd_kernel(dims, idx_ref, gl_ref, qkv_ref, bias_ref, *rest):
    heads, nblocks, slots_n, first, parts, chunk, wide = dims
    out_refs, lse_ref, sbuf, s_v, e_v, l_v, out_v = rest[:parts], rest[parts], *rest[parts + 1 :]
    n = nblocks * BL
    lane = lax.broadcasted_iota(jnp.int32, (BL, 128), 1)

    def finish(row, outs, lses):
        low = low_lanes(BL)
        for p in range((heads + 1) // 2):
            if 2 * p + 1 < heads:
                both = jnp.where(low, outs[2 * p], outs[2 * p + 1])
                out_v[pl.ds(row, BL), p * 128 : (p + 1) * 128] = both.astype(bf16)
            else:
                out_v[pl.ds(row, BL), p * 128 : p * 128 + HD] = outs[2 * p][:, :HD].astype(bf16)
        total = jnp.zeros((BL, 128), f32)
        for h in range(heads):
            total = jnp.where(lane == h, lses[h], total)
        lse_ref[pl.ds(row, BL), :] = total

    def queries(r, h):
        return pick(qkv_ref[pl.ds(r, BL), (heads + h // 2) * 128 : (heads + h // 2 + 1) * 128], h % 2 == 1)

    blocks = parts * chunk

    def clamp(b):
        return jnp.minimum(jnp.maximum(b, 0), blocks - 1)

    def gathered(a, h):
        base = (h * nblocks + a) * slots_n
        return jnp.concatenate(
            [
                qkv_ref[pl.ds(pl.multiple_of(idx_ref[base + j] * BL, BL), BL), h * 128 : (h + 1) * 128]
                for j in range(slots_n)
            ],
            0,
        )

    def body(b, _):
        last, now, new = clamp(b - 2), clamp(b - 1), clamp(b)
        outs, lses = [], []
        for h in range(heads):
            o = jnp.dot(e_v[h], gathered(first + last, h), preferred_element_type=f32)
            outs.append(o)
            lses.append(l_v[h])
        finish(pl.multiple_of(last * BL, BL), outs, lses)
        for h in range(heads):
            s = s_v[h] + bias_ref[pl.ds(h * nblocks + first + now, 1), :]
            m = jnp.max(s, -1, keepdims=True)
            e = jnp.exp(s - m)
            l = jnp.sum(e, -1, keepdims=True)
            e_v[h] = (e * (1.0 / l)).astype(bf16)
            l_v[h] = jnp.broadcast_to(m + jnp.log(l), (BL, 128))
        for h in range(heads):
            a = first + new
            s_v[h] = lax.dot_general(
                queries(pl.multiple_of(a * BL, BL), h), gathered(a, h), NT, preferred_element_type=f32
            )
        return 0

    lax.fori_loop(0, blocks + 2, body, 0)

    def whole_row(g, _):
        a = gl_ref[1 + g]
        local = a - first

        @pl.when((local >= 0) & (local < parts * chunk))
        def _():
            r = pl.multiple_of(a * BL, BL)
            outs, lses = [], []
            for h in range(heads):
                q = queries(r, h)
                m = None
                for c in range(n // wide):
                    cs = slice(c * wide, (c + 1) * wide)
                    s = lax.dot_general(q, qkv_ref[cs, h * 128 : (h + 1) * 128], NT, preferred_element_type=f32)
                    sbuf[h, :, cs] = s
                    mc = jnp.max(s, -1, keepdims=True)
                    m = mc if m is None else jnp.maximum(m, mc)
                l = 0.0
                for c in range(n // wide):
                    cs = slice(c * wide, (c + 1) * wide)
                    e = jnp.exp(sbuf[h, :, cs] - m)
                    sbuf[h, :, cs] = e
                    l = l + jnp.sum(e, -1, keepdims=True)
                inv = 1.0 / l
                o = 0.0
                for c in range(n // wide):
                    cs = slice(c * wide, (c + 1) * wide)
                    p = (sbuf[h, :, cs] * inv).astype(bf16)
                    o = o + jnp.dot(p, qkv_ref[cs, h * 128 : (h + 1) * 128], preferred_element_type=f32)
                outs.append(o)
                lses.append(m + jnp.log(l))
            finish(pl.multiple_of(local * BL, BL), outs, lses)

        return 0

    lax.fori_loop(0, gl_ref[0], whole_row, 0)
    for part in range(parts):
        out_refs[part][...] = out_v[part * chunk * BL : (part + 1) * chunk * BL, :]


def attn_fwd(idx, gl, qkv, bias, heads, first_part, parts):
    n = qkv.shape[0]
    nblocks = n // BL
    chunk = nblocks // 4
    slots_n = bias.shape[1] // BL
    vmem = pl.BlockSpec(memory_space=pltpu.VMEM)
    smem = pl.BlockSpec(memory_space=pltpu.SMEM)
    dims = (heads, nblocks, slots_n, first_part * chunk, parts, chunk, 512)
    return pl.pallas_call(
        functools.partial(fwd_kernel, dims),
        out_shape=tuple([jax.ShapeDtypeStruct((n // 4, heads * HD), bf16)] * parts)
        + (jax.ShapeDtypeStruct((parts * n // 4, 128), f32),),
        in_specs=[smem, smem, vmem, vmem],
        out_specs=tuple([vmem] * (parts + 1)),
        scratch_shapes=[
            pltpu.VMEM((heads, BL, n), f32),
            pltpu.VMEM((heads, BL, slots_n * BL), f32),
            pltpu.VMEM((heads, BL, slots_n * BL), bf16),
            pltpu.VMEM((heads, BL, 128), f32),
            pltpu.VMEM((parts * n // 4, heads * HD), bf16),
        ],
        compiler_params=pltpu.CompilerParams(vmem_limit_bytes=24 << 20),
        cost_estimate=pl.CostEstimate(flops=10 * parts * 10**9, bytes_accessed=10**7, transcendentals=0),
        name="attn_fwd",
    )(idx, gl, qkv, bias)


def bwd_kernel(dims, idx_ref, gl_ref, qkv_ref, bias_ref, *rest):
    heads, nblocks, slots_n, first, parts, chunk, wide, begin, end = dims
    g_refs, rest = rest[:parts], rest[parts:]
    lse_ref, rest = rest[0], rest[1:]
    if not begin:
        acc_in, dq_in, rest = rest[0], rest[1], rest[2:]
    if end:
        out_ref, acc, pbuf, dbuf, sd_v, w_v, g_v = rest
    else:
        acc, dq_ref, pbuf, dbuf, sd_v, w_v, g_v = rest
    n = nblocks * BL
    pairs = (heads + 1) // 2
    kvw = heads * 128

    def start(i, _):
        rr = pl.ds(pl.multiple_of(i * 256, 256), 256)
        if begin:
            acc[rr, :] = jnp.zeros((256, kvw), f32)
        else:
            acc[rr, :] = acc_in[rr, :]
        return 0

    lax.fori_loop(0, n // 256, start, 0)
    if end and not begin:
        out_ref[0 : first * BL, kvw:] = dq_in[...]

    for part in range(parts):
        g_v[part * chunk * BL : (part + 1) * chunk * BL, :] = g_refs[part][...]

    def grads(at, h):
        w = min(128, heads * HD - (h // 2) * 128)
        g = g_v[pl.ds(at, BL), (h // 2) * 128 : (h // 2) * 128 + w]
        if w < 128:
            return jnp.concatenate([g, jnp.zeros((BL, 128 - w), bf16)], 1)
        return pick(g, h % 2 == 0)

    def queries(r, h):
        return pick(qkv_ref[pl.ds(r, BL), (heads + h // 2) * 128 : (heads + h // 2 + 1) * 128], h % 2 == 1)

    def finish(r, dqs):
        low = low_lanes(BL)
        for p in range(pairs):
            high = dqs[2 * p]
            odd = dqs[2 * p + 1] if 2 * p + 1 < heads else jnp.zeros_like(high)
            both = jnp.where(low, odd, high).astype(bf16)
            if end:
                out_ref[pl.ds(r, BL), kvw + p * 128 : kvw + (p + 1) * 128] = both
            else:
                dq_ref[pl.ds(pl.multiple_of(r - first * BL, BL), BL), p * 128 : (p + 1) * 128] = both

    blocks = parts * chunk

    def clamp(b):
        return jnp.minimum(jnp.maximum(b, 0), blocks - 1)

    def slot_rows(a, h):
        base = (h * nblocks + a) * slots_n
        return [pl.multiple_of(idx_ref[base + j] * BL, BL) for j in range(slots_n)]

    def stacked(b, h):
        r = pl.multiple_of((first + b) * BL, BL)
        return jnp.concatenate([queries(r, h), grads(pl.multiple_of(b * BL, BL), h)], 0)

    def body(b, _):
        last, now, new = clamp(b - 2), clamp(b - 1), clamp(b)
        dqs = []
        for h in range(heads):
            hs = slice(h * 128, (h + 1) * 128)
            rows = slot_rows(first + last, h)
            kv = jnp.concatenate([qkv_ref[pl.ds(rows[j], BL), hs] for j in range(slots_n)], 0)
            dqs.append(jnp.dot(w_v[h, :BL], kv, preferred_element_type=f32))
            dkv = lax.dot_general(w_v[h], stacked(last, h), TN, preferred_element_type=f32)
            dkv = jnp.where(b >= 2, dkv, 0.0)
            for j in range(slots_n):
                acc[pl.ds(rows[j], BL), hs] += dkv[j * BL : (j + 1) * BL]
        finish(pl.multiple_of((first + last) * BL, BL), dqs)
        for h in range(heads):
            sd = sd_v[h]
            row = pl.multiple_of(now * BL, BL)
            p = jnp.exp(
                sd[:BL] + bias_ref[pl.ds(h * nblocks + first + now, 1), :] - lse_ref[pl.ds(row, BL), h : h + 1]
            )
            dp = sd[BL:]
            ds = p * (dp - jnp.sum(dp * p, -1, keepdims=True))
            w_v[h, :BL] = ds.astype(bf16)
            w_v[h, BL:] = p.astype(bf16)
        for h in range(heads):
            rows = slot_rows(first + new, h)
            kv = jnp.concatenate(
                [qkv_ref[pl.ds(rows[j], BL), h * 128 : (h + 1) * 128] for j in range(slots_n)], 0
            )
            sd_v[h] = lax.dot_general(stacked(new, h), kv, NT, preferred_element_type=f32)
        return 0

    sd_v[...] = jnp.zeros_like(sd_v)
    w_v[...] = jnp.zeros_like(w_v)
    lax.fori_loop(0, blocks + 2, body, 0)

    def whole_row(g, _):
        a = gl_ref[1 + g]
        local = a - first

        @pl.when((local >= 0) & (local < parts * chunk))
        def _():
            r = pl.multiple_of(a * BL, BL)
            row = pl.multiple_of(local * BL, BL)
            dqs = []
            for h in range(heads):
                hs = slice(h * 128, (h + 1) * 128)
                x = jnp.concatenate([queries(r, h), grads(row, h)], 0)
                lse = lse_ref[pl.ds(row, BL), h : h + 1]
                inner = 0.0
                for c in range(n // wide):
                    cs = slice(c * wide, (c + 1) * wide)
                    sd = lax.dot_general(x, qkv_ref[cs, hs], NT, preferred_element_type=f32)
                    p = jnp.exp(sd[:BL] - lse)
                    dp = sd[BL:]
                    pbuf[h, :, cs] = p
                    dbuf[h, :, cs] = dp
                    inner = inner + jnp.sum(dp * p, -1, keepdims=True)
                dq = 0.0
                for c in range(n // wide):
                    cs = slice(c * wide, (c + 1) * wide)
                    p = pbuf[h, :, cs]
                    ds = (p * (dbuf[h, :, cs] - inner)).astype(bf16)
                    w = jnp.concatenate([ds, p.astype(bf16)], 0)
                    dq = dq + jnp.dot(ds, qkv_ref[cs, hs], preferred_element_type=f32)
                    acc[cs, hs] += lax.dot_general(w, x, TN, preferred_element_type=f32)
                dqs.append(dq)
            finish(r, dqs)

        return 0

    lax.fori_loop(0, gl_ref[0], whole_row, 0)
    if end:

        def flush(i, _):
            rr = pl.ds(pl.multiple_of(i * 256, 256), 256)
            out_ref[rr, :kvw] = acc[rr, :].astype(bf16)
            return 0

        lax.fori_loop(0, n // 256, flush, 0)


def attn_bwd(idx, gl, qkv, bias, grads, lse, heads, first_part, carried, end):
    n = qkv.shape[0]
    nblocks = n // BL
    chunk = nblocks // 4
    slots_n = bias.shape[1] // BL
    parts = len(grads)
    vmem = pl.BlockSpec(memory_space=pltpu.VMEM)
    smem = pl.BlockSpec(memory_space=pltpu.SMEM)
    dims = (heads, nblocks, slots_n, first_part * chunk, parts, chunk, 512, not carried, end)
    pairs = (heads + 1) // 2
    scratch = [pltpu.VMEM((heads, BL, n), f32)] * 2 + [
        pltpu.VMEM((heads, 2 * BL, slots_n * BL), f32),
        pltpu.VMEM((heads, 2 * BL, slots_n * BL), bf16),
        pltpu.VMEM((parts * n // 4, heads * HD), bf16),
    ]
    if end:
        out_shape = jax.ShapeDtypeStruct((n, (heads + pairs) * 128), bf16)
        out_specs = vmem
        scratch = [pltpu.VMEM((n, heads * 128), f32)] + scratch
    else:
        out_shape = (
            jax.ShapeDtypeStruct((n, heads * 128), f32),
            jax.ShapeDtypeStruct((parts * n // 4, pairs * 128), bf16),
        )
        out_specs = (vmem, vmem)
    return pl.pallas_call(
        functools.partial(bwd_kernel, dims),
        out_shape=out_shape,
        in_specs=[smem, smem] + [vmem] * (3 + parts + len(carried)),
        out_specs=out_specs,
        scratch_shapes=scratch,
        compiler_params=pltpu.CompilerParams(vmem_limit_bytes=36 << 20),
        cost_estimate=pl.CostEstimate(flops=11 * parts * 10**9, bytes_accessed=10**7, transcendentals=0),
        name="attn_bwd",
    )(idx, gl, qkv, bias, *grads, lse, *carried)


MESH_ID = pl.DeviceIdType.MESH


def flip(index, number):
    total = 0
    for bit in (1, 2, 4):
        digit = (index // bit) % 2
        total = total + bit * ((1 - digit) if number & bit else digit)
    return total


def blend(a, b):
    return sum(bit * (((a // bit) % 2 + (b // bit) % 2) % 2) for bit in (1, 2, 4))


def greet(item, place, items):
    barrier = pltpu.get_barrier_semaphore()
    for t in range(1, 4):
        pl.semaphore_signal(barrier, inc=1, device_id=(item, flip(place, t)), device_id_type=MESH_ID)
    for k in range(1, items):
        pl.semaphore_signal(barrier, inc=1, device_id=(flip(item, k), place), device_id_type=MESH_ID)
    pl.semaphore_wait(barrier, 3 + items - 1)


def tail_kernel(
    items, query_columns, x0, x1, x2, x3, gq_ref, slab_ref, first_ref, small_ref, uk_ref, ur_ref, dk_ref, d1_ref, d2_ref, d3_ref,
    din_ref, group_ref, sgroup_ref, total_ref, squares_ref,
    near_out, near_in, far_out, far_in, grad_v, side_out, side_in, part_out, part_in, z_out, z_in, d_out, d_in, small_in, small_mid, small_side, small_both, small_items, small_sum, sq_out, sq_in, sq_mid, sq_items,
    near_send, near_recv, far_send, far_recv, side_send, side_recv, part_send, part_recv, z_send, z_recv, d_send, d_recv, sg_send, sg_recv, sx_send, sx_recv, si_send, si_recv, st_send, st_recv,
    gr_send, gr_recv, sl_send, sl_recv, qg_send, qg_recv, qi_send, qi_recv,
):
    xs = (x0, x1, x2, x3)
    item, place = lax.axis_index("item"), lax.axis_index("seq")
    tokens, width = x0.shape
    rows = width // items
    tile = tokens // 2
    chunks = tokens // tile
    columns = gq_ref.shape[1]
    levels = items // 2
    up_rows = uk_ref.shape[1]
    greet(item, place, items)

    def to_group(src, dst, send, recv, t):
        return pltpu.make_async_remote_copy(
            src_ref=src, dst_ref=dst, send_sem=send, recv_sem=recv,
            device_id=(item, flip(place, t)), device_id_type=MESH_ID,
        )

    def to_item(src, dst, send, recv, k):
        return pltpu.make_async_remote_copy(
            src_ref=src, dst_ref=dst, send_sem=send, recv_sem=recv,
            device_id=(flip(item, k), place), device_id_type=MESH_ID,
        )

    small_copies = [
        to_group(small_ref.at[flip(place, t)], small_in.at[t], sg_send.at[t], sg_recv.at[t], t) for t in range(1, 4)
    ]
    for copy in small_copies:
        copy.start()

    z_copies = []
    for kz in range(levels - 1, 0, -1):
        z_out[kz] = uk_ref[kz] + ur_ref[kz]
        copy = to_item(z_out.at[kz], z_in.at[kz], z_send.at[kz], z_recv.at[kz], 2 * kz)
        copy.start()
        z_copies.append(copy)

    def down_sum(kx):
        return (
            dk_ref[kx].astype(f32) + d1_ref[kx].astype(f32) + d2_ref[kx].astype(f32) + d3_ref[kx].astype(f32)
        )

    d_out[...] = down_sum(1).astype(bf16)
    d_copy = to_item(d_out, d_in, d_send.at[0], d_recv.at[0], 1)
    d_copy.start()

    def token_part(t, c):
        return lax.dot_general(
            gq_ref[t * tokens + c * tile : t * tokens + (c + 1) * tile, :], slab_ref[...], NT, preferred_element_type=f32
        )

    near_copies = {}
    far_copies = []

    def send_near(t, *which):
        for c in which:
            cs = pl.ds(c * tile, tile)
            near_out[t // 2, c * tile : (c + 1) * tile, :] = token_part(t, c).astype(bf16)
            copy = to_group(
                near_out.at[t // 2, cs], near_in.at[t // 2, cs], near_send.at[t // 2, c], near_recv.at[t // 2, c], 1
            )
            copy.start()
            near_copies[(t // 2, c)] = copy

    def send_far(c):
        cs = slice(c * tile, (c + 1) * tile)
        part = token_part(2, c)
        near_copies[(1, c)].wait_recv()
        far_out[cs, :] = (part.astype(bf16).astype(f32) + near_in[1, cs, :].astype(f32)).astype(bf16)
        copy = to_group(far_out.at[pl.ds(c * tile, tile)], far_in.at[pl.ds(c * tile, tile)], far_send.at[c], far_recv.at[c], 2)
        copy.start()
        far_copies.append(copy)

    send_near(3, 0)
    send_far(0)
    for copy in small_copies:
        copy.wait()
    small_mid[...] = small_ref[place] + small_in[1] + small_in[2] + small_in[3]
    small_x = to_item(small_mid, small_side, sx_send.at[0], sx_recv.at[0], 1)
    small_x.start()
    grads = 0.0
    for t in range(4):
        grads = grads + lax.dot_general(
            xs[t][...], gq_ref[t * tokens : (t + 1) * tokens, :], TN, preferred_element_type=f32
        )
    grad_v[...] = grads

    def sums(r, line):
        at = pl.multiple_of(r * tile, tile)
        return line + jnp.sum(gq_ref[pl.ds(at, tile), :].astype(f32), 0, keepdims=True)

    line = lax.fori_loop(0, 4 * chunks, sums, jnp.zeros((1, columns), f32))
    high = line.astype(bf16)
    rest = (line - high.astype(f32)).astype(bf16)
    which = lax.broadcasted_iota(jnp.int32, (16, columns), 0)
    lines = jnp.where(which == 0, high.astype(f32), jnp.where(which == 1, rest.astype(f32), 0.0)).astype(bf16)
    level = item // 2
    side = item % 2

    def slab_part(kz, kx):
        at = pl.multiple_of((2 * flip(level, kz) + (side + kx) % 2) * rows, 8)
        return grad_v[pl.ds(at, rows), :]

    side_copies = []
    for kz in range(levels - 1, -1, -1):
        side_out[kz, 0:rows, :] = slab_part(kz, 1).astype(bf16)
        side_out[kz, rows : rows + 16, :] = lines
        copy = to_item(side_out.at[kz], side_in.at[kz], side_send.at[kz], side_recv.at[kz], 1)
        copy.start()
        side_copies.append((kz, copy))

    send_near(3, 1)
    send_far(1)
    small_x.wait()
    small_both[...] = small_mid[...] + small_side[...]
    item_copies = [
        to_item(small_both, small_items.at[kz], si_send.at[kz], si_recv.at[kz], 2 * kz) for kz in range(1, levels)
    ]
    for copy in item_copies:
        copy.start()

    send_near(1, *range(chunks))
    for c in range(chunks):
        cs = slice(c * tile, (c + 1) * tile)
        din_ref[cs, :] = first_ref[cs, :] + token_part(0, c).astype(bf16).astype(f32)

    for copy in item_copies:
        copy.wait()
    small_sum[...] = small_both[...] + small_items[1] + small_items[2] + small_items[3]
    total_ref[place] = small_sum[...]
    total_copies = [to_group(small_sum, total_ref.at[place], st_send.at[t], st_recv.at[t], t) for t in range(1, 4)]
    for copy in total_copies:
        copy.start()

    def square_sum(values):
        return jnp.sum(jnp.sum(values * values, 0, keepdims=True), -1, keepdims=True)

    part_copies = []
    for kz, copy in side_copies:
        copy.wait()
        part = slab_part(kz, 0) + side_in[kz, 0:rows, :].astype(f32)
        both = lines.astype(f32) + side_in[kz, rows : rows + 16, :].astype(f32)
        if kz:
            part_out[kz, 0:rows, :] = part.astype(bf16)
            whole = jnp.sum(both, 0, keepdims=True)
            short = whole.astype(bf16).astype(f32)
            which_row = jnp.where(which == 0, short, jnp.where(which == 1, whole - short, 0.0))
            part_out[kz, rows : rows + 16, :] = which_row.astype(bf16)
            copy = to_item(part_out.at[kz], part_in.at[kz], part_send.at[kz], part_recv.at[kz], 2 * kz)
            copy.start()
            part_copies.append(copy)
        else:
            own_part, own_lines = part, both

    for copy in z_copies:
        copy.wait()

    up = uk_ref[0].astype(f32) + ur_ref[0].astype(f32)
    for kz in range(1, levels):
        up = up + z_in[kz].astype(f32)
    d_copy.wait()
    down = down_sum(0) + d_in[...].astype(f32)
    group_ref[0, 0:up_rows, :] = up.astype(bf16)
    group_ref[0, up_rows:, :] = down.astype(bf16)
    big_copies = [to_group(group_ref.at[0], group_ref.at[t], gr_send.at[t], gr_recv.at[t], t) for t in (2, 1)]
    for copy in big_copies:
        copy.start()
    squares = square_sum(up) + square_sum(down)
    for copy in part_copies:
        copy.wait()
    own, whole = own_part, jnp.sum(own_lines, 0, keepdims=True)
    for kz in range(1, levels):
        own = own + part_in[kz, 0:rows, :].astype(f32)
        whole = whole + jnp.sum(part_in[kz, rows : rows + 16, :].astype(f32), 0, keepdims=True)
    column = lax.broadcasted_iota(jnp.int32, (1, columns), 1)
    squares = squares + square_sum(own * jnp.where(column < query_columns, 1.0, HD**-0.5))
    sq_out[...] = jnp.broadcast_to(squares, (8, 128))
    sq_copies = [to_group(sq_out, sq_in.at[t], qg_send.at[t], qg_recv.at[t], t) for t in range(1, 4)]
    for copy in sq_copies:
        copy.start()
    short = whole.astype(bf16).astype(f32)
    sgroup_ref[0, 0:rows, :] = own.astype(bf16)
    sgroup_ref[0, rows : rows + 16, :] = jnp.where(which == 0, short, jnp.where(which == 1, whole - short, 0.0)).astype(bf16)
    group_copies = [to_group(sgroup_ref.at[0], sgroup_ref.at[t], sl_send.at[t], sl_recv.at[t], t) for t in (2, 1)]
    for copy in group_copies:
        copy.start()
    for copy in sq_copies:
        copy.wait()
    sq_mid[...] = sq_out[...] + sq_in[1] + sq_in[2] + sq_in[3]
    sq_item_copies = [to_item(sq_mid, sq_items.at[k], qi_send.at[k], qi_recv.at[k], k) for k in range(1, items)]
    for copy in sq_item_copies:
        copy.start()

    group_copies[0].wait()
    cross = to_group(sgroup_ref.at[2], sgroup_ref.at[3], sl_send.at[3], sl_recv.at[3], 1)
    cross.start()
    big_copies[0].wait()
    big_cross = to_group(group_ref.at[2], group_ref.at[3], gr_send.at[3], gr_recv.at[3], 1)
    big_cross.start()
    for t in range(1, 4):
        total_copies[t - 1].wait_send()
        to_group(small_sum, total_ref.at[flip(place, t)], st_send.at[t], st_recv.at[t], t).wait_recv()
    for c in range(chunks):
        cs = slice(c * tile, (c + 1) * tile)
        near_copies[(1, c)].wait_send()
        near_copies[(0, c)].wait()
        far_copies[c].wait()
        din_ref[cs, :] = din_ref[cs, :] + near_in[0, cs, :].astype(f32) + far_in[cs, :].astype(f32)
    for copy in sq_item_copies:
        copy.wait()
    answer = sq_mid[...]
    for k in range(1, items):
        answer = answer + sq_items[k]
    squares_ref[...] = answer
    group_copies[1].wait()
    cross.wait()
    big_copies[1].wait()
    big_cross.wait()


def tail(xs, gq, slab, first, small, shards, items, query_columns):
    tokens, width = xs[0].shape
    columns = gq.shape[1]
    rows = width // items
    vmem = pl.BlockSpec(memory_space=pltpu.VMEM)
    dma = pltpu.SemaphoreType.DMA
    chunks, levels = 2, items // 2
    up_rows = shards[0].shape[1]
    quarter = up_rows + rows
    slab_part = (levels, rows + 16, columns)
    return pl.pallas_call(
        functools.partial(tail_kernel, items, query_columns),
        out_shape=(
            jax.ShapeDtypeStruct((tokens, width), f32),
            jax.ShapeDtypeStruct((4, quarter, width), bf16),
            jax.ShapeDtypeStruct((4, rows + 16, columns), bf16),
            jax.ShapeDtypeStruct(small.shape, f32),
            jax.ShapeDtypeStruct((8, 128), f32),
        ),
        in_specs=[vmem] * 14,
        out_specs=(vmem,) * 5,
        scratch_shapes=[
            pltpu.VMEM((2, tokens, width), bf16),
            pltpu.VMEM((2, tokens, width), bf16),
            pltpu.VMEM((tokens, width), bf16),
            pltpu.VMEM((tokens, width), bf16),
            pltpu.VMEM((width, columns), f32),
            pltpu.VMEM(slab_part, bf16),
            pltpu.VMEM(slab_part, bf16),
            pltpu.VMEM(slab_part, bf16),
            pltpu.VMEM(slab_part, bf16),
            pltpu.VMEM((levels, up_rows, width), bf16),
            pltpu.VMEM((levels, up_rows, width), bf16),
            pltpu.VMEM((rows, width), bf16),
            pltpu.VMEM((rows, width), bf16),
            pltpu.VMEM((4, 8, width), f32),
            pltpu.VMEM((8, width), f32),
            pltpu.VMEM((8, width), f32),
            pltpu.VMEM((8, width), f32),
            pltpu.VMEM((levels, 8, width), f32),
            pltpu.VMEM((8, width), f32),
            pltpu.VMEM((8, 128), f32),
            pltpu.VMEM((4, 8, 128), f32),
            pltpu.VMEM((8, 128), f32),
            pltpu.VMEM((items, 8, 128), f32),
            dma((2, chunks)), dma((2, chunks)), dma((chunks,)), dma((chunks,)),
            dma((levels,)), dma((levels,)), dma((levels,)), dma((levels,)), dma((levels,)), dma((levels,)), dma((1,)), dma((1,)),
            dma((4,)), dma((4,)), dma((1,)), dma((1,)), dma((levels,)), dma((levels,)), dma((4,)), dma((4,)),
            dma((4,)), dma((4,)), dma((4,)), dma((4,)), dma((4,)), dma((4,)), dma((items,)), dma((items,)),
        ],
        compiler_params=pltpu.CompilerParams(vmem_limit_bytes=42 << 20, collective_id=3, has_side_effects=True),
        cost_estimate=pl.CostEstimate(flops=60 * 10**9, bytes_accessed=10**7, transcendentals=0),
        name="tail",
    )(*xs, gq, slab, first, small, *shards)


def update_kernel(place_of, heads, *refs):
    group_ref, sgroup_ref, total_ref, squares_ref, made_out, made_in = refs[:6]
    given, norm_ref, out_ref, din_ref, new = refs[6:21], refs[21], refs[22], refs[23], refs[24:39]
    held, grad_q, grad_s, out_v, din_v, in_sem, out_sem, made_sem = refs[39:54], *refs[54:]
    made = [
        pltpu.make_async_copy(made_out, out_v, made_sem.at[0]),
        pltpu.make_async_copy(made_in, din_v, made_sem.at[1]),
    ]
    order = (12, 13, 14, 3, 4, 5, 0, 1, 2, 6, 7, 8, 9, 10, 11)
    loads = {n: pltpu.make_async_copy(given[n], held[n], in_sem.at[n]) for n in order}
    for n in order:
        loads[n].start()
    for copy in made:
        copy.start()
    stores = []
    place = place_of()
    rows, width = held[3].shape
    third = rows // 3
    small_rows = held[12].shape[0]
    for row in range(small_rows):
        grad_s[row : row + 1, :] = total_ref[row // 3, row % 3 : row % 3 + 1, :]
    for q in range(4):
        t = flip(place, q)
        piece = sgroup_ref.at[t]
        for h in range(heads):
            at = (q * heads + h) * HD
            pair = h * 128
            value, key = (pair, pair + HD) if h % 2 == 0 else (pair + HD, pair)
            query = (heads + h // 2) * 128 + (HD if h % 2 == 0 else 0)
            for part, base, scale in ((0, query, HD**-0.5), (1, key, 1.0), (2, value, 1.0)):
                grad_q[:, part * width + at : part * width + at + HD] = piece[0:rows, base : base + HD].astype(f32) * scale
            for row, base, scale in ((2, query, HD**-0.5), (3, value, 1.0)):
                line = piece[rows : rows + 16, base : base + HD].astype(f32)
                grad_s[row : row + 1, at : at + HD] = (line[0:1] + line[1:2]) * scale
    small = grad_s[0:small_rows, :]
    squares = jnp.sum(jnp.sum(small * small, 0, keepdims=True), -1, keepdims=True) + squares_ref[0:1, 0:1]
    norm = jnp.sqrt(squares)
    norm_ref[...] = norm
    factor = jnp.minimum(1.0, clip_level / (norm + 1e-06))

    def apply(base, index, grad, decay, rate):
        w, f, s = held[base : base + 3]
        fresh = adam_update(w[index], f[index], s[index], grad * factor, decay, rate)
        w[index], f[index], s[index] = fresh

    def arrive(base):
        for n in range(base, base + 3):
            loads[n].wait()

    def leave(base):
        for n in range(base, base + 3):
            copy = pltpu.make_async_copy(held[n], new[n], out_sem.at[n])
            copy.start()
            stores.append(copy)

    everything = (slice(None), slice(None))
    arrive(12)
    apply(12, everything, small, 0.0, small_rate)
    leave(12)
    arrive(3)
    for q in range(3):
        os = (slice(q * third, (q + 1) * third), slice(None))
        apply(3, os, group_ref[flip(place, q), rows : rows + third, :].astype(f32), weight_decay, learn_rate)
    leave(3)
    arrive(0)
    for part in range(3):
        cs = slice(part * width, (part + 1) * width)
        apply(0, (slice(None), cs), grad_q[:, cs], weight_decay, learn_rate)
    leave(0)
    arrive(6)
    for q in range(4):
        cs = slice(q * width, (q + 1) * width)
        apply(6, (slice(None), cs), group_ref[flip(place, q), 0:rows, :].astype(f32), weight_decay, learn_rate)
    leave(6)
    for copy in made:
        copy.wait()
    made = [
        pltpu.make_async_copy(out_v, out_ref, made_sem.at[2]),
        pltpu.make_async_copy(din_v, din_ref, made_sem.at[3]),
    ]
    for copy in made:
        copy.start()
    arrive(9)
    for q in range(4):
        ds = (slice(q * rows, (q + 1) * rows), slice(None))
        apply(9, ds, group_ref[flip(place, q), rows + third :, :].astype(f32), weight_decay, learn_rate)
    leave(9)
    for copy in stores + made:
        copy.wait()


def update(place_of, heads, group, sgroup, total, squares, made, states):
    vmem = pl.BlockSpec(memory_space=pltpu.VMEM)
    anywhere = pl.BlockSpec(memory_space=pl.ANY)
    count = len(states)
    dma = pltpu.SemaphoreType.DMA
    return pl.pallas_call(
        functools.partial(update_kernel, place_of, heads),
        out_shape=(jax.ShapeDtypeStruct((1, 1), f32),)
        + tuple(jax.ShapeDtypeStruct(a.shape, a.dtype) for a in made)
        + tuple(jax.ShapeDtypeStruct(a.shape, f32) for a in states),
        in_specs=[vmem] * 4 + [anywhere] * (2 + count),
        out_specs=(vmem,) + (anywhere,) * (2 + count),
        scratch_shapes=[pltpu.VMEM(a.shape, f32) for a in states]
        + [pltpu.VMEM(states[0].shape, f32), pltpu.VMEM((16, total.shape[2]), f32)]
        + [pltpu.VMEM(a.shape, a.dtype) for a in made]
        + [dma((count,)), dma((count,)), dma((4,))],
        compiler_params=pltpu.CompilerParams(vmem_limit_bytes=60 << 20),
        cost_estimate=pl.CostEstimate(flops=10**9, bytes_accessed=25 * 10**6, transcendentals=0),
        name="update",
    )(group, sgroup, total, squares, *made, *states)


def line_place(z):
    return (z + 2) % 3 + (z // 3) * (3 - (z + 2) % 3)


def head_kernel(
    items, heads, x_ref, wq_ref, small_ref, wo_ref, wu_ref, wd_ref,
    near_out, far_out, cross_out, qkv_out, slab_out, line_ref, side_ref, wfar_ref,
    near_ref, far_ref, cross_ref, qkv_ref, slab_ref, piece_ref, bias_ref, raw_v, quarter_ref, pieces_v, x_send, x_recv, far_send, far_recv, cross_send, cross_recv,
    s_up_send, s_up_recv, s_down_send, s_down_recv, s_side_send, s_side_recv,
    w_up_send, w_up_recv, w_down_send, w_down_recv, w_side_send, w_side_recv, w_own, y_send, y_recv, keep_sem, raw_sem, qkv_sem,
):
    item, place = lax.axis_index("item"), lax.axis_index("seq")
    side, level = item % 2, item // 2
    levels = items // 2
    tokens = x_ref.shape[0]
    rows, width = wo_ref.shape
    third = rows // 3
    raws = (
        (wu_ref.at[:, pl.ds(pl.multiple_of(place * width, 128), width)], 0, rows),
        (wd_ref.at[pl.ds(pl.multiple_of(place * rows, 8), rows)], rows, rows),
        (wo_ref.at[pl.ds(pl.multiple_of((place - place // 3) * third, 8), third)], 2 * rows, third),
    )
    for n, (src, at, count) in enumerate(raws):
        pltpu.make_async_copy(src, raw_v.at[pl.ds(at, count)], raw_sem.at[n]).start()
    bias_ref[...] = jnp.zeros_like(bias_ref)
    piece_ref[...] = jnp.zeros_like(piece_ref)
    for g in range(4):

        @pl.when(place == g)
        def _():
            for h in range(heads):
                at = (g * heads + h) * HD
                pair = h * 128
                value, key = (pair, pair + HD) if h % 2 == 0 else (pair + HD, pair)
                query = (heads + h // 2) * 128 + (HD if h % 2 == 0 else 0)
                for part, base, scale in ((0, query, HD**-0.5), (1, key, 1.0), (2, value, 1.0)):
                    cut = wq_ref[:, part * width + at : part * width + at + HD]
                    piece_ref[:, base : base + HD] = (cut * scale).astype(bf16)
                bias_ref[:, query : query + HD] = small_ref[2:3, at : at + HD] * HD**-0.5
                bias_ref[:, value : value + HD] = small_ref[3:4, at : at + HD]

    tile = 256
    chunks = tokens // tile
    greet(item, place, items)

    def to_group(src, dst, send, recv, t):
        return pltpu.make_async_remote_copy(
            src_ref=src, dst_ref=dst, send_sem=send, recv_sem=recv,
            device_id=(item, flip(place, t)), device_id_type=MESH_ID,
        )

    class Flow:
        def __init__(self, slot, side_slot, other_slot, arrived, sems):
            self.slot, self.side_slot, self.other_slot, self.arrived = slot, side_slot, other_slot, arrived
            self.up_send, self.up_recv, self.down_send, self.down_recv, self.side_send, self.side_recv = sems

        def up(self, d):
            part = self.slot(-d)
            return pltpu.make_async_remote_copy(
                src_ref=part, dst_ref=part, send_sem=self.up_send.at[d], recv_sem=self.up_recv.at[d],
                device_id=(item + 2, place), device_id_type=MESH_ID,
            )

        def down(self, d):
            part = self.slot(d)
            return pltpu.make_async_remote_copy(
                src_ref=part, dst_ref=part, send_sem=self.down_send.at[d], recv_sem=self.down_recv.at[d],
                device_id=(item - 2, place), device_id_type=MESH_ID,
            )

        def across(self, d):
            part = self.slot(d)
            return pltpu.make_async_remote_copy(
                src_ref=part, dst_ref=self.side_slot(d), send_sem=self.side_send.at[level + d], recv_sem=self.side_recv.at[level + d],
                device_id=(item + 1 - 2 * side, place), device_id_type=MESH_ID,
            )

        def begin(self):
            @pl.when(level < levels - 1)
            def _():
                self.up(0).start()

            @pl.when(level > 0)
            def _():
                self.down(0).start()

            self.across(0).start()
            self.arrived(0)

        def step(self, d):
            @pl.when(level >= d)
            def _():
                part = self.slot(-d)
                pltpu.make_async_remote_copy(
                    src_ref=part, dst_ref=part, send_sem=self.up_send.at[d - 1], recv_sem=self.up_recv.at[d - 1],
                    device_id=(item + 1 - 2 * side, place), device_id_type=MESH_ID,
                ).wait_recv()

                @pl.when(level < levels - 1)
                def _():
                    self.up(d).start()

                self.across(-d).start()
                self.arrived(-d)

            @pl.when(level < levels - d)
            def _():
                part = self.slot(d)
                pltpu.make_async_remote_copy(
                    src_ref=part, dst_ref=part, send_sem=self.down_send.at[d - 1], recv_sem=self.down_recv.at[d - 1],
                    device_id=(item + 1 - 2 * side, place), device_id_type=MESH_ID,
                ).wait_recv()

                @pl.when(level > 0)
                def _():
                    self.down(d).start()

                self.across(d).start()
                self.arrived(d)

        def other_side(self):
            for z in range(levels):
                part = self.other_slot(z)
                pltpu.make_async_remote_copy(
                    src_ref=part, dst_ref=part, send_sem=self.side_send.at[z], recv_sem=self.side_recv.at[z],
                    device_id=(item + 1 - 2 * side, place), device_id_type=MESH_ID,
                ).wait_recv()

        def finish(self):
            for d in range(levels - 1):

                @pl.when((level >= d) & (level < levels - 1))
                def _():
                    self.up(d).wait_send()

                @pl.when((level < levels - d) & (level > 0))
                def _():
                    self.down(d).wait_send()

            for z in range(levels):
                part = self.slot(z - level)
                pltpu.make_async_remote_copy(
                    src_ref=part, dst_ref=part, send_sem=self.side_send.at[z], recv_sem=self.side_recv.at[z],
                    device_id=(item + 1 - 2 * side, place), device_id_type=MESH_ID,
                ).wait_send()

    def far_copy(z):
        at = line_place(z)
        return to_group(line_ref.at[at], wfar_ref.at[at], y_send.at[at], y_recv.at[at], 2)

    def to_far(z):
        @pl.when((z > 0) & (z < levels - 1))
        def _():
            far_copy(z).start()

    def piece_slot(d):
        return pieces_v.at[item + 2 * d]

    slab_flow = Flow(piece_slot, piece_slot, lambda z: pieces_v.at[2 * z + 1 - side], lambda d: None, (s_up_send, s_up_recv, s_down_send, s_down_recv, s_side_send, s_side_recv))
    w_flow = Flow(
        lambda d: line_ref.at[line_place(level + d)], lambda d: side_ref.at[line_place(level + d)],
        lambda z: side_ref.at[line_place(z)], lambda d: to_far(level + d), (w_up_send, w_up_recv, w_down_send, w_down_recv, w_side_send, w_side_recv))
    pieces_v[item] = piece_ref[...]
    slab_flow.begin()
    far_copies, near_copies, cross_copies = [], [], []
    for c in range(chunks):
        cs = pl.ds(c * tile, tile)
        far_copies.append(to_group(x_ref.at[cs], far_ref.at[cs], far_send.at[c], far_recv.at[c], 2))
        far_copies[-1].start()
    near_copies = [to_group(x_ref, near_ref, x_send.at[0], x_recv.at[0], 1)]
    near_copies[0].start()
    for n, (src, at, count) in enumerate(raws):
        pltpu.make_async_copy(src, raw_v.at[pl.ds(at, count)], raw_sem.at[n]).wait()
    quarter_ref[...] = raw_v[...].astype(bf16)
    own = pltpu.make_async_copy(quarter_ref, line_ref.at[line_place(level)], w_own.at[0])
    own.start()
    for d in range(1, levels):
        slab_flow.step(d)
    own.wait()
    w_flow.begin()
    slab_flow.other_side()
    for j in range(items):
        slab_ref[j * rows : (j + 1) * rows, :] = pieces_v[j]

    keeps = [pltpu.make_async_copy(slab_ref, slab_out, keep_sem.at[0])]
    keeps[0].start()

    def project_rows(src, t, c):
        part = jnp.dot(src[c * tile : (c + 1) * tile, :], slab_ref[...], preferred_element_type=f32)
        at = t * tokens + c * tile
        qkv_ref[at : at + tile, :] = (part + bias_ref[...]).astype(bf16)
        copy = pltpu.make_async_copy(qkv_ref.at[pl.ds(at, tile)], qkv_out.at[pl.ds(at, tile)], qkv_sem.at[t, c])
        copy.start()
        keeps.append(copy)

    def pass_on(c):
        cs = pl.ds(c * tile, tile)
        far_copies[c].wait_recv()
        copy = to_group(far_ref.at[cs], cross_ref.at[cs], cross_send.at[c], cross_recv.at[c], 1)
        copy.start()
        cross_copies.append(copy)

    for c in range(chunks):
        project_rows(x_ref, 0, c)
        pass_on(c)
        if c + 1 < levels:
            w_flow.step(c + 1)
        if c == 0:
            near_copies[0].wait_recv()
            keeps.append(pltpu.make_async_copy(near_ref, near_out, keep_sem.at[1]))
            keeps[-1].start()
        project_rows(near_ref, 1, c)
        project_rows(far_ref, 2, c)
        cross_copies[c].wait_recv()
        project_rows(cross_ref, 3, c)
    keeps.append(pltpu.make_async_copy(far_ref, far_out, keep_sem.at[2]))
    keeps.append(pltpu.make_async_copy(cross_ref, cross_out, keep_sem.at[3]))
    for copy in keeps[-2:]:
        copy.start()
    for d in range(chunks + 1, levels):
        w_flow.step(d)
    w_flow.other_side()
    near_copies[0].wait_send()
    for c in range(chunks):
        far_copies[c].wait_send()
        cross_copies[c].wait_send()
    for z in range(1, levels - 1):
        far_copy(z).wait()
    for copy in keeps:
        copy.wait()
    slab_flow.finish()
    w_flow.finish()


def head(x, wq, small, wo, wu, wd, items, heads):
    tokens, width = x.shape
    rows = wo.shape[0]
    columns = (heads + (heads + 1) // 2) * 128
    quarter = (2 * rows + rows // 3, width)
    vmem = pl.BlockSpec(memory_space=pltpu.VMEM)
    hbm = pl.BlockSpec(memory_space=pltpu.HBM)
    dma = pltpu.SemaphoreType.DMA
    chunks, levels = tokens // 256, items // 2
    tokens_shape = jax.ShapeDtypeStruct((tokens, width), bf16)
    return pl.pallas_call(
        functools.partial(head_kernel, items, heads),
        out_shape=(
            tokens_shape, tokens_shape, tokens_shape,
            jax.ShapeDtypeStruct((4 * tokens, columns), bf16),
            jax.ShapeDtypeStruct((rows * items, columns), bf16),
            jax.ShapeDtypeStruct((levels,) + quarter, bf16),
            jax.ShapeDtypeStruct((levels,) + quarter, bf16),
            jax.ShapeDtypeStruct((levels - 2,) + quarter, bf16),
        ),
        in_specs=[vmem] * 3 + [hbm] * 3,
        out_specs=(hbm,) * 8,
        scratch_shapes=[pltpu.VMEM((tokens, width), bf16)] * 3
        + [
            pltpu.VMEM((4 * tokens, columns), bf16),
            pltpu.VMEM((rows * items, columns), bf16),
            pltpu.VMEM((rows, columns), bf16),
            pltpu.VMEM((1, columns), f32),
            pltpu.VMEM(quarter, f32),
            pltpu.VMEM(quarter, bf16),
            pltpu.VMEM((items, rows, columns), bf16),
            dma((1,)), dma((1,)), dma((chunks,)), dma((chunks,)), dma((chunks,)), dma((chunks,)),
        ]
        + [dma((levels,))] * 12
        + [dma((1,)), dma((levels,)), dma((levels,)), dma((4,)), dma((3,)), dma((4, chunks))],
        compiler_params=pltpu.CompilerParams(vmem_limit_bytes=61 << 20, collective_id=1, has_side_effects=True),
        cost_estimate=pl.CostEstimate(flops=40 * 10**9, bytes_accessed=10**7, transcendentals=0),
        name="head",
    )(x, wq, small, wo, wu, wd)


def gelu_parts(u):
    half = 0.5 * (1.0 + lax.erf(u * 0.7071067811865476))
    return u * half, half + u * jnp.exp(-0.5 * u * u) * 0.3989422804014327


def middle_kernel(
    dims, line_ref, side_ref, fmid_ref, fends_ref, gmid_ref, gends_ref, x_ref, mix0_ref, mix1_ref, mix2_ref, mix3_ref, dout_ref, small_ref,
    out_ref, first_ref, gmix0_ref, gmix1_ref, gmix2_ref, gmix3_ref, ukeep_ref, usend_ref, dkeep_ref, dfar_ref, dsend_ref, sgrad_ref,
    wo_v, wu_v, wd_v, xhat_v, hid_v, act_v, slope_v, ffn_v, gffn_v, gup_v, rstd_v, stage_d, stage_u,
    got_u, got_d, got_o, mixn_v,
    wsem, wsend, wrecv, mix_send, mix_recv, usend, urecv, dsend, drecv, osend, orecv, flush, fsend, frecv,
):
    items, rows, width, tile = dims
    item, place = lax.axis_index("item"), lax.axis_index("seq")
    side, level = item % 2, item // 2
    core, far = place % 2, place // 2
    third = rows // 3
    tokens = x_ref.shape[0]
    tiles = tokens // tile
    near = (item, flip(place, 1))
    barrier = pltpu.get_barrier_semaphore()
    across = (item, flip(place, 2))
    for device in (near, across):
        pl.semaphore_signal(barrier, inc=1, device_id=device, device_id_type=MESH_ID)
    pl.semaphore_wait(barrier, 2)

    def remote(src, dst, send, recv):
        return pltpu.make_async_remote_copy(
            src_ref=src, dst_ref=dst, send_sem=send, recv_sem=recv, device_id=near, device_id_type=MESH_ID
        )

    mix_copy = remote(mix1_ref, mixn_v, mix_send.at[0], mix_recv.at[0])
    mix_copy.start()

    def load(which):
        for t in (0, 2):
            q = flip(place, t)
            for n in range(items):
                z, kx = n // 2, n % 2
                j = 2 * z + (side + kx) % 2
                at = line_place(z)
                if t == 0:
                    src = (line_ref, side_ref)[kx].at[at]
                elif at < items // 2 - 2:
                    src = (fmid_ref, gmid_ref)[kx].at[at]
                else:
                    src = (fends_ref, gends_ref)[kx].at[at - (items // 2 - 2)]
                if which == 0:
                    src = src.at[pl.ds(2 * rows, third)]
                    dst = wo_v.at[j, pl.ds(pl.multiple_of(q * third, 16), third)]
                elif which == 1:
                    src = src.at[pl.ds(0, rows)]
                    dst = wu_v.at[q, pl.ds(pl.multiple_of(j * rows, 16), rows)]
                else:
                    src = src.at[pl.ds(rows, rows)]
                    dst = wd_v.at[j // 2, pl.ds(pl.multiple_of((j % 2) * 4 * rows + q * rows, 16), rows)]
                remote(src, dst, wsend.at[which], wrecv.at[which]).start()
                pltpu.make_async_copy(src, dst, wsem.at[which]).start()

    for which in range(3):
        load(which)

    def loaded(which):
        half = (wo_v.at[pl.ds(0, items // 2)], wu_v.at[pl.ds(0, 2)], wd_v.at[pl.ds(0, 2)])[which]
        pltpu.make_async_copy(half, half, wsem.at[which]).wait()
        remote(half, half, wsend.at[which], wrecv.at[which]).wait_recv()

    def rowsl(r):
        return pl.ds(pl.multiple_of(r * tile, tile), tile)

    def wo_rows(q):
        return jnp.concatenate([wo_v[2 * q, 0:rows], wo_v[2 * q + 1, 0:rows]], 0)

    mixes = (mix0_ref, mixn_v, mix2_ref, mix3_ref)
    gmixes = (gmix0_ref, gmix1_ref, gmix2_ref, gmix3_ref)
    mix_copy.wait_recv()
    loaded(0)

    def norm_one(r, _):
        rs = rowsl(r)
        total = x_ref[rs, :].astype(f32) + small_ref[4:5, :]
        for t in range(4):
            total += jnp.dot(mixes[t][rs, :], wo_rows(flip(place, t)), preferred_element_type=f32)
        centered = total - jnp.mean(total, -1, keepdims=True)
        rstd = lax.rsqrt(jnp.mean(centered * centered, -1, keepdims=True) + norm_epsilon)
        xhat = centered * rstd
        xhat_v[rs, :] = xhat
        rstd_v[rs, :] = jnp.broadcast_to(rstd, (tile, 128))
        hid_v[rs, :] = (xhat * small_ref[0:1, :] + small_ref[1:2, :]).astype(bf16)
        return 0

    lax.fori_loop(0, tiles, norm_one, 0)
    loaded(1)
    loaded(2)

    def ffn(n, _):
        p, r = n // tiles, n % tiles
        rs = rowsl(r)
        up = jnp.dot(hid_v[rs, :], wu_v[p], preferred_element_type=f32) + small_ref[pl.ds(8 + p, 1), :]
        act, slope = gelu_parts(up)
        act = act.astype(bf16)
        act_v[p, rs, :] = act
        slope_v[p, rs, :] = slope
        part = jnp.dot(act, wd_v[p], preferred_element_type=f32)

        @pl.when(p == 0)
        def _():
            ffn_v[rs, :] = part

        @pl.when(p > 0)
        def _():
            ffn_v[rs, :] += part

        return 0

    lax.fori_loop(0, 4 * tiles, ffn, 0)
    zero = jnp.zeros((1, width), f32)

    def norm_two(r, sums):
        rs = rowsl(r)
        dg, db, dd = sums
        hidden = xhat_v[rs, :] * small_ref[0:1, :] + small_ref[1:2, :]
        total = hidden + (ffn_v[rs, :] + small_ref[7:8, :])
        centered = total - jnp.mean(total, -1, keepdims=True)
        rstd = lax.rsqrt(jnp.mean(centered * centered, -1, keepdims=True) + norm_epsilon)
        xhat = centered * rstd
        out_ref[rs, :] = (xhat * small_ref[5:6, :] + small_ref[6:7, :]).astype(bf16)
        dy = dout_ref[rs, :].astype(f32)
        dg = dg + jnp.sum(dy * xhat, 0, keepdims=True)
        db = db + jnp.sum(dy, 0, keepdims=True)
        dx = dy * small_ref[5:6, :]
        dx = rstd * (dx - jnp.mean(dx, -1, keepdims=True) - xhat * jnp.mean(dx * xhat, -1, keepdims=True))
        ffn_v[rs, :] = dx
        short = dx.astype(bf16)
        gffn_v[rs, :] = short
        dd = dd + jnp.sum(short.astype(f32), 0, keepdims=True)
        return dg, db, dd

    dg2, db2, dd = lax.fori_loop(0, tiles, norm_two, (zero, zero, zero))
    sgrad_ref[...] = jnp.zeros_like(sgrad_ref)
    sgrad_ref[1, 2:3, :] = dg2
    sgrad_ref[2, 0:1, :] = db2
    sgrad_ref[2, 1:2, :] = dd
    nt = (((1,), (1,)), ((), ()))
    tn = (((0,), (0,)), ((), ()))
    pieces = width // tile

    def spread(src, yrel, row, count, sem):
        for n in range(items):
            z, kx = n // 2, n % 2
            j = 2 * z + (side + kx) % 2
            dst = (ukeep_ref, usend_ref)[kx].at[yrel, flip(level, z), pl.ds(row, count)]
            pltpu.make_async_copy(src(j), dst, sem).start()

    def chunk_at(n):
        return blend(level, 3 - n)

    def finish_chunk(n, par):
        p = chunk_at(n)
        remote(got_d.at[p], got_d.at[p], dsend.at[p], drecv.at[p]).wait_recv()
        for jj in range(2):
            for yy in range(2):
                at = pl.multiple_of((4 * jj + 2 * yy + core) * rows, 16)
                got_d[p, jj, yy] = stage_d[par, pl.ds(at, rows), :] + got_d[p, jj, yy]

        kz = 3 - n
        for jj in range(2):
            kx = (jj + side) % 2
            for yy in range(2):

                @pl.when(far == yy)
                def _():
                    pltpu.make_async_copy(got_d.at[p, jj, yy], dkeep_ref.at[kz, kx], flush.at[0]).start()

                    @pl.when(n < 2)
                    def _():
                        pltpu.make_async_remote_copy(
                            src_ref=got_d.at[p, jj, 1 - yy], dst_ref=dfar_ref.at[n, kx],
                            send_sem=fsend.at[n], recv_sem=frecv.at[n], device_id=across, device_id_type=MESH_ID,
                        ).start()

                    @pl.when(n >= 2)
                    def _():
                        pltpu.make_async_copy(got_d.at[p, jj, 1 - yy], dsend_ref.at[n - 2, kx], flush.at[3]).start()

        half = p // 2

        @pl.when(p % 2 == core)
        def _():
            remote(got_u.at[half], got_u.at[half], usend.at[half], urecv.at[half]).wait_recv()
            for m in range(tiles):
                ms = slice(m * tile, (m + 1) * tile)
                got_u[half, ms, :] = stage_u[par, ms, :] + got_u[half, ms, :]
            spread(
                lambda j: got_u.at[half, pl.ds(pl.multiple_of(j * rows, 16), rows)],
                (half + far) % 2, 0, rows, flush.at[1],
            )

    def back(n, _):
        par = n % 2
        p = chunk_at(n)

        def back_rows(r, total):
            rs = rowsl(r)
            ga = lax.dot_general(gffn_v[rs, :], wd_v[p], nt, preferred_element_type=f32)
            gup = (ga * slope_v[p, rs, :]).astype(bf16)
            gup_v[rs, :] = gup
            ffn_v[rs, :] += lax.dot_general(gup, wu_v[p], nt, preferred_element_type=f32)
            return total + jnp.sum(gup.astype(f32), 0, keepdims=True)

        sgrad_ref[(8 + p) // 3, pl.ds((8 + p) % 3, 1), :] = lax.fori_loop(0, tiles, back_rows, zero)

        @pl.when(n >= 2)
        def _():
            before = chunk_at(n - 2)
            remote(got_d.at[before], got_d.at[before], dsend.at[before], drecv.at[before]).wait_send()

            @pl.when(p % 2 != core)
            def _():
                half = before // 2
                remote(got_u.at[half], got_u.at[half], usend.at[half], urecv.at[half]).wait_send()

        for m in range(pieces):
            cs = slice(m * tile, (m + 1) * tile)
            stage_d[par, cs, :] = lax.dot_general(act_v[p, :, cs], gffn_v[...], tn, preferred_element_type=f32).astype(bf16)
        for jj in range(2):
            for yy in range(2):
                at = pl.multiple_of((4 * jj + 2 * yy + 1 - core) * rows, 16)
                remote(stage_d.at[par, pl.ds(at, rows)], got_d.at[p, jj, yy], dsend.at[p], drecv.at[p]).start()
        for m in range(pieces):
            cs = slice(m * tile, (m + 1) * tile)
            stage_u[par, cs, :] = lax.dot_general(hid_v[:, cs], gup_v[...], tn, preferred_element_type=f32).astype(bf16)

        @pl.when(p % 2 != core)
        def _():
            remote(stage_u.at[par], got_u.at[p // 2], usend.at[p // 2], urecv.at[p // 2]).start()

        @pl.when(n > 0)
        def _():
            finish_chunk(n - 1, 1 - par)

        return 0

    lax.fori_loop(0, 4, back, 0)
    finish_chunk(3, 1)

    def norm_back(r, sums):
        rs = rowsl(r)
        dg, db, da = sums
        dy = ffn_v[rs, :]
        xhat = xhat_v[rs, :]
        dg = dg + jnp.sum(dy * xhat, 0, keepdims=True)
        db = db + jnp.sum(dy, 0, keepdims=True)
        dx = dy * small_ref[0:1, :]
        dx = rstd_v[rs, 0:1] * (dx - jnp.mean(dx, -1, keepdims=True) - xhat * jnp.mean(dx * xhat, -1, keepdims=True))
        first_ref[rs, :] = dx
        short = dx.astype(bf16)
        hid_v[rs, :] = short
        da = da + jnp.sum(short.astype(f32), 0, keepdims=True)
        for t in range(4):
            gmixes[t][rs, :] = lax.dot_general(
                short, wo_rows(flip(place, t)), nt, preferred_element_type=f32
            ).astype(bf16)
        return dg, db, da

    dg1, db1, da = lax.fori_loop(0, tiles, norm_back, (zero, zero, zero))
    sgrad_ref[0, 0:1, :] = dg1
    sgrad_ref[0, 1:2, :] = db1
    sgrad_ref[1, 1:2, :] = da
    for j in range(items):
        wo_v[j, pl.ds(rows, third)] = jnp.zeros((third, width), bf16)
    for t in range(4):
        q = flip(place, t)
        part = lax.dot_general(mixes[t][...], hid_v[...], tn, preferred_element_type=f32).astype(bf16)
        wo_v[2 * q, pl.ds(0, rows)] = part[:rows]
        wo_v[2 * q + 1, pl.ds(0, rows)] = part[rows:]
    o_copies = []
    for yy in range(2):
        at = pl.multiple_of((2 * yy + 1 - core) * third, 16)
        copy = remote(wo_v.at[:, pl.ds(at, third)], got_o.at[yy], osend.at[yy], orecv.at[yy])
        copy.start()
        o_copies.append(copy)
    for yy in range(2):
        o_copies[yy].wait_recv()
        at = pl.multiple_of((2 * yy + core) * third, 16)
        for j in range(items):
            got_o[yy, j] = wo_v[j, pl.ds(at, third)] + got_o[yy, j]
        spread(lambda j: got_o.at[yy, j], (yy + far) % 2, rows, third, flush.at[2])

    mix_copy.wait_send()
    for which in range(3):
        half = (wo_v.at[pl.ds(0, items // 2)], wu_v.at[pl.ds(0, 2)], wd_v.at[pl.ds(0, 2)])[which]
        remote(half, half, wsend.at[which], wrecv.at[which]).wait_send()
    for n in (2, 3):
        p = chunk_at(n)
        remote(got_d.at[p], got_d.at[p], dsend.at[p], drecv.at[p]).wait_send()

        @pl.when(p % 2 != core)
        def _():
            remote(got_u.at[p // 2], got_u.at[p // 2], usend.at[p // 2], urecv.at[p // 2]).wait_send()

    for yy in range(2):
        o_copies[yy].wait_send()
    pltpu.make_async_copy(dkeep_ref, dkeep_ref, flush.at[0]).wait()
    pltpu.make_async_copy(dsend_ref, dsend_ref, flush.at[3]).wait()
    for n in range(2):
        sent = dfar_ref.at[n]
        copy = pltpu.make_async_remote_copy(
            src_ref=sent, dst_ref=sent, send_sem=fsend.at[n], recv_sem=frecv.at[n],
            device_id=across, device_id_type=MESH_ID,
        )
        copy.wait_send()
        copy.wait_recv()
    pltpu.make_async_copy(got_u, got_u, flush.at[1]).wait()
    pltpu.make_async_copy(got_o, got_o, flush.at[2]).wait()


def middle(weights, x, mixes, dout, small, tile=768):
    levels, quarter, width = weights[0].shape
    items = 2 * levels
    rows = quarter * 3 // 7
    third = rows // 3
    tokens = x.shape[0]
    any_space = pl.BlockSpec(memory_space=pltpu.HBM)
    vmem = pl.BlockSpec(memory_space=pltpu.VMEM)
    square = (tokens, width)
    dma = pltpu.SemaphoreType.DMA
    head_part = jax.ShapeDtypeStruct((tokens, width // 4), bf16)
    u_shape = jax.ShapeDtypeStruct((2, levels, rows + third, width), bf16)
    d_half = jax.ShapeDtypeStruct((2, 2, rows, width), bf16)
    d_shape = jax.ShapeDtypeStruct((levels, 2, rows, width), bf16)
    return pl.pallas_call(
        functools.partial(middle_kernel, (items, rows, width, tile)),
        out_shape=(
            jax.ShapeDtypeStruct(square, bf16),
            jax.ShapeDtypeStruct(square, f32),
            head_part, head_part, head_part, head_part,
            u_shape, u_shape, d_shape, d_half, d_half,
            jax.ShapeDtypeStruct((4, 8, width), f32),
        ),
        in_specs=[any_space] * 6 + [vmem] * 7,
        out_specs=(vmem,) * 6 + (any_space,) * 5 + (vmem,),
        scratch_shapes=[
            pltpu.VMEM((items, 4 * third, width), bf16),
            pltpu.VMEM((4, width, width), bf16),
            pltpu.VMEM((4, width, width), bf16),
            pltpu.VMEM(square, f32),
            pltpu.VMEM(square, bf16),
            pltpu.VMEM((4, tokens, width), bf16),
            pltpu.VMEM((4, tokens, width), f32),
            pltpu.VMEM(square, f32),
            pltpu.VMEM(square, bf16),
            pltpu.VMEM(square, bf16),
            pltpu.VMEM((tokens, 128), f32),
            pltpu.VMEM((2, width, width), bf16),
            pltpu.VMEM((2, width, width), bf16),
            pltpu.VMEM((2, width, width), bf16),
            pltpu.VMEM((4, 2, 2, rows, width), bf16),
            pltpu.VMEM((2, items, third, width), bf16),
            pltpu.VMEM((tokens, width // 4), bf16),
            dma((3,)), dma((3,)), dma((3,)), dma((1,)), dma((1,)), dma((2,)), dma((2,)), dma((4,)), dma((4,)),
            dma((2,)), dma((2,)), dma((4,)), dma((2,)), dma((2,)),
        ],
        compiler_params=pltpu.CompilerParams(vmem_limit_bytes=61 << 20, collective_id=2, has_side_effects=True),
        cost_estimate=pl.CostEstimate(flops=60 * 10**9, bytes_accessed=10**7, transcendentals=0),
        name="middle",
    )(*weights, x, *mixes, dout, small)


def swap(values, axis, bit):
    size = lax.axis_size(axis)
    return lax.ppermute(values, axis, [(i, i ^ bit) for i in range(size)])


def take(values, at, dim):
    return lax.dynamic_index_in_dim(values, at, dim, keepdims=False)


def add_short(a, b):
    return (a.astype(f32) + b.astype(f32)).astype(bf16)


def layer_norm(values, gain, bias):
    average = jnp.mean(values, -1, keepdims=True)
    centered = values - average
    spread = jnp.mean(centered * centered, -1, keepdims=True)
    return centered * lax.rsqrt(spread + norm_epsilon) * gain + bias


def exact_gelu(values):
    return jax.nn.gelu(values, approximate=False)


def packed_columns(own):
    heads = own.shape[2]
    cols = []
    for h in range(heads):
        pair = [own[:, 2, h], own[:, 1, h]]
        cols += pair if h % 2 == 0 else pair[::-1]
    for p in range((heads + 1) // 2):
        odd = own[:, 0, 2 * p + 1] if 2 * p + 1 < heads else jnp.zeros_like(own[:, 0, 0])
        cols += [odd * HD**-0.5, own[:, 0, 2 * p] * HD**-0.5]
    return jnp.concatenate(cols, -1)


def natural_columns(values, heads):
    parts = [[], [], []]
    for h in range(heads):
        first, second = values[:, h * 128 : h * 128 + HD], values[:, h * 128 + HD : h * 128 + 128]
        base = (heads + h // 2) * 128
        if h % 2 == 0:
            parts[2].append(first)
            parts[1].append(second)
            parts[0].append(values[:, base + HD : base + 128] * HD**-0.5)
        else:
            parts[1].append(first)
            parts[2].append(second)
            parts[0].append(values[:, base : base + HD] * HD**-0.5)
    return jnp.concatenate(parts[0] + parts[1] + parts[2], -1)


def on_device(
    inputs,
    d_output,
    glob_count,
    glob_pos,
    rand_blocks,
    w_qkv,
    w_out,
    w_up,
    w_down,
    small_params,
    first_qkv,
    second_qkv,
    first_out,
    second_out,
    first_up,
    second_up,
    first_down,
    second_down,
    first_small,
    second_small,
):
    _, tok_rows, width = inputs.shape
    items = lax.axis_size("item")
    place = lax.axis_index("seq")
    heads = rand_blocks.shape[1]

    tokens_b = inputs.reshape(tok_rows, width)
    *others, qkv, slab, w_line, w_side, w_far = head(
        tokens_b, w_qkv, small_params, w_out, w_up, w_down, items, heads
    )
    xs = [tokens_b, *others]
    w_far_ends = swap(w_line[2:], "seq", 2)
    w_side_mid = swap(w_far, "item", 1)
    idx, bias, gl = slots(glob_count[0], glob_pos[0], rand_blocks[0], place)
    mix2, mix3, lse_far = attn_fwd(idx, gl, qkv, bias, heads, 2, 2)
    w_far_ends, w_side_mid, mix2, mix3, qkv = lax.optimization_barrier((w_far_ends, w_side_mid, mix2, mix3, qkv))
    mix2_in, mix3_in = swap(mix2, "seq", 2), swap(mix3, "seq", 3)
    w_side_ends = swap(w_far_ends, "item", 1)
    mix0, mix1, lse_near = attn_fwd(idx, gl, qkv, bias, heads, 0, 2)
    w_side_ends, mix0, mix1, mix2_in, mix3_in = lax.optimization_barrier((w_side_ends, mix0, mix1, mix2_in, mix3_in))
    outputs, grad_first, *grad_mixed, u_keep, u_send, d_keep, d_far, d_send, small_part = middle(
        (w_line, w_side, w_far, w_far_ends, w_side_mid, w_side_ends), tokens_b, (mix0, mix1, mix2_in, mix3_in), d_output.reshape(tok_rows, width), small_params
    )
    grads_in = [grad_mixed[0]] + [swap(grad_mixed[t], "seq", t) for t in range(1, 4)]
    u_in = swap(u_send, "item", 1)
    d_in = swap(d_send, "seq", 2)
    d_next = [swap(add_short(d_keep[3 - n], d_far[n]), "item", 2 * (3 - n)) for n in range(2)]
    acc, dq_near = attn_bwd(idx, gl, qkv, bias, grads_in[:2], lse_near, heads, 0, (), False)
    u_in, d_in, d_next, acc, dq_near = lax.optimization_barrier((u_in, d_in, d_next, acc, dq_near))
    u_next = swap(add_short(u_keep[1], u_in[1]), "seq", 2)
    d_last = swap(add_short(d_keep[1], d_in[0]), "item", 2)
    u_here = add_short(u_keep[0], u_in[0])
    d_here = add_short(d_keep[0], d_in[1])
    grad_qkv = attn_bwd(idx, gl, qkv, bias, grads_in[2:], lse_far, heads, 2, (acc, dq_near), True)
    d_last, u_next, grad_qkv = lax.optimization_barrier((d_last, u_next, grad_qkv))
    grad_inputs, group, slab_group, small_total, squares = tail(
        xs, grad_qkv, slab, grad_first, small_part, (u_here, u_next, d_here, d_last, *d_next), items, heads * 128
    )
    norm, outputs, grad_inputs, *states = update(
        lambda: lax.axis_index("seq"),
        heads,
        group,
        slab_group,
        small_total,
        squares,
        (outputs, grad_inputs),
        (
            w_qkv, first_qkv, second_qkv, w_out, first_out, second_out, w_up, first_up, second_up,
            w_down, first_down, second_down, small_params, first_small, second_small,
        ),
    )
    return (outputs[None], grad_inputs[None], norm.reshape(()), *states)


def on_device_many(
    inputs,
    d_output,
    glob_count,
    glob_pos,
    rand_blocks,
    w_qkv,
    w_out,
    w_up,
    w_down,
    small_params,
    first_qkv,
    second_qkv,
    first_out,
    second_out,
    first_up,
    second_up,
    first_down,
    second_down,
    first_small,
    second_small,
):
    items_n, tok_rows, width = inputs.shape
    groups = lax.axis_size("seq")
    place = lax.axis_index("seq")
    heads = rand_blocks.shape[1]
    row_count = tok_rows

    own = lax.dynamic_index_in_dim(
        w_qkv.reshape(-1, 3, groups, heads, HD), place, 2, keepdims=False
    )
    slab = lax.all_gather(packed_columns(own).astype(bf16), "item", axis=0, tiled=True)
    full_out, full_up, full_down = (
        lax.all_gather(w_out.astype(bf16), "item", axis=0, tiled=True),
        lax.all_gather(w_up.astype(bf16), "item", axis=0, tiled=True),
        lax.all_gather(w_down.astype(bf16), "item", axis=0, tiled=True),
    )
    bias3 = jnp.stack([small_params[2], jnp.zeros((width,), f32), small_params[3]])
    own_bias = lax.dynamic_index_in_dim(
        bias3.reshape(1, 3, groups, heads, HD), place, 2, keepdims=False
    )
    slab_bias = packed_columns(own_bias)
    tokens_b = inputs.reshape(tok_rows, width)
    tokens_all = lax.all_gather(tokens_b, "seq", axis=0, tiled=True)
    tokens_f = tokens_b.astype(f32)
    qkv = (jnp.dot(tokens_all, slab, preferred_element_type=f32) + slab_bias).astype(bf16)
    idx, bias, gl = slots(glob_count[0], glob_pos[0], rand_blocks[0], jnp.int32(0))
    *mixed_parts, lse = attn_fwd(idx, gl, qkv, bias, heads, 0, 4)
    mixed_heads = jnp.concatenate(mixed_parts, 0)
    mixed = lax.all_to_all(mixed_heads, "seq", split_axis=0, concat_axis=1, tiled=True)
    attn_out = jnp.dot(mixed, full_out, preferred_element_type=f32) + small_params[4]
    hidden, norm_one_back = jax.vjp(
        layer_norm, tokens_f + attn_out, small_params[0], small_params[1]
    )
    hidden_b = hidden.astype(bf16)
    up_pre = jnp.dot(hidden_b, full_up, preferred_element_type=f32) + small_params[8:12].reshape(-1)
    active, gelu_back = jax.vjp(exact_gelu, up_pre)
    active_b = active.astype(bf16)
    ffn_out = jnp.dot(active_b, full_down, preferred_element_type=f32) + small_params[7]
    outputs, norm_two_back = jax.vjp(layer_norm, hidden + ffn_out, small_params[5], small_params[6])
    grad_second, grad_gain_two, grad_bias_two = norm_two_back(
        d_output.reshape(row_count, width).astype(f32)
    )
    grad_ffn = grad_second.astype(bf16)
    grad_w_down = jnp.einsum("rf,rd->fd", active_b, grad_ffn, preferred_element_type=f32)
    grad_active = jnp.einsum("rd,fd->rf", grad_ffn, full_down, preferred_element_type=f32)
    (grad_up_pre,) = gelu_back(grad_active)
    grad_up_b = grad_up_pre.astype(bf16)
    grad_w_up = jnp.einsum("rd,rf->df", hidden_b, grad_up_b, preferred_element_type=f32)
    grad_hidden = grad_second + jnp.einsum(
        "rf,df->rd", grad_up_b, full_up, preferred_element_type=f32
    )
    grad_first, grad_gain_one, grad_bias_one = norm_one_back(grad_hidden)
    grad_attn = grad_first.astype(bf16)
    grad_w_out = jnp.einsum("rm,rd->md", mixed, grad_attn, preferred_element_type=f32)
    grad_mixed = jnp.einsum("rd,md->rm", grad_attn, full_out, preferred_element_type=f32).astype(
        bf16
    )
    grad_heads = lax.all_to_all(grad_mixed, "seq", split_axis=1, concat_axis=0, tiled=True)
    grads_in = [grad_heads[t * tok_rows : (t + 1) * tok_rows] for t in range(4)]
    grad_qkv = attn_bwd(idx, gl, qkv, bias, grads_in, lse, heads, 0, (), True)
    grad_slab = jnp.einsum("rd,re->de", tokens_all, grad_qkv, preferred_element_type=f32)
    grad_tokens = jnp.einsum("re,de->rd", grad_qkv, slab, preferred_element_type=f32).astype(bf16)
    grad_inputs = grad_first + lax.psum_scatter(
        grad_tokens, "seq", scatter_dimension=0, tiled=True
    ).astype(f32)
    slab_sum = natural_columns(jnp.sum(grad_qkv.astype(f32), 0)[None], heads)[0]
    bias_grads = lax.dynamic_update_index_in_dim(
        jnp.zeros((3, groups, heads * HD), f32), slab_sum.reshape(3, heads * HD), place, 1
    ).reshape(3, width)
    small_rows = jnp.stack(
        [
            grad_gain_one,
            grad_bias_one,
            bias_grads[0],
            bias_grads[2],
            jnp.sum(grad_attn.astype(f32), 0),
            grad_gain_two,
            grad_bias_two,
            jnp.sum(grad_ffn.astype(f32), 0),
        ]
    )
    small_part = jnp.concatenate(
        [small_rows, jnp.sum(grad_up_b.astype(f32), 0).reshape(4, width)], 0
    )
    small_total = lax.psum(small_part, ("item", "seq"))
    shard_down = lax.psum_scatter(grad_w_down.astype(bf16), "item", scatter_dimension=0, tiled=True)
    shard_up = lax.psum_scatter(grad_w_up.astype(bf16), "item", scatter_dimension=0, tiled=True)
    shard_out = lax.psum_scatter(grad_w_out.astype(bf16), "item", scatter_dimension=0, tiled=True)
    shard_slab = lax.psum_scatter(grad_slab.astype(bf16), "item", scatter_dimension=0, tiled=True)
    shard_slab = natural_columns(shard_slab.astype(f32), heads).reshape(-1, 3, 1, heads * HD)
    shard_qkv = lax.all_gather(shard_slab, "seq", axis=2, tiled=True).reshape(-1, 3 * width)
    shard_out, shard_up, shard_down = lax.psum(
        (shard_out.astype(f32), shard_up.astype(f32), shard_down.astype(f32)), "seq"
    )
    local_squares = (
        jnp.sum(shard_qkv * shard_qkv)
        + jnp.sum(shard_out * shard_out)
        + jnp.sum(shard_up * shard_up)
        + jnp.sum(shard_down * shard_down)
    )
    matrix_squares = lax.psum(local_squares, "item")
    grad_norm = jnp.sqrt(matrix_squares + jnp.sum(small_total * small_total))
    factor = jnp.minimum(1.0, clip_level / (grad_norm + 1e-06))
    new_qkv = adam_update(
        w_qkv, first_qkv, second_qkv, shard_qkv * factor, weight_decay, learn_rate
    )
    new_out = adam_update(
        w_out, first_out, second_out, shard_out * factor, weight_decay, learn_rate
    )
    new_up = adam_update(w_up, first_up, second_up, shard_up * factor, weight_decay, learn_rate)
    new_down = adam_update(
        w_down, first_down, second_down, shard_down * factor, weight_decay, learn_rate
    )
    new_small = adam_update(
        small_params, first_small, second_small, small_total * factor, 0.0, small_rate
    )
    return (
        outputs.astype(bf16).reshape(items_n, tok_rows, width),
        grad_inputs.reshape(items_n, tok_rows, width),
        grad_norm,
        new_qkv[0],
        new_qkv[1],
        new_qkv[2],
        new_out[0],
        new_out[1],
        new_out[2],
        new_up[0],
        new_up[1],
        new_up[2],
        new_down[0],
        new_down[1],
        new_down[2],
        new_small[0],
        new_small[1],
        new_small[2],
    )


def solution(mesh):
    few = mesh.shape["item"] == 8 and mesh.shape["seq"] == 4
    return jax.shard_map(
        on_device if few else on_device_many,
        mesh=mesh,
        in_specs=(
            P("item", "seq", None),
            P("item", "seq", None),
            P("item"),
            P("item", None),
            P("item", "seq", None, None),
            P("item", None),
            P("item", None),
            P("item", None),
            P("item", None),
            P(),
            P("item", None),
            P("item", None),
            P("item", None),
            P("item", None),
            P("item", None),
            P("item", None),
            P("item", None),
            P("item", None),
            P(),
            P(),
        ),
        out_specs=(
            P("item", "seq", None),
            P("item", "seq", None),
            P(),
            P("item", None),
            P("item", None),
            P("item", None),
            P("item", None),
            P("item", None),
            P("item", None),
            P("item", None),
            P("item", None),
            P("item", None),
            P("item", None),
            P("item", None),
            P("item", None),
            P(),
            P(),
            P(),
        ),
        check_vma=False,
    )
```

```python
import functools

import jax
import jax.numpy as jnp
from jax import lax
from jax.experimental import pallas as pl
from jax.experimental.pallas import tpu as pltpu
from jax.sharding import PartitionSpec as P

ADAM_STEP = 10
norm_epsilon = 1e-06
beta_first = 0.9
beta_second = 0.999
adam_epsilon = 1e-08
learn_rate = 0.1
small_rate = 0.5
weight_decay = 0.01
clip_level = 1.0


def adam_update(weight, first, second, grad, decay, rate):
    first_new = beta_first * first + (1.0 - beta_first) * grad
    second_new = beta_second * second + (1.0 - beta_second) * grad * grad
    first_hat = first_new / (1.0 - beta_first**ADAM_STEP)
    second_hat = second_new / (1.0 - beta_second**ADAM_STEP)
    weight_new = weight - rate * (
        first_hat / (jnp.sqrt(second_hat) + adam_epsilon) + decay * weight
    )
    return (weight_new, first_new, second_new)


HD = 64
BL = 64
NEG = -1e30
bf16 = jnp.bfloat16
f32 = jnp.float32
NT = (((1,), (1,)), ((), ()))
TN = (((0,), (0,)), ((), ()))


def slots(count, positions, table, place):
    heads, nblocks, picks = table.shape
    chunk = nblocks // 4
    globals_n = positions.shape[0]
    here = jnp.arange(nblocks, dtype=jnp.int32)

    def turned(b):
        return ((b // chunk) ^ place) * chunk + b % chunk

    block = turned(here)
    rows = table.reshape(heads, 2, 2, chunk, picks)
    rows = jnp.where(place % 2 == 1, rows[:, :, ::-1], rows)
    rows = jnp.where(place // 2 == 1, rows[:, ::-1], rows).reshape(heads, nblocks, picks)
    window = jnp.stack([block - 1, block, block + 1], -1)
    active = jnp.arange(globals_n, dtype=jnp.int32) < count
    parts = jnp.concatenate(
        [
            jnp.broadcast_to(window[None], (heads, nblocks, 3)),
            jnp.broadcast_to(jnp.where(active, positions, -1)[None, None], (heads, nblocks, globals_n)),
            rows,
        ],
        -1,
    )
    count_slots = 3 + globals_n + picks
    valid = (parts >= 0) & (parts < nblocks)
    same = parts[..., :, None] == parts[..., None, :]
    earlier = jnp.arange(count_slots)[:, None] > jnp.arange(count_slots)[None, :]
    repeated = jnp.any(same & earlier, -1)
    is_global = jnp.any((positions[None, :] == block[:, None]) & active[None], -1)
    valid = valid & ~repeated & ~is_global[None, :, None]
    idx = turned(jnp.clip(parts, 0, nblocks - 1))
    bias = jnp.where(valid, 0.0, NEG).astype(f32)
    bias = jnp.broadcast_to(bias[..., None], (heads, nblocks, count_slots, BL))
    glob = jnp.concatenate([count[None], turned(positions)])
    return idx.reshape(-1), bias.reshape(heads * nblocks, count_slots * BL), glob


def low_lanes(rows):
    return lax.broadcasted_iota(jnp.int32, (rows, 2 * HD), 1) < HD


def pick(block, keep_low):
    low = low_lanes(block.shape[0])
    return jnp.where(low if keep_low else ~low, block, jnp.zeros_like(block))


def fwd_kernel(dims, idx_ref, gl_ref, qkv_ref, bias_ref, *rest):
    heads, nblocks, slots_n, first, parts, chunk, wide = dims
    out_refs, lse_ref, sbuf, s_v, e_v, l_v, out_v = rest[:parts], rest[parts], *rest[parts + 1 :]
    n = nblocks * BL
    lane = lax.broadcasted_iota(jnp.int32, (BL, 128), 1)

    def finish(row, outs, lses):
        low = low_lanes(BL)
        for p in range((heads + 1) // 2):
            if 2 * p + 1 < heads:
                both = jnp.where(low, outs[2 * p], outs[2 * p + 1])
                out_v[pl.ds(row, BL), p * 128 : (p + 1) * 128] = both.astype(bf16)
            else:
                out_v[pl.ds(row, BL), p * 128 : p * 128 + HD] = outs[2 * p][:, :HD].astype(bf16)
        total = jnp.zeros((BL, 128), f32)
        for h in range(heads):
            total = jnp.where(lane == h, lses[h], total)
        lse_ref[pl.ds(row, BL), :] = total

    def queries(r, h):
        return pick(qkv_ref[pl.ds(r, BL), (heads + h // 2) * 128 : (heads + h // 2 + 1) * 128], h % 2 == 1)

    blocks = parts * chunk

    def clamp(b):
        return jnp.minimum(jnp.maximum(b, 0), blocks - 1)

    def gathered(a, h):
        base = (h * nblocks + a) * slots_n
        return jnp.concatenate(
            [
                qkv_ref[pl.ds(pl.multiple_of(idx_ref[base + j] * BL, BL), BL), h * 128 : (h + 1) * 128]
                for j in range(slots_n)
            ],
            0,
        )

    def body(b, _):
        last, now, new = clamp(b - 2), clamp(b - 1), clamp(b)
        outs, lses = [], []
        for h in range(heads):
            o = jnp.dot(e_v[h], gathered(first + last, h), preferred_element_type=f32)
            outs.append(o)
            lses.append(l_v[h])
        finish(pl.multiple_of(last * BL, BL), outs, lses)
        for h in range(heads):
            s = s_v[h] + bias_ref[pl.ds(h * nblocks + first + now, 1), :]
            m = jnp.max(s, -1, keepdims=True)
            e = jnp.exp(s - m)
            l = jnp.sum(e, -1, keepdims=True)
            e_v[h] = (e * (1.0 / l)).astype(bf16)
            l_v[h] = jnp.broadcast_to(m + jnp.log(l), (BL, 128))
        for h in range(heads):
            a = first + new
            s_v[h] = lax.dot_general(
                queries(pl.multiple_of(a * BL, BL), h), gathered(a, h), NT, preferred_element_type=f32
            )
        return 0

    lax.fori_loop(0, blocks + 2, body, 0, unroll=2)

    def whole_row(g, _):
        a = gl_ref[1 + g]
        local = a - first

        @pl.when((local >= 0) & (local < parts * chunk))
        def _():
            r = pl.multiple_of(a * BL, BL)
            outs, lses = [], []
            for h in range(heads):
                q = queries(r, h)
                m = None
                for c in range(n // wide):
                    cs = slice(c * wide, (c + 1) * wide)
                    s = lax.dot_general(q, qkv_ref[cs, h * 128 : (h + 1) * 128], NT, preferred_element_type=f32)
                    sbuf[h, :, cs] = s
                    mc = jnp.max(s, -1, keepdims=True)
                    m = mc if m is None else jnp.maximum(m, mc)
                l = 0.0
                for c in range(n // wide):
                    cs = slice(c * wide, (c + 1) * wide)
                    e = jnp.exp(sbuf[h, :, cs] - m)
                    sbuf[h, :, cs] = e
                    l = l + jnp.sum(e, -1, keepdims=True)
                inv = 1.0 / l
                o = 0.0
                for c in range(n // wide):
                    cs = slice(c * wide, (c + 1) * wide)
                    p = (sbuf[h, :, cs] * inv).astype(bf16)
                    o = o + jnp.dot(p, qkv_ref[cs, h * 128 : (h + 1) * 128], preferred_element_type=f32)
                outs.append(o)
                lses.append(m + jnp.log(l))
            finish(pl.multiple_of(local * BL, BL), outs, lses)

        return 0

    lax.fori_loop(0, gl_ref[0], whole_row, 0)
    for part in range(parts):
        out_refs[part][...] = out_v[part * chunk * BL : (part + 1) * chunk * BL, :]


def attn_fwd(idx, gl, qkv, bias, heads, first_part, parts):
    n = qkv.shape[0]
    nblocks = n // BL
    chunk = nblocks // 4
    slots_n = bias.shape[1] // BL
    vmem = pl.BlockSpec(memory_space=pltpu.VMEM)
    smem = pl.BlockSpec(memory_space=pltpu.SMEM)
    dims = (heads, nblocks, slots_n, first_part * chunk, parts, chunk, 512)
    return pl.pallas_call(
        functools.partial(fwd_kernel, dims),
        out_shape=tuple([jax.ShapeDtypeStruct((n // 4, heads * HD), bf16)] * parts)
        + (jax.ShapeDtypeStruct((parts * n // 4, 128), f32),),
        in_specs=[smem, smem, vmem, vmem],
        out_specs=tuple([vmem] * (parts + 1)),
        scratch_shapes=[
            pltpu.VMEM((heads, BL, n), f32),
            pltpu.VMEM((heads, BL, slots_n * BL), f32),
            pltpu.VMEM((heads, BL, slots_n * BL), bf16),
            pltpu.VMEM((heads, BL, 128), f32),
            pltpu.VMEM((parts * n // 4, heads * HD), bf16),
        ],
        compiler_params=pltpu.CompilerParams(vmem_limit_bytes=24 << 20),
        cost_estimate=pl.CostEstimate(flops=10 * parts * 10**9, bytes_accessed=10**7, transcendentals=0),
        name="attn_fwd",
    )(idx, gl, qkv, bias)


def bwd_kernel(dims, idx_ref, gl_ref, qkv_ref, bias_ref, *rest):
    heads, nblocks, slots_n, first, parts, chunk, wide, begin, end = dims
    g_refs, rest = rest[:parts], rest[parts:]
    lse_ref, rest = rest[0], rest[1:]
    if not begin:
        acc_in, dq_in, rest = rest[0], rest[1], rest[2:]
    if end:
        out_ref, acc, pbuf, dbuf, sd_v, w_v, g_v = rest
    else:
        acc, dq_ref, pbuf, dbuf, sd_v, w_v, g_v = rest
    n = nblocks * BL
    pairs = (heads + 1) // 2
    kvw = heads * 128

    def start(i, _):
        rr = pl.ds(pl.multiple_of(i * 256, 256), 256)
        if begin:
            acc[rr, :] = jnp.zeros((256, kvw), f32)
        else:
            acc[rr, :] = acc_in[rr, :]
        return 0

    lax.fori_loop(0, n // 256, start, 0)
    if end and not begin:
        out_ref[0 : first * BL, kvw:] = dq_in[...]

    for part in range(parts):
        g_v[part * chunk * BL : (part + 1) * chunk * BL, :] = g_refs[part][...]

    def grads(at, h):
        w = min(128, heads * HD - (h // 2) * 128)
        g = g_v[pl.ds(at, BL), (h // 2) * 128 : (h // 2) * 128 + w]
        if w < 128:
            return jnp.concatenate([g, jnp.zeros((BL, 128 - w), bf16)], 1)
        return pick(g, h % 2 == 0)

    def queries(r, h):
        return pick(qkv_ref[pl.ds(r, BL), (heads + h // 2) * 128 : (heads + h // 2 + 1) * 128], h % 2 == 1)

    def finish(r, dqs):
        low = low_lanes(BL)
        for p in range(pairs):
            high = dqs[2 * p]
            odd = dqs[2 * p + 1] if 2 * p + 1 < heads else jnp.zeros_like(high)
            both = jnp.where(low, odd, high).astype(bf16)
            if end:
                out_ref[pl.ds(r, BL), kvw + p * 128 : kvw + (p + 1) * 128] = both
            else:
                dq_ref[pl.ds(pl.multiple_of(r - first * BL, BL), BL), p * 128 : (p + 1) * 128] = both

    blocks = parts * chunk

    def clamp(b):
        return jnp.minimum(jnp.maximum(b, 0), blocks - 1)

    def slot_rows(a, h):
        base = (h * nblocks + a) * slots_n
        return [pl.multiple_of(idx_ref[base + j] * BL, BL) for j in range(slots_n)]

    def stacked(b, h):
        r = pl.multiple_of((first + b) * BL, BL)
        return jnp.concatenate([queries(r, h), grads(pl.multiple_of(b * BL, BL), h)], 0)

    def body(b, _):
        last, now, new = clamp(b - 2), clamp(b - 1), clamp(b)
        dqs = []
        for h in range(heads):
            hs = slice(h * 128, (h + 1) * 128)
            rows = slot_rows(first + last, h)
            kv = jnp.concatenate([qkv_ref[pl.ds(rows[j], BL), hs] for j in range(slots_n)], 0)
            dqs.append(jnp.dot(w_v[h, :BL], kv, preferred_element_type=f32))
            dkv = lax.dot_general(w_v[h], stacked(last, h), TN, preferred_element_type=f32)
            dkv = jnp.where(b >= 2, dkv, 0.0)
            for j in range(slots_n):
                acc[pl.ds(rows[j], BL), hs] += dkv[j * BL : (j + 1) * BL]
        finish(pl.multiple_of((first + last) * BL, BL), dqs)
        for h in range(heads):
            sd = sd_v[h]
            row = pl.multiple_of(now * BL, BL)
            p = jnp.exp(
                sd[:BL] + bias_ref[pl.ds(h * nblocks + first + now, 1), :] - lse_ref[pl.ds(row, BL), h : h + 1]
            )
            dp = sd[BL:]
            ds = p * (dp - jnp.sum(dp * p, -1, keepdims=True))
            w_v[h, :BL] = ds.astype(bf16)
            w_v[h, BL:] = p.astype(bf16)
        for h in range(heads):
            rows = slot_rows(first + new, h)
            kv = jnp.concatenate(
                [qkv_ref[pl.ds(rows[j], BL), h * 128 : (h + 1) * 128] for j in range(slots_n)], 0
            )
            sd_v[h] = lax.dot_general(stacked(new, h), kv, NT, preferred_element_type=f32)
        return 0

    sd_v[...] = jnp.zeros_like(sd_v)
    w_v[...] = jnp.zeros_like(w_v)
    lax.fori_loop(0, blocks + 2, body, 0)

    def whole_row(g, _):
        a = gl_ref[1 + g]
        local = a - first

        @pl.when((local >= 0) & (local < parts * chunk))
        def _():
            r = pl.multiple_of(a * BL, BL)
            row = pl.multiple_of(local * BL, BL)
            dqs = []
            for h in range(heads):
                hs = slice(h * 128, (h + 1) * 128)
                x = jnp.concatenate([queries(r, h), grads(row, h)], 0)
                lse = lse_ref[pl.ds(row, BL), h : h + 1]
                inner = 0.0
                for c in range(n // wide):
                    cs = slice(c * wide, (c + 1) * wide)
                    sd = lax.dot_general(x, qkv_ref[cs, hs], NT, preferred_element_type=f32)
                    p = jnp.exp(sd[:BL] - lse)
                    dp = sd[BL:]
                    pbuf[h, :, cs] = p
                    dbuf[h, :, cs] = dp
                    inner = inner + jnp.sum(dp * p, -1, keepdims=True)
                dq = 0.0
                for c in range(n // wide):
                    cs = slice(c * wide, (c + 1) * wide)
                    p = pbuf[h, :, cs]
                    ds = (p * (dbuf[h, :, cs] - inner)).astype(bf16)
                    w = jnp.concatenate([ds, p.astype(bf16)], 0)
                    dq = dq + jnp.dot(ds, qkv_ref[cs, hs], preferred_element_type=f32)
                    acc[cs, hs] += lax.dot_general(w, x, TN, preferred_element_type=f32)
                dqs.append(dq)
            finish(r, dqs)

        return 0

    lax.fori_loop(0, gl_ref[0], whole_row, 0)
    if end:

        def flush(i, _):
            rr = pl.ds(pl.multiple_of(i * 256, 256), 256)
            out_ref[rr, :kvw] = acc[rr, :].astype(bf16)
            return 0

        lax.fori_loop(0, n // 256, flush, 0)


def attn_bwd(idx, gl, qkv, bias, grads, lse, heads, first_part, carried, end):
    n = qkv.shape[0]
    nblocks = n // BL
    chunk = nblocks // 4
    slots_n = bias.shape[1] // BL
    parts = len(grads)
    vmem = pl.BlockSpec(memory_space=pltpu.VMEM)
    smem = pl.BlockSpec(memory_space=pltpu.SMEM)
    dims = (heads, nblocks, slots_n, first_part * chunk, parts, chunk, 512, not carried, end)
    pairs = (heads + 1) // 2
    scratch = [pltpu.VMEM((heads, BL, n), f32)] * 2 + [
        pltpu.VMEM((heads, 2 * BL, slots_n * BL), f32),
        pltpu.VMEM((heads, 2 * BL, slots_n * BL), bf16),
        pltpu.VMEM((parts * n // 4, heads * HD), bf16),
    ]
    if end:
        out_shape = jax.ShapeDtypeStruct((n, (heads + pairs) * 128), bf16)
        out_specs = vmem
        scratch = [pltpu.VMEM((n, heads * 128), f32)] + scratch
    else:
        out_shape = (
            jax.ShapeDtypeStruct((n, heads * 128), f32),
            jax.ShapeDtypeStruct((parts * n // 4, pairs * 128), bf16),
        )
        out_specs = (vmem, vmem)
    return pl.pallas_call(
        functools.partial(bwd_kernel, dims),
        out_shape=out_shape,
        in_specs=[smem, smem] + [vmem] * (3 + parts + len(carried)),
        out_specs=out_specs,
        scratch_shapes=scratch,
        compiler_params=pltpu.CompilerParams(vmem_limit_bytes=36 << 20),
        cost_estimate=pl.CostEstimate(flops=11 * parts * 10**9, bytes_accessed=10**7, transcendentals=0),
        name="attn_bwd",
    )(idx, gl, qkv, bias, *grads, lse, *carried)


MESH_ID = pl.DeviceIdType.MESH


def flip(index, number):
    total = 0
    for bit in (1, 2, 4):
        digit = (index // bit) % 2
        total = total + bit * ((1 - digit) if number & bit else digit)
    return total


def blend(a, b):
    return sum(bit * (((a // bit) % 2 + (b // bit) % 2) % 2) for bit in (1, 2, 4))


def greet(item, place, items):
    barrier = pltpu.get_barrier_semaphore()
    for t in range(1, 4):
        pl.semaphore_signal(barrier, inc=1, device_id=(item, flip(place, t)), device_id_type=MESH_ID)
    for k in range(1, items):
        pl.semaphore_signal(barrier, inc=1, device_id=(flip(item, k), place), device_id_type=MESH_ID)
    pl.semaphore_wait(barrier, 3 + items - 1)


def tail_kernel(
    items, query_columns, x0, x1, x2, x3, gq_ref, slab_ref, first_ref, small_ref, uk_ref, ur_ref, dk_ref, d1_ref, d2_ref, d3_ref,
    din_ref, group_ref, sgroup_ref, total_ref, squares_ref,
    near_out, near_in, far_out, far_in, grad_v, side_out, side_in, part_out, part_in, z_out, z_in, d_out, d_in, small_in, small_mid, small_side, small_both, small_items, small_sum, sq_out, sq_in, sq_mid, sq_items,
    near_send, near_recv, far_send, far_recv, side_send, side_recv, part_send, part_recv, z_send, z_recv, d_send, d_recv, sg_send, sg_recv, sx_send, sx_recv, si_send, si_recv, st_send, st_recv,
    gr_send, gr_recv, sl_send, sl_recv, qg_send, qg_recv, qi_send, qi_recv,
):
    xs = (x0, x1, x2, x3)
    item, place = lax.axis_index("item"), lax.axis_index("seq")
    tokens, width = x0.shape
    rows = width // items
    tile = tokens // 2
    chunks = tokens // tile
    columns = gq_ref.shape[1]
    levels = items // 2
    up_rows = uk_ref.shape[1]
    greet(item, place, items)

    def to_group(src, dst, send, recv, t):
        return pltpu.make_async_remote_copy(
            src_ref=src, dst_ref=dst, send_sem=send, recv_sem=recv,
            device_id=(item, flip(place, t)), device_id_type=MESH_ID,
        )

    def to_item(src, dst, send, recv, k):
        return pltpu.make_async_remote_copy(
            src_ref=src, dst_ref=dst, send_sem=send, recv_sem=recv,
            device_id=(flip(item, k), place), device_id_type=MESH_ID,
        )

    small_copies = [
        to_group(small_ref.at[flip(place, t)], small_in.at[t], sg_send.at[t], sg_recv.at[t], t) for t in range(1, 4)
    ]
    for copy in small_copies:
        copy.start()

    z_copies = []
    for kz in range(levels - 1, 0, -1):
        z_out[kz] = uk_ref[kz] + ur_ref[kz]
        copy = to_item(z_out.at[kz], z_in.at[kz], z_send.at[kz], z_recv.at[kz], 2 * kz)
        copy.start()
        z_copies.append(copy)

    def down_sum(kx):
        return (
            dk_ref[kx].astype(f32) + d1_ref[kx].astype(f32) + d2_ref[kx].astype(f32) + d3_ref[kx].astype(f32)
        )

    d_out[...] = down_sum(1).astype(bf16)
    d_copy = to_item(d_out, d_in, d_send.at[0], d_recv.at[0], 1)
    d_copy.start()

    def token_part(t, c):
        return lax.dot_general(
            gq_ref[t * tokens + c * tile : t * tokens + (c + 1) * tile, :], slab_ref[...], NT, preferred_element_type=f32
        )

    near_copies = {}
    far_copies = []

    def send_near(t, *which):
        for c in which:
            cs = pl.ds(c * tile, tile)
            near_out[t // 2, c * tile : (c + 1) * tile, :] = token_part(t, c).astype(bf16)
            copy = to_group(
                near_out.at[t // 2, cs], near_in.at[t // 2, cs], near_send.at[t // 2, c], near_recv.at[t // 2, c], 1
            )
            copy.start()
            near_copies[(t // 2, c)] = copy

    def send_far(c):
        cs = slice(c * tile, (c + 1) * tile)
        part = token_part(2, c)
        near_copies[(1, c)].wait_recv()
        far_out[cs, :] = (part.astype(bf16).astype(f32) + near_in[1, cs, :].astype(f32)).astype(bf16)
        copy = to_group(far_out.at[pl.ds(c * tile, tile)], far_in.at[pl.ds(c * tile, tile)], far_send.at[c], far_recv.at[c], 2)
        copy.start()
        far_copies.append(copy)

    send_near(3, 0)
    send_far(0)
    for copy in small_copies:
        copy.wait()
    small_mid[...] = small_ref[place] + small_in[1] + small_in[2] + small_in[3]
    small_x = to_item(small_mid, small_side, sx_send.at[0], sx_recv.at[0], 1)
    small_x.start()
    grads = 0.0
    for t in range(4):
        grads = grads + lax.dot_general(
            xs[t][...], gq_ref[t * tokens : (t + 1) * tokens, :], TN, preferred_element_type=f32
        )
    grad_v[...] = grads

    def sums(r, line):
        at = pl.multiple_of(r * tile, tile)
        return line + jnp.sum(gq_ref[pl.ds(at, tile), :].astype(f32), 0, keepdims=True)

    line = lax.fori_loop(0, 4 * chunks, sums, jnp.zeros((1, columns), f32))
    high = line.astype(bf16)
    rest = (line - high.astype(f32)).astype(bf16)
    which = lax.broadcasted_iota(jnp.int32, (16, columns), 0)
    lines = jnp.where(which == 0, high.astype(f32), jnp.where(which == 1, rest.astype(f32), 0.0)).astype(bf16)
    level = item // 2
    side = item % 2

    def slab_part(kz, kx):
        at = pl.multiple_of((2 * flip(level, kz) + (side + kx) % 2) * rows, 8)
        return grad_v[pl.ds(at, rows), :]

    side_copies = []
    for kz in range(levels - 1, -1, -1):
        side_out[kz, 0:rows, :] = slab_part(kz, 1).astype(bf16)
        side_out[kz, rows : rows + 16, :] = lines
        copy = to_item(side_out.at[kz], side_in.at[kz], side_send.at[kz], side_recv.at[kz], 1)
        copy.start()
        side_copies.append((kz, copy))

    send_near(3, 1)
    send_far(1)
    small_x.wait()
    small_both[...] = small_mid[...] + small_side[...]
    item_copies = [
        to_item(small_both, small_items.at[kz], si_send.at[kz], si_recv.at[kz], 2 * kz) for kz in range(1, levels)
    ]
    for copy in item_copies:
        copy.start()

    send_near(1, *range(chunks))
    for c in range(chunks):
        cs = slice(c * tile, (c + 1) * tile)
        din_ref[cs, :] = first_ref[cs, :] + token_part(0, c).astype(bf16).astype(f32)

    for copy in item_copies:
        copy.wait()
    small_sum[...] = small_both[...] + small_items[1] + small_items[2] + small_items[3]
    total_ref[place] = small_sum[...]
    total_copies = [to_group(small_sum, total_ref.at[place], st_send.at[t], st_recv.at[t], t) for t in range(1, 4)]
    for copy in total_copies:
        copy.start()

    def square_sum(values):
        return jnp.sum(jnp.sum(values * values, 0, keepdims=True), -1, keepdims=True)

    part_copies = []
    for kz, copy in side_copies:
        copy.wait()
        part = slab_part(kz, 0) + side_in[kz, 0:rows, :].astype(f32)
        both = lines.astype(f32) + side_in[kz, rows : rows + 16, :].astype(f32)
        if kz:
            part_out[kz, 0:rows, :] = part.astype(bf16)
            whole = jnp.sum(both, 0, keepdims=True)
            short = whole.astype(bf16).astype(f32)
            which_row = jnp.where(which == 0, short, jnp.where(which == 1, whole - short, 0.0))
            part_out[kz, rows : rows + 16, :] = which_row.astype(bf16)
            copy = to_item(part_out.at[kz], part_in.at[kz], part_send.at[kz], part_recv.at[kz], 2 * kz)
            copy.start()
            part_copies.append(copy)
        else:
            own_part, own_lines = part, both

    for copy in z_copies:
        copy.wait()

    up = uk_ref[0].astype(f32) + ur_ref[0].astype(f32)
    for kz in range(1, levels):
        up = up + z_in[kz].astype(f32)
    d_copy.wait()
    down = down_sum(0) + d_in[...].astype(f32)
    group_ref[0, 0:up_rows, :] = up.astype(bf16)
    group_ref[0, up_rows:, :] = down.astype(bf16)
    big_copies = [to_group(group_ref.at[0], group_ref.at[t], gr_send.at[t], gr_recv.at[t], t) for t in (2, 1)]
    for copy in big_copies:
        copy.start()
    squares = square_sum(up) + square_sum(down)
    for copy in part_copies:
        copy.wait()
    own, whole = own_part, jnp.sum(own_lines, 0, keepdims=True)
    for kz in range(1, levels):
        own = own + part_in[kz, 0:rows, :].astype(f32)
        whole = whole + jnp.sum(part_in[kz, rows : rows + 16, :].astype(f32), 0, keepdims=True)
    column = lax.broadcasted_iota(jnp.int32, (1, columns), 1)
    squares = squares + square_sum(own * jnp.where(column < query_columns, 1.0, HD**-0.5))
    sq_out[...] = jnp.broadcast_to(squares, (8, 128))
    sq_copies = [to_group(sq_out, sq_in.at[t], qg_send.at[t], qg_recv.at[t], t) for t in range(1, 4)]
    for copy in sq_copies:
        copy.start()
    short = whole.astype(bf16).astype(f32)
    sgroup_ref[0, 0:rows, :] = own.astype(bf16)
    sgroup_ref[0, rows : rows + 16, :] = jnp.where(which == 0, short, jnp.where(which == 1, whole - short, 0.0)).astype(bf16)
    group_copies = [to_group(sgroup_ref.at[0], sgroup_ref.at[t], sl_send.at[t], sl_recv.at[t], t) for t in (2, 1)]
    for copy in group_copies:
        copy.start()
    for copy in sq_copies:
        copy.wait()
    sq_mid[...] = sq_out[...] + sq_in[1] + sq_in[2] + sq_in[3]
    sq_item_copies = [to_item(sq_mid, sq_items.at[k], qi_send.at[k], qi_recv.at[k], k) for k in range(1, items)]
    for copy in sq_item_copies:
        copy.start()

    group_copies[0].wait()
    cross = to_group(sgroup_ref.at[2], sgroup_ref.at[3], sl_send.at[3], sl_recv.at[3], 1)
    cross.start()
    big_copies[0].wait()
    big_cross = to_group(group_ref.at[2], group_ref.at[3], gr_send.at[3], gr_recv.at[3], 1)
    big_cross.start()
    for t in range(1, 4):
        total_copies[t - 1].wait_send()
        to_group(small_sum, total_ref.at[flip(place, t)], st_send.at[t], st_recv.at[t], t).wait_recv()
    for c in range(chunks):
        cs = slice(c * tile, (c + 1) * tile)
        near_copies[(1, c)].wait_send()
        near_copies[(0, c)].wait()
        far_copies[c].wait()
        din_ref[cs, :] = din_ref[cs, :] + near_in[0, cs, :].astype(f32) + far_in[cs, :].astype(f32)
    for copy in sq_item_copies:
        copy.wait()
    answer = sq_mid[...]
    for k in range(1, items):
        answer = answer + sq_items[k]
    squares_ref[...] = answer
    group_copies[1].wait()
    cross.wait()
    big_copies[1].wait()
    big_cross.wait()


def tail(xs, gq, slab, first, small, shards, items, query_columns):
    tokens, width = xs[0].shape
    columns = gq.shape[1]
    rows = width // items
    vmem = pl.BlockSpec(memory_space=pltpu.VMEM)
    dma = pltpu.SemaphoreType.DMA
    chunks, levels = 2, items // 2
    up_rows = shards[0].shape[1]
    quarter = up_rows + rows
    slab_part = (levels, rows + 16, columns)
    return pl.pallas_call(
        functools.partial(tail_kernel, items, query_columns),
        out_shape=(
            jax.ShapeDtypeStruct((tokens, width), f32),
            jax.ShapeDtypeStruct((4, quarter, width), bf16),
            jax.ShapeDtypeStruct((4, rows + 16, columns), bf16),
            jax.ShapeDtypeStruct(small.shape, f32),
            jax.ShapeDtypeStruct((8, 128), f32),
        ),
        in_specs=[vmem] * 14,
        out_specs=(vmem,) * 5,
        scratch_shapes=[
            pltpu.VMEM((2, tokens, width), bf16),
            pltpu.VMEM((2, tokens, width), bf16),
            pltpu.VMEM((tokens, width), bf16),
            pltpu.VMEM((tokens, width), bf16),
            pltpu.VMEM((width, columns), f32),
            pltpu.VMEM(slab_part, bf16),
            pltpu.VMEM(slab_part, bf16),
            pltpu.VMEM(slab_part, bf16),
            pltpu.VMEM(slab_part, bf16),
            pltpu.VMEM((levels, up_rows, width), bf16),
            pltpu.VMEM((levels, up_rows, width), bf16),
            pltpu.VMEM((rows, width), bf16),
            pltpu.VMEM((rows, width), bf16),
            pltpu.VMEM((4, 8, width), f32),
            pltpu.VMEM((8, width), f32),
            pltpu.VMEM((8, width), f32),
            pltpu.VMEM((8, width), f32),
            pltpu.VMEM((levels, 8, width), f32),
            pltpu.VMEM((8, width), f32),
            pltpu.VMEM((8, 128), f32),
            pltpu.VMEM((4, 8, 128), f32),
            pltpu.VMEM((8, 128), f32),
            pltpu.VMEM((items, 8, 128), f32),
            dma((2, chunks)), dma((2, chunks)), dma((chunks,)), dma((chunks,)),
            dma((levels,)), dma((levels,)), dma((levels,)), dma((levels,)), dma((levels,)), dma((levels,)), dma((1,)), dma((1,)),
            dma((4,)), dma((4,)), dma((1,)), dma((1,)), dma((levels,)), dma((levels,)), dma((4,)), dma((4,)),
            dma((4,)), dma((4,)), dma((4,)), dma((4,)), dma((4,)), dma((4,)), dma((items,)), dma((items,)),
        ],
        compiler_params=pltpu.CompilerParams(vmem_limit_bytes=42 << 20, collective_id=3, has_side_effects=True),
        cost_estimate=pl.CostEstimate(flops=60 * 10**9, bytes_accessed=10**7, transcendentals=0),
        name="tail",
    )(*xs, gq, slab, first, small, *shards)


def update_kernel(place_of, heads, *refs):
    group_ref, sgroup_ref, total_ref, squares_ref, made_out, made_in = refs[:6]
    given, norm_ref, out_ref, din_ref, new = refs[6:21], refs[21], refs[22], refs[23], refs[24:39]
    held, grad_q, grad_s, out_v, din_v, in_sem, out_sem, made_sem = refs[39:54], *refs[54:]
    made = [
        pltpu.make_async_copy(made_out, out_v, made_sem.at[0]),
        pltpu.make_async_copy(made_in, din_v, made_sem.at[1]),
    ]
    order = (12, 13, 14, 3, 4, 5, 0, 1, 2, 6, 7, 8, 9, 10, 11)
    loads = {n: pltpu.make_async_copy(given[n], held[n], in_sem.at[n]) for n in order}
    for n in order:
        loads[n].start()
    for copy in made:
        copy.start()
    stores = []
    place = place_of()
    rows, width = held[3].shape
    third = rows // 3
    small_rows = held[12].shape[0]
    for row in range(small_rows):
        grad_s[row : row + 1, :] = total_ref[row // 3, row % 3 : row % 3 + 1, :]
    for q in range(4):
        t = flip(place, q)
        piece = sgroup_ref.at[t]
        for h in range(heads):
            at = (q * heads + h) * HD
            pair = h * 128
            value, key = (pair, pair + HD) if h % 2 == 0 else (pair + HD, pair)
            query = (heads + h // 2) * 128 + (HD if h % 2 == 0 else 0)
            for part, base, scale in ((0, query, HD**-0.5), (1, key, 1.0), (2, value, 1.0)):
                grad_q[:, part * width + at : part * width + at + HD] = piece[0:rows, base : base + HD].astype(f32) * scale
            for row, base, scale in ((2, query, HD**-0.5), (3, value, 1.0)):
                line = piece[rows : rows + 16, base : base + HD].astype(f32)
                grad_s[row : row + 1, at : at + HD] = (line[0:1] + line[1:2]) * scale
    small = grad_s[0:small_rows, :]
    squares = jnp.sum(jnp.sum(small * small, 0, keepdims=True), -1, keepdims=True) + squares_ref[0:1, 0:1]
    norm = jnp.sqrt(squares)
    norm_ref[...] = norm
    factor = jnp.minimum(1.0, clip_level / (norm + 1e-06))

    def apply(base, index, grad, decay, rate):
        w, f, s = held[base : base + 3]
        fresh = adam_update(w[index], f[index], s[index], grad * factor, decay, rate)
        w[index], f[index], s[index] = fresh

    def arrive(base):
        for n in range(base, base + 3):
            loads[n].wait()

    def leave(base):
        for n in range(base, base + 3):
            copy = pltpu.make_async_copy(held[n], new[n], out_sem.at[n])
            copy.start()
            stores.append(copy)

    everything = (slice(None), slice(None))
    arrive(12)
    apply(12, everything, small, 0.0, small_rate)
    leave(12)
    arrive(3)
    for q in range(3):
        os = (slice(q * third, (q + 1) * third), slice(None))
        apply(3, os, group_ref[flip(place, q), rows : rows + third, :].astype(f32), weight_decay, learn_rate)
    leave(3)
    arrive(0)
    for part in range(3):
        cs = slice(part * width, (part + 1) * width)
        apply(0, (slice(None), cs), grad_q[:, cs], weight_decay, learn_rate)
    leave(0)
    arrive(6)
    for q in range(4):
        cs = slice(q * width, (q + 1) * width)
        apply(6, (slice(None), cs), group_ref[flip(place, q), 0:rows, :].astype(f32), weight_decay, learn_rate)
    leave(6)
    for copy in made:
        copy.wait()
    made = [
        pltpu.make_async_copy(out_v, out_ref, made_sem.at[2]),
        pltpu.make_async_copy(din_v, din_ref, made_sem.at[3]),
    ]
    for copy in made:
        copy.start()
    arrive(9)
    for q in range(4):
        ds = (slice(q * rows, (q + 1) * rows), slice(None))
        apply(9, ds, group_ref[flip(place, q), rows + third :, :].astype(f32), weight_decay, learn_rate)
    leave(9)
    for copy in stores + made:
        copy.wait()


def update(place_of, heads, group, sgroup, total, squares, made, states):
    vmem = pl.BlockSpec(memory_space=pltpu.VMEM)
    anywhere = pl.BlockSpec(memory_space=pl.ANY)
    count = len(states)
    dma = pltpu.SemaphoreType.DMA
    return pl.pallas_call(
        functools.partial(update_kernel, place_of, heads),
        out_shape=(jax.ShapeDtypeStruct((1, 1), f32),)
        + tuple(jax.ShapeDtypeStruct(a.shape, a.dtype) for a in made)
        + tuple(jax.ShapeDtypeStruct(a.shape, f32) for a in states),
        in_specs=[vmem] * 4 + [anywhere] * (2 + count),
        out_specs=(vmem,) + (anywhere,) * (2 + count),
        scratch_shapes=[pltpu.VMEM(a.shape, f32) for a in states]
        + [pltpu.VMEM(states[0].shape, f32), pltpu.VMEM((16, total.shape[2]), f32)]
        + [pltpu.VMEM(a.shape, a.dtype) for a in made]
        + [dma((count,)), dma((count,)), dma((4,))],
        compiler_params=pltpu.CompilerParams(vmem_limit_bytes=60 << 20),
        cost_estimate=pl.CostEstimate(flops=10**9, bytes_accessed=25 * 10**6, transcendentals=0),
        name="update",
    )(group, sgroup, total, squares, *made, *states)


def line_place(z):
    return (z + 2) % 3 + (z // 3) * (3 - (z + 2) % 3)


def head_kernel(
    items, heads, x_ref, wq_ref, small_ref, wo_ref, wu_ref, wd_ref,
    near_out, far_out, cross_out, qkv_out, slab_out, line_ref, side_ref, wfar_ref,
    near_ref, far_ref, cross_ref, qkv_ref, slab_ref, piece_ref, bias_ref, raw_v, quarter_ref, pieces_v, x_send, x_recv, far_send, far_recv, cross_send, cross_recv,
    s_up_send, s_up_recv, s_down_send, s_down_recv, s_side_send, s_side_recv,
    w_up_send, w_up_recv, w_down_send, w_down_recv, w_side_send, w_side_recv, w_own, y_send, y_recv, keep_sem, raw_sem, qkv_sem,
):
    item, place = lax.axis_index("item"), lax.axis_index("seq")
    side, level = item % 2, item // 2
    levels = items // 2
    tokens = x_ref.shape[0]
    rows, width = wo_ref.shape
    third = rows // 3
    raws = (
        (wu_ref.at[:, pl.ds(pl.multiple_of(place * width, 128), width)], 0, rows),
        (wd_ref.at[pl.ds(pl.multiple_of(place * rows, 8), rows)], rows, rows),
        (wo_ref.at[pl.ds(pl.multiple_of((place - place // 3) * third, 8), third)], 2 * rows, third),
    )
    for n, (src, at, count) in enumerate(raws):
        pltpu.make_async_copy(src, raw_v.at[pl.ds(at, count)], raw_sem.at[n]).start()
    bias_ref[...] = jnp.zeros_like(bias_ref)
    piece_ref[...] = jnp.zeros_like(piece_ref)
    for g in range(4):

        @pl.when(place == g)
        def _():
            for h in range(heads):
                at = (g * heads + h) * HD
                pair = h * 128
                value, key = (pair, pair + HD) if h % 2 == 0 else (pair + HD, pair)
                query = (heads + h // 2) * 128 + (HD if h % 2 == 0 else 0)
                for part, base, scale in ((0, query, HD**-0.5), (1, key, 1.0), (2, value, 1.0)):
                    cut = wq_ref[:, part * width + at : part * width + at + HD]
                    piece_ref[:, base : base + HD] = (cut * scale).astype(bf16)
                bias_ref[:, query : query + HD] = small_ref[2:3, at : at + HD] * HD**-0.5
                bias_ref[:, value : value + HD] = small_ref[3:4, at : at + HD]

    tile = 256
    chunks = tokens // tile
    greet(item, place, items)

    def to_group(src, dst, send, recv, t):
        return pltpu.make_async_remote_copy(
            src_ref=src, dst_ref=dst, send_sem=send, recv_sem=recv,
            device_id=(item, flip(place, t)), device_id_type=MESH_ID,
        )

    class Flow:
        def __init__(self, slot, side_slot, other_slot, arrived, sems):
            self.slot, self.side_slot, self.other_slot, self.arrived = slot, side_slot, other_slot, arrived
            self.up_send, self.up_recv, self.down_send, self.down_recv, self.side_send, self.side_recv = sems

        def up(self, d):
            part = self.slot(-d)
            return pltpu.make_async_remote_copy(
                src_ref=part, dst_ref=part, send_sem=self.up_send.at[d], recv_sem=self.up_recv.at[d],
                device_id=(item + 2, place), device_id_type=MESH_ID,
            )

        def down(self, d):
            part = self.slot(d)
            return pltpu.make_async_remote_copy(
                src_ref=part, dst_ref=part, send_sem=self.down_send.at[d], recv_sem=self.down_recv.at[d],
                device_id=(item - 2, place), device_id_type=MESH_ID,
            )

        def across(self, d):
            part = self.slot(d)
            return pltpu.make_async_remote_copy(
                src_ref=part, dst_ref=self.side_slot(d), send_sem=self.side_send.at[level + d], recv_sem=self.side_recv.at[level + d],
                device_id=(item + 1 - 2 * side, place), device_id_type=MESH_ID,
            )

        def begin(self):
            @pl.when(level < levels - 1)
            def _():
                self.up(0).start()

            @pl.when(level > 0)
            def _():
                self.down(0).start()

            self.across(0).start()
            self.arrived(0)

        def step(self, d):
            @pl.when(level >= d)
            def _():
                part = self.slot(-d)
                pltpu.make_async_remote_copy(
                    src_ref=part, dst_ref=part, send_sem=self.up_send.at[d - 1], recv_sem=self.up_recv.at[d - 1],
                    device_id=(item + 1 - 2 * side, place), device_id_type=MESH_ID,
                ).wait_recv()

                @pl.when(level < levels - 1)
                def _():
                    self.up(d).start()

                self.across(-d).start()
                self.arrived(-d)

            @pl.when(level < levels - d)
            def _():
                part = self.slot(d)
                pltpu.make_async_remote_copy(
                    src_ref=part, dst_ref=part, send_sem=self.down_send.at[d - 1], recv_sem=self.down_recv.at[d - 1],
                    device_id=(item + 1 - 2 * side, place), device_id_type=MESH_ID,
                ).wait_recv()

                @pl.when(level > 0)
                def _():
                    self.down(d).start()

                self.across(d).start()
                self.arrived(d)

        def other_side(self):
            for z in range(levels):
                part = self.other_slot(z)
                pltpu.make_async_remote_copy(
                    src_ref=part, dst_ref=part, send_sem=self.side_send.at[z], recv_sem=self.side_recv.at[z],
                    device_id=(item + 1 - 2 * side, place), device_id_type=MESH_ID,
                ).wait_recv()

        def finish(self):
            for d in range(levels - 1):

                @pl.when((level >= d) & (level < levels - 1))
                def _():
                    self.up(d).wait_send()

                @pl.when((level < levels - d) & (level > 0))
                def _():
                    self.down(d).wait_send()

            for z in range(levels):
                part = self.slot(z - level)
                pltpu.make_async_remote_copy(
                    src_ref=part, dst_ref=part, send_sem=self.side_send.at[z], recv_sem=self.side_recv.at[z],
                    device_id=(item + 1 - 2 * side, place), device_id_type=MESH_ID,
                ).wait_send()

    def far_copy(z):
        at = line_place(z)
        return to_group(line_ref.at[at], wfar_ref.at[at], y_send.at[at], y_recv.at[at], 2)

    def to_far(z):
        @pl.when((z > 0) & (z < levels - 1))
        def _():
            far_copy(z).start()

    def piece_slot(d):
        return pieces_v.at[item + 2 * d]

    slab_flow = Flow(piece_slot, piece_slot, lambda z: pieces_v.at[2 * z + 1 - side], lambda d: None, (s_up_send, s_up_recv, s_down_send, s_down_recv, s_side_send, s_side_recv))
    w_flow = Flow(
        lambda d: line_ref.at[line_place(level + d)], lambda d: side_ref.at[line_place(level + d)],
        lambda z: side_ref.at[line_place(z)], lambda d: to_far(level + d), (w_up_send, w_up_recv, w_down_send, w_down_recv, w_side_send, w_side_recv))
    pieces_v[item] = piece_ref[...]
    slab_flow.begin()
    far_copies, near_copies, cross_copies = [], [], []
    for c in range(chunks):
        cs = pl.ds(c * tile, tile)
        far_copies.append(to_group(x_ref.at[cs], far_ref.at[cs], far_send.at[c], far_recv.at[c], 2))
        far_copies[-1].start()
    near_copies = [to_group(x_ref, near_ref, x_send.at[0], x_recv.at[0], 1)]
    near_copies[0].start()
    for n, (src, at, count) in enumerate(raws):
        pltpu.make_async_copy(src, raw_v.at[pl.ds(at, count)], raw_sem.at[n]).wait()
    quarter_ref[...] = raw_v[...].astype(bf16)
    own = pltpu.make_async_copy(quarter_ref, line_ref.at[line_place(level)], w_own.at[0])
    own.start()
    for d in range(1, levels):
        slab_flow.step(d)
    own.wait()
    w_flow.begin()
    slab_flow.other_side()
    for j in range(items):
        slab_ref[j * rows : (j + 1) * rows, :] = pieces_v[j]

    keeps = [pltpu.make_async_copy(slab_ref, slab_out, keep_sem.at[0])]
    keeps[0].start()

    def project_rows(src, t, c):
        part = jnp.dot(src[c * tile : (c + 1) * tile, :], slab_ref[...], preferred_element_type=f32)
        at = t * tokens + c * tile
        qkv_ref[at : at + tile, :] = (part + bias_ref[...]).astype(bf16)
        copy = pltpu.make_async_copy(qkv_ref.at[pl.ds(at, tile)], qkv_out.at[pl.ds(at, tile)], qkv_sem.at[t, c])
        copy.start()
        keeps.append(copy)

    def pass_on(c):
        cs = pl.ds(c * tile, tile)
        far_copies[c].wait_recv()
        copy = to_group(far_ref.at[cs], cross_ref.at[cs], cross_send.at[c], cross_recv.at[c], 1)
        copy.start()
        cross_copies.append(copy)

    for c in range(chunks):
        project_rows(x_ref, 0, c)
        pass_on(c)
        if c + 1 < levels:
            w_flow.step(c + 1)
        if c == 0:
            near_copies[0].wait_recv()
            keeps.append(pltpu.make_async_copy(near_ref, near_out, keep_sem.at[1]))
            keeps[-1].start()
        project_rows(near_ref, 1, c)
        project_rows(far_ref, 2, c)
        cross_copies[c].wait_recv()
        project_rows(cross_ref, 3, c)
    keeps.append(pltpu.make_async_copy(far_ref, far_out, keep_sem.at[2]))
    keeps.append(pltpu.make_async_copy(cross_ref, cross_out, keep_sem.at[3]))
    for copy in keeps[-2:]:
        copy.start()
    for d in range(chunks + 1, levels):
        w_flow.step(d)
    w_flow.other_side()
    near_copies[0].wait_send()
    for c in range(chunks):
        far_copies[c].wait_send()
        cross_copies[c].wait_send()
    for z in range(1, levels - 1):
        far_copy(z).wait()
    for copy in keeps:
        copy.wait()
    slab_flow.finish()
    w_flow.finish()


def head(x, wq, small, wo, wu, wd, items, heads):
    tokens, width = x.shape
    rows = wo.shape[0]
    columns = (heads + (heads + 1) // 2) * 128
    quarter = (2 * rows + rows // 3, width)
    vmem = pl.BlockSpec(memory_space=pltpu.VMEM)
    hbm = pl.BlockSpec(memory_space=pltpu.HBM)
    dma = pltpu.SemaphoreType.DMA
    chunks, levels = tokens // 256, items // 2
    tokens_shape = jax.ShapeDtypeStruct((tokens, width), bf16)
    return pl.pallas_call(
        functools.partial(head_kernel, items, heads),
        out_shape=(
            tokens_shape, tokens_shape, tokens_shape,
            jax.ShapeDtypeStruct((4 * tokens, columns), bf16),
            jax.ShapeDtypeStruct((rows * items, columns), bf16),
            jax.ShapeDtypeStruct((levels,) + quarter, bf16),
            jax.ShapeDtypeStruct((levels,) + quarter, bf16),
            jax.ShapeDtypeStruct((levels - 2,) + quarter, bf16),
        ),
        in_specs=[vmem] * 3 + [hbm] * 3,
        out_specs=(hbm,) * 8,
        scratch_shapes=[pltpu.VMEM((tokens, width), bf16)] * 3
        + [
            pltpu.VMEM((4 * tokens, columns), bf16),
            pltpu.VMEM((rows * items, columns), bf16),
            pltpu.VMEM((rows, columns), bf16),
            pltpu.VMEM((1, columns), f32),
            pltpu.VMEM(quarter, f32),
            pltpu.VMEM(quarter, bf16),
            pltpu.VMEM((items, rows, columns), bf16),
            dma((1,)), dma((1,)), dma((chunks,)), dma((chunks,)), dma((chunks,)), dma((chunks,)),
        ]
        + [dma((levels,))] * 12
        + [dma((1,)), dma((levels,)), dma((levels,)), dma((4,)), dma((3,)), dma((4, chunks))],
        compiler_params=pltpu.CompilerParams(vmem_limit_bytes=61 << 20, collective_id=1, has_side_effects=True),
        cost_estimate=pl.CostEstimate(flops=40 * 10**9, bytes_accessed=10**7, transcendentals=0),
        name="head",
    )(x, wq, small, wo, wu, wd)


def gelu_parts(u):
    half = 0.5 * (1.0 + lax.erf(u * 0.7071067811865476))
    return u * half, half + u * jnp.exp(-0.5 * u * u) * 0.3989422804014327


def middle_kernel(
    dims, line_ref, side_ref, fmid_ref, fends_ref, gmid_ref, gends_ref, x_ref, mix0_ref, mix1_ref, mix2_ref, mix3_ref, dout_ref, small_ref,
    out_ref, first_ref, gmix0_ref, gmix1_ref, gmix2_ref, gmix3_ref, ukeep_ref, usend_ref, dkeep_ref, dfar_ref, dsend_ref, sgrad_ref,
    wo_v, wu_v, wd_v, xhat_v, hid_v, act_v, slope_v, ffn_v, gffn_v, gup_v, rstd_v, stage_d, stage_u,
    got_u, got_d, got_o, mixn_v,
    wsem, wsend, wrecv, mix_send, mix_recv, usend, urecv, dsend, drecv, osend, orecv, flush, fsend, frecv,
):
    items, rows, width, tile = dims
    item, place = lax.axis_index("item"), lax.axis_index("seq")
    side, level = item % 2, item // 2
    core, far = place % 2, place // 2
    third = rows // 3
    tokens = x_ref.shape[0]
    tiles = tokens // tile
    near = (item, flip(place, 1))
    barrier = pltpu.get_barrier_semaphore()
    across = (item, flip(place, 2))
    for device in (near, across):
        pl.semaphore_signal(barrier, inc=1, device_id=device, device_id_type=MESH_ID)
    pl.semaphore_wait(barrier, 2)

    def remote(src, dst, send, recv):
        return pltpu.make_async_remote_copy(
            src_ref=src, dst_ref=dst, send_sem=send, recv_sem=recv, device_id=near, device_id_type=MESH_ID
        )

    mix_copy = remote(mix1_ref, mixn_v, mix_send.at[0], mix_recv.at[0])
    mix_copy.start()

    def load(which):
        for t in (0, 2):
            q = flip(place, t)
            for n in range(items):
                z, kx = n // 2, n % 2
                j = 2 * z + (side + kx) % 2
                at = line_place(z)
                if t == 0:
                    src = (line_ref, side_ref)[kx].at[at]
                elif at < items // 2 - 2:
                    src = (fmid_ref, gmid_ref)[kx].at[at]
                else:
                    src = (fends_ref, gends_ref)[kx].at[at - (items // 2 - 2)]
                if which == 0:
                    src = src.at[pl.ds(2 * rows, third)]
                    dst = wo_v.at[j, pl.ds(pl.multiple_of(q * third, 16), third)]
                elif which == 1:
                    src = src.at[pl.ds(0, rows)]
                    dst = wu_v.at[q, pl.ds(pl.multiple_of(j * rows, 16), rows)]
                else:
                    src = src.at[pl.ds(rows, rows)]
                    dst = wd_v.at[j // 2, pl.ds(pl.multiple_of((j % 2) * 4 * rows + q * rows, 16), rows)]
                remote(src, dst, wsend.at[which], wrecv.at[which]).start()
                pltpu.make_async_copy(src, dst, wsem.at[which]).start()

    for which in range(3):
        load(which)

    def loaded(which):
        half = (wo_v.at[pl.ds(0, items // 2)], wu_v.at[pl.ds(0, 2)], wd_v.at[pl.ds(0, 2)])[which]
        pltpu.make_async_copy(half, half, wsem.at[which]).wait()
        remote(half, half, wsend.at[which], wrecv.at[which]).wait_recv()

    def rowsl(r):
        return pl.ds(pl.multiple_of(r * tile, tile), tile)

    def wo_rows(q):
        return jnp.concatenate([wo_v[2 * q, 0:rows], wo_v[2 * q + 1, 0:rows]], 0)

    mixes = (mix0_ref, mixn_v, mix2_ref, mix3_ref)
    gmixes = (gmix0_ref, gmix1_ref, gmix2_ref, gmix3_ref)
    mix_copy.wait_recv()
    loaded(0)

    def norm_one(r, _):
        rs = rowsl(r)
        total = x_ref[rs, :].astype(f32) + small_ref[4:5, :]
        for t in range(4):
            total += jnp.dot(mixes[t][rs, :], wo_rows(flip(place, t)), preferred_element_type=f32)
        centered = total - jnp.mean(total, -1, keepdims=True)
        rstd = lax.rsqrt(jnp.mean(centered * centered, -1, keepdims=True) + norm_epsilon)
        xhat = centered * rstd
        xhat_v[rs, :] = xhat
        rstd_v[rs, :] = jnp.broadcast_to(rstd, (tile, 128))
        hid_v[rs, :] = (xhat * small_ref[0:1, :] + small_ref[1:2, :]).astype(bf16)
        return 0

    lax.fori_loop(0, tiles, norm_one, 0)
    loaded(1)
    loaded(2)

    def ffn(n, _):
        p, r = n // tiles, n % tiles
        rs = rowsl(r)
        up = jnp.dot(hid_v[rs, :], wu_v[p], preferred_element_type=f32) + small_ref[pl.ds(8 + p, 1), :]
        act, slope = gelu_parts(up)
        act = act.astype(bf16)
        act_v[p, rs, :] = act
        slope_v[p, rs, :] = slope
        part = jnp.dot(act, wd_v[p], preferred_element_type=f32)

        @pl.when(p == 0)
        def _():
            ffn_v[rs, :] = part

        @pl.when(p > 0)
        def _():
            ffn_v[rs, :] += part

        return 0

    lax.fori_loop(0, 4 * tiles, ffn, 0)
    zero = jnp.zeros((1, width), f32)

    def norm_two(r, sums):
        rs = rowsl(r)
        dg, db, dd = sums
        hidden = xhat_v[rs, :] * small_ref[0:1, :] + small_ref[1:2, :]
        total = hidden + (ffn_v[rs, :] + small_ref[7:8, :])
        centered = total - jnp.mean(total, -1, keepdims=True)
        rstd = lax.rsqrt(jnp.mean(centered * centered, -1, keepdims=True) + norm_epsilon)
        xhat = centered * rstd
        out_ref[rs, :] = (xhat * small_ref[5:6, :] + small_ref[6:7, :]).astype(bf16)
        dy = dout_ref[rs, :].astype(f32)
        dg = dg + jnp.sum(dy * xhat, 0, keepdims=True)
        db = db + jnp.sum(dy, 0, keepdims=True)
        dx = dy * small_ref[5:6, :]
        dx = rstd * (dx - jnp.mean(dx, -1, keepdims=True) - xhat * jnp.mean(dx * xhat, -1, keepdims=True))
        ffn_v[rs, :] = dx
        short = dx.astype(bf16)
        gffn_v[rs, :] = short
        dd = dd + jnp.sum(short.astype(f32), 0, keepdims=True)
        return dg, db, dd

    dg2, db2, dd = lax.fori_loop(0, tiles, norm_two, (zero, zero, zero))
    sgrad_ref[...] = jnp.zeros_like(sgrad_ref)
    sgrad_ref[1, 2:3, :] = dg2
    sgrad_ref[2, 0:1, :] = db2
    sgrad_ref[2, 1:2, :] = dd
    nt = (((1,), (1,)), ((), ()))
    tn = (((0,), (0,)), ((), ()))
    pieces = width // tile

    def spread(src, yrel, row, count, sem):
        for n in range(items):
            z, kx = n // 2, n % 2
            j = 2 * z + (side + kx) % 2
            dst = (ukeep_ref, usend_ref)[kx].at[yrel, flip(level, z), pl.ds(row, count)]
            pltpu.make_async_copy(src(j), dst, sem).start()

    def chunk_at(n):
        return blend(level, 3 - n)

    def finish_chunk(n, par):
        p = chunk_at(n)
        remote(got_d.at[p], got_d.at[p], dsend.at[p], drecv.at[p]).wait_recv()
        for jj in range(2):
            for yy in range(2):
                at = pl.multiple_of((4 * jj + 2 * yy + core) * rows, 16)
                got_d[p, jj, yy] = stage_d[par, pl.ds(at, rows), :] + got_d[p, jj, yy]

        kz = 3 - n
        for jj in range(2):
            kx = (jj + side) % 2
            for yy in range(2):

                @pl.when(far == yy)
                def _():
                    pltpu.make_async_copy(got_d.at[p, jj, yy], dkeep_ref.at[kz, kx], flush.at[0]).start()

                    @pl.when(n < 2)
                    def _():
                        pltpu.make_async_remote_copy(
                            src_ref=got_d.at[p, jj, 1 - yy], dst_ref=dfar_ref.at[n, kx],
                            send_sem=fsend.at[n], recv_sem=frecv.at[n], device_id=across, device_id_type=MESH_ID,
                        ).start()

                    @pl.when(n >= 2)
                    def _():
                        pltpu.make_async_copy(got_d.at[p, jj, 1 - yy], dsend_ref.at[n - 2, kx], flush.at[3]).start()

        half = p // 2

        @pl.when(p % 2 == core)
        def _():
            remote(got_u.at[half], got_u.at[half], usend.at[half], urecv.at[half]).wait_recv()
            for m in range(tiles):
                ms = slice(m * tile, (m + 1) * tile)
                got_u[half, ms, :] = stage_u[par, ms, :] + got_u[half, ms, :]
            spread(
                lambda j: got_u.at[half, pl.ds(pl.multiple_of(j * rows, 16), rows)],
                (half + far) % 2, 0, rows, flush.at[1],
            )

    def back(n, _):
        par = n % 2
        p = chunk_at(n)

        def back_rows(r, total):
            rs = rowsl(r)
            ga = lax.dot_general(gffn_v[rs, :], wd_v[p], nt, preferred_element_type=f32)
            gup = (ga * slope_v[p, rs, :]).astype(bf16)
            gup_v[rs, :] = gup
            ffn_v[rs, :] += lax.dot_general(gup, wu_v[p], nt, preferred_element_type=f32)
            return total + jnp.sum(gup.astype(f32), 0, keepdims=True)

        sgrad_ref[(8 + p) // 3, pl.ds((8 + p) % 3, 1), :] = lax.fori_loop(0, tiles, back_rows, zero)

        @pl.when(n >= 2)
        def _():
            before = chunk_at(n - 2)
            remote(got_d.at[before], got_d.at[before], dsend.at[before], drecv.at[before]).wait_send()

            @pl.when(p % 2 != core)
            def _():
                half = before // 2
                remote(got_u.at[half], got_u.at[half], usend.at[half], urecv.at[half]).wait_send()

        for m in range(pieces):
            cs = slice(m * tile, (m + 1) * tile)
            stage_d[par, cs, :] = lax.dot_general(act_v[p, :, cs], gffn_v[...], tn, preferred_element_type=f32).astype(bf16)
        for jj in range(2):
            for yy in range(2):
                at = pl.multiple_of((4 * jj + 2 * yy + 1 - core) * rows, 16)
                remote(stage_d.at[par, pl.ds(at, rows)], got_d.at[p, jj, yy], dsend.at[p], drecv.at[p]).start()
        for m in range(pieces):
            cs = slice(m * tile, (m + 1) * tile)
            stage_u[par, cs, :] = lax.dot_general(hid_v[:, cs], gup_v[...], tn, preferred_element_type=f32).astype(bf16)

        @pl.when(p % 2 != core)
        def _():
            remote(stage_u.at[par], got_u.at[p // 2], usend.at[p // 2], urecv.at[p // 2]).start()

        @pl.when(n > 0)
        def _():
            finish_chunk(n - 1, 1 - par)

        return 0

    lax.fori_loop(0, 4, back, 0)
    finish_chunk(3, 1)

    def norm_back(r, sums):
        rs = rowsl(r)
        dg, db, da = sums
        dy = ffn_v[rs, :]
        xhat = xhat_v[rs, :]
        dg = dg + jnp.sum(dy * xhat, 0, keepdims=True)
        db = db + jnp.sum(dy, 0, keepdims=True)
        dx = dy * small_ref[0:1, :]
        dx = rstd_v[rs, 0:1] * (dx - jnp.mean(dx, -1, keepdims=True) - xhat * jnp.mean(dx * xhat, -1, keepdims=True))
        first_ref[rs, :] = dx
        short = dx.astype(bf16)
        hid_v[rs, :] = short
        da = da + jnp.sum(short.astype(f32), 0, keepdims=True)
        for t in range(4):
            gmixes[t][rs, :] = lax.dot_general(
                short, wo_rows(flip(place, t)), nt, preferred_element_type=f32
            ).astype(bf16)
        return dg, db, da

    dg1, db1, da = lax.fori_loop(0, tiles, norm_back, (zero, zero, zero))
    sgrad_ref[0, 0:1, :] = dg1
    sgrad_ref[0, 1:2, :] = db1
    sgrad_ref[1, 1:2, :] = da
    for j in range(items):
        wo_v[j, pl.ds(rows, third)] = jnp.zeros((third, width), bf16)
    for t in range(4):
        q = flip(place, t)
        part = lax.dot_general(mixes[t][...], hid_v[...], tn, preferred_element_type=f32).astype(bf16)
        wo_v[2 * q, pl.ds(0, rows)] = part[:rows]
        wo_v[2 * q + 1, pl.ds(0, rows)] = part[rows:]
    o_copies = []
    for yy in range(2):
        at = pl.multiple_of((2 * yy + 1 - core) * third, 16)
        copy = remote(wo_v.at[:, pl.ds(at, third)], got_o.at[yy], osend.at[yy], orecv.at[yy])
        copy.start()
        o_copies.append(copy)
    for yy in range(2):
        o_copies[yy].wait_recv()
        at = pl.multiple_of((2 * yy + core) * third, 16)
        for j in range(items):
            got_o[yy, j] = wo_v[j, pl.ds(at, third)] + got_o[yy, j]
        spread(lambda j: got_o.at[yy, j], (yy + far) % 2, rows, third, flush.at[2])

    mix_copy.wait_send()
    for which in range(3):
        half = (wo_v.at[pl.ds(0, items // 2)], wu_v.at[pl.ds(0, 2)], wd_v.at[pl.ds(0, 2)])[which]
        remote(half, half, wsend.at[which], wrecv.at[which]).wait_send()
    for n in (2, 3):
        p = chunk_at(n)
        remote(got_d.at[p], got_d.at[p], dsend.at[p], drecv.at[p]).wait_send()

        @pl.when(p % 2 != core)
        def _():
            remote(got_u.at[p // 2], got_u.at[p // 2], usend.at[p // 2], urecv.at[p // 2]).wait_send()

    for yy in range(2):
        o_copies[yy].wait_send()
    pltpu.make_async_copy(dkeep_ref, dkeep_ref, flush.at[0]).wait()
    pltpu.make_async_copy(dsend_ref, dsend_ref, flush.at[3]).wait()
    for n in range(2):
        sent = dfar_ref.at[n]
        copy = pltpu.make_async_remote_copy(
            src_ref=sent, dst_ref=sent, send_sem=fsend.at[n], recv_sem=frecv.at[n],
            device_id=across, device_id_type=MESH_ID,
        )
        copy.wait_send()
        copy.wait_recv()
    pltpu.make_async_copy(got_u, got_u, flush.at[1]).wait()
    pltpu.make_async_copy(got_o, got_o, flush.at[2]).wait()


def middle(weights, x, mixes, dout, small, tile=768):
    levels, quarter, width = weights[0].shape
    items = 2 * levels
    rows = quarter * 3 // 7
    third = rows // 3
    tokens = x.shape[0]
    any_space = pl.BlockSpec(memory_space=pltpu.HBM)
    vmem = pl.BlockSpec(memory_space=pltpu.VMEM)
    square = (tokens, width)
    dma = pltpu.SemaphoreType.DMA
    head_part = jax.ShapeDtypeStruct((tokens, width // 4), bf16)
    u_shape = jax.ShapeDtypeStruct((2, levels, rows + third, width), bf16)
    d_half = jax.ShapeDtypeStruct((2, 2, rows, width), bf16)
    d_shape = jax.ShapeDtypeStruct((levels, 2, rows, width), bf16)
    return pl.pallas_call(
        functools.partial(middle_kernel, (items, rows, width, tile)),
        out_shape=(
            jax.ShapeDtypeStruct(square, bf16),
            jax.ShapeDtypeStruct(square, f32),
            head_part, head_part, head_part, head_part,
            u_shape, u_shape, d_shape, d_half, d_half,
            jax.ShapeDtypeStruct((4, 8, width), f32),
        ),
        in_specs=[any_space] * 6 + [vmem] * 7,
        out_specs=(vmem,) * 6 + (any_space,) * 5 + (vmem,),
        scratch_shapes=[
            pltpu.VMEM((items, 4 * third, width), bf16),
            pltpu.VMEM((4, width, width), bf16),
            pltpu.VMEM((4, width, width), bf16),
            pltpu.VMEM(square, f32),
            pltpu.VMEM(square, bf16),
            pltpu.VMEM((4, tokens, width), bf16),
            pltpu.VMEM((4, tokens, width), f32),
            pltpu.VMEM(square, f32),
            pltpu.VMEM(square, bf16),
            pltpu.VMEM(square, bf16),
            pltpu.VMEM((tokens, 128), f32),
            pltpu.VMEM((2, width, width), bf16),
            pltpu.VMEM((2, width, width), bf16),
            pltpu.VMEM((2, width, width), bf16),
            pltpu.VMEM((4, 2, 2, rows, width), bf16),
            pltpu.VMEM((2, items, third, width), bf16),
            pltpu.VMEM((tokens, width // 4), bf16),
            dma((3,)), dma((3,)), dma((3,)), dma((1,)), dma((1,)), dma((2,)), dma((2,)), dma((4,)), dma((4,)),
            dma((2,)), dma((2,)), dma((4,)), dma((2,)), dma((2,)),
        ],
        compiler_params=pltpu.CompilerParams(vmem_limit_bytes=61 << 20, collective_id=2, has_side_effects=True),
        cost_estimate=pl.CostEstimate(flops=60 * 10**9, bytes_accessed=10**7, transcendentals=0),
        name="middle",
    )(*weights, x, *mixes, dout, small)


def swap(values, axis, bit):
    size = lax.axis_size(axis)
    return lax.ppermute(values, axis, [(i, i ^ bit) for i in range(size)])


def take(values, at, dim):
    return lax.dynamic_index_in_dim(values, at, dim, keepdims=False)


def add_short(a, b):
    return (a.astype(f32) + b.astype(f32)).astype(bf16)


def layer_norm(values, gain, bias):
    average = jnp.mean(values, -1, keepdims=True)
    centered = values - average
    spread = jnp.mean(centered * centered, -1, keepdims=True)
    return centered * lax.rsqrt(spread + norm_epsilon) * gain + bias


def exact_gelu(values):
    return jax.nn.gelu(values, approximate=False)


def packed_columns(own):
    heads = own.shape[2]
    cols = []
    for h in range(heads):
        pair = [own[:, 2, h], own[:, 1, h]]
        cols += pair if h % 2 == 0 else pair[::-1]
    for p in range((heads + 1) // 2):
        odd = own[:, 0, 2 * p + 1] if 2 * p + 1 < heads else jnp.zeros_like(own[:, 0, 0])
        cols += [odd * HD**-0.5, own[:, 0, 2 * p] * HD**-0.5]
    return jnp.concatenate(cols, -1)


def natural_columns(values, heads):
    parts = [[], [], []]
    for h in range(heads):
        first, second = values[:, h * 128 : h * 128 + HD], values[:, h * 128 + HD : h * 128 + 128]
        base = (heads + h // 2) * 128
        if h % 2 == 0:
            parts[2].append(first)
            parts[1].append(second)
            parts[0].append(values[:, base + HD : base + 128] * HD**-0.5)
        else:
            parts[1].append(first)
            parts[2].append(second)
            parts[0].append(values[:, base : base + HD] * HD**-0.5)
    return jnp.concatenate(parts[0] + parts[1] + parts[2], -1)


def on_device(
    inputs,
    d_output,
    glob_count,
    glob_pos,
    rand_blocks,
    w_qkv,
    w_out,
    w_up,
    w_down,
    small_params,
    first_qkv,
    second_qkv,
    first_out,
    second_out,
    first_up,
    second_up,
    first_down,
    second_down,
    first_small,
    second_small,
):
    _, tok_rows, width = inputs.shape
    items = lax.axis_size("item")
    place = lax.axis_index("seq")
    heads = rand_blocks.shape[1]

    tokens_b = inputs.reshape(tok_rows, width)
    *others, qkv, slab, w_line, w_side, w_far = head(
        tokens_b, w_qkv, small_params, w_out, w_up, w_down, items, heads
    )
    xs = [tokens_b, *others]
    w_far_ends = swap(w_line[2:], "seq", 2)
    w_side_mid = swap(w_far, "item", 1)
    idx, bias, gl = slots(glob_count[0], glob_pos[0], rand_blocks[0], place)
    mix2, mix3, lse_far = attn_fwd(idx, gl, qkv, bias, heads, 2, 2)
    w_far_ends, w_side_mid, mix2, mix3, qkv = lax.optimization_barrier((w_far_ends, w_side_mid, mix2, mix3, qkv))
    mix2_in, mix3_in = swap(mix2, "seq", 2), swap(mix3, "seq", 3)
    w_side_ends = swap(w_far_ends, "item", 1)
    mix0, mix1, lse_near = attn_fwd(idx, gl, qkv, bias, heads, 0, 2)
    w_side_ends, mix0, mix1, mix2_in, mix3_in = lax.optimization_barrier((w_side_ends, mix0, mix1, mix2_in, mix3_in))
    outputs, grad_first, *grad_mixed, u_keep, u_send, d_keep, d_far, d_send, small_part = middle(
        (w_line, w_side, w_far, w_far_ends, w_side_mid, w_side_ends), tokens_b, (mix0, mix1, mix2_in, mix3_in), d_output.reshape(tok_rows, width), small_params
    )
    grads_in = [grad_mixed[0]] + [swap(grad_mixed[t], "seq", t) for t in range(1, 4)]
    u_in = swap(u_send, "item", 1)
    d_in = swap(d_send, "seq", 2)
    d_next = [swap(add_short(d_keep[3 - n], d_far[n]), "item", 2 * (3 - n)) for n in range(2)]
    acc, dq_near = attn_bwd(idx, gl, qkv, bias, grads_in[:2], lse_near, heads, 0, (), False)
    u_in, d_in, d_next, acc, dq_near = lax.optimization_barrier((u_in, d_in, d_next, acc, dq_near))
    u_next = swap(add_short(u_keep[1], u_in[1]), "seq", 2)
    d_last = swap(add_short(d_keep[1], d_in[0]), "item", 2)
    u_here = add_short(u_keep[0], u_in[0])
    d_here = add_short(d_keep[0], d_in[1])
    grad_qkv = attn_bwd(idx, gl, qkv, bias, grads_in[2:], lse_far, heads, 2, (acc, dq_near), True)
    d_last, u_next, grad_qkv = lax.optimization_barrier((d_last, u_next, grad_qkv))
    grad_inputs, group, slab_group, small_total, squares = tail(
        xs, grad_qkv, slab, grad_first, small_part, (u_here, u_next, d_here, d_last, *d_next), items, heads * 128
    )
    norm, outputs, grad_inputs, *states = update(
        lambda: lax.axis_index("seq"),
        heads,
        group,
        slab_group,
        small_total,
        squares,
        (outputs, grad_inputs),
        (
            w_qkv, first_qkv, second_qkv, w_out, first_out, second_out, w_up, first_up, second_up,
            w_down, first_down, second_down, small_params, first_small, second_small,
        ),
    )
    return (outputs[None], grad_inputs[None], norm.reshape(()), *states)


def on_device_many(
    inputs,
    d_output,
    glob_count,
    glob_pos,
    rand_blocks,
    w_qkv,
    w_out,
    w_up,
    w_down,
    small_params,
    first_qkv,
    second_qkv,
    first_out,
    second_out,
    first_up,
    second_up,
    first_down,
    second_down,
    first_small,
    second_small,
):
    items_n, tok_rows, width = inputs.shape
    groups = lax.axis_size("seq")
    place = lax.axis_index("seq")
    heads = rand_blocks.shape[1]
    row_count = tok_rows

    own = lax.dynamic_index_in_dim(
        w_qkv.reshape(-1, 3, groups, heads, HD), place, 2, keepdims=False
    )
    slab = lax.all_gather(packed_columns(own).astype(bf16), "item", axis=0, tiled=True)
    full_out, full_up, full_down = (
        lax.all_gather(w_out.astype(bf16), "item", axis=0, tiled=True),
        lax.all_gather(w_up.astype(bf16), "item", axis=0, tiled=True),
        lax.all_gather(w_down.astype(bf16), "item", axis=0, tiled=True),
    )
    bias3 = jnp.stack([small_params[2], jnp.zeros((width,), f32), small_params[3]])
    own_bias = lax.dynamic_index_in_dim(
        bias3.reshape(1, 3, groups, heads, HD), place, 2, keepdims=False
    )
    slab_bias = packed_columns(own_bias)
    tokens_b = inputs.reshape(tok_rows, width)
    tokens_all = lax.all_gather(tokens_b, "seq", axis=0, tiled=True)
    tokens_f = tokens_b.astype(f32)
    qkv = (jnp.dot(tokens_all, slab, preferred_element_type=f32) + slab_bias).astype(bf16)
    idx, bias, gl = slots(glob_count[0], glob_pos[0], rand_blocks[0], jnp.int32(0))
    *mixed_parts, lse = attn_fwd(idx, gl, qkv, bias, heads, 0, 4)
    mixed_heads = jnp.concatenate(mixed_parts, 0)
    mixed = lax.all_to_all(mixed_heads, "seq", split_axis=0, concat_axis=1, tiled=True)
    attn_out = jnp.dot(mixed, full_out, preferred_element_type=f32) + small_params[4]
    hidden, norm_one_back = jax.vjp(
        layer_norm, tokens_f + attn_out, small_params[0], small_params[1]
    )
    hidden_b = hidden.astype(bf16)
    up_pre = jnp.dot(hidden_b, full_up, preferred_element_type=f32) + small_params[8:12].reshape(-1)
    active, gelu_back = jax.vjp(exact_gelu, up_pre)
    active_b = active.astype(bf16)
    ffn_out = jnp.dot(active_b, full_down, preferred_element_type=f32) + small_params[7]
    outputs, norm_two_back = jax.vjp(layer_norm, hidden + ffn_out, small_params[5], small_params[6])
    grad_second, grad_gain_two, grad_bias_two = norm_two_back(
        d_output.reshape(row_count, width).astype(f32)
    )
    grad_ffn = grad_second.astype(bf16)
    grad_w_down = jnp.einsum("rf,rd->fd", active_b, grad_ffn, preferred_element_type=f32)
    grad_active = jnp.einsum("rd,fd->rf", grad_ffn, full_down, preferred_element_type=f32)
    (grad_up_pre,) = gelu_back(grad_active)
    grad_up_b = grad_up_pre.astype(bf16)
    grad_w_up = jnp.einsum("rd,rf->df", hidden_b, grad_up_b, preferred_element_type=f32)
    grad_hidden = grad_second + jnp.einsum(
        "rf,df->rd", grad_up_b, full_up, preferred_element_type=f32
    )
    grad_first, grad_gain_one, grad_bias_one = norm_one_back(grad_hidden)
    grad_attn = grad_first.astype(bf16)
    grad_w_out = jnp.einsum("rm,rd->md", mixed, grad_attn, preferred_element_type=f32)
    grad_mixed = jnp.einsum("rd,md->rm", grad_attn, full_out, preferred_element_type=f32).astype(
        bf16
    )
    grad_heads = lax.all_to_all(grad_mixed, "seq", split_axis=1, concat_axis=0, tiled=True)
    grads_in = [grad_heads[t * tok_rows : (t + 1) * tok_rows] for t in range(4)]
    grad_qkv = attn_bwd(idx, gl, qkv, bias, grads_in, lse, heads, 0, (), True)
    grad_slab = jnp.einsum("rd,re->de", tokens_all, grad_qkv, preferred_element_type=f32)
    grad_tokens = jnp.einsum("re,de->rd", grad_qkv, slab, preferred_element_type=f32).astype(bf16)
    grad_inputs = grad_first + lax.psum_scatter(
        grad_tokens, "seq", scatter_dimension=0, tiled=True
    ).astype(f32)
    slab_sum = natural_columns(jnp.sum(grad_qkv.astype(f32), 0)[None], heads)[0]
    bias_grads = lax.dynamic_update_index_in_dim(
        jnp.zeros((3, groups, heads * HD), f32), slab_sum.reshape(3, heads * HD), place, 1
    ).reshape(3, width)
    small_rows = jnp.stack(
        [
            grad_gain_one,
            grad_bias_one,
            bias_grads[0],
            bias_grads[2],
            jnp.sum(grad_attn.astype(f32), 0),
            grad_gain_two,
            grad_bias_two,
            jnp.sum(grad_ffn.astype(f32), 0),
        ]
    )
    small_part = jnp.concatenate(
        [small_rows, jnp.sum(grad_up_b.astype(f32), 0).reshape(4, width)], 0
    )
    small_total = lax.psum(small_part, ("item", "seq"))
    shard_down = lax.psum_scatter(grad_w_down.astype(bf16), "item", scatter_dimension=0, tiled=True)
    shard_up = lax.psum_scatter(grad_w_up.astype(bf16), "item", scatter_dimension=0, tiled=True)
    shard_out = lax.psum_scatter(grad_w_out.astype(bf16), "item", scatter_dimension=0, tiled=True)
    shard_slab = lax.psum_scatter(grad_slab.astype(bf16), "item", scatter_dimension=0, tiled=True)
    shard_slab = natural_columns(shard_slab.astype(f32), heads).reshape(-1, 3, 1, heads * HD)
    shard_qkv = lax.all_gather(shard_slab, "seq", axis=2, tiled=True).reshape(-1, 3 * width)
    shard_out, shard_up, shard_down = lax.psum(
        (shard_out.astype(f32), shard_up.astype(f32), shard_down.astype(f32)), "seq"
    )
    local_squares = (
        jnp.sum(shard_qkv * shard_qkv)
        + jnp.sum(shard_out * shard_out)
        + jnp.sum(shard_up * shard_up)
        + jnp.sum(shard_down * shard_down)
    )
    matrix_squares = lax.psum(local_squares, "item")
    grad_norm = jnp.sqrt(matrix_squares + jnp.sum(small_total * small_total))
    factor = jnp.minimum(1.0, clip_level / (grad_norm + 1e-06))
    new_qkv = adam_update(
        w_qkv, first_qkv, second_qkv, shard_qkv * factor, weight_decay, learn_rate
    )
    new_out = adam_update(
        w_out, first_out, second_out, shard_out * factor, weight_decay, learn_rate
    )
    new_up = adam_update(w_up, first_up, second_up, shard_up * factor, weight_decay, learn_rate)
    new_down = adam_update(
        w_down, first_down, second_down, shard_down * factor, weight_decay, learn_rate
    )
    new_small = adam_update(
        small_params, first_small, second_small, small_total * factor, 0.0, small_rate
    )
    return (
        outputs.astype(bf16).reshape(items_n, tok_rows, width),
        grad_inputs.reshape(items_n, tok_rows, width),
        grad_norm,
        new_qkv[0],
        new_qkv[1],
        new_qkv[2],
        new_out[0],
        new_out[1],
        new_out[2],
        new_up[0],
        new_up[1],
        new_up[2],
        new_down[0],
        new_down[1],
        new_down[2],
        new_small[0],
        new_small[1],
        new_small[2],
    )


def solution(mesh):
    few = mesh.shape["item"] == 8 and mesh.shape["seq"] == 4
    return jax.shard_map(
        on_device if few else on_device_many,
        mesh=mesh,
        in_specs=(
            P("item", "seq", None),
            P("item", "seq", None),
            P("item"),
            P("item", None),
            P("item", "seq", None, None),
            P("item", None),
            P("item", None),
            P("item", None),
            P("item", None),
            P(),
            P("item", None),
            P("item", None),
            P("item", None),
            P("item", None),
            P("item", None),
            P("item", None),
            P("item", None),
            P("item", None),
            P(),
            P(),
        ),
        out_specs=(
            P("item", "seq", None),
            P("item", "seq", None),
            P(),
            P("item", None),
            P("item", None),
            P("item", None),
            P("item", None),
            P("item", None),
            P("item", None),
            P("item", None),
            P("item", None),
            P("item", None),
            P("item", None),
            P("item", None),
            P("item", None),
            P(),
            P(),
            P(),
        ),
        check_vma=False,
    )
```
